32 devices in a mesh: dp: 16 (over z, y, core), mp: 2 (over x).
Axes of the slice: x: 2, y: 2, z: 4, core: 2. Of those that a mesh axis runs over, the one named last changes fastest.
Arguments:
- residual_in: bfloat16 [8192, 1024], P(('dp', 'mp')), may hold values from -6 to 6
- cotangent: bfloat16 [8192, 1024], P(('dp', 'mp')), may hold values from -6 to 6
- ln_gain: float32 [1024], replicated, may hold values from 0.5 to 1.5
- ln_bias: float32 [1024], replicated, may hold values from -3 to 3
- w_qkv: bfloat16 [3, 1024, 1024], P(None, 'dp', 'mp'), may hold values from -0.1875 to 0.1875
- w_out: bfloat16 [1024, 1024], P('mp', 'dp'), may hold values from -1.5 to 1.5
- w_in: bfloat16 [1024, 4096], P('dp', 'mp'), may hold values from -0.1875 to 0.1875
- b_in: bfloat16 [4096], P(('mp', 'dp')), may hold values from -3 to 3
- w_back: bfloat16 [4096, 1024], P('mp', 'dp'), may hold values from -0.09375 to 0.09375
- b_back: float32 [1024], replicated, may hold values from -3 to 3
- bucket_ids: int32 [16], P('dp'), may hold values from 0 to 3, as said below
- residue_counts: int32 [16, 16], P('dp'), may hold values from 30 to 256
Outputs:
- block_out: bfloat16 [8192, 1024], P(('dp', 'mp'))
- grad_input: bfloat16 [8192, 1024], P(('dp', 'mp'))
- grad_ln_gain: float32 [1024], P(('dp', 'mp'))
- grad_ln_bias: float32 [1024], P(('dp', 'mp'))
- grad_w_qkv: float32 [3, 1024, 1024], P(None, 'dp', 'mp')
- grad_w_out: float32 [1024, 1024], P('mp', 'dp')
- grad_w_in: float32 [1024, 4096], P('dp', 'mp')
- grad_b_in: float32 [4096], P(('mp', 'dp'))
- grad_w_back: float32 [4096, 1024], P('mp', 'dp')
- grad_b_back: float32 [1024], P(('dp', 'mp'))
The draws below stay inside these ranges and needn't reach their ends.
Inputs may be any that keep to these rules, and one draw needn't show every extreme that they name: `bucket_ids`: every bucket number is held by the same number of groups.
All inputs are finite; a program needn't handle non-finite values.
Results may differ from the reference program's by a relative error of at most 0.017.
Values may be sent and summed in bfloat16 or wider, within the bound.
A program may use at most 192 MiB of HBM per device.

```python
from functools import partial
import jax
import jax.numpy as jnp
from jax import lax

D = 1024
H = 16
HD = 64
ROT = 32
FF = 4096
NB = 4
SEQ_MIN = 30
TOK_DEV = 256
GROUPS = 16
TOKENS = 8192
SLOTS = 16
SEQ_MAX = 256
N_MP = 2


def draw_bucket_ids(key, part):
    key = jax.random.fold_in(key, 11)
    shuffled = jax.random.permutation(key, GROUPS)
    return (shuffled % NB).astype(jnp.int32)


def draw_residue_counts(key, part):
    key = jax.random.fold_in(key, 23)
    main_key, pick_key = jax.random.split(key)
    counts = jax.random.randint(main_key, (GROUPS, SLOTS), SEQ_MIN, SEQ_MAX + 1, dtype=jnp.int32)
    chosen = jax.random.randint(pick_key, (2,), 0, GROUPS, dtype=jnp.int32)
    counts = counts.at[chosen[0], 0].set(SEQ_MAX)
    counts = counts.at[chosen[1], 1].set(SEQ_MIN)
    return counts.astype(jnp.int32)


def level_of(stream_key, dims, cuts, smallest, largest):
    def one(position, shards_of):
        heights = jax.random.uniform(jax.random.fold_in(jax.random.fold_in(stream_key, 6), position), (shards_of,), jnp.float32, smallest / len(cuts), largest / len(cuts))
        return jnp.repeat(jnp.exp(heights), dims[position] // shards_of).reshape((-1,) + (1,) * (len(dims) - position - 1))

    factor_of = one(*cuts[0])
    for cut in cuts[1:]:
        factor_of = factor_of * one(*cut)
    return factor_of


def bell_draw(stream_key, dims, deviation, bound, shards=(), kind=jnp.bfloat16):
    level = level_of(stream_key, dims, shards, -0.22, 0.18) if shards else 1.0
    values = jax.random.normal(stream_key, dims, jnp.float32) * deviation * level
    return jnp.minimum(jnp.maximum(values, -bound), bound).astype(kind)


def setup_inputs(seed: int = 0) -> dict:
    arg_keys = jax.random.split(jax.random.key(seed), 13)
    return {
        "residual_in": bell_draw(arg_keys[0], (TOKENS, D), 1.0, 6.0, ((0, 32),)),
        "cotangent": bell_draw(arg_keys[1], (TOKENS, D), 1.0, 6.0, ((0, 32),)),
        "ln_gain": jnp.clip(1.0 + 0.1 * jax.random.normal(arg_keys[2], (D,), jnp.float32), 0.5, 1.5),
        "ln_bias": bell_draw(arg_keys[3], (D,), 0.5, 3.0, (), jnp.float32),
        "w_qkv": bell_draw(arg_keys[4], (3, D, D), D ** -0.5, 0.1875, ((1, 16), (2, 2))),
        "w_out": bell_draw(arg_keys[5], (D, D), (D // 64) ** -0.5, 1.5, ((0, 2), (1, 16))),
        "w_in": bell_draw(arg_keys[6], (D, FF), D ** -0.5, 0.1875, ((0, 16), (1, 2))),
        "b_in": bell_draw(arg_keys[7], (FF,), 0.5, 3.0, ((0, 32),)),
        "w_back": bell_draw(arg_keys[8], (FF, D), FF ** -0.5, 0.09375, ((0, 2), (1, 16))),
        "b_back": bell_draw(arg_keys[9], (D,), 0.5, 3.0, (), jnp.float32),
        "bucket_ids": draw_bucket_ids(jax.random.fold_in(arg_keys[12], 71), 0),
        "residue_counts": draw_residue_counts(jax.random.fold_in(arg_keys[12], 71), 0),
    }


@jax.custom_vjp
def low(v):
    return lax.optimization_barrier(v.astype(jnp.bfloat16)).astype(jnp.float32)

@jax.custom_vjp
def low_back(v):
    return v

def low_keep(v):
    return (low(v), None)

def low_pass(kept, grad):
    return (grad,)

def back_keep(v):
    return (v, None)

def back_low(kept, grad):
    return (low(grad),)
low.defvjp(low_keep, low_pass)
low_back.defvjp(back_keep, back_low)
NORM_EPS = 1e-05
MASKED_SCORE = -1e+30
FULL_PRECISION = lax.Precision.HIGHEST

def norm_rows(inputs_now, norm_gain, norm_shift):
    centred = inputs_now - lax.optimization_barrier(jnp.mean(inputs_now, axis=-1, keepdims=True))
    spread = lax.optimization_barrier(jnp.mean(centred * centred, axis=-1, keepdims=True))
    return centred * lax.rsqrt(spread + NORM_EPS) * norm_gain + norm_shift

def slot_tables(bucket_one, residue_row, group_rows):
    slot_length = jnp.right_shift(jnp.int32(group_rows // 2), bucket_one.astype(jnp.int32))
    places = jnp.arange(group_rows, dtype=jnp.int32)
    slot_ids = (places // slot_length).astype(jnp.int32)
    inside = (places - slot_ids * slot_length).astype(jnp.int32)
    match_table = slot_ids[:, None] == jnp.arange(SLOTS, dtype=jnp.int32)[None, :]
    picked = lax.optimization_barrier(jnp.sum(jnp.where(match_table, residue_row.astype(jnp.int32)[None, :], 0), axis=1)).astype(jnp.int32)
    live_rows = jnp.minimum(picked, slot_length)
    return (slot_ids, inside, inside < live_rows)

def rope_tables(inside):
    half_steps = jnp.arange(ROT // 2, dtype=jnp.float32)
    inverse_rates = 10000.0 ** (-2.0 * half_steps / ROT)
    angles = inside.astype(jnp.float32)[:, None] * inverse_rates[None, :]
    return (jnp.cos(angles), jnp.sin(angles))

def rotate(values, cosine_table, sine_table):
    row_count = values.shape[0]
    head_count = values.shape[1]
    paired = values[..., :ROT].reshape(row_count, head_count, ROT // 2, 2)
    even_part = paired[..., 0]
    odd_part = paired[..., 1]
    cosine_now = cosine_table[:, None, :]
    sine_now = sine_table[:, None, :]
    turned = jnp.stack([even_part * cosine_now - odd_part * sine_now, odd_part * cosine_now + even_part * sine_now], axis=-1)
    return jnp.concatenate([turned.reshape(row_count, head_count, ROT), values[..., ROT:]], axis=-1)

def mask_block(block_start, block_rows, slot_ids):
    query_places = block_start + jnp.arange(block_rows, dtype=jnp.int32)
    query_slots = lax.dynamic_slice_in_dim(slot_ids, block_start, block_rows, 0)
    key_places = jnp.arange(slot_ids.shape[0], dtype=jnp.int32)
    return (query_slots[:, None] == slot_ids[None, :]) & (key_places[None, :] <= query_places[:, None])

def attend_block(query_block, block_start, key_rows, value_rows, slot_ids):
    allowed = mask_block(block_start, query_block.shape[0], slot_ids)
    scores = jnp.einsum('qhd,khd->hqk', query_block, key_rows, precision=FULL_PRECISION) * HD ** (-0.5)
    scores = low_back(scores)
    scores = jnp.where(allowed[None], scores, MASKED_SCORE)
    weights_now = low(jax.nn.softmax(scores, axis=-1))
    return jnp.einsum('hqk,khd->qhd', weights_now, value_rows, precision=FULL_PRECISION)

def block_forward(residual_rows, ln_gain, ln_bias, w_qkv, w_out, w_in, b_in, w_back, b_back, slot_ids=None, cosine_table=None, sine_table=None):
    group_rows = residual_rows.shape[0]
    normed = low(norm_rows(residual_rows, ln_gain, ln_bias))

    def project(member_index):
        return jnp.dot(normed, w_qkv[member_index], precision=FULL_PRECISION).reshape(group_rows, H, HD)
    queries = low(rotate(low_back(project(0)), cosine_table, sine_table))
    key_rows = low(rotate(low_back(project(1)), cosine_table, sine_table))
    value_rows = low(low_back(project(2)))
    block_rows = min(512, group_rows)
    count_blocks = group_rows // block_rows
    starts = jnp.arange(count_blocks, dtype=jnp.int32) * block_rows

    def one_block(inputs_now):
        return attend_block(inputs_now[0], inputs_now[1], key_rows, value_rows, slot_ids)
    attended = lax.map(jax.checkpoint(one_block), (queries.reshape(count_blocks, block_rows, H, HD), starts))
    mixed_rows = low(low_back(attended.reshape(group_rows, H * HD)))
    hidden = low_back(jnp.dot(normed, w_in, precision=FULL_PRECISION) + b_in)
    active = low(jax.nn.gelu(hidden, approximate=True))
    attention = jnp.dot(mixed_rows, w_out, precision=FULL_PRECISION)
    feed_out = jnp.dot(active, w_back, precision=FULL_PRECISION)
    return residual_rows + attention + feed_out + b_back

def reference(residual_in, cotangent, ln_gain, ln_bias, w_qkv, w_out, w_in, b_in, w_back, b_back, bucket_ids, residue_counts):
    group_rows = TOK_DEV * N_MP
    params = (ln_gain.astype(jnp.float32), ln_bias.astype(jnp.float32), w_qkv.astype(jnp.float32), w_out.astype(jnp.float32), w_in.astype(jnp.float32), b_in.astype(jnp.float32), w_back.astype(jnp.float32), b_back.astype(jnp.float32))
    inputs_all = (residual_in.reshape(GROUPS, group_rows, D), cotangent.reshape(GROUPS, group_rows, D), bucket_ids, residue_counts)

    def one_group(totals, inputs_now):
        residual_rows, cot_rows, bucket_one, residue_row = inputs_now
        slot_ids, inside, valid_rows = slot_tables(bucket_one, residue_row, group_rows)
        cosine_table, sine_table = rope_tables(inside)
        forward_now = partial(block_forward, slot_ids=slot_ids, cosine_table=cosine_table, sine_table=sine_table)
        result, pullback = jax.vjp(forward_now, residual_rows.astype(jnp.float32), *params)
        seed_rows = jnp.where(valid_rows[:, None], cot_rows.astype(jnp.float32), jnp.float32(0.0))
        gradients = pullback(seed_rows)
        totals = tuple((running + current for running, current in zip(totals, gradients[1:])))
        return (totals, (result.astype(jnp.bfloat16), gradients[0].astype(jnp.bfloat16)))
    start_totals = tuple((jnp.zeros(member.shape, jnp.float32) for member in params))
    totals, outputs = lax.scan(one_group, start_totals, inputs_all)
    block_out = outputs[0].reshape(TOKENS, D)
    grad_input = outputs[1].reshape(TOKENS, D)
    return (block_out, grad_input, totals[0], totals[1], totals[2], totals[3], totals[4], totals[5], totals[6], totals[7])
```

```python
from functools import partial

import jax
import jax.numpy as jnp
import numpy as np
from jax import lax
from jax.experimental import pallas as pl
from jax.experimental.pallas import tpu as pltpu
from jax.sharding import PartitionSpec as P

HD = 64
ROT = 32
SLOTS = 16


NORM_EPS = 1e-05
MASKED_SCORE = -1e30


def norm_rows(inputs_now, norm_gain, norm_shift):
    centred = inputs_now - jnp.mean(inputs_now, axis=-1, keepdims=True)
    spread = jnp.mean(centred * centred, axis=-1, keepdims=True)
    return centred * lax.rsqrt(spread + NORM_EPS) * norm_gain + norm_shift


def slot_tables(bucket_one, residue_row, group_rows):
    slot_length = jnp.right_shift(jnp.int32(group_rows // 2), bucket_one)
    places = jnp.arange(group_rows, dtype=jnp.int32)
    slot_ids = places // slot_length
    inside = places - slot_ids * slot_length
    match_table = slot_ids[:, None] == jnp.arange(SLOTS, dtype=jnp.int32)[None, :]
    picked = jnp.sum(jnp.where(match_table, residue_row[None, :], 0), axis=1)
    live_rows = jnp.minimum(picked, slot_length)
    return (slot_ids, inside, inside < live_rows)


def rope_tables(inside):
    half_steps = jnp.arange(ROT // 2, dtype=jnp.float32)
    inverse_rates = 10000.0 ** (-2.0 * half_steps / ROT)
    angles = inside.astype(jnp.float32)[:, None] * inverse_rates[None, :]
    return (jnp.cos(angles), jnp.sin(angles))


def rotate(values, cosine_table, sine_table):
    row_count = values.shape[0]
    head_count = values.shape[1]
    paired = values[..., :ROT].reshape(row_count, head_count, ROT // 2, 2)
    even_part = paired[..., 0]
    odd_part = paired[..., 1]
    cosine_now = cosine_table[:, None, :]
    sine_now = sine_table[:, None, :]
    turned = jnp.stack(
        [
            even_part * cosine_now - odd_part * sine_now,
            odd_part * cosine_now + even_part * sine_now,
        ],
        axis=-1,
    )
    return jnp.concatenate([turned.reshape(row_count, head_count, ROT), values[..., ROT:]], axis=-1)


def mask_block(block_start, block_rows, slot_ids):
    query_places = block_start + jnp.arange(block_rows, dtype=jnp.int32)
    query_slots = lax.dynamic_slice_in_dim(slot_ids, block_start, block_rows, 0)
    key_places = jnp.arange(slot_ids.shape[0], dtype=jnp.int32)
    return (query_slots[:, None] == slot_ids[None, :]) & (
        key_places[None, :] <= query_places[:, None]
    )


def over_rows(first_op, second_op):
    return lax.dot_general(
        first_op, second_op, (((0,), (0,)), ((), ())), preferred_element_type=jnp.float32
    )


def against_weight(first_op, second_op):
    return lax.dot_general(
        first_op, second_op, (((1,), (1,)), ((), ())), preferred_element_type=jnp.float32
    )


def on_device(
    residual_in,
    cotangent,
    ln_gain,
    ln_bias,
    w_qkv,
    w_out,
    w_in,
    b_in,
    w_back,
    b_back,
    bucket_ids,
    residue_counts,
):
    model_count = lax.axis_size("mp")
    model_rank = lax.axis_index("mp")
    local_rows = residual_in.shape[0]
    group_rows = local_rows * model_count
    slot_ids, inside, valid_rows = slot_tables(bucket_ids[0], residue_counts[0], group_rows)
    cosine_table, sine_table = rope_tables(inside)
    qkv_all, out_all, in_all, bias_in, back_all = (
        lax.all_gather(w_qkv, "dp", axis=1, tiled=True),
        lax.all_gather(w_out, "dp", axis=1, tiled=True),
        lax.all_gather(w_in, "dp", axis=0, tiled=True),
        lax.all_gather(b_in, "dp", axis=0, tiled=True),
        lax.all_gather(w_back, "dp", axis=1, tiled=True),
    )
    x_local = residual_in.astype(jnp.float32)
    x_group = lax.all_gather(residual_in, "mp", axis=0, tiled=True).astype(jnp.float32)
    normed = norm_rows(x_group, ln_gain, ln_bias).astype(jnp.bfloat16)
    head_width = qkv_all.shape[2]
    head_count = head_width // HD
    score_scale = HD ** (-0.5)

    def project(member_index):
        return jnp.dot(normed, qkv_all[member_index], preferred_element_type=jnp.float32).reshape(
            group_rows, head_count, HD
        )

    queries = rotate(project(0), cosine_table, sine_table).astype(jnp.bfloat16)
    key_rows = rotate(project(1), cosine_table, sine_table).astype(jnp.bfloat16)
    value_rows = project(2).astype(jnp.bfloat16)
    block_rows = min(512, group_rows)
    starts = jnp.arange(group_rows // block_rows, dtype=jnp.int32) * block_rows

    def block_scores(block_start):
        query_block = lax.dynamic_slice_in_dim(queries, block_start, block_rows, 0)
        allowed = mask_block(block_start, block_rows, slot_ids)
        scores = (
            jnp.einsum("qhd,khd->hqk", query_block, key_rows, preferred_element_type=jnp.float32)
            * score_scale
        )
        return (query_block, jnp.where(allowed[None], scores, MASKED_SCORE))

    def forward_block(block_start):
        query_block, scores = block_scores(block_start)
        row_peak = jnp.max(scores, axis=-1, keepdims=True)
        exp_scores = jnp.exp(scores - row_peak)
        row_total = jnp.sum(exp_scores, axis=-1, keepdims=True)
        weights_now = (exp_scores / row_total).astype(jnp.bfloat16)
        attended = jnp.einsum(
            "hqk,khd->qhd", weights_now, value_rows, preferred_element_type=jnp.float32
        )
        return (attended.astype(jnp.bfloat16), (row_peak + jnp.log(row_total))[..., 0])

    attended_blocks, log_totals = lax.map(forward_block, starts)
    mixed_rows = attended_blocks.reshape(group_rows, head_width)
    hidden = jnp.dot(normed, in_all, preferred_element_type=jnp.float32) + bias_in.astype(
        jnp.float32
    )
    gelu_tanh = partial(jax.nn.gelu, approximate=True)
    active_value, gelu_pull = jax.vjp(gelu_tanh, hidden)
    active = active_value.astype(jnp.bfloat16)
    partial_out = jnp.dot(mixed_rows, out_all, preferred_element_type=jnp.float32) + jnp.dot(
        active, back_all, preferred_element_type=jnp.float32
    )
    summed_all = lax.psum(partial_out.astype(jnp.bfloat16), "mp").astype(jnp.float32)
    summed = lax.dynamic_slice_in_dim(summed_all, model_rank * local_rows, local_rows, 0)
    block_out = (x_local + summed + b_back).astype(jnp.bfloat16)
    cot_group = lax.all_gather(cotangent, "mp", axis=0, tiled=True)
    seed_rows = jnp.where(valid_rows[:, None], cot_group, jnp.zeros_like(cot_group))
    qkv_all, out_all, in_all, back_all = (
        lax.all_gather(w_qkv, "dp", axis=1, tiled=True),
        lax.all_gather(w_out, "dp", axis=1, tiled=True),
        lax.all_gather(w_in, "dp", axis=0, tiled=True),
        lax.all_gather(w_back, "dp", axis=1, tiled=True),
    )
    active_grad = against_weight(seed_rows, back_all)
    hidden_grad = gelu_pull(active_grad)[0].astype(jnp.bfloat16)
    grad_in_local = over_rows(normed, hidden_grad)
    grad_bias_in = jnp.sum(hidden_grad.astype(jnp.float32), axis=0)
    grad_back_local = over_rows(active, seed_rows)
    grad_out_local = over_rows(mixed_rows, seed_rows)
    normed_grad = against_weight(hidden_grad, in_all)
    mixed_grad = (
        against_weight(seed_rows, out_all).astype(jnp.bfloat16).reshape(group_rows, head_count, HD)
    )

    def backward_block(carry, inputs_now):
        key_acc, value_acc = carry
        block_start, log_total = inputs_now
        query_block, scores = block_scores(block_start)
        grad_block = lax.dynamic_slice_in_dim(mixed_grad, block_start, block_rows, 0)
        probs = jnp.exp(scores - log_total[..., None])
        probs_low = probs.astype(jnp.bfloat16)
        value_acc = value_acc + jnp.einsum(
            "hqk,qhd->khd", probs_low, grad_block, preferred_element_type=jnp.float32
        )
        probs_grad = jnp.einsum(
            "qhd,khd->hqk", grad_block, value_rows, preferred_element_type=jnp.float32
        )
        score_grad = probs * (probs_grad - jnp.sum(probs * probs_grad, axis=-1, keepdims=True))
        score_low = score_grad.astype(jnp.bfloat16)
        query_grad = (
            jnp.einsum("hqk,khd->qhd", score_low, key_rows, preferred_element_type=jnp.float32)
            * score_scale
        )
        key_acc = (
            key_acc
            + jnp.einsum("hqk,qhd->khd", score_low, query_block, preferred_element_type=jnp.float32)
            * score_scale
        )
        return ((key_acc, value_acc), query_grad)

    empty_heads = jnp.zeros((group_rows, head_count, HD), jnp.float32)
    (key_acc, value_acc), query_blocks = lax.scan(
        backward_block, (empty_heads, empty_heads), (starts, log_totals)
    )
    turn_back = partial(rotate, cosine_table=cosine_table, sine_table=sine_table)
    unturn = jax.vjp(turn_back, empty_heads)[1]
    query_pre_grad = (
        unturn(query_blocks.reshape(group_rows, head_count, HD))[0]
        .astype(jnp.bfloat16)
        .reshape(group_rows, head_width)
    )
    key_pre_grad = unturn(key_acc)[0].astype(jnp.bfloat16).reshape(group_rows, head_width)
    value_grad = value_acc.astype(jnp.bfloat16).reshape(group_rows, head_width)
    grad_qkv_local = jnp.stack(
        [
            over_rows(normed, query_pre_grad),
            over_rows(normed, key_pre_grad),
            over_rows(normed, value_grad),
        ],
        axis=0,
    )
    normed_grad = (
        normed_grad
        + against_weight(query_pre_grad, qkv_all[0])
        + against_weight(key_pre_grad, qkv_all[1])
        + against_weight(value_grad, qkv_all[2])
    )
    share_grad = lax.psum(normed_grad.astype(jnp.bfloat16), "mp").astype(jnp.float32)
    seed_group = seed_rows.astype(jnp.float32)
    norm_pull = jax.vjp(norm_rows, x_group, ln_gain, ln_bias)[1]
    input_part, gain_part, shift_part = norm_pull(share_grad)
    input_group = seed_group + input_part
    grad_input = lax.dynamic_slice_in_dim(
        input_group, model_rank * local_rows, local_rows, 0
    ).astype(jnp.bfloat16)
    back_part = jnp.sum(seed_group, axis=0)
    grad_w_qkv, grad_w_out, grad_w_in, grad_b_in, grad_w_back, gain_rows, shift_rows, back_rows = (
        lax.psum_scatter(
            grad_qkv_local.astype(jnp.bfloat16), "dp", scatter_dimension=1, tiled=True
        ).astype(jnp.float32),
        lax.psum_scatter(
            grad_out_local.astype(jnp.bfloat16), "dp", scatter_dimension=1, tiled=True
        ).astype(jnp.float32),
        lax.psum_scatter(
            grad_in_local.astype(jnp.bfloat16), "dp", scatter_dimension=0, tiled=True
        ).astype(jnp.float32),
        lax.psum_scatter(
            grad_bias_in.astype(jnp.bfloat16), "dp", scatter_dimension=0, tiled=True
        ).astype(jnp.float32),
        lax.psum_scatter(
            grad_back_local.astype(jnp.bfloat16), "dp", scatter_dimension=1, tiled=True
        ).astype(jnp.float32),
        lax.psum_scatter(
            gain_part.astype(jnp.bfloat16), "dp", scatter_dimension=0, tiled=True
        ).astype(jnp.float32),
        lax.psum_scatter(
            shift_part.astype(jnp.bfloat16), "dp", scatter_dimension=0, tiled=True
        ).astype(jnp.float32),
        lax.psum_scatter(
            back_part.astype(jnp.bfloat16), "dp", scatter_dimension=0, tiled=True
        ).astype(jnp.float32),
    )
    piece_width = gain_rows.shape[0] // model_count
    grad_ln_gain = lax.dynamic_slice_in_dim(gain_rows, model_rank * piece_width, piece_width, 0)
    grad_ln_bias = lax.dynamic_slice_in_dim(shift_rows, model_rank * piece_width, piece_width, 0)
    grad_b_back = lax.dynamic_slice_in_dim(back_rows, model_rank * piece_width, piece_width, 0)
    return (
        block_out,
        grad_input,
        grad_ln_gain,
        grad_ln_bias,
        grad_w_qkv,
        grad_w_out,
        grad_w_in,
        grad_b_in,
        grad_w_back,
        grad_b_back,
    )


MESH = pl.DeviceIdType.MESH
NZ = 4
TILE = 256
N_HEADS = TILE // HD
NQ = 4
NJ = 4
NK = NQ + 2 * NJ
VROWS = 56


def fits_quad(mesh):
    return mesh.shape["mp"] == 2 and mesh.shape["dp"] == 4 * NZ


def dot_nn(a, b):
    return lax.dot_general(a, b, (((1,), (0,)), ((), ())), preferred_element_type=jnp.float32)


def dot_nt(a, b):
    return lax.dot_general(a, b, (((1,), (1,)), ((), ())), preferred_element_type=jnp.float32)


def dot_tn(a, b):
    return lax.dot_general(a, b, (((0,), (0,)), ((), ())), preferred_element_type=jnp.float32)


def layer_kernel(
    bucket_ref,
    counts_ref,
    x_ref,
    cot_ref,
    gain_ref,
    bias_ref,
    bback_ref,
    cos_ref,
    sin_ref,
    bin_ref,
    wqkv_ref,
    wot_ref,
    win_ref,
    wbt_ref,
    block_ref,
    gin_ref,
    go_ref,
    lng_ref,
    lnb_ref,
    bbk_ref,
    gbin_ref,
    B,
    W,
    NA,
    SA,
    NT,
    ST,
    CT,
    SN,
    BM,
    QR,
    KR,
    VR,
    DQ,
    DK,
    DV,
    ATT,
    DA,
    ACT,
    HG,
    OUT,
    DN,
    GP,
    GC,
    RZ,
    FS,
    YS,
    YR,
    XH,
    RSTD,
    EXS,
    EYS,
    EXR,
    EYR,
    EXS2,
    EYS2,
    EXR2,
    EYR2,
    V,
    VS,
    VRV,
    loc_sem,
    ays,
    ayr,
    azs,
    azr,
    acs,
    acr,
    gs,
    gr,
    rcs,
    rcr,
    rzs,
    rzr,
    rys,
    ryr,
    exs,
    exr,
    vs,
    vr,
):
    f32, bf16 = jnp.float32, jnp.bfloat16
    dp, x = lax.axis_index("dp"), lax.axis_index("mp")
    z = dp // 4
    y = lax.rem(dp // 2, 2)
    c = lax.rem(dp, 2)
    rows = x_ref.shape[0]
    width = x_ref.shape[1]
    dev_x = (dp, 1 - x)
    dev_y = (dp + 2 - 4 * y, x)
    dev_c = (dp + 1 - 2 * c, x)
    dev_r = (lax.rem(dp + 4, 4 * NZ), x)
    dev_l = (lax.rem(dp + 4 * NZ - 4, 4 * NZ), x)
    dev_z = [(lax.rem(dp + 4 * i, 4 * NZ), x) for i in (1, 2, 3)]
    m_own = 2 * y + x
    m_x = 2 * y + 1 - x
    m_y = 2 - 2 * y + x
    m_d = 3 - m_own

    def rcp(src, dst, ss, rs, dev):
        return pltpu.make_async_remote_copy(
            src_ref=src, dst_ref=dst, send_sem=ss, recv_sem=rs, device_id=dev, device_id_type=MESH
        )

    barrier = pltpu.get_barrier_semaphore()
    peers = [dev_x, dev_y, dev_c] + dev_z
    for peer in peers:
        pl.semaphore_signal(barrier, inc=1, device_id=peer, device_id_type=MESH)

    def wsrc(k, q):
        if k == NK:
            return None
        if k < 3:
            return wqkv_ref.at[k, :, pl.ds(pl.multiple_of(q * TILE, TILE), TILE)]
        if k == 3:
            return wot_ref.at[:, pl.ds(pl.multiple_of(q * TILE, TILE), TILE)]
        ref = win_ref if k % 2 == 0 else wbt_ref
        j = (k - NQ) // 2
        return ref.at[:, pl.ds(pl.multiple_of(q * (NJ * TILE) + j * TILE, TILE), TILE)]

    def wv(k):
        return B if isinstance(k, int) and k == NK else W.at[k]

    def own_copy(k):
        return pltpu.make_async_copy(wsrc(k, y), W.at[k, z, y, c], loc_sem.at[k])

    def y_copy(k):
        if k == NK:
            return rcp(B.at[z, y, c], B.at[z, y, c], ays.at[k], ayr.at[k], dev_y)
        return rcp(wsrc(k, 1 - y), W.at[k, z, y, c], ays.at[k], ayr.at[k], dev_y)

    def y_arrived(k):
        here = wv(k).at[z, 1 - y, c]
        rcp(here, here, ays.at[k], ayr.at[k], dev_y).wait_recv()

    def z_copy(k, way, s, e):
        block = wv(k).at[e, :, c]
        return rcp(
            block, block, azs.at[k, way, s], azr.at[k, way, s], dev_r if way == 0 else dev_l
        )

    def c_copy(k, e):
        block = wv(k).at[e, :, c]
        return rcp(block, block, acs.at[k, e], acr.at[k, e], dev_c)

    def ag_own(k, copied=True):
        if copied:
            pltpu.make_async_copy(
                W.at[k, z, y, c], W.at[k, z, y, c], loc_sem.at[k]
            ).wait()
        y_arrived(k)

        @pl.when(z < NZ - 1)
        def _():
            z_copy(k, 0, 0, z).start()

        @pl.when(z > 0)
        def _():
            z_copy(k, 1, 0, z).start()

        c_copy(k, z).start()

    def ag_step(k, s):
        @pl.when(z - 1 - s >= 0)
        def _():
            e = z - 1 - s
            z_copy(k, 0, s, e).wait_recv()
            if s < NZ - 2:

                @pl.when(z < NZ - 1)
                def _():
                    z_copy(k, 0, s + 1, e).start()

            c_copy(k, e).start()

        @pl.when(z + 1 + s <= NZ - 1)
        def _():
            e = z + 1 + s
            z_copy(k, 1, s, e).wait_recv()
            if s < NZ - 2:

                @pl.when(z > 0)
                def _():
                    z_copy(k, 1, s + 1, e).start()

            c_copy(k, e).start()

    def ag_done(k):
        for e in range(NZ):
            block = wv(k).at[e, :, 1 - c]
            rcp(block, block, acs.at[k, e], acr.at[k, e], dev_c).wait_recv()

    def ag_sent(k, copied=True):
        y_copy(k).wait_send() if isinstance(k, int) else None
        for s in range(NZ - 1):

            @pl.when((z < NZ - 1) & (z - s >= 0))
            def _():
                z_copy(k, 0, s, z - s).wait_send()

            @pl.when((z > 0) & (z + s <= NZ - 1))
            def _():
                z_copy(k, 1, s, z + s).wait_send()

        for e in range(NZ):
            c_copy(k, e).wait_send()

    def ag_diag(t):
        if t < NK:
            ag_own(t)
        for s in range(NZ - 1):
            if 0 <= t - 1 - s < NK:
                ag_step(t - 1 - s, s)

    P0 = 64
    parts = (pl.ds(0, P0), pl.ds(P0, rows - P0))
    BUF = (NA, SA)

    def g_copy(t, p, way, m):
        block = BUF[t].at[m, parts[p]]
        i = (t * 2 + p) * 3 + way
        dev = (dev_x, dev_y)[way] if way < 2 else (dev_y, dev_x)[p]
        return rcp(block, block, gs.at[i], gr.at[i], dev)

    def g_send(t):
        g_copy(t, 0, 0, m_own).start()
        g_copy(t, 1, 1, m_own).start()
        g_copy(t, 1, 0, m_own).start()
        g_copy(t, 0, 1, m_own).start()

    def g_forward(t):
        g_copy(t, 0, 0, m_x).wait_recv()
        g_copy(t, 0, 2, m_x).start()
        g_copy(t, 1, 1, m_y).wait_recv()
        g_copy(t, 1, 2, m_y).start()

    def g_done(t):
        g_copy(t, 1, 0, m_x).wait_recv()
        g_copy(t, 0, 1, m_y).wait_recv()
        g_copy(t, 0, 2, m_d).wait_recv()
        g_copy(t, 1, 2, m_d).wait_recv()

    def g_sent(t):
        for p in (0, 1):
            for way in (0, 1):
                g_copy(t, p, way, m_own).wait_send()
        g_copy(t, 0, 2, m_x).wait_send()
        g_copy(t, 1, 2, m_y).wait_send()

    def rs_c(k):
        return rcp(GP.at[k, :, :, 1 - c], GC.at[k], rcs.at[k], rcr.at[k], dev_c)

    def rs_z(k, way, e, slot):
        return rcp(
            GP.at[k, e, :, c],
            RZ.at[k, slot],
            rzs.at[k, e],
            rzr.at[k, slot],
            dev_r if way == 0 else dev_l,
        )

    def rs_begin(k):
        rs_c(k).wait_recv()
        for e in range(NZ):
            GP[k, e, :, c] = (GP[k, e, :, c].astype(f32) + GC[k, e].astype(f32)).astype(bf16)

        @pl.when(z == 0)
        def _():
            for e in range(NZ - 1, 0, -1):
                rs_z(k, 0, e, e).start()

        @pl.when(z == NZ - 1)
        def _():
            for e in range(NZ - 1):
                rs_z(k, 1, e, e if e < NZ - 2 else 4).start()

    def pass_on(k, way, e, slot):
        rs_z(k, way, e, e).wait_recv()
        GP[k, e, :, c] = (GP[k, e, :, c].astype(f32) + RZ[k, e].astype(f32)).astype(bf16)
        rs_z(k, way, e, slot).start()

    def rs_hop1(k):
        @pl.when(z == 1)
        def _():
            pass_on(k, 0, 3, 3)
            pass_on(k, 0, 2, 2)

        @pl.when(z == 2)
        def _():
            pass_on(k, 1, 0, 0)
            pass_on(k, 1, 1, 4)

    def rs_hop2(k):
        @pl.when(z == 2)
        def _():
            pass_on(k, 0, 3, 3)

        @pl.when(z == 1)
        def _():
            pass_on(k, 1, 0, 4)

    def rs_y(k):
        return rcp(YS.at[k], YR.at[k], rys.at[k], ryr.at[k], dev_y)

    def rs_final(k):
        FS[...] = GP[k, z, :, c].astype(f32)

        @pl.when(z > 0)
        def _():
            rs_z(k, 0, z, z).wait_recv()
            FS[...] += RZ[k, z].astype(f32)

        @pl.when(z < NZ - 1)
        def _():
            rs_z(k, 1, z, 4).wait_recv()
            FS[...] += RZ[k, 4].astype(f32)

        YS[k] = FS[1 - y].astype(bf16)
        rs_y(k).start()
        go_ref[k, y] = FS[y]

    def rs_out(k):
        rs_y(k).wait_recv()
        go_ref[k, 1 - y] = YR[k].astype(f32)

    def rs_sent(k):
        rs_c(k).wait_send()
        for e in range(NZ):

            @pl.when(z != e)
            def _():
                rs_z(k, 0, e, e).wait_send()

        rs_y(k).wait_send()

    def e_copy(t, u, i):
        src, dst, dev = (
            (EXS, EXR, dev_x),
            (EYS, EYR, dev_y),
            (EXS2, EXR2, dev_x),
            (EYS2, EYR2, dev_y),
        )[i]
        return rcp(src.at[t, u], dst.at[t, u], exs.at[t, u, i], exr.at[t, u, i], dev)

    def cols(u, half):
        return pl.ds(half * (width // 2) + u * TILE, TILE)

    def e_first(t, u, P):
        for i in range(2):
            EXS[t, u, i] = P[2 * i + 1 - x, :, cols(u, 0)].astype(bf16)
        e_copy(t, u, 0).start()
        for i in range(2):
            EYS[t, u, i] = P[2 - 2 * y + i, :, cols(u, 1)].astype(bf16)
        e_copy(t, u, 1).start()

    def e_second(t, u, P):
        e_copy(t, u, 0).wait_recv()
        EYS2[t, u] = (P[m_y, :, cols(u, 0)] + EXR[t, u, 1 - y].astype(f32)).astype(bf16)
        e_copy(t, u, 3).start()
        e_copy(t, u, 1).wait_recv()
        EXS2[t, u] = (P[m_x, :, cols(u, 1)] + EYR[t, u, 1 - x].astype(f32)).astype(bf16)
        e_copy(t, u, 2).start()

    def e_last(t, u, P):
        e_copy(t, u, 3).wait_recv()
        P[m_own, :, cols(u, 0)] += EXR[t, u, y].astype(f32) + EYR2[t, u].astype(f32)
        e_copy(t, u, 2).wait_recv()
        P[m_own, :, cols(u, 1)] += EYR[t, u, x].astype(f32) + EXR2[t, u].astype(f32)

    def e_sent(t):
        for u in range(2):
            for i in range(4):
                e_copy(t, u, i).wait_send()

    for k in range(NK):
        own_copy(k).start()
    xf = x_ref[...].astype(f32)
    centred = xf - jnp.mean(xf, axis=-1, keepdims=True)
    rstd = lax.rsqrt(jnp.mean(centred * centred, axis=-1, keepdims=True) + NORM_EPS)
    xhat = centred * rstd
    XH[...] = xhat
    RSTD[...] = jnp.broadcast_to(rstd, RSTD.shape)
    NA[m_own] = (xhat * gain_ref[...] + bias_ref[...]).astype(bf16)

    bucket = bucket_ref[0]
    B[z, y, c, 0:8] = jnp.broadcast_to(bin_ref[...].astype(f32), (8, 128)).astype(bf16)
    B[z, y, c, 8:16] = jnp.full((8, 128), bucket.astype(f32), f32).astype(bf16)

    pl.semaphore_wait(barrier, len(peers))
    y_copy(NK).start()
    for k in range(NQ):
        y_copy(k).start()
    g_send(0)

    slot = lax.shift_right_logical(jnp.int32(rows), bucket)
    shift_of = (rows.bit_length() - 1) - bucket
    row = x * rows + lax.broadcasted_iota(jnp.int32, (rows, 128), 0)
    slot_of = lax.shift_right_logical(row, jnp.full(row.shape, shift_of, jnp.int32))
    place = row & jnp.full(row.shape, slot - 1, jnp.int32)
    limit = jnp.zeros((rows, 128), jnp.int32)
    for s in range(SLOTS):
        limit = jnp.where(slot_of == s, counts_ref[s], limit)
    valid = jnp.where(place < limit, 1.0, 0.0)[:, 0:1]
    seeds = cot_ref[...].astype(f32) * valid
    SA[m_own] = seeds.astype(bf16)
    back_sum = jnp.sum(seeds, axis=0, keepdims=True)
    V[...] = jnp.zeros_like(V)
    for i in range(8):
        V[16 + i : 17 + i, :] = back_sum[:, i * 128 : (i + 1) * 128]
    for k in range(NQ, NK):
        y_copy(k).start()
    g_send(1)

    ag_own(NK, copied=False)
    for s in range(NZ - 1):
        ag_step(NK, s)
    g_forward(0)
    for t in range(4):
        ag_diag(t)
    g_forward(1)
    for t in range(4, NK + NZ - 1):
        ag_diag(t)
    ag_done(NK)
    g_done(0)
    g_done(1)
    for k in range(NK):
        ag_done(k)

    lane = lax.broadcasted_iota(jnp.int32, (rows, TILE), 1)
    even = (lane & 1) == 0
    for g in range(2):
        brow = B[z, g, c].astype(f32)[8:9, :]
        ba = jnp.broadcast_to(brow, (rows, 128))

        def pick(ref):
            full = ref[...]
            out = full
            for b in range(1, 4):
                n = rows >> b
                out = jnp.where(ba == float(b), jnp.concatenate([full[:n]] * (1 << b), axis=0), out)
            return out

        cg, sg = pick(cos_ref), pick(sin_ref)
        CT[g] = jnp.concatenate([cg, cg], axis=1)
        SN[g] = jnp.concatenate([sg, sg], axis=1)
        size = jnp.full((rows, 128), rows, jnp.int32)
        for b in range(1, 4):
            size = jnp.where(ba == float(b), rows >> b, size)
        size = jnp.concatenate([size, size], axis=1)
        qi = lax.broadcasted_iota(jnp.int32, (rows, rows), 0)
        ki = lax.broadcasted_iota(jnp.int32, (rows, rows), 1)
        BM[g] = jnp.where((ki <= qi) & ((qi ^ ki) < size), 0.0, MASKED_SCORE)

    def turn(v, g, sign):
        other = jnp.where(even, -pltpu.roll(v, TILE - 1, 1), pltpu.roll(v, 1, 1))
        return v * CT[g] + (sign * other) * SN[g]

    def flip(m, _):
        cs = pl.ds(pl.multiple_of(m * rows, rows), rows)
        for d in range(4):
            NT[d, :, cs] = NA[m, :, d * TILE : (d + 1) * TILE].T
            ST[d, :, cs] = SA[m, :, d * TILE : (d + 1) * TILE].T
        return 0

    lax.fori_loop(0, 4, flip, 0)

    def weight(k):
        return W[k].reshape(width, TILE)

    scale = HD ** (-0.5)

    def attend(m, _):
        g = m // 2
        nb = NA[m]
        q = turn(dot_nn(nb, weight(0)), g, 1.0).astype(bf16)
        kk = turn(dot_nn(nb, weight(1)), g, 1.0).astype(bf16)
        v = dot_nn(nb, weight(2)).astype(bf16)
        da = dot_nn(SA[m], weight(3)).astype(bf16)
        QR[...] = q
        KR[...] = kk
        VR[...] = v
        DA[...] = da
        zero = jnp.zeros((rows, TILE), bf16)

        def head(h, acc):
            att, dq, dk, dv = acc
            mine = (lane // HD) == h
            qh = jnp.where(mine, QR[...], zero)
            kh = jnp.where(mine, KR[...], zero)
            vh = jnp.where(mine, VR[...], zero)
            dh = jnp.where(mine, DA[...], zero)
            s = dot_nt(qh, KR[...]) * scale + BM[g]
            e = jnp.exp(s - jnp.max(s, axis=-1, keepdims=True))
            p = e * (1.0 / jnp.sum(e, axis=-1, keepdims=True))
            pb = p.astype(bf16)
            att += dot_nn(pb, vh)
            pg = dot_nt(dh, VR[...])
            sg = p * (pg - jnp.sum(p * pg, axis=-1, keepdims=True))
            sb = sg.astype(bf16)
            dv += dot_tn(pb, dh)
            dq += dot_nn(sb, kh)
            dk += dot_tn(sb, qh)
            return att, dq, dk, dv

        none = jnp.zeros((rows, TILE), f32)
        att, dq, dk, dv = lax.fori_loop(0, N_HEADS, head, (none,) * 4)
        at = att.astype(bf16)
        dqb = turn(dq * scale, g, -1.0).astype(bf16)
        dkb = turn(dk * scale, g, -1.0).astype(bf16)
        dvb = dv.astype(bf16)
        rs = pl.ds(pl.multiple_of(m * rows, rows), rows)
        ATT[rs, :] = at
        DQ[rs, :] = dqb
        DK[rs, :] = dkb
        DV[rs, :] = dvb
        OUT[m] = dot_nt(at, weight(3))
        DN[m] = dot_nt(dqb, weight(0)) + dot_nt(dkb, weight(1)) + dot_nt(dvb, weight(2))
        return 0

    lax.fori_loop(0, 4, attend, 0)

    def grad_of(k, left, right):
        def block(d, _):
            GP[k, d] = dot_nn(left[d], right[...]).astype(bf16).reshape(2, 2, 64, TILE)
            return 0

        lax.fori_loop(0, 4, block, 0)
        rs_c(k).start()

    grad_of(0, NT, DQ)
    grad_of(1, NT, DK)
    grad_of(2, NT, DV)
    grad_of(3, ST, ATT)

    def feed(j, _):
        ki, kb = NQ + 2 * j, NQ + 1 + 2 * j
        n0 = 2 * j
        zz = 2 * y + n0 // 4
        yy = lax.rem(n0 // 2, 2)
        b0 = B[zz, yy, 0].astype(f32)[0:1, :]
        b1 = B[zz, yy, 1].astype(f32)[0:1, :]
        bias_j = jnp.concatenate([b0, b1], axis=1)

        def rowsof(m, total):
            u = dot_nn(NA[m], weight(ki)) + bias_j
            u2 = u * u
            k0 = float(np.sqrt(2.0 / np.pi))
            t = jnp.tanh(k0 * u * (1.0 + 0.044715 * u2))
            act = (0.5 * u * (1.0 + t)).astype(bf16)
            slope = 0.5 * (1.0 + t) + (0.5 * k0) * u * (1.0 - t * t) * (1.0 + 0.134145 * u2)
            hg = (dot_nn(SA[m], weight(kb)) * slope).astype(bf16)
            rs = pl.ds(pl.multiple_of(m * rows, rows), rows)
            ACT[rs, :] = act
            HG[rs, :] = hg
            OUT[m] += dot_nt(act, weight(kb))
            DN[m] += dot_nt(hg, weight(ki))
            return total + jnp.sum(hg.astype(f32), axis=0, keepdims=True)

        total = lax.fori_loop(0, 4, rowsof, jnp.zeros((1, TILE), f32))
        at = 24 + x * 16 + y * 8 + 2 * j
        V[pl.ds(at, 1), :] = total[:, :128]
        V[pl.ds(at + 1, 1), :] = total[:, 128:]
        grad_of(ki, NT, HG)
        grad_of(kb, ST, ACT)
        return 0

    lax.fori_loop(0, NJ, feed, 0)

    for t, P in ((0, OUT), (1, DN)):
        for u in range(2):
            e_first(t, u, P)

    def later(f):
        lax.fori_loop(0, NK, lambda k, _: (f(k), 0)[1], 0)

    later(rs_begin)
    later(rs_hop1)
    later(rs_hop2)
    for t, P in ((0, OUT), (1, DN)):
        for u in range(2):
            e_second(t, u, P)
        for u in range(2):
            e_last(t, u, P)
    block_ref[...] = (x_ref[...].astype(f32) + OUT[m_own] + bback_ref[...]).astype(bf16)
    dn = DN[m_own]
    xhat = XH[...]
    e = dn * gain_ref[...]
    me = jnp.mean(e, axis=-1, keepdims=True)
    mex = jnp.mean(e * xhat, axis=-1, keepdims=True)
    gin_ref[...] = (SA[m_own].astype(f32) + RSTD[:, 0:1] * (e - me - xhat * mex)).astype(bf16)
    gsum = jnp.sum(dn * xhat, axis=0, keepdims=True)
    bsum = jnp.sum(dn, axis=0, keepdims=True)
    for i in range(8):
        V[i : i + 1, :] = gsum[:, i * 128 : (i + 1) * 128]
        V[8 + i : 9 + i, :] = bsum[:, i * 128 : (i + 1) * 128]

    def v_copy(i, dev):
        return rcp(VS.at[min(i, 3)], VRV.at[i], vs.at[i], vr.at[i], dev)

    VS[0] = V[...]
    for i, dev in enumerate((dev_c, dev_x, dev_y)):
        v_copy(i, dev).start()
        v_copy(i, dev).wait_recv()
        VS[i + 1] = VS[i] + VRV[i]
    for i, dev in enumerate(dev_z):
        v_copy(3 + i, dev).start()
    later(rs_final)
    later(rs_out)
    for i, dev in enumerate(dev_z):
        v_copy(3 + i, dev).wait_recv()
    V[...] = VS[3] + VRV[3] + VRV[4] + VRV[5]
    index = 2 * dp + x
    lane4 = lax.rem(index, 4)
    for base, ref in ((0, lng_ref), (8, lnb_ref), (16, bbk_ref)):
        line = V[pl.ds(base + index // 4, 1), :]
        out = line[:, 0:32]
        for n in range(1, 4):
            out = jnp.where(lane4 == n, line[:, 32 * n : 32 * n + 32], out)
        ref[...] = out
    gbin_ref[...] = V[pl.ds(24 + 16 * x + dp, 1), :]

    for k in range(NK + 1):
        ag_sent(k)
    for t in range(2):
        g_sent(t)
        e_sent(t)
    later(rs_sent)
    for i, dev in enumerate([dev_c, dev_x, dev_y] + dev_z):
        v_copy(i, dev).wait_send()


def rope_constants(rows):
    half = np.arange(ROT // 2, dtype=np.float32)
    rates = (10000.0 ** (-2.0 * half / ROT)).astype(np.float32)
    angle = np.arange(rows, dtype=np.float32)[:, None] * rates[None, :]
    angle = np.repeat(angle, 2, axis=1)
    cos = np.concatenate([np.cos(angle), np.ones((rows, HD - ROT))], axis=1)
    sin = np.concatenate([np.sin(angle), np.zeros((rows, HD - ROT))], axis=1)
    two = lambda t: np.concatenate([t, t], axis=1).astype(np.float32)
    return two(cos), two(sin)


def on_quad(
    residual_in,
    cotangent,
    ln_gain,
    ln_bias,
    w_qkv,
    w_out,
    w_in,
    b_in,
    w_back,
    b_back,
    bucket_ids,
    residue_counts,
):
    rows, width = residual_in.shape
    cos, sin = rope_constants(rows)
    f32, bf16 = jnp.float32, jnp.bfloat16
    vm = pl.BlockSpec(memory_space=pltpu.VMEM)
    sm = pl.BlockSpec(memory_space=pltpu.SMEM)
    anyspace = pl.BlockSpec(memory_space=pl.ANY)
    shard = width // (4 * NZ)
    sem = pltpu.SemaphoreType.DMA
    block = (2, 2, rows, TILE)
    outs = pl.pallas_call(
        layer_kernel,
        out_shape=(
            jax.ShapeDtypeStruct((rows, width), bf16),
            jax.ShapeDtypeStruct((rows, width), bf16),
            jax.ShapeDtypeStruct((NK, 2, shard, TILE), f32),
            jax.ShapeDtypeStruct((1, 32), f32),
            jax.ShapeDtypeStruct((1, 32), f32),
            jax.ShapeDtypeStruct((1, 32), f32),
            jax.ShapeDtypeStruct((1, 128), f32),
        ),
        in_specs=[sm, sm] + [vm] * 8 + [anyspace] * 4,
        out_specs=(vm,) * 7,
        scratch_shapes=[
            pltpu.VMEM((NZ, 2, 2, 16, 128), bf16),
            pltpu.VMEM((NK, NZ, 2, 2, shard, TILE), bf16),
            pltpu.VMEM((4, rows, width), bf16),
            pltpu.VMEM((4, rows, width), bf16),
            pltpu.VMEM((4, TILE, 4 * rows), bf16),
            pltpu.VMEM((4, TILE, 4 * rows), bf16),
            pltpu.VMEM((2, rows, TILE), f32),
            pltpu.VMEM((2, rows, TILE), f32),
            pltpu.VMEM((2, rows, rows), f32),
            pltpu.VMEM((rows, TILE), bf16),
            pltpu.VMEM((rows, TILE), bf16),
            pltpu.VMEM((rows, TILE), bf16),
            pltpu.VMEM((4 * rows, TILE), bf16),
            pltpu.VMEM((4 * rows, TILE), bf16),
            pltpu.VMEM((4 * rows, TILE), bf16),
            pltpu.VMEM((4 * rows, TILE), bf16),
            pltpu.VMEM((rows, TILE), bf16),
            pltpu.VMEM((4 * rows, TILE), bf16),
            pltpu.VMEM((4 * rows, TILE), bf16),
            pltpu.VMEM((4, rows, width), f32),
            pltpu.VMEM((4, rows, width), f32),
            pltpu.VMEM((NK, NZ, 2, 2, shard, TILE), bf16),
            pltpu.VMEM((NK, NZ, 2, shard, TILE), bf16),
            pltpu.VMEM((NK, 5, 2, shard, TILE), bf16),
            pltpu.VMEM((2, shard, TILE), f32),
            pltpu.VMEM((NK, shard, TILE), bf16),
            pltpu.VMEM((NK, shard, TILE), bf16),
            pltpu.VMEM((rows, width), f32),
            pltpu.VMEM((rows, 128), f32),
            pltpu.VMEM((2,) + block, bf16),
            pltpu.VMEM((2,) + block, bf16),
            pltpu.VMEM((2,) + block, bf16),
            pltpu.VMEM((2,) + block, bf16),
            pltpu.VMEM((2, 2, rows, TILE), bf16),
            pltpu.VMEM((2, 2, rows, TILE), bf16),
            pltpu.VMEM((2, 2, rows, TILE), bf16),
            pltpu.VMEM((2, 2, rows, TILE), bf16),
            pltpu.VMEM((VROWS, 128), f32),
            pltpu.VMEM((4, VROWS, 128), f32),
            pltpu.VMEM((6, VROWS, 128), f32),
            sem((NK,)),
            sem((NK + 1,)),
            sem((NK + 1,)),
            sem((NK + 1, 2, 3)),
            sem((NK + 1, 2, 3)),
            sem((NK + 1, NZ)),
            sem((NK + 1, NZ)),
            sem((12,)),
            sem((12,)),
            sem((NK,)),
            sem((NK,)),
            sem((NK, NZ)),
            sem((NK, 5)),
            sem((NK,)),
            sem((NK,)),
            sem((2, 2, 4)),
            sem((2, 2, 4)),
            sem((6,)),
            sem((6,)),
        ],
        compiler_params=pltpu.CompilerParams(
            collective_id=0, has_side_effects=True, vmem_limit_bytes=63 << 20
        ),
        cost_estimate=pl.CostEstimate(
            flops=20 * 2**30, bytes_accessed=8 * 2**20, transcendentals=2**21
        ),
    )(
        bucket_ids,
        residue_counts.reshape(SLOTS),
        residual_in,
        cotangent,
        ln_gain.reshape(1, width),
        ln_bias.reshape(1, width),
        b_back.reshape(1, width),
        jnp.asarray(cos),
        jnp.asarray(sin),
        b_in.reshape(1, 128),
        w_qkv,
        w_out.T,
        w_in,
        w_back.T,
    )
    block_out, grad_input, go, lng, lnb, bbk, gbin = outs
    half = 2 * TILE
    grad_w_qkv = go[:3].transpose(0, 2, 1, 3).reshape(3, shard, half)
    grad_w_out = go[3].transpose(0, 2, 1).reshape(half, shard)
    gi = go[NQ::2]
    gb = go[NQ + 1 :: 2]
    grad_w_in = gi.transpose(2, 1, 0, 3).reshape(shard, NJ * half)
    grad_w_back = gb.transpose(1, 0, 3, 2).reshape(NJ * half, shard)
    return (
        block_out,
        grad_input,
        lng.reshape(32),
        lnb.reshape(32),
        grad_w_qkv,
        grad_w_out,
        grad_w_in,
        gbin.reshape(128),
        grad_w_back,
        bbk.reshape(32),
    )


def solution(mesh):
    placed = (
        P(("dp", "mp"), None),
        P(("dp", "mp"), None),
        P(),
        P(),
        P(None, "dp", "mp"),
        P("mp", "dp"),
        P("dp", "mp"),
        P(("mp", "dp")),
        P("mp", "dp"),
        P(),
        P("dp"),
        P("dp", None),
    )
    return jax.shard_map(
        on_quad if fits_quad(mesh) else on_device,
        mesh=mesh,
        in_specs=placed,
        out_specs=(
            P(("dp", "mp"), None),
            P(("dp", "mp"), None),
            P(("dp", "mp")),
            P(("dp", "mp")),
            P(None, "dp", "mp"),
            P("mp", "dp"),
            P("dp", "mp"),
            P(("mp", "dp")),
            P("mp", "dp"),
            P(("dp", "mp")),
        ),
        check_vma=False,
    )
```

```python
from functools import partial

import jax
import jax.numpy as jnp
import numpy as np
from jax import lax
from jax.experimental import pallas as pl
from jax.experimental.pallas import tpu as pltpu
from jax.sharding import PartitionSpec as P

HD = 64
ROT = 32
SLOTS = 16


NORM_EPS = 1e-05
MASKED_SCORE = -1e30


def norm_rows(inputs_now, norm_gain, norm_shift):
    centred = inputs_now - jnp.mean(inputs_now, axis=-1, keepdims=True)
    spread = jnp.mean(centred * centred, axis=-1, keepdims=True)
    return centred * lax.rsqrt(spread + NORM_EPS) * norm_gain + norm_shift


def slot_tables(bucket_one, residue_row, group_rows):
    slot_length = jnp.right_shift(jnp.int32(group_rows // 2), bucket_one)
    places = jnp.arange(group_rows, dtype=jnp.int32)
    slot_ids = places // slot_length
    inside = places - slot_ids * slot_length
    match_table = slot_ids[:, None] == jnp.arange(SLOTS, dtype=jnp.int32)[None, :]
    picked = jnp.sum(jnp.where(match_table, residue_row[None, :], 0), axis=1)
    live_rows = jnp.minimum(picked, slot_length)
    return (slot_ids, inside, inside < live_rows)


def rope_tables(inside):
    half_steps = jnp.arange(ROT // 2, dtype=jnp.float32)
    inverse_rates = 10000.0 ** (-2.0 * half_steps / ROT)
    angles = inside.astype(jnp.float32)[:, None] * inverse_rates[None, :]
    return (jnp.cos(angles), jnp.sin(angles))


def rotate(values, cosine_table, sine_table):
    row_count = values.shape[0]
    head_count = values.shape[1]
    paired = values[..., :ROT].reshape(row_count, head_count, ROT // 2, 2)
    even_part = paired[..., 0]
    odd_part = paired[..., 1]
    cosine_now = cosine_table[:, None, :]
    sine_now = sine_table[:, None, :]
    turned = jnp.stack(
        [
            even_part * cosine_now - odd_part * sine_now,
            odd_part * cosine_now + even_part * sine_now,
        ],
        axis=-1,
    )
    return jnp.concatenate([turned.reshape(row_count, head_count, ROT), values[..., ROT:]], axis=-1)


def mask_block(block_start, block_rows, slot_ids):
    query_places = block_start + jnp.arange(block_rows, dtype=jnp.int32)
    query_slots = lax.dynamic_slice_in_dim(slot_ids, block_start, block_rows, 0)
    key_places = jnp.arange(slot_ids.shape[0], dtype=jnp.int32)
    return (query_slots[:, None] == slot_ids[None, :]) & (
        key_places[None, :] <= query_places[:, None]
    )


def over_rows(first_op, second_op):
    return lax.dot_general(
        first_op, second_op, (((0,), (0,)), ((), ())), preferred_element_type=jnp.float32
    )


def against_weight(first_op, second_op):
    return lax.dot_general(
        first_op, second_op, (((1,), (1,)), ((), ())), preferred_element_type=jnp.float32
    )


def on_device(
    residual_in,
    cotangent,
    ln_gain,
    ln_bias,
    w_qkv,
    w_out,
    w_in,
    b_in,
    w_back,
    b_back,
    bucket_ids,
    residue_counts,
):
    model_count = lax.axis_size("mp")
    model_rank = lax.axis_index("mp")
    local_rows = residual_in.shape[0]
    group_rows = local_rows * model_count
    slot_ids, inside, valid_rows = slot_tables(bucket_ids[0], residue_counts[0], group_rows)
    cosine_table, sine_table = rope_tables(inside)
    qkv_all, out_all, in_all, bias_in, back_all = (
        lax.all_gather(w_qkv, "dp", axis=1, tiled=True),
        lax.all_gather(w_out, "dp", axis=1, tiled=True),
        lax.all_gather(w_in, "dp", axis=0, tiled=True),
        lax.all_gather(b_in, "dp", axis=0, tiled=True),
        lax.all_gather(w_back, "dp", axis=1, tiled=True),
    )
    x_local = residual_in.astype(jnp.float32)
    x_group = lax.all_gather(residual_in, "mp", axis=0, tiled=True).astype(jnp.float32)
    normed = norm_rows(x_group, ln_gain, ln_bias).astype(jnp.bfloat16)
    head_width = qkv_all.shape[2]
    head_count = head_width // HD
    score_scale = HD ** (-0.5)

    def project(member_index):
        return jnp.dot(normed, qkv_all[member_index], preferred_element_type=jnp.float32).reshape(
            group_rows, head_count, HD
        )

    queries = rotate(project(0), cosine_table, sine_table).astype(jnp.bfloat16)
    key_rows = rotate(project(1), cosine_table, sine_table).astype(jnp.bfloat16)
    value_rows = project(2).astype(jnp.bfloat16)
    block_rows = min(512, group_rows)
    starts = jnp.arange(group_rows // block_rows, dtype=jnp.int32) * block_rows

    def block_scores(block_start):
        query_block = lax.dynamic_slice_in_dim(queries, block_start, block_rows, 0)
        allowed = mask_block(block_start, block_rows, slot_ids)
        scores = (
            jnp.einsum("qhd,khd->hqk", query_block, key_rows, preferred_element_type=jnp.float32)
            * score_scale
        )
        return (query_block, jnp.where(allowed[None], scores, MASKED_SCORE))

    def forward_block(block_start):
        query_block, scores = block_scores(block_start)
        row_peak = jnp.max(scores, axis=-1, keepdims=True)
        exp_scores = jnp.exp(scores - row_peak)
        row_total = jnp.sum(exp_scores, axis=-1, keepdims=True)
        weights_now = (exp_scores / row_total).astype(jnp.bfloat16)
        attended = jnp.einsum(
            "hqk,khd->qhd", weights_now, value_rows, preferred_element_type=jnp.float32
        )
        return (attended.astype(jnp.bfloat16), (row_peak + jnp.log(row_total))[..., 0])

    attended_blocks, log_totals = lax.map(forward_block, starts)
    mixed_rows = attended_blocks.reshape(group_rows, head_width)
    hidden = jnp.dot(normed, in_all, preferred_element_type=jnp.float32) + bias_in.astype(
        jnp.float32
    )
    gelu_tanh = partial(jax.nn.gelu, approximate=True)
    active_value, gelu_pull = jax.vjp(gelu_tanh, hidden)
    active = active_value.astype(jnp.bfloat16)
    partial_out = jnp.dot(mixed_rows, out_all, preferred_element_type=jnp.float32) + jnp.dot(
        active, back_all, preferred_element_type=jnp.float32
    )
    summed_all = lax.psum(partial_out.astype(jnp.bfloat16), "mp").astype(jnp.float32)
    summed = lax.dynamic_slice_in_dim(summed_all, model_rank * local_rows, local_rows, 0)
    block_out = (x_local + summed + b_back).astype(jnp.bfloat16)
    cot_group = lax.all_gather(cotangent, "mp", axis=0, tiled=True)
    seed_rows = jnp.where(valid_rows[:, None], cot_group, jnp.zeros_like(cot_group))
    qkv_all, out_all, in_all, back_all = (
        lax.all_gather(w_qkv, "dp", axis=1, tiled=True),
        lax.all_gather(w_out, "dp", axis=1, tiled=True),
        lax.all_gather(w_in, "dp", axis=0, tiled=True),
        lax.all_gather(w_back, "dp", axis=1, tiled=True),
    )
    active_grad = against_weight(seed_rows, back_all)
    hidden_grad = gelu_pull(active_grad)[0].astype(jnp.bfloat16)
    grad_in_local = over_rows(normed, hidden_grad)
    grad_bias_in = jnp.sum(hidden_grad.astype(jnp.float32), axis=0)
    grad_back_local = over_rows(active, seed_rows)
    grad_out_local = over_rows(mixed_rows, seed_rows)
    normed_grad = against_weight(hidden_grad, in_all)
    mixed_grad = (
        against_weight(seed_rows, out_all).astype(jnp.bfloat16).reshape(group_rows, head_count, HD)
    )

    def backward_block(carry, inputs_now):
        key_acc, value_acc = carry
        block_start, log_total = inputs_now
        query_block, scores = block_scores(block_start)
        grad_block = lax.dynamic_slice_in_dim(mixed_grad, block_start, block_rows, 0)
        probs = jnp.exp(scores - log_total[..., None])
        probs_low = probs.astype(jnp.bfloat16)
        value_acc = value_acc + jnp.einsum(
            "hqk,qhd->khd", probs_low, grad_block, preferred_element_type=jnp.float32
        )
        probs_grad = jnp.einsum(
            "qhd,khd->hqk", grad_block, value_rows, preferred_element_type=jnp.float32
        )
        score_grad = probs * (probs_grad - jnp.sum(probs * probs_grad, axis=-1, keepdims=True))
        score_low = score_grad.astype(jnp.bfloat16)
        query_grad = (
            jnp.einsum("hqk,khd->qhd", score_low, key_rows, preferred_element_type=jnp.float32)
            * score_scale
        )
        key_acc = (
            key_acc
            + jnp.einsum("hqk,qhd->khd", score_low, query_block, preferred_element_type=jnp.float32)
            * score_scale
        )
        return ((key_acc, value_acc), query_grad)

    empty_heads = jnp.zeros((group_rows, head_count, HD), jnp.float32)
    (key_acc, value_acc), query_blocks = lax.scan(
        backward_block, (empty_heads, empty_heads), (starts, log_totals)
    )
    turn_back = partial(rotate, cosine_table=cosine_table, sine_table=sine_table)
    unturn = jax.vjp(turn_back, empty_heads)[1]
    query_pre_grad = (
        unturn(query_blocks.reshape(group_rows, head_count, HD))[0]
        .astype(jnp.bfloat16)
        .reshape(group_rows, head_width)
    )
    key_pre_grad = unturn(key_acc)[0].astype(jnp.bfloat16).reshape(group_rows, head_width)
    value_grad = value_acc.astype(jnp.bfloat16).reshape(group_rows, head_width)
    grad_qkv_local = jnp.stack(
        [
            over_rows(normed, query_pre_grad),
            over_rows(normed, key_pre_grad),
            over_rows(normed, value_grad),
        ],
        axis=0,
    )
    normed_grad = (
        normed_grad
        + against_weight(query_pre_grad, qkv_all[0])
        + against_weight(key_pre_grad, qkv_all[1])
        + against_weight(value_grad, qkv_all[2])
    )
    share_grad = lax.psum(normed_grad.astype(jnp.bfloat16), "mp").astype(jnp.float32)
    seed_group = seed_rows.astype(jnp.float32)
    norm_pull = jax.vjp(norm_rows, x_group, ln_gain, ln_bias)[1]
    input_part, gain_part, shift_part = norm_pull(share_grad)
    input_group = seed_group + input_part
    grad_input = lax.dynamic_slice_in_dim(
        input_group, model_rank * local_rows, local_rows, 0
    ).astype(jnp.bfloat16)
    back_part = jnp.sum(seed_group, axis=0)
    grad_w_qkv, grad_w_out, grad_w_in, grad_b_in, grad_w_back, gain_rows, shift_rows, back_rows = (
        lax.psum_scatter(
            grad_qkv_local.astype(jnp.bfloat16), "dp", scatter_dimension=1, tiled=True
        ).astype(jnp.float32),
        lax.psum_scatter(
            grad_out_local.astype(jnp.bfloat16), "dp", scatter_dimension=1, tiled=True
        ).astype(jnp.float32),
        lax.psum_scatter(
            grad_in_local.astype(jnp.bfloat16), "dp", scatter_dimension=0, tiled=True
        ).astype(jnp.float32),
        lax.psum_scatter(
            grad_bias_in.astype(jnp.bfloat16), "dp", scatter_dimension=0, tiled=True
        ).astype(jnp.float32),
        lax.psum_scatter(
            grad_back_local.astype(jnp.bfloat16), "dp", scatter_dimension=1, tiled=True
        ).astype(jnp.float32),
        lax.psum_scatter(
            gain_part.astype(jnp.bfloat16), "dp", scatter_dimension=0, tiled=True
        ).astype(jnp.float32),
        lax.psum_scatter(
            shift_part.astype(jnp.bfloat16), "dp", scatter_dimension=0, tiled=True
        ).astype(jnp.float32),
        lax.psum_scatter(
            back_part.astype(jnp.bfloat16), "dp", scatter_dimension=0, tiled=True
        ).astype(jnp.float32),
    )
    piece_width = gain_rows.shape[0] // model_count
    grad_ln_gain = lax.dynamic_slice_in_dim(gain_rows, model_rank * piece_width, piece_width, 0)
    grad_ln_bias = lax.dynamic_slice_in_dim(shift_rows, model_rank * piece_width, piece_width, 0)
    grad_b_back = lax.dynamic_slice_in_dim(back_rows, model_rank * piece_width, piece_width, 0)
    return (
        block_out,
        grad_input,
        grad_ln_gain,
        grad_ln_bias,
        grad_w_qkv,
        grad_w_out,
        grad_w_in,
        grad_b_in,
        grad_w_back,
        grad_b_back,
    )


MESH = pl.DeviceIdType.MESH
NZ = 4
TILE = 256
N_HEADS = TILE // HD
NQ = 4
NJ = 4
NK = NQ + 2 * NJ
VROWS = 56


def fits_quad(mesh):
    return mesh.shape["mp"] == 2 and mesh.shape["dp"] == 4 * NZ


def dot_nn(a, b):
    return lax.dot_general(a, b, (((1,), (0,)), ((), ())), preferred_element_type=jnp.float32)


def dot_nt(a, b):
    return lax.dot_general(a, b, (((1,), (1,)), ((), ())), preferred_element_type=jnp.float32)


def dot_tn(a, b):
    return lax.dot_general(a, b, (((0,), (0,)), ((), ())), preferred_element_type=jnp.float32)


def layer_kernel(
    bucket_ref,
    counts_ref,
    x_ref,
    cot_ref,
    gain_ref,
    bias_ref,
    bback_ref,
    cos_ref,
    sin_ref,
    bin_ref,
    wqkv_ref,
    wot_ref,
    win_ref,
    wbt_ref,
    block_ref,
    gin_ref,
    go_ref,
    lng_ref,
    lnb_ref,
    bbk_ref,
    gbin_ref,
    B,
    W,
    NA,
    SA,
    NT,
    ST,
    CT,
    SN,
    BM,
    QR,
    KR,
    VR,
    DQ,
    DK,
    DV,
    ATT,
    DA,
    ACT,
    HG,
    OUT,
    DN,
    GP,
    GC,
    RZ,
    FS,
    YS,
    YR,
    XH,
    RSTD,
    EXS,
    EYS,
    EXR,
    EYR,
    EXS2,
    EYS2,
    EXR2,
    EYR2,
    V,
    VS,
    VRV,
    loc_sem,
    ays,
    ayr,
    azs,
    azr,
    acs,
    acr,
    gs,
    gr,
    rcs,
    rcr,
    rzs,
    rzr,
    rys,
    ryr,
    exs,
    exr,
    vs,
    vr,
):
    f32, bf16 = jnp.float32, jnp.bfloat16
    dp, x = lax.axis_index("dp"), lax.axis_index("mp")
    z = dp // 4
    y = lax.rem(dp // 2, 2)
    c = lax.rem(dp, 2)
    rows = x_ref.shape[0]
    width = x_ref.shape[1]
    dev_x = (dp, 1 - x)
    dev_y = (dp + 2 - 4 * y, x)
    dev_c = (dp + 1 - 2 * c, x)
    dev_r = (lax.rem(dp + 4, 4 * NZ), x)
    dev_l = (lax.rem(dp + 4 * NZ - 4, 4 * NZ), x)
    dev_z = [(lax.rem(dp + 4 * i, 4 * NZ), x) for i in (1, 2, 3)]
    m_own = 2 * y + x
    m_x = 2 * y + 1 - x
    m_y = 2 - 2 * y + x
    m_d = 3 - m_own

    def rcp(src, dst, ss, rs, dev):
        return pltpu.make_async_remote_copy(
            src_ref=src, dst_ref=dst, send_sem=ss, recv_sem=rs, device_id=dev, device_id_type=MESH
        )

    barrier = pltpu.get_barrier_semaphore()
    peers = [dev_x, dev_y, dev_c] + dev_z
    for peer in peers:
        pl.semaphore_signal(barrier, inc=1, device_id=peer, device_id_type=MESH)

    def wsrc(k, q):
        if k == NK:
            return None
        if 2 <= k < 5:
            return wqkv_ref.at[k - 2, :, pl.ds(pl.multiple_of(q * TILE, TILE), TILE)]
        if k == 5:
            return wot_ref.at[:, pl.ds(pl.multiple_of(q * TILE, TILE), TILE)]
        ref = win_ref if k % 2 == 0 else wbt_ref
        j = 0 if k < 2 else (k - NQ) // 2
        return ref.at[:, pl.ds(pl.multiple_of(q * (NJ * TILE) + j * TILE, TILE), TILE)]

    def wv(k):
        return B if isinstance(k, int) and k == NK else W.at[k]

    def own_copy(k):
        return pltpu.make_async_copy(wsrc(k, y), W.at[k, z, y, c], loc_sem.at[k])

    def y_copy(k):
        if k == NK:
            return rcp(B.at[z, y, c], B.at[z, y, c], ays.at[k], ayr.at[k], dev_y)
        return rcp(wsrc(k, 1 - y), W.at[k, z, y, c], ays.at[k], ayr.at[k], dev_y)

    def y_arrived(k):
        here = wv(k).at[z, 1 - y, c]
        rcp(here, here, ays.at[k], ayr.at[k], dev_y).wait_recv()

    def z_copy(k, way, s, e):
        block = wv(k).at[e, :, c]
        return rcp(
            block, block, azs.at[k, way, s], azr.at[k, way, s], dev_r if way == 0 else dev_l
        )

    def c_copy(k, e):
        block = wv(k).at[e, :, c]
        return rcp(block, block, acs.at[k, e], acr.at[k, e], dev_c)

    def ag_own(k, copied=True):
        if copied:
            pltpu.make_async_copy(
                W.at[k, z, y, c], W.at[k, z, y, c], loc_sem.at[k]
            ).wait()
        y_arrived(k)

        @pl.when(z < NZ - 1)
        def _():
            z_copy(k, 0, 0, z).start()

        @pl.when(z > 0)
        def _():
            z_copy(k, 1, 0, z).start()

        c_copy(k, z).start()

    def ag_step(k, s):
        @pl.when(z - 1 - s >= 0)
        def _():
            e = z - 1 - s
            z_copy(k, 0, s, e).wait_recv()
            if s < NZ - 2:

                @pl.when(z < NZ - 1)
                def _():
                    z_copy(k, 0, s + 1, e).start()

            c_copy(k, e).start()

        @pl.when(z + 1 + s <= NZ - 1)
        def _():
            e = z + 1 + s
            z_copy(k, 1, s, e).wait_recv()
            if s < NZ - 2:

                @pl.when(z > 0)
                def _():
                    z_copy(k, 1, s + 1, e).start()

            c_copy(k, e).start()

    def ag_done(k):
        for e in range(NZ):
            block = wv(k).at[e, :, 1 - c]
            rcp(block, block, acs.at[k, e], acr.at[k, e], dev_c).wait_recv()

    def ag_sent(k, copied=True):
        y_copy(k).wait_send() if isinstance(k, int) else None
        for s in range(NZ - 1):

            @pl.when((z < NZ - 1) & (z - s >= 0))
            def _():
                z_copy(k, 0, s, z - s).wait_send()

            @pl.when((z > 0) & (z + s <= NZ - 1))
            def _():
                z_copy(k, 1, s, z + s).wait_send()

        for e in range(NZ):
            c_copy(k, e).wait_send()

    order = [NK] + list(range(NK))
    turns = iter(range(NK + NZ))

    def ag_turn():
        t = next(turns, None)
        if t is None:
            return
        if t + 3 <= NK:
            y_copy(order[t + 3]).start()
        if t <= NK:
            ag_own(order[t], copied=t > 0)
        for s in range(NZ - 1):
            if 0 <= t - 1 - s <= NK:
                ag_step(order[t - 1 - s], s)

    P0 = 64
    parts = (pl.ds(0, P0), pl.ds(P0, rows - P0))
    BUF = (NA, SA)

    def g_copy(t, p, way, m):
        block = BUF[t].at[m, parts[p]]
        i = (t * 2 + p) * 3 + way
        dev = (dev_x, dev_y)[way] if way < 2 else (dev_y, dev_x)[p]
        return rcp(block, block, gs.at[i], gr.at[i], dev)

    def g_send(t):
        g_copy(t, 0, 0, m_own).start()
        g_copy(t, 1, 1, m_own).start()
        g_copy(t, 1, 0, m_own).start()
        g_copy(t, 0, 1, m_own).start()

    def g_near(t):
        g_copy(t, 0, 0, m_x).wait_recv()
        g_copy(t, 1, 1, m_y).wait_recv()

    def g_forward(t):
        g_copy(t, 0, 2, m_x).start()
        g_copy(t, 1, 2, m_y).start()

    def g_rest(t):
        g_copy(t, 1, 0, m_x).wait_recv()
        g_copy(t, 0, 1, m_y).wait_recv()

    def g_far(t):
        g_copy(t, 0, 2, m_d).wait_recv()
        g_copy(t, 1, 2, m_d).wait_recv()

    def g_sent(t):
        for p in (0, 1):
            for way in (0, 1):
                g_copy(t, p, way, m_own).wait_send()
        g_copy(t, 0, 2, m_x).wait_send()
        g_copy(t, 1, 2, m_y).wait_send()

    def rs_c(k):
        return rcp(GP.at[k, :, :, 1 - c], GC.at[k], rcs.at[k], rcr.at[k], dev_c)

    def rs_z(k, way, e, slot):
        return rcp(
            GP.at[k, e, :, c],
            RZ.at[k, slot],
            rzs.at[k, e],
            rzr.at[k, slot],
            dev_r if way == 0 else dev_l,
        )

    def rs_begin(k):
        rs_c(k).wait_recv()
        for e in range(NZ):
            GP[k, e, :, c] = (GP[k, e, :, c].astype(f32) + GC[k, e].astype(f32)).astype(bf16)

        @pl.when(z == 0)
        def _():
            for e in range(NZ - 1, 0, -1):
                rs_z(k, 0, e, e).start()

        @pl.when(z == NZ - 1)
        def _():
            for e in range(NZ - 1):
                rs_z(k, 1, e, e if e < NZ - 2 else 4).start()

    def pass_on(k, way, e, slot):
        rs_z(k, way, e, e).wait_recv()
        GP[k, e, :, c] = (GP[k, e, :, c].astype(f32) + RZ[k, e].astype(f32)).astype(bf16)
        rs_z(k, way, e, slot).start()

    def rs_hop1(k):
        @pl.when(z == 1)
        def _():
            pass_on(k, 0, 3, 3)
            pass_on(k, 0, 2, 2)

        @pl.when(z == 2)
        def _():
            pass_on(k, 1, 0, 0)
            pass_on(k, 1, 1, 4)

    def rs_hop2(k):
        @pl.when(z == 2)
        def _():
            pass_on(k, 0, 3, 3)

        @pl.when(z == 1)
        def _():
            pass_on(k, 1, 0, 4)

    def rs_y(k):
        return rcp(YS.at[k], YR.at[k], rys.at[k], ryr.at[k], dev_y)

    def rs_final(k):
        FS[...] = GP[k, z, :, c].astype(f32)

        @pl.when(z > 0)
        def _():
            rs_z(k, 0, z, z).wait_recv()
            FS[...] += RZ[k, z].astype(f32)

        @pl.when(z < NZ - 1)
        def _():
            rs_z(k, 1, z, 4).wait_recv()
            FS[...] += RZ[k, 4].astype(f32)

        YS[k] = FS[1 - y].astype(bf16)
        rs_y(k).start()
        go_ref[k, y] = FS[y]

    def rs_out(k):
        rs_y(k).wait_recv()
        go_ref[k, 1 - y] = YR[k].astype(f32)

    rturns = iter(range(NK + 4))

    def rs_turn():
        r = next(rturns, None)
        if r is None:
            return
        for s, f in enumerate((rs_begin, rs_hop1, rs_hop2, rs_final, rs_out)):
            if 0 <= r - s < NK:
                f(r - s)

    def rs_sent(k):
        rs_c(k).wait_send()
        for e in range(NZ):

            @pl.when(z != e)
            def _():
                rs_z(k, 0, e, e).wait_send()

        rs_y(k).wait_send()

    def e_copy(t, u, i):
        src, dst, dev = (
            (EXS, EXR, dev_x),
            (EYS, EYR, dev_y),
            (EXS2, EXR2, dev_x),
            (EYS2, EYR2, dev_y),
        )[i]
        return rcp(src.at[t, u], dst.at[t, u], exs.at[t, u, i], exr.at[t, u, i], dev)

    def cols(u, half):
        return pl.ds(half * (width // 2) + u * TILE, TILE)

    def e_first(t, u, P):
        for i in range(2):
            EXS[t, u, i] = P[2 * i + 1 - x, :, cols(u, 0)].astype(bf16)
        e_copy(t, u, 0).start()
        for i in range(2):
            EYS[t, u, i] = P[2 - 2 * y + i, :, cols(u, 1)].astype(bf16)
        e_copy(t, u, 1).start()

    def e_second(t, u, P):
        e_copy(t, u, 0).wait_recv()
        EYS2[t, u] = (P[m_y, :, cols(u, 0)] + EXR[t, u, 1 - y].astype(f32)).astype(bf16)
        e_copy(t, u, 3).start()
        e_copy(t, u, 1).wait_recv()
        EXS2[t, u] = (P[m_x, :, cols(u, 1)] + EYR[t, u, 1 - x].astype(f32)).astype(bf16)
        e_copy(t, u, 2).start()

    def e_last(t, u, P):
        e_copy(t, u, 3).wait_recv()
        P[m_own, :, cols(u, 0)] += EXR[t, u, y].astype(f32) + EYR2[t, u].astype(f32)
        e_copy(t, u, 2).wait_recv()
        P[m_own, :, cols(u, 1)] += EYR[t, u, x].astype(f32) + EXR2[t, u].astype(f32)

    def e_sent(t):
        for u in range(2):
            for i in range(4):
                e_copy(t, u, i).wait_send()

    for k in range(NK):
        own_copy(k).start()
    xf = x_ref[...].astype(f32)
    centred = xf - jnp.mean(xf, axis=-1, keepdims=True)
    rstd = lax.rsqrt(jnp.mean(centred * centred, axis=-1, keepdims=True) + NORM_EPS)
    xhat = centred * rstd
    XH[...] = xhat
    RSTD[...] = jnp.broadcast_to(rstd, RSTD.shape)
    NA[m_own] = (xhat * gain_ref[...] + bias_ref[...]).astype(bf16)

    bucket = bucket_ref[0]
    B[z, y, c, 0:8] = jnp.broadcast_to(bin_ref[...].astype(f32), (8, 128)).astype(bf16)
    B[z, y, c, 8:16] = jnp.full((8, 128), bucket.astype(f32), f32).astype(bf16)

    pl.semaphore_wait(barrier, len(peers))
    for k in order[:3]:
        y_copy(k).start()
    g_send(0)

    slot = lax.shift_right_logical(jnp.int32(rows), bucket)
    shift_of = (rows.bit_length() - 1) - bucket
    row = x * rows + lax.broadcasted_iota(jnp.int32, (rows, 128), 0)
    slot_of = lax.shift_right_logical(row, jnp.full(row.shape, shift_of, jnp.int32))
    place = row & jnp.full(row.shape, slot - 1, jnp.int32)
    limit = jnp.zeros((rows, 128), jnp.int32)
    for s in range(SLOTS):
        limit = jnp.where(slot_of == s, counts_ref[s], limit)
    valid = jnp.where(place < limit, 1.0, 0.0)[:, 0:1]
    seeds = cot_ref[...].astype(f32) * valid
    SA[m_own] = seeds.astype(bf16)
    back_sum = jnp.sum(seeds, axis=0, keepdims=True)
    V[...] = jnp.zeros_like(V)
    for i in range(8):
        V[16 + i : 17 + i, :] = back_sum[:, i * 128 : (i + 1) * 128]
    ag_turn()
    ag_turn()

    lane = lax.broadcasted_iota(jnp.int32, (rows, TILE), 1)
    even = (lane & 1) == 0
    for g in range(2):
        brow = B[z, g, c].astype(f32)[8:9, :]
        ba = jnp.broadcast_to(brow, (rows, 128))

        def pick(ref):
            full = ref[...]
            out = full
            for b in range(1, 4):
                n = rows >> b
                out = jnp.where(ba == float(b), jnp.concatenate([full[:n]] * (1 << b), axis=0), out)
            return out

        cg, sg = pick(cos_ref), pick(sin_ref)
        CT[g] = jnp.concatenate([cg, cg], axis=1)
        SN[g] = jnp.concatenate([sg, sg], axis=1)
        size = jnp.full((rows, 128), rows, jnp.int32)
        for b in range(1, 4):
            size = jnp.where(ba == float(b), rows >> b, size)
        size = jnp.concatenate([size, size], axis=1)
        qi = lax.broadcasted_iota(jnp.int32, (rows, rows), 0)
        ki = lax.broadcasted_iota(jnp.int32, (rows, rows), 1)
        BM[g] = jnp.where((ki <= qi) & ((qi ^ ki) < size), 0.0, MASKED_SCORE)

    def turn(v, g, sign):
        other = jnp.where(even, -pltpu.roll(v, TILE - 1, 1), pltpu.roll(v, 1, 1))
        return v * CT[g] + (sign * other) * SN[g]

    def flip(src, dst, m):
        cs = pl.ds(pl.multiple_of(m * rows, rows), rows)
        for d in range(4):
            dst[d, :, cs] = src[m, :, d * TILE : (d + 1) * TILE].T

    def weight(k):
        return W[k].reshape(width, TILE)

    scale = HD ** (-0.5)

    def attend(m):
        g = m // 2
        nb = NA[m]
        q = turn(dot_nn(nb, weight(2)), g, 1.0).astype(bf16)
        kk = turn(dot_nn(nb, weight(3)), g, 1.0).astype(bf16)
        v = dot_nn(nb, weight(4)).astype(bf16)
        da = dot_nn(SA[m], weight(5)).astype(bf16)
        QR[...] = q
        KR[...] = kk
        VR[...] = v
        DA[...] = da
        zero = jnp.zeros((rows, TILE), bf16)

        def head(h, acc):
            att, dq, dk, dv = acc
            mine = (lane // HD) == h
            qh = jnp.where(mine, QR[...], zero)
            kh = jnp.where(mine, KR[...], zero)
            vh = jnp.where(mine, VR[...], zero)
            dh = jnp.where(mine, DA[...], zero)
            s = dot_nt(qh, KR[...]) * scale + BM[g]
            e = jnp.exp(s - jnp.max(s, axis=-1, keepdims=True))
            p = e * (1.0 / jnp.sum(e, axis=-1, keepdims=True))
            pb = p.astype(bf16)
            att += dot_nn(pb, vh)
            pg = dot_nt(dh, VR[...])
            sg = p * (pg - jnp.sum(p * pg, axis=-1, keepdims=True))
            sb = sg.astype(bf16)
            dv += dot_tn(pb, dh)
            dq += dot_nn(sb, kh)
            dk += dot_tn(sb, qh)
            return att, dq, dk, dv

        none = jnp.zeros((rows, TILE), f32)
        acc = lax.fori_loop(0, N_HEADS // 2, head, (none,) * 4)
        ag_turn()
        att, dq, dk, dv = lax.fori_loop(N_HEADS // 2, N_HEADS, head, acc)
        at = att.astype(bf16)
        dqb = turn(dq * scale, g, -1.0).astype(bf16)
        dkb = turn(dk * scale, g, -1.0).astype(bf16)
        dvb = dv.astype(bf16)
        rs = pl.ds(pl.multiple_of(m * rows, rows), rows)
        ATT[rs, :] = at
        DQ[rs, :] = dqb
        DK[rs, :] = dkb
        DV[rs, :] = dvb
        OUT[m] += dot_nt(at, weight(5))
        DN[m] += dot_nt(dqb, weight(2)) + dot_nt(dkb, weight(3)) + dot_nt(dvb, weight(4))

    def grad_of(k, left, right):
        def block(d, _):
            GP[k, d] = dot_nn(left[d], right[...]).astype(bf16).reshape(2, 2, 64, TILE)
            return 0

        lax.fori_loop(0, 4, block, 0)
        rs_c(k).start()

    def slice_of(j):
        return (0, 1) if j == 0 else (NQ + 2 * j, NQ + 1 + 2 * j)

    def feed(j, m, first=False):
        ki, kb = slice_of(j)
        b0 = B[2 * y + j // 2, j % 2, 0].astype(f32)[0:1, :]
        b1 = B[2 * y + j // 2, j % 2, 1].astype(f32)[0:1, :]
        u = dot_nn(NA[m], weight(ki)) + jnp.concatenate([b0, b1], axis=1)
        u2 = u * u
        k0 = float(np.sqrt(2.0 / np.pi))
        t = jnp.tanh(k0 * u * (1.0 + 0.044715 * u2))
        act = (0.5 * u * (1.0 + t)).astype(bf16)
        slope = 0.5 * (1.0 + t) + (0.5 * k0) * u * (1.0 - t * t) * (1.0 + 0.134145 * u2)
        hg = (dot_nn(SA[m], weight(kb)) * slope).astype(bf16)
        rs = pl.ds(pl.multiple_of(m * rows, rows), rows)
        ACT[rs, :] = act
        HG[rs, :] = hg
        out, dn = dot_nt(act, weight(kb)), dot_nt(hg, weight(ki))
        if first:
            OUT[m] = out
            DN[m] = dn
        else:
            OUT[m] += out
            DN[m] += dn
        at = 24 + x * 16 + y * 8 + 2 * j
        total = jnp.sum(hg.astype(f32), axis=0, keepdims=True)
        V[pl.ds(at, 1), :] += total[:, :128]
        V[pl.ds(at + 1, 1), :] += total[:, 128:]

    def feed_grads(j):
        ki, kb = slice_of(j)
        grad_of(ki, NT, HG)
        grad_of(kb, ST, ACT)

    def feed_rows(j):
        for i in (0, 1):
            lax.fori_loop(2 * i, 2 * i + 2, lambda m, _: (feed(j, m), 0)[1], 0)
            ag_turn()

    def arrived(*chunks):
        for k in chunks:
            ag_done(k)

    flip(NA, NT, m_own)
    flip(SA, ST, m_own)
    ag_turn()
    g_near(0)
    g_send(1)
    g_forward(0)
    ag_turn()
    ag_turn()
    ag_turn()
    arrived(NK, 0, 1)
    feed(0, m_own, True)
    g_rest(0)
    flip(NA, NT, m_x)
    flip(NA, NT, m_y)
    ag_turn()
    g_near(1)
    g_forward(1)
    g_rest(1)
    feed(0, m_x, True)
    feed(0, m_y, True)
    flip(SA, ST, m_x)
    flip(SA, ST, m_y)
    ag_turn()
    ag_turn()
    ag_turn()
    arrived(2, 3, 4, 5)
    attend(m_own)
    ag_turn()
    attend(m_x)
    g_far(0)
    flip(NA, NT, m_d)
    attend(m_y)
    g_far(1)
    flip(SA, ST, m_d)
    feed(0, m_d, True)
    feed_grads(0)
    attend(m_d)
    ag_turn()
    rs_turn()
    grad_of(2, NT, DQ)
    grad_of(3, NT, DK)
    rs_turn()
    grad_of(4, NT, DV)
    grad_of(5, ST, ATT)
    ag_turn()
    rs_turn()
    arrived(6, 7)
    feed_rows(1)
    rs_turn()
    feed_grads(1)
    rs_turn()
    arrived(8, 9)
    feed_rows(2)
    rs_turn()
    feed_grads(2)
    rs_turn()
    ag_turn()
    ag_turn()
    arrived(10, 11)
    feed_rows(3)
    rs_turn()

    for t, P in ((0, OUT), (1, DN)):
        for u in range(2):
            e_first(t, u, P)

    def later(f):
        lax.fori_loop(0, NK, lambda k, _: (f(k), 0)[1], 0)

    feed_grads(3)
    rs_turn()
    e_second(0, 0, OUT)
    rs_turn()
    e_second(0, 1, OUT)
    rs_turn()
    rs_turn()
    e_second(1, 0, DN)
    rs_turn()
    e_second(1, 1, DN)
    for _ in range(NK + 4):
        rs_turn()
    for t, P in ((0, OUT), (1, DN)):
        for u in range(2):
            e_last(t, u, P)
    block_ref[...] = (x_ref[...].astype(f32) + OUT[m_own] + bback_ref[...]).astype(bf16)
    dn = DN[m_own]
    xhat = XH[...]
    e = dn * gain_ref[...]
    me = jnp.mean(e, axis=-1, keepdims=True)
    mex = jnp.mean(e * xhat, axis=-1, keepdims=True)
    gin_ref[...] = (SA[m_own].astype(f32) + RSTD[:, 0:1] * (e - me - xhat * mex)).astype(bf16)
    gsum = jnp.sum(dn * xhat, axis=0, keepdims=True)
    bsum = jnp.sum(dn, axis=0, keepdims=True)
    for i in range(8):
        V[i : i + 1, :] = gsum[:, i * 128 : (i + 1) * 128]
        V[8 + i : 9 + i, :] = bsum[:, i * 128 : (i + 1) * 128]

    def v_copy(i, dev):
        return rcp(VS.at[min(i, 3)], VRV.at[i], vs.at[i], vr.at[i], dev)

    VS[0] = V[...]
    for i, dev in enumerate((dev_c, dev_x, dev_y)):
        v_copy(i, dev).start()
        v_copy(i, dev).wait_recv()
        VS[i + 1] = VS[i] + VRV[i]
    for i, dev in enumerate(dev_z):
        v_copy(3 + i, dev).start()
    for i, dev in enumerate(dev_z):
        v_copy(3 + i, dev).wait_recv()
    V[...] = VS[3] + VRV[3] + VRV[4] + VRV[5]
    index = 2 * dp + x
    lane4 = lax.rem(index, 4)
    for base, ref in ((0, lng_ref), (8, lnb_ref), (16, bbk_ref)):
        line = V[pl.ds(base + index // 4, 1), :]
        out = line[:, 0:32]
        for n in range(1, 4):
            out = jnp.where(lane4 == n, line[:, 32 * n : 32 * n + 32], out)
        ref[...] = out
    gbin_ref[...] = V[pl.ds(24 + 16 * x + dp, 1), :]

    for k in range(NK + 1):
        ag_sent(k)
    for t in range(2):
        g_sent(t)
        e_sent(t)
    later(rs_sent)
    for i, dev in enumerate([dev_c, dev_x, dev_y] + dev_z):
        v_copy(i, dev).wait_send()


def rope_constants(rows):
    half = np.arange(ROT // 2, dtype=np.float32)
    rates = (10000.0 ** (-2.0 * half / ROT)).astype(np.float32)
    angle = np.arange(rows, dtype=np.float32)[:, None] * rates[None, :]
    angle = np.repeat(angle, 2, axis=1)
    cos = np.concatenate([np.cos(angle), np.ones((rows, HD - ROT))], axis=1)
    sin = np.concatenate([np.sin(angle), np.zeros((rows, HD - ROT))], axis=1)
    two = lambda t: np.concatenate([t, t], axis=1).astype(np.float32)
    return two(cos), two(sin)


def on_quad(
    residual_in,
    cotangent,
    ln_gain,
    ln_bias,
    w_qkv,
    w_out,
    w_in,
    b_in,
    w_back,
    b_back,
    bucket_ids,
    residue_counts,
):
    rows, width = residual_in.shape
    cos, sin = rope_constants(rows)
    f32, bf16 = jnp.float32, jnp.bfloat16
    vm = pl.BlockSpec(memory_space=pltpu.VMEM)
    sm = pl.BlockSpec(memory_space=pltpu.SMEM)
    anyspace = pl.BlockSpec(memory_space=pl.ANY)
    shard = width // (4 * NZ)
    sem = pltpu.SemaphoreType.DMA
    block = (2, 2, rows, TILE)
    outs = pl.pallas_call(
        layer_kernel,
        out_shape=(
            jax.ShapeDtypeStruct((rows, width), bf16),
            jax.ShapeDtypeStruct((rows, width), bf16),
            jax.ShapeDtypeStruct((NK, 2, shard, TILE), f32),
            jax.ShapeDtypeStruct((1, 32), f32),
            jax.ShapeDtypeStruct((1, 32), f32),
            jax.ShapeDtypeStruct((1, 32), f32),
            jax.ShapeDtypeStruct((1, 128), f32),
        ),
        in_specs=[sm, sm] + [vm] * 8 + [anyspace] * 4,
        out_specs=(vm,) * 7,
        scratch_shapes=[
            pltpu.VMEM((NZ, 2, 2, 16, 128), bf16),
            pltpu.VMEM((NK, NZ, 2, 2, shard, TILE), bf16),
            pltpu.VMEM((4, rows, width), bf16),
            pltpu.VMEM((4, rows, width), bf16),
            pltpu.VMEM((4, TILE, 4 * rows), bf16),
            pltpu.VMEM((4, TILE, 4 * rows), bf16),
            pltpu.VMEM((2, rows, TILE), f32),
            pltpu.VMEM((2, rows, TILE), f32),
            pltpu.VMEM((2, rows, rows), f32),
            pltpu.VMEM((rows, TILE), bf16),
            pltpu.VMEM((rows, TILE), bf16),
            pltpu.VMEM((rows, TILE), bf16),
            pltpu.VMEM((4 * rows, TILE), bf16),
            pltpu.VMEM((4 * rows, TILE), bf16),
            pltpu.VMEM((4 * rows, TILE), bf16),
            pltpu.VMEM((4 * rows, TILE), bf16),
            pltpu.VMEM((rows, TILE), bf16),
            pltpu.VMEM((4 * rows, TILE), bf16),
            pltpu.VMEM((4 * rows, TILE), bf16),
            pltpu.VMEM((4, rows, width), f32),
            pltpu.VMEM((4, rows, width), f32),
            pltpu.VMEM((NK, NZ, 2, 2, shard, TILE), bf16),
            pltpu.VMEM((NK, NZ, 2, shard, TILE), bf16),
            pltpu.VMEM((NK, 5, 2, shard, TILE), bf16),
            pltpu.VMEM((2, shard, TILE), f32),
            pltpu.VMEM((NK, shard, TILE), bf16),
            pltpu.VMEM((NK, shard, TILE), bf16),
            pltpu.VMEM((rows, width), f32),
            pltpu.VMEM((rows, 128), f32),
            pltpu.VMEM((2,) + block, bf16),
            pltpu.VMEM((2,) + block, bf16),
            pltpu.VMEM((2,) + block, bf16),
            pltpu.VMEM((2,) + block, bf16),
            pltpu.VMEM((2, 2, rows, TILE), bf16),
            pltpu.VMEM((2, 2, rows, TILE), bf16),
            pltpu.VMEM((2, 2, rows, TILE), bf16),
            pltpu.VMEM((2, 2, rows, TILE), bf16),
            pltpu.VMEM((VROWS, 128), f32),
            pltpu.VMEM((4, VROWS, 128), f32),
            pltpu.VMEM((6, VROWS, 128), f32),
            sem((NK,)),
            sem((NK + 1,)),
            sem((NK + 1,)),
            sem((NK + 1, 2, 3)),
            sem((NK + 1, 2, 3)),
            sem((NK + 1, NZ)),
            sem((NK + 1, NZ)),
            sem((12,)),
            sem((12,)),
            sem((NK,)),
            sem((NK,)),
            sem((NK, NZ)),
            sem((NK, 5)),
            sem((NK,)),
            sem((NK,)),
            sem((2, 2, 4)),
            sem((2, 2, 4)),
            sem((6,)),
            sem((6,)),
        ],
        compiler_params=pltpu.CompilerParams(
            collective_id=0, has_side_effects=True, vmem_limit_bytes=63 << 20
        ),
        cost_estimate=pl.CostEstimate(
            flops=20 * 2**30, bytes_accessed=8 * 2**20, transcendentals=2**21
        ),
    )(
        bucket_ids,
        residue_counts.reshape(SLOTS),
        residual_in,
        cotangent,
        ln_gain.reshape(1, width),
        ln_bias.reshape(1, width),
        b_back.reshape(1, width),
        jnp.asarray(cos),
        jnp.asarray(sin),
        b_in.reshape(1, 128),
        w_qkv,
        w_out.T,
        w_in,
        w_back.T,
    )
    block_out, grad_input, go, lng, lnb, bbk, gbin = outs
    half = 2 * TILE
    grad_w_qkv = go[2:5].transpose(0, 2, 1, 3).reshape(3, shard, half)
    grad_w_out = go[5].transpose(0, 2, 1).reshape(half, shard)
    gi = jnp.concatenate([go[0:1], go[6::2]])
    gb = jnp.concatenate([go[1:2], go[7::2]])
    grad_w_in = gi.transpose(2, 1, 0, 3).reshape(shard, NJ * half)
    grad_w_back = gb.transpose(1, 0, 3, 2).reshape(NJ * half, shard)
    return (
        block_out,
        grad_input,
        lng.reshape(32),
        lnb.reshape(32),
        grad_w_qkv,
        grad_w_out,
        grad_w_in,
        gbin.reshape(128),
        grad_w_back,
        bbk.reshape(32),
    )


def solution(mesh):
    placed = (
        P(("dp", "mp"), None),
        P(("dp", "mp"), None),
        P(),
        P(),
        P(None, "dp", "mp"),
        P("mp", "dp"),
        P("dp", "mp"),
        P(("mp", "dp")),
        P("mp", "dp"),
        P(),
        P("dp"),
        P("dp", None),
    )
    return jax.shard_map(
        on_quad if fits_quad(mesh) else on_device,
        mesh=mesh,
        in_specs=placed,
        out_specs=(
            P(("dp", "mp"), None),
            P(("dp", "mp"), None),
            P(("dp", "mp")),
            P(("dp", "mp")),
            P(None, "dp", "mp"),
            P("mp", "dp"),
            P("dp", "mp"),
            P(("mp", "dp")),
            P("mp", "dp"),
            P(("dp", "mp")),
        ),
        check_vma=False,
    )
```

```python
from functools import partial

import jax
import jax.numpy as jnp
import numpy as np
from jax import lax
from jax.experimental import pallas as pl
from jax.experimental.pallas import tpu as pltpu
from jax.sharding import PartitionSpec as P

HD = 64
ROT = 32
SLOTS = 16


NORM_EPS = 1e-05
MASKED_SCORE = -1e30


def norm_rows(inputs_now, norm_gain, norm_shift):
    centred = inputs_now - jnp.mean(inputs_now, axis=-1, keepdims=True)
    spread = jnp.mean(centred * centred, axis=-1, keepdims=True)
    return centred * lax.rsqrt(spread + NORM_EPS) * norm_gain + norm_shift


def slot_tables(bucket_one, residue_row, group_rows):
    slot_length = jnp.right_shift(jnp.int32(group_rows // 2), bucket_one)
    places = jnp.arange(group_rows, dtype=jnp.int32)
    slot_ids = places // slot_length
    inside = places - slot_ids * slot_length
    match_table = slot_ids[:, None] == jnp.arange(SLOTS, dtype=jnp.int32)[None, :]
    picked = jnp.sum(jnp.where(match_table, residue_row[None, :], 0), axis=1)
    live_rows = jnp.minimum(picked, slot_length)
    return (slot_ids, inside, inside < live_rows)


def rope_tables(inside):
    half_steps = jnp.arange(ROT // 2, dtype=jnp.float32)
    inverse_rates = 10000.0 ** (-2.0 * half_steps / ROT)
    angles = inside.astype(jnp.float32)[:, None] * inverse_rates[None, :]
    return (jnp.cos(angles), jnp.sin(angles))


def rotate(values, cosine_table, sine_table):
    row_count = values.shape[0]
    head_count = values.shape[1]
    paired = values[..., :ROT].reshape(row_count, head_count, ROT // 2, 2)
    even_part = paired[..., 0]
    odd_part = paired[..., 1]
    cosine_now = cosine_table[:, None, :]
    sine_now = sine_table[:, None, :]
    turned = jnp.stack(
        [
            even_part * cosine_now - odd_part * sine_now,
            odd_part * cosine_now + even_part * sine_now,
        ],
        axis=-1,
    )
    return jnp.concatenate([turned.reshape(row_count, head_count, ROT), values[..., ROT:]], axis=-1)


def mask_block(block_start, block_rows, slot_ids):
    query_places = block_start + jnp.arange(block_rows, dtype=jnp.int32)
    query_slots = lax.dynamic_slice_in_dim(slot_ids, block_start, block_rows, 0)
    key_places = jnp.arange(slot_ids.shape[0], dtype=jnp.int32)
    return (query_slots[:, None] == slot_ids[None, :]) & (
        key_places[None, :] <= query_places[:, None]
    )


def over_rows(first_op, second_op):
    return lax.dot_general(
        first_op, second_op, (((0,), (0,)), ((), ())), preferred_element_type=jnp.float32
    )


def against_weight(first_op, second_op):
    return lax.dot_general(
        first_op, second_op, (((1,), (1,)), ((), ())), preferred_element_type=jnp.float32
    )


def on_device(
    residual_in,
    cotangent,
    ln_gain,
    ln_bias,
    w_qkv,
    w_out,
    w_in,
    b_in,
    w_back,
    b_back,
    bucket_ids,
    residue_counts,
):
    model_count = lax.axis_size("mp")
    model_rank = lax.axis_index("mp")
    local_rows = residual_in.shape[0]
    group_rows = local_rows * model_count
    slot_ids, inside, valid_rows = slot_tables(bucket_ids[0], residue_counts[0], group_rows)
    cosine_table, sine_table = rope_tables(inside)
    qkv_all, out_all, in_all, bias_in, back_all = (
        lax.all_gather(w_qkv, "dp", axis=1, tiled=True),
        lax.all_gather(w_out, "dp", axis=1, tiled=True),
        lax.all_gather(w_in, "dp", axis=0, tiled=True),
        lax.all_gather(b_in, "dp", axis=0, tiled=True),
        lax.all_gather(w_back, "dp", axis=1, tiled=True),
    )
    x_local = residual_in.astype(jnp.float32)
    x_group = lax.all_gather(residual_in, "mp", axis=0, tiled=True).astype(jnp.float32)
    normed = norm_rows(x_group, ln_gain, ln_bias).astype(jnp.bfloat16)
    head_width = qkv_all.shape[2]
    head_count = head_width // HD
    score_scale = HD ** (-0.5)

    def project(member_index):
        return jnp.dot(normed, qkv_all[member_index], preferred_element_type=jnp.float32).reshape(
            group_rows, head_count, HD
        )

    queries = rotate(project(0), cosine_table, sine_table).astype(jnp.bfloat16)
    key_rows = rotate(project(1), cosine_table, sine_table).astype(jnp.bfloat16)
    value_rows = project(2).astype(jnp.bfloat16)
    block_rows = min(512, group_rows)
    starts = jnp.arange(group_rows // block_rows, dtype=jnp.int32) * block_rows

    def block_scores(block_start):
        query_block = lax.dynamic_slice_in_dim(queries, block_start, block_rows, 0)
        allowed = mask_block(block_start, block_rows, slot_ids)
        scores = (
            jnp.einsum("qhd,khd->hqk", query_block, key_rows, preferred_element_type=jnp.float32)
            * score_scale
        )
        return (query_block, jnp.where(allowed[None], scores, MASKED_SCORE))

    def forward_block(block_start):
        query_block, scores = block_scores(block_start)
        row_peak = jnp.max(scores, axis=-1, keepdims=True)
        exp_scores = jnp.exp(scores - row_peak)
        row_total = jnp.sum(exp_scores, axis=-1, keepdims=True)
        weights_now = (exp_scores / row_total).astype(jnp.bfloat16)
        attended = jnp.einsum(
            "hqk,khd->qhd", weights_now, value_rows, preferred_element_type=jnp.float32
        )
        return (attended.astype(jnp.bfloat16), (row_peak + jnp.log(row_total))[..., 0])

    attended_blocks, log_totals = lax.map(forward_block, starts)
    mixed_rows = attended_blocks.reshape(group_rows, head_width)
    hidden = jnp.dot(normed, in_all, preferred_element_type=jnp.float32) + bias_in.astype(
        jnp.float32
    )
    gelu_tanh = partial(jax.nn.gelu, approximate=True)
    active_value, gelu_pull = jax.vjp(gelu_tanh, hidden)
    active = active_value.astype(jnp.bfloat16)
    partial_out = jnp.dot(mixed_rows, out_all, preferred_element_type=jnp.float32) + jnp.dot(
        active, back_all, preferred_element_type=jnp.float32
    )
    summed_all = lax.psum(partial_out.astype(jnp.bfloat16), "mp").astype(jnp.float32)
    summed = lax.dynamic_slice_in_dim(summed_all, model_rank * local_rows, local_rows, 0)
    block_out = (x_local + summed + b_back).astype(jnp.bfloat16)
    cot_group = lax.all_gather(cotangent, "mp", axis=0, tiled=True)
    seed_rows = jnp.where(valid_rows[:, None], cot_group, jnp.zeros_like(cot_group))
    qkv_all, out_all, in_all, back_all = (
        lax.all_gather(w_qkv, "dp", axis=1, tiled=True),
        lax.all_gather(w_out, "dp", axis=1, tiled=True),
        lax.all_gather(w_in, "dp", axis=0, tiled=True),
        lax.all_gather(w_back, "dp", axis=1, tiled=True),
    )
    active_grad = against_weight(seed_rows, back_all)
    hidden_grad = gelu_pull(active_grad)[0].astype(jnp.bfloat16)
    grad_in_local = over_rows(normed, hidden_grad)
    grad_bias_in = jnp.sum(hidden_grad.astype(jnp.float32), axis=0)
    grad_back_local = over_rows(active, seed_rows)
    grad_out_local = over_rows(mixed_rows, seed_rows)
    normed_grad = against_weight(hidden_grad, in_all)
    mixed_grad = (
        against_weight(seed_rows, out_all).astype(jnp.bfloat16).reshape(group_rows, head_count, HD)
    )

    def backward_block(carry, inputs_now):
        key_acc, value_acc = carry
        block_start, log_total = inputs_now
        query_block, scores = block_scores(block_start)
        grad_block = lax.dynamic_slice_in_dim(mixed_grad, block_start, block_rows, 0)
        probs = jnp.exp(scores - log_total[..., None])
        probs_low = probs.astype(jnp.bfloat16)
        value_acc = value_acc + jnp.einsum(
            "hqk,qhd->khd", probs_low, grad_block, preferred_element_type=jnp.float32
        )
        probs_grad = jnp.einsum(
            "qhd,khd->hqk", grad_block, value_rows, preferred_element_type=jnp.float32
        )
        score_grad = probs * (probs_grad - jnp.sum(probs * probs_grad, axis=-1, keepdims=True))
        score_low = score_grad.astype(jnp.bfloat16)
        query_grad = (
            jnp.einsum("hqk,khd->qhd", score_low, key_rows, preferred_element_type=jnp.float32)
            * score_scale
        )
        key_acc = (
            key_acc
            + jnp.einsum("hqk,qhd->khd", score_low, query_block, preferred_element_type=jnp.float32)
            * score_scale
        )
        return ((key_acc, value_acc), query_grad)

    empty_heads = jnp.zeros((group_rows, head_count, HD), jnp.float32)
    (key_acc, value_acc), query_blocks = lax.scan(
        backward_block, (empty_heads, empty_heads), (starts, log_totals)
    )
    turn_back = partial(rotate, cosine_table=cosine_table, sine_table=sine_table)
    unturn = jax.vjp(turn_back, empty_heads)[1]
    query_pre_grad = (
        unturn(query_blocks.reshape(group_rows, head_count, HD))[0]
        .astype(jnp.bfloat16)
        .reshape(group_rows, head_width)
    )
    key_pre_grad = unturn(key_acc)[0].astype(jnp.bfloat16).reshape(group_rows, head_width)
    value_grad = value_acc.astype(jnp.bfloat16).reshape(group_rows, head_width)
    grad_qkv_local = jnp.stack(
        [
            over_rows(normed, query_pre_grad),
            over_rows(normed, key_pre_grad),
            over_rows(normed, value_grad),
        ],
        axis=0,
    )
    normed_grad = (
        normed_grad
        + against_weight(query_pre_grad, qkv_all[0])
        + against_weight(key_pre_grad, qkv_all[1])
        + against_weight(value_grad, qkv_all[2])
    )
    share_grad = lax.psum(normed_grad.astype(jnp.bfloat16), "mp").astype(jnp.float32)
    seed_group = seed_rows.astype(jnp.float32)
    norm_pull = jax.vjp(norm_rows, x_group, ln_gain, ln_bias)[1]
    input_part, gain_part, shift_part = norm_pull(share_grad)
    input_group = seed_group + input_part
    grad_input = lax.dynamic_slice_in_dim(
        input_group, model_rank * local_rows, local_rows, 0
    ).astype(jnp.bfloat16)
    back_part = jnp.sum(seed_group, axis=0)
    grad_w_qkv, grad_w_out, grad_w_in, grad_b_in, grad_w_back, gain_rows, shift_rows, back_rows = (
        lax.psum_scatter(
            grad_qkv_local.astype(jnp.bfloat16), "dp", scatter_dimension=1, tiled=True
        ).astype(jnp.float32),
        lax.psum_scatter(
            grad_out_local.astype(jnp.bfloat16), "dp", scatter_dimension=1, tiled=True
        ).astype(jnp.float32),
        lax.psum_scatter(
            grad_in_local.astype(jnp.bfloat16), "dp", scatter_dimension=0, tiled=True
        ).astype(jnp.float32),
        lax.psum_scatter(
            grad_bias_in.astype(jnp.bfloat16), "dp", scatter_dimension=0, tiled=True
        ).astype(jnp.float32),
        lax.psum_scatter(
            grad_back_local.astype(jnp.bfloat16), "dp", scatter_dimension=1, tiled=True
        ).astype(jnp.float32),
        lax.psum_scatter(
            gain_part.astype(jnp.bfloat16), "dp", scatter_dimension=0, tiled=True
        ).astype(jnp.float32),
        lax.psum_scatter(
            shift_part.astype(jnp.bfloat16), "dp", scatter_dimension=0, tiled=True
        ).astype(jnp.float32),
        lax.psum_scatter(
            back_part.astype(jnp.bfloat16), "dp", scatter_dimension=0, tiled=True
        ).astype(jnp.float32),
    )
    piece_width = gain_rows.shape[0] // model_count
    grad_ln_gain = lax.dynamic_slice_in_dim(gain_rows, model_rank * piece_width, piece_width, 0)
    grad_ln_bias = lax.dynamic_slice_in_dim(shift_rows, model_rank * piece_width, piece_width, 0)
    grad_b_back = lax.dynamic_slice_in_dim(back_rows, model_rank * piece_width, piece_width, 0)
    return (
        block_out,
        grad_input,
        grad_ln_gain,
        grad_ln_bias,
        grad_w_qkv,
        grad_w_out,
        grad_w_in,
        grad_b_in,
        grad_w_back,
        grad_b_back,
    )


MESH = pl.DeviceIdType.MESH
NZ = 4
TILE = 256
N_HEADS = TILE // HD
NQ = 4
NJ = 4
NK = NQ + 2 * NJ
VROWS = 56


def fits_quad(mesh):
    return mesh.shape["mp"] == 2 and mesh.shape["dp"] == 4 * NZ


def dot_nn(a, b):
    return lax.dot_general(a, b, (((1,), (0,)), ((), ())), preferred_element_type=jnp.float32)


def dot_nt(a, b):
    return lax.dot_general(a, b, (((1,), (1,)), ((), ())), preferred_element_type=jnp.float32)


def dot_tn(a, b):
    return lax.dot_general(a, b, (((0,), (0,)), ((), ())), preferred_element_type=jnp.float32)


def layer_kernel(
    bucket_ref,
    counts_ref,
    x_ref,
    cot_ref,
    gain_ref,
    bias_ref,
    bback_ref,
    cos_ref,
    sin_ref,
    bin_ref,
    wqkv_ref,
    wot_ref,
    win_ref,
    wbt_ref,
    block_ref,
    gin_ref,
    gqkv_ref,
    got_ref,
    gi_ref,
    gbt_ref,
    lng_ref,
    lnb_ref,
    bbk_ref,
    gbin_ref,
    B,
    W,
    NA,
    SA,
    NT,
    ST,
    CT,
    SN,
    BM,
    QR,
    KR,
    VR,
    DQ,
    DK,
    DV,
    ATT,
    ACT,
    HG,
    OUT,
    DN,
    GP,
    GC,
    RZ,
    FS,
    YS,
    YR,
    XH,
    RSTD,
    EXS,
    EYS,
    EXR,
    EYR,
    EXS2,
    EYS2,
    EXR2,
    EYR2,
    V,
    VS,
    VRV,
    loc_sem,
    ays,
    ayr,
    azs,
    azr,
    acs,
    acr,
    gs,
    gr,
    rcs,
    rcr,
    rzs,
    rzr,
    rys,
    ryr,
    exs,
    exr,
    vs,
    vr,
):
    f32, bf16 = jnp.float32, jnp.bfloat16
    dp, x = lax.axis_index("dp"), lax.axis_index("mp")
    z = dp // 4
    y = lax.rem(dp // 2, 2)
    c = lax.rem(dp, 2)
    rows = x_ref.shape[0]
    width = x_ref.shape[1]
    dev_x = (dp, 1 - x)
    dev_y = (dp + 2 - 4 * y, x)
    dev_c = (dp + 1 - 2 * c, x)
    dev_r = (lax.rem(dp + 4, 4 * NZ), x)
    dev_l = (lax.rem(dp + 4 * NZ - 4, 4 * NZ), x)
    dev_z = [(lax.rem(dp + 4 * i, 4 * NZ), x) for i in (1, 2, 3)]
    m_own = 2 * y + x
    m_x = 2 * y + 1 - x
    m_y = 2 - 2 * y + x
    m_d = 3 - m_own

    def rcp(src, dst, ss, rs, dev):
        return pltpu.make_async_remote_copy(
            src_ref=src, dst_ref=dst, send_sem=ss, recv_sem=rs, device_id=dev, device_id_type=MESH
        )

    barrier = pltpu.get_barrier_semaphore()
    peers = [dev_x, dev_y, dev_c] + dev_z
    for peer in peers:
        pl.semaphore_signal(barrier, inc=1, device_id=peer, device_id_type=MESH)

    def wsrc(k, q):
        if k == NK:
            return None
        if k < 3:
            return wqkv_ref.at[k, :, pl.ds(pl.multiple_of(q * TILE, TILE), TILE)]
        if k == 3:
            return wot_ref.at[:, pl.ds(pl.multiple_of(q * TILE, TILE), TILE)]
        ref = win_ref if k % 2 == 0 else wbt_ref
        j = (k - NQ) // 2
        return ref.at[:, pl.ds(pl.multiple_of(q * (NJ * TILE) + j * TILE, TILE), TILE)]

    def wv(k):
        return B if isinstance(k, int) and k == NK else W.at[k]

    def own_copy(k):
        return pltpu.make_async_copy(wsrc(k, y), W.at[k, z, y, c], loc_sem.at[k])

    def y_copy(k):
        if k == NK:
            return rcp(B.at[z, y, c], B.at[z, y, c], ays.at[k], ayr.at[k], dev_y)
        return rcp(wsrc(k, 1 - y), W.at[k, z, y, c], ays.at[k], ayr.at[k], dev_y)

    def y_arrived(k):
        here = wv(k).at[z, 1 - y, c]
        rcp(here, here, ays.at[k], ayr.at[k], dev_y).wait_recv()

    def z_copy(k, way, s, e):
        block = wv(k).at[e, :, c]
        return rcp(
            block, block, azs.at[k, way, s], azr.at[k, way, s], dev_r if way == 0 else dev_l
        )

    def c_copy(k, e):
        block = wv(k).at[e, :, c]
        return rcp(block, block, acs.at[k, e], acr.at[k, e], dev_c)

    def ag_own(k, copied=True):
        if copied:
            pltpu.make_async_copy(
                W.at[k, z, y, c], W.at[k, z, y, c], loc_sem.at[k]
            ).wait()
        y_arrived(k)

        @pl.when(z < NZ - 1)
        def _():
            z_copy(k, 0, 0, z).start()

        @pl.when(z > 0)
        def _():
            z_copy(k, 1, 0, z).start()

        c_copy(k, z).start()

    def ag_step(k, s):
        @pl.when(z - 1 - s >= 0)
        def _():
            e = z - 1 - s
            z_copy(k, 0, s, e).wait_recv()
            if s < NZ - 2:

                @pl.when(z < NZ - 1)
                def _():
                    z_copy(k, 0, s + 1, e).start()

            c_copy(k, e).start()

        @pl.when(z + 1 + s <= NZ - 1)
        def _():
            e = z + 1 + s
            z_copy(k, 1, s, e).wait_recv()
            if s < NZ - 2:

                @pl.when(z > 0)
                def _():
                    z_copy(k, 1, s + 1, e).start()

            c_copy(k, e).start()

    def ag_done(k):
        for e in range(NZ):
            block = wv(k).at[e, :, 1 - c]
            rcp(block, block, acs.at[k, e], acr.at[k, e], dev_c).wait_recv()

    def ag_sent(k, copied=True):
        y_copy(k).wait_send() if isinstance(k, int) else None
        for s in range(NZ - 1):

            @pl.when((z < NZ - 1) & (z - s >= 0))
            def _():
                z_copy(k, 0, s, z - s).wait_send()

            @pl.when((z > 0) & (z + s <= NZ - 1))
            def _():
                z_copy(k, 1, s, z + s).wait_send()

        for e in range(NZ):
            c_copy(k, e).wait_send()

    order = [NK] + list(range(NK))
    turns = iter(range(NK + NZ))

    def ag_turn():
        t = next(turns, None)
        if t is None:
            return
        if t + 3 <= NK:
            y_copy(order[t + 3]).start()
        if t <= NK:
            ag_own(order[t], copied=t > 0)
        for s in range(NZ - 1):
            if 0 <= t - 1 - s <= NK:
                ag_step(order[t - 1 - s], s)

    P0 = 64
    parts = (pl.ds(0, P0), pl.ds(P0, rows - P0))
    BUF = (NA, SA)

    def g_copy(t, p, way, m):
        block = BUF[t].at[m, parts[p]]
        i = (t * 2 + p) * 3 + way
        dev = (dev_x, dev_y)[way] if way < 2 else (dev_y, dev_x)[p]
        return rcp(block, block, gs.at[i], gr.at[i], dev)

    def g_send(t):
        g_copy(t, 0, 0, m_own).start()
        g_copy(t, 1, 1, m_own).start()
        g_copy(t, 1, 0, m_own).start()
        g_copy(t, 0, 1, m_own).start()

    def g_near(t):
        g_copy(t, 0, 0, m_x).wait_recv()
        g_copy(t, 1, 1, m_y).wait_recv()

    def g_forward(t):
        g_copy(t, 0, 2, m_x).start()
        g_copy(t, 1, 2, m_y).start()

    def g_rest(t):
        g_copy(t, 1, 0, m_x).wait_recv()
        g_copy(t, 0, 1, m_y).wait_recv()

    def g_far(t):
        g_copy(t, 0, 2, m_d).wait_recv()
        g_copy(t, 1, 2, m_d).wait_recv()

    def g_sent(t):
        for p in (0, 1):
            for way in (0, 1):
                g_copy(t, p, way, m_own).wait_send()
        g_copy(t, 0, 2, m_x).wait_send()
        g_copy(t, 1, 2, m_y).wait_send()

    def rs_c(k):
        return rcp(GP.at[k, :, :, 1 - c], GC.at[k], rcs.at[k], rcr.at[k], dev_c)

    def rs_z(k, way, e, slot):
        return rcp(
            GP.at[k, e, :, c],
            RZ.at[k, slot],
            rzs.at[k, e],
            rzr.at[k, slot],
            dev_r if way == 0 else dev_l,
        )

    def rs_begin(k):
        rs_c(k).wait_recv()
        for e in range(NZ):
            GP[k, e, :, c] = (GP[k, e, :, c].astype(f32) + GC[k, e].astype(f32)).astype(bf16)

        @pl.when(z == 0)
        def _():
            for e in range(NZ - 1, 0, -1):
                rs_z(k, 0, e, e).start()

        @pl.when(z == NZ - 1)
        def _():
            for e in range(NZ - 1):
                rs_z(k, 1, e, e if e < NZ - 2 else 4).start()

    def pass_on(k, way, e, slot):
        rs_z(k, way, e, e).wait_recv()
        GP[k, e, :, c] = (GP[k, e, :, c].astype(f32) + RZ[k, e].astype(f32)).astype(bf16)
        rs_z(k, way, e, slot).start()

    def rs_hop1(k):
        @pl.when(z == 1)
        def _():
            pass_on(k, 0, 3, 3)
            pass_on(k, 0, 2, 2)

        @pl.when(z == 2)
        def _():
            pass_on(k, 1, 0, 0)
            pass_on(k, 1, 1, 4)

    def rs_hop2(k):
        @pl.when(z == 2)
        def _():
            pass_on(k, 0, 3, 3)

        @pl.when(z == 1)
        def _():
            pass_on(k, 1, 0, 4)

    def rs_y(k):
        return rcp(YS.at[k], YR.at[k], rys.at[k], ryr.at[k], dev_y)

    def put(k, q, value):
        if k < 3:
            gqkv_ref[k, :, pl.ds(pl.multiple_of(q * TILE, TILE), TILE)] = value
        elif k == 3:
            got_ref[:, pl.ds(pl.multiple_of(q * TILE, TILE), TILE)] = value
        else:
            ref = gi_ref if k % 2 == 0 else gbt_ref
            j = (k - NQ) // 2
            ref[:, pl.ds(pl.multiple_of(q * (NJ * TILE) + j * TILE, TILE), TILE)] = value

    def rs_final(k):
        FS[...] = GP[k, z, :, c].astype(f32)

        @pl.when(z > 0)
        def _():
            rs_z(k, 0, z, z).wait_recv()
            FS[...] += RZ[k, z].astype(f32)

        @pl.when(z < NZ - 1)
        def _():
            rs_z(k, 1, z, 4).wait_recv()
            FS[...] += RZ[k, 4].astype(f32)

        YS[k] = FS[1 - y].astype(bf16)
        rs_y(k).start()
        put(k, y, FS[y])

    def rs_out(k):
        rs_y(k).wait_recv()
        put(k, 1 - y, YR[k].astype(f32))

    rturns = iter(range(NK + 4))

    def rs_turn():
        r = next(rturns, None)
        if r is None:
            return
        for s, f in enumerate((rs_begin, rs_hop1, rs_hop2, rs_final, rs_out)):
            if 0 <= r - s < NK:
                f(r - s)

    def rs_sent(k):
        rs_c(k).wait_send()
        for e in range(NZ):

            @pl.when(z != e)
            def _():
                rs_z(k, 0, e, e).wait_send()

        rs_y(k).wait_send()

    def e_copy(t, u, i):
        src, dst, dev = (
            (EXS, EXR, dev_x),
            (EYS, EYR, dev_y),
            (EXS2, EXR2, dev_x),
            (EYS2, EYR2, dev_y),
        )[i]
        return rcp(src.at[t, u], dst.at[t, u], exs.at[t, u, i], exr.at[t, u, i], dev)

    def cols(u, half):
        return pl.ds(half * (width // 2) + u * TILE, TILE)

    def e_first(t, u, P):
        for i in range(2):
            EXS[t, u, i] = P[2 * i + 1 - x, :, cols(u, 0)].astype(bf16)
        e_copy(t, u, 0).start()
        for i in range(2):
            EYS[t, u, i] = P[2 - 2 * y + i, :, cols(u, 1)].astype(bf16)
        e_copy(t, u, 1).start()

    def e_second(t, u, P):
        e_copy(t, u, 0).wait_recv()
        EYS2[t, u] = (P[m_y, :, cols(u, 0)] + EXR[t, u, 1 - y].astype(f32)).astype(bf16)
        e_copy(t, u, 3).start()
        e_copy(t, u, 1).wait_recv()
        EXS2[t, u] = (P[m_x, :, cols(u, 1)] + EYR[t, u, 1 - x].astype(f32)).astype(bf16)
        e_copy(t, u, 2).start()

    def e_last(t, u, P):
        e_copy(t, u, 3).wait_recv()
        P[m_own, :, cols(u, 0)] += EXR[t, u, y].astype(f32) + EYR2[t, u].astype(f32)
        e_copy(t, u, 2).wait_recv()
        P[m_own, :, cols(u, 1)] += EYR[t, u, x].astype(f32) + EXR2[t, u].astype(f32)

    def e_sent(t):
        for u in range(2):
            for i in range(4):
                e_copy(t, u, i).wait_send()

    for k in range(NK):
        own_copy(k).start()
    xf = x_ref[...].astype(f32)
    centred = xf - jnp.mean(xf, axis=-1, keepdims=True)
    rstd = lax.rsqrt(jnp.mean(centred * centred, axis=-1, keepdims=True) + NORM_EPS)
    xhat = centred * rstd
    XH[...] = xhat
    RSTD[...] = jnp.broadcast_to(rstd, RSTD.shape)
    NA[m_own] = (xhat * gain_ref[...] + bias_ref[...]).astype(bf16)

    bucket = bucket_ref[0]
    B[z, y, c, 0:8] = jnp.broadcast_to(bin_ref[...].astype(f32), (8, 128)).astype(bf16)
    B[z, y, c, 8:16] = jnp.full((8, 128), bucket.astype(f32), f32).astype(bf16)

    pl.semaphore_wait(barrier, len(peers))
    for k in order[:3]:
        y_copy(k).start()
    g_send(0)

    slot = lax.shift_right_logical(jnp.int32(rows), bucket)
    shift_of = (rows.bit_length() - 1) - bucket
    row = x * rows + lax.broadcasted_iota(jnp.int32, (rows, 128), 0)
    slot_of = lax.shift_right_logical(row, jnp.full(row.shape, shift_of, jnp.int32))
    place = row & jnp.full(row.shape, slot - 1, jnp.int32)
    limit = jnp.zeros((rows, 128), jnp.int32)
    for s in range(SLOTS):
        limit = jnp.where(slot_of == s, counts_ref[s], limit)
    valid = jnp.where(place < limit, 1.0, 0.0)[:, 0:1]
    seeds = cot_ref[...].astype(f32) * valid
    SA[m_own] = seeds.astype(bf16)
    back_sum = jnp.sum(seeds, axis=0, keepdims=True)
    V[...] = jnp.zeros_like(V)
    for i in range(8):
        V[16 + i : 17 + i, :] = back_sum[:, i * 128 : (i + 1) * 128]
    ag_turn()
    ag_turn()

    lane = lax.broadcasted_iota(jnp.int32, (rows, TILE), 1)
    even = (lane & 1) == 0

    def table(g):
        brow = B[z, g, c].astype(f32)[8:9, :]
        ba = jnp.broadcast_to(brow, (rows, 128))

        def pick(ref):
            full = ref[...]
            out = full
            for b in range(1, 4):
                n = rows >> b
                out = jnp.where(ba == float(b), jnp.concatenate([full[:n]] * (1 << b), axis=0), out)
            return out

        cg, sg = pick(cos_ref), pick(sin_ref)
        CT[g] = jnp.concatenate([cg, cg], axis=1)
        SN[g] = jnp.concatenate([sg, sg], axis=1)
        size = jnp.full((rows, 128), rows, jnp.int32)
        for b in range(1, 4):
            size = jnp.where(ba == float(b), rows >> b, size)
        size = jnp.concatenate([size, size], axis=1)
        qi = lax.broadcasted_iota(jnp.int32, (rows, rows), 0)
        ki = lax.broadcasted_iota(jnp.int32, (rows, rows), 1)
        BM[g] = jnp.where((ki <= qi) & ((qi ^ ki) < size), 0.0, MASKED_SCORE)

    def tables():
        for g in range(2):
            table(g)

    def turn(v, g, sign):
        other = jnp.where(even, -pltpu.roll(v, TILE - 1, 1), pltpu.roll(v, 1, 1))
        return v * CT[g] + (sign * other) * SN[g]

    def flip(src, dst, m):
        cs = pl.ds(pl.multiple_of(m * rows, rows), rows)
        for d in range(4):
            dst[d, :, cs] = src[m, :, d * TILE : (d + 1) * TILE].T

    def weight(k):
        return W[k].reshape(width, TILE)

    scale = HD ** (-0.5)

    def project(m):
        g = m // 2
        nb = NA[m]
        QR[m] = turn(dot_nn(nb, weight(0)), g, 1.0).astype(bf16)
        KR[m] = turn(dot_nn(nb, weight(1)), g, 1.0).astype(bf16)
        VR[m] = dot_nn(nb, weight(2)).astype(bf16)

    def attend(m):
        g = m // 2
        q, kk, v = QR[m], KR[m], VR[m]
        da = dot_nn(SA[m], weight(3)).astype(bf16)
        zero = jnp.zeros((rows, TILE), bf16)
        att = dq = dk = dv = None
        for h in range(N_HEADS):
            mine = (lane // HD) == h
            qh = jnp.where(mine, q, zero)
            kh = jnp.where(mine, kk, zero)
            vh = jnp.where(mine, v, zero)
            dh = jnp.where(mine, da, zero)
            s = dot_nt(qh, kk) * scale + BM[g]
            e = jnp.exp(s - jnp.max(s, axis=-1, keepdims=True))
            p = e * (1.0 / jnp.sum(e, axis=-1, keepdims=True))
            pb = p.astype(bf16)
            pg = dot_nt(dh, v)
            sg = p * (pg - jnp.sum(p * pg, axis=-1, keepdims=True))
            sb = sg.astype(bf16)
            now = (dot_nn(pb, vh), dot_nn(sb, kh), dot_tn(sb, qh), dot_tn(pb, dh))
            if h == 0:
                att, dq, dk, dv = now
            else:
                att, dq, dk, dv = (a + b for a, b in zip((att, dq, dk, dv), now))
        at = att.astype(bf16)
        dqb = turn(dq * scale, g, -1.0).astype(bf16)
        dkb = turn(dk * scale, g, -1.0).astype(bf16)
        dvb = dv.astype(bf16)
        rs = pl.ds(pl.multiple_of(m * rows, rows), rows)
        ATT[rs, :] = at
        DQ[rs, :] = dqb
        DK[rs, :] = dkb
        DV[rs, :] = dvb
        OUT[m] = dot_nt(at, weight(3))
        DN[m] = dot_nt(dqb, weight(0)) + dot_nt(dkb, weight(1)) + dot_nt(dvb, weight(2))

    def grad_of(k, left, right):
        total = dot_nn(left[...].reshape(4 * TILE, 4 * rows), right)
        GP[k] = total.astype(bf16).reshape(NZ, 2, 2, 64, TILE)
        rs_c(k).start()

    def slice_of(j):
        return NQ + 2 * j, NQ + 1 + 2 * j

    def feed(j, m):
        ki, kb = slice_of(j)
        b0 = B[2 * y + j // 2, j % 2, 0].astype(f32)[0:1, :]
        b1 = B[2 * y + j // 2, j % 2, 1].astype(f32)[0:1, :]
        u = dot_nn(NA[m], weight(ki)) + jnp.concatenate([b0, b1], axis=1)
        u2 = u * u
        k0 = float(np.sqrt(2.0 / np.pi))
        t = jnp.tanh(k0 * u * (1.0 + 0.044715 * u2))
        act = (0.5 * u * (1.0 + t)).astype(bf16)
        slope = 0.5 * (1.0 + t) + (0.5 * k0) * u * (1.0 - t * t) * (1.0 + 0.134145 * u2)
        hg = (dot_nn(SA[m], weight(kb)) * slope).astype(bf16)
        rs = pl.ds(pl.multiple_of(m * rows, rows), rows)
        ACT[j, rs, :] = act
        HG[j, rs, :] = hg
        OUT[m] += dot_nt(act, weight(kb))
        DN[m] += dot_nt(hg, weight(ki))
        at = 24 + x * 16 + y * 8 + 2 * j
        total = jnp.sum(hg.astype(f32), axis=0, keepdims=True)
        V[pl.ds(at, 1), :] += total[:, :128]
        V[pl.ds(at + 1, 1), :] += total[:, 128:]

    def feed_grads(j):
        ki, kb = slice_of(j)
        grad_of(ki, NT, HG[j])
        grad_of(kb, ST, ACT[j])

    def feed_rows(j, *between):
        for i in (0, 1):
            feed(j, 2 * i)
            feed(j, 2 * i + 1)
            if i < len(between):
                between[i]()

    def v_copy(i, dev):
        return rcp(VS.at[min(i, 3)], VRV.at[i], vs.at[i], vr.at[i], dev)

    v_devs = (dev_c, dev_x, dev_y)

    def v_step(i):
        v_copy(i, v_devs[i]).wait_recv()
        VS[i + 1] = VS[i] + VRV[i]
        if i < 2:
            v_copy(i + 1, v_devs[i + 1]).start()
        else:
            for n, dev in enumerate(dev_z):
                v_copy(3 + n, dev).start()

    def arrived(*chunks):
        for k in chunks:
            ag_done(k)

    flip(NA, NT, m_own)
    flip(SA, ST, m_own)
    ag_turn()
    g_near(0)
    g_send(1)
    g_forward(0)
    tables()
    ag_turn()
    g_rest(0)
    flip(NA, NT, m_x)
    flip(NA, NT, m_y)
    ag_turn()
    ag_turn()
    arrived(NK)
    ag_turn()
    arrived(0, 1, 2)
    project(m_own)
    project(m_x)
    g_near(1)
    g_forward(1)
    project(m_y)
    ag_turn()
    arrived(3)
    attend(m_own)
    g_rest(1)
    ag_turn()
    attend(m_x)
    flip(SA, ST, m_x)
    flip(SA, ST, m_y)
    attend(m_y)
    g_far(0)
    flip(NA, NT, m_d)
    project(m_d)
    ag_turn()
    g_far(1)
    flip(SA, ST, m_d)
    attend(m_d)
    grad_of(0, NT, DQ[...])
    grad_of(1, NT, DK[...])
    ag_turn()
    grad_of(2, NT, DV[...])
    grad_of(3, ST, ATT[...])
    rs_turn()
    arrived(4, 5)
    feed_rows(0, ag_turn)
    rs_turn()
    feed_grads(0)
    ag_turn()
    rs_turn()
    arrived(6, 7)
    feed_rows(1)
    ag_turn()
    rs_turn()
    feed_grads(1)
    arrived(8, 9)
    feed_rows(2, ag_turn, rs_turn)
    feed_grads(2)
    ag_turn()
    rs_turn()
    arrived(10, 11)
    feed_rows(3)

    for u in range(2):
        e_first(1, u, DN)
    feed_grads(3)
    rs_turn()
    e_second(1, 0, DN)
    rs_turn()
    e_second(1, 1, DN)
    for u in range(2):
        e_first(0, u, OUT)
    rs_turn()
    for u in range(2):
        e_last(1, u, DN)
    dn = DN[m_own]
    xhat = XH[...]
    gsum = jnp.sum(dn * xhat, axis=0, keepdims=True)
    bsum = jnp.sum(dn, axis=0, keepdims=True)
    for i in range(8):
        V[i : i + 1, :] = gsum[:, i * 128 : (i + 1) * 128]
        V[8 + i : 9 + i, :] = bsum[:, i * 128 : (i + 1) * 128]
    VS[0] = V[...]
    v_copy(0, dev_c).start()
    e = dn * gain_ref[...]
    me = jnp.mean(e, axis=-1, keepdims=True)
    mex = jnp.mean(e * xhat, axis=-1, keepdims=True)
    gin_ref[...] = (SA[m_own].astype(f32) + RSTD[:, 0:1] * (e - me - xhat * mex)).astype(bf16)
    v_step(0)
    rs_turn()
    e_second(0, 0, OUT)
    v_step(1)
    rs_turn()
    e_second(0, 1, OUT)
    v_step(2)
    for _ in range(NK + 4):
        rs_turn()
    for i in range(3):
        v_copy(3 + i, dev_z[i]).wait_recv()
    V[...] = VS[3] + VRV[3] + VRV[4] + VRV[5]
    index = 2 * dp + x
    lane4 = lax.rem(index, 4)
    for base, ref in ((0, lng_ref), (8, lnb_ref), (16, bbk_ref)):
        line = V[pl.ds(base + index // 4, 1), :]
        out = line[:, 0:32]
        for n in range(1, 4):
            out = jnp.where(lane4 == n, line[:, 32 * n : 32 * n + 32], out)
        ref[...] = out
    gbin_ref[...] = V[pl.ds(24 + 16 * x + dp, 1), :]
    for u in range(2):
        e_last(0, u, OUT)
    block_ref[...] = (x_ref[...].astype(f32) + OUT[m_own] + bback_ref[...]).astype(bf16)

    def later(f):
        lax.fori_loop(0, NK, lambda k, _: (f(k), 0)[1], 0)

    for k in range(NK + 1):
        ag_sent(k)
    for t in range(2):
        g_sent(t)
        e_sent(t)
    later(rs_sent)
    for i, dev in enumerate([dev_c, dev_x, dev_y] + dev_z):
        v_copy(i, dev).wait_send()


def rope_constants(rows):
    half = np.arange(ROT // 2, dtype=np.float32)
    rates = (10000.0 ** (-2.0 * half / ROT)).astype(np.float32)
    angle = np.arange(rows, dtype=np.float32)[:, None] * rates[None, :]
    angle = np.repeat(angle, 2, axis=1)
    cos = np.concatenate([np.cos(angle), np.ones((rows, HD - ROT))], axis=1)
    sin = np.concatenate([np.sin(angle), np.zeros((rows, HD - ROT))], axis=1)
    two = lambda t: np.concatenate([t, t], axis=1).astype(np.float32)
    return two(cos), two(sin)


def on_quad(
    residual_in,
    cotangent,
    ln_gain,
    ln_bias,
    w_qkv,
    w_out,
    w_in,
    b_in,
    w_back,
    b_back,
    bucket_ids,
    residue_counts,
):
    rows, width = residual_in.shape
    cos, sin = rope_constants(rows)
    f32, bf16 = jnp.float32, jnp.bfloat16
    vm = pl.BlockSpec(memory_space=pltpu.VMEM)
    sm = pl.BlockSpec(memory_space=pltpu.SMEM)
    anyspace = pl.BlockSpec(memory_space=pl.ANY)
    shard = width // (4 * NZ)
    sem = pltpu.SemaphoreType.DMA
    block = (2, 2, rows, TILE)
    outs = pl.pallas_call(
        layer_kernel,
        out_shape=(
            jax.ShapeDtypeStruct((rows, width), bf16),
            jax.ShapeDtypeStruct((rows, width), bf16),
            jax.ShapeDtypeStruct((3, shard, 2 * TILE), f32),
            jax.ShapeDtypeStruct((shard, 2 * TILE), f32),
            jax.ShapeDtypeStruct((shard, 2 * NJ * TILE), f32),
            jax.ShapeDtypeStruct((shard, 2 * NJ * TILE), f32),
            jax.ShapeDtypeStruct((1, 32), f32),
            jax.ShapeDtypeStruct((1, 32), f32),
            jax.ShapeDtypeStruct((1, 32), f32),
            jax.ShapeDtypeStruct((1, 128), f32),
        ),
        in_specs=[sm, sm] + [vm] * 8 + [anyspace] * 4,
        out_specs=(vm,) * 10,
        scratch_shapes=[
            pltpu.VMEM((NZ, 2, 2, 16, 128), bf16),
            pltpu.VMEM((NK, NZ, 2, 2, shard, TILE), bf16),
            pltpu.VMEM((4, rows, width), bf16),
            pltpu.VMEM((4, rows, width), bf16),
            pltpu.VMEM((4, TILE, 4 * rows), bf16),
            pltpu.VMEM((4, TILE, 4 * rows), bf16),
            pltpu.VMEM((2, rows, TILE), f32),
            pltpu.VMEM((2, rows, TILE), f32),
            pltpu.VMEM((2, rows, rows), f32),
            pltpu.VMEM((4, rows, TILE), bf16),
            pltpu.VMEM((4, rows, TILE), bf16),
            pltpu.VMEM((4, rows, TILE), bf16),
            pltpu.VMEM((4 * rows, TILE), bf16),
            pltpu.VMEM((4 * rows, TILE), bf16),
            pltpu.VMEM((4 * rows, TILE), bf16),
            pltpu.VMEM((4 * rows, TILE), bf16),
            pltpu.VMEM((NJ, 4 * rows, TILE), bf16),
            pltpu.VMEM((NJ, 4 * rows, TILE), bf16),
            pltpu.VMEM((4, rows, width), f32),
            pltpu.VMEM((4, rows, width), f32),
            pltpu.VMEM((NK, NZ, 2, 2, shard, TILE), bf16),
            pltpu.VMEM((NK, NZ, 2, shard, TILE), bf16),
            pltpu.VMEM((NK, 5, 2, shard, TILE), bf16),
            pltpu.VMEM((2, shard, TILE), f32),
            pltpu.VMEM((NK, shard, TILE), bf16),
            pltpu.VMEM((NK, shard, TILE), bf16),
            pltpu.VMEM((rows, width), f32),
            pltpu.VMEM((rows, 128), f32),
            pltpu.VMEM((2,) + block, bf16),
            pltpu.VMEM((2,) + block, bf16),
            pltpu.VMEM((2,) + block, bf16),
            pltpu.VMEM((2,) + block, bf16),
            pltpu.VMEM((2, 2, rows, TILE), bf16),
            pltpu.VMEM((2, 2, rows, TILE), bf16),
            pltpu.VMEM((2, 2, rows, TILE), bf16),
            pltpu.VMEM((2, 2, rows, TILE), bf16),
            pltpu.VMEM((VROWS, 128), f32),
            pltpu.VMEM((4, VROWS, 128), f32),
            pltpu.VMEM((6, VROWS, 128), f32),
            sem((NK,)),
            sem((NK + 1,)),
            sem((NK + 1,)),
            sem((NK + 1, 2, 3)),
            sem((NK + 1, 2, 3)),
            sem((NK + 1, NZ)),
            sem((NK + 1, NZ)),
            sem((12,)),
            sem((12,)),
            sem((NK,)),
            sem((NK,)),
            sem((NK, NZ)),
            sem((NK, 5)),
            sem((NK,)),
            sem((NK,)),
            sem((2, 2, 4)),
            sem((2, 2, 4)),
            sem((6,)),
            sem((6,)),
        ],
        compiler_params=pltpu.CompilerParams(
            collective_id=0, has_side_effects=True, vmem_limit_bytes=63 << 20
        ),
        cost_estimate=pl.CostEstimate(
            flops=20 * 2**30, bytes_accessed=8 * 2**20, transcendentals=2**21
        ),
    )(
        bucket_ids,
        residue_counts.reshape(SLOTS),
        residual_in,
        cotangent,
        ln_gain.reshape(1, width),
        ln_bias.reshape(1, width),
        b_back.reshape(1, width),
        jnp.asarray(cos),
        jnp.asarray(sin),
        b_in.reshape(1, 128),
        w_qkv,
        w_out.T,
        w_in,
        w_back.T,
    )
    block_out, grad_input, grad_w_qkv, gwo, grad_w_in, gwb, lng, lnb, bbk, gbin = outs
    return (
        block_out,
        grad_input,
        lng.reshape(32),
        lnb.reshape(32),
        grad_w_qkv,
        gwo.T,
        grad_w_in,
        gbin.reshape(128),
        gwb.T,
        bbk.reshape(32),
    )


def solution(mesh):
    placed = (
        P(("dp", "mp"), None),
        P(("dp", "mp"), None),
        P(),
        P(),
        P(None, "dp", "mp"),
        P("mp", "dp"),
        P("dp", "mp"),
        P(("mp", "dp")),
        P("mp", "dp"),
        P(),
        P("dp"),
        P("dp", None),
    )
    return jax.shard_map(
        on_quad if fits_quad(mesh) else on_device,
        mesh=mesh,
        in_specs=placed,
        out_specs=(
            P(("dp", "mp"), None),
            P(("dp", "mp"), None),
            P(("dp", "mp")),
            P(("dp", "mp")),
            P(None, "dp", "mp"),
            P("mp", "dp"),
            P("dp", "mp"),
            P(("mp", "dp")),
            P("mp", "dp"),
            P(("dp", "mp")),
        ),
        check_vma=False,
    )
```

```python
from functools import partial

import jax
import jax.numpy as jnp
import numpy as np
from jax import lax
from jax.experimental import pallas as pl
from jax.experimental.pallas import tpu as pltpu
from jax.sharding import PartitionSpec as P

HD = 64
ROT = 32
SLOTS = 16


NORM_EPS = 1e-05
MASKED_SCORE = -1e30


def norm_rows(inputs_now, norm_gain, norm_shift):
    centred = inputs_now - jnp.mean(inputs_now, axis=-1, keepdims=True)
    spread = jnp.mean(centred * centred, axis=-1, keepdims=True)
    return centred * lax.rsqrt(spread + NORM_EPS) * norm_gain + norm_shift


def slot_tables(bucket_one, residue_row, group_rows):
    slot_length = jnp.right_shift(jnp.int32(group_rows // 2), bucket_one)
    places = jnp.arange(group_rows, dtype=jnp.int32)
    slot_ids = places // slot_length
    inside = places - slot_ids * slot_length
    match_table = slot_ids[:, None] == jnp.arange(SLOTS, dtype=jnp.int32)[None, :]
    picked = jnp.sum(jnp.where(match_table, residue_row[None, :], 0), axis=1)
    live_rows = jnp.minimum(picked, slot_length)
    return (slot_ids, inside, inside < live_rows)


def rope_tables(inside):
    half_steps = jnp.arange(ROT // 2, dtype=jnp.float32)
    inverse_rates = 10000.0 ** (-2.0 * half_steps / ROT)
    angles = inside.astype(jnp.float32)[:, None] * inverse_rates[None, :]
    return (jnp.cos(angles), jnp.sin(angles))


def rotate(values, cosine_table, sine_table):
    row_count = values.shape[0]
    head_count = values.shape[1]
    paired = values[..., :ROT].reshape(row_count, head_count, ROT // 2, 2)
    even_part = paired[..., 0]
    odd_part = paired[..., 1]
    cosine_now = cosine_table[:, None, :]
    sine_now = sine_table[:, None, :]
    turned = jnp.stack(
        [
            even_part * cosine_now - odd_part * sine_now,
            odd_part * cosine_now + even_part * sine_now,
        ],
        axis=-1,
    )
    return jnp.concatenate([turned.reshape(row_count, head_count, ROT), values[..., ROT:]], axis=-1)


def mask_block(block_start, block_rows, slot_ids):
    query_places = block_start + jnp.arange(block_rows, dtype=jnp.int32)
    query_slots = lax.dynamic_slice_in_dim(slot_ids, block_start, block_rows, 0)
    key_places = jnp.arange(slot_ids.shape[0], dtype=jnp.int32)
    return (query_slots[:, None] == slot_ids[None, :]) & (
        key_places[None, :] <= query_places[:, None]
    )


def over_rows(first_op, second_op):
    return lax.dot_general(
        first_op, second_op, (((0,), (0,)), ((), ())), preferred_element_type=jnp.float32
    )


def against_weight(first_op, second_op):
    return lax.dot_general(
        first_op, second_op, (((1,), (1,)), ((), ())), preferred_element_type=jnp.float32
    )


def on_device(
    residual_in,
    cotangent,
    ln_gain,
    ln_bias,
    w_qkv,
    w_out,
    w_in,
    b_in,
    w_back,
    b_back,
    bucket_ids,
    residue_counts,
):
    model_count = lax.axis_size("mp")
    model_rank = lax.axis_index("mp")
    local_rows = residual_in.shape[0]
    group_rows = local_rows * model_count
    slot_ids, inside, valid_rows = slot_tables(bucket_ids[0], residue_counts[0], group_rows)
    cosine_table, sine_table = rope_tables(inside)
    qkv_all, out_all, in_all, bias_in, back_all = (
        lax.all_gather(w_qkv, "dp", axis=1, tiled=True),
        lax.all_gather(w_out, "dp", axis=1, tiled=True),
        lax.all_gather(w_in, "dp", axis=0, tiled=True),
        lax.all_gather(b_in, "dp", axis=0, tiled=True),
        lax.all_gather(w_back, "dp", axis=1, tiled=True),
    )
    x_local = residual_in.astype(jnp.float32)
    x_group = lax.all_gather(residual_in, "mp", axis=0, tiled=True).astype(jnp.float32)
    normed = norm_rows(x_group, ln_gain, ln_bias).astype(jnp.bfloat16)
    head_width = qkv_all.shape[2]
    head_count = head_width // HD
    score_scale = HD ** (-0.5)

    def project(member_index):
        return jnp.dot(normed, qkv_all[member_index], preferred_element_type=jnp.float32).reshape(
            group_rows, head_count, HD
        )

    queries = rotate(project(0), cosine_table, sine_table).astype(jnp.bfloat16)
    key_rows = rotate(project(1), cosine_table, sine_table).astype(jnp.bfloat16)
    value_rows = project(2).astype(jnp.bfloat16)
    block_rows = min(512, group_rows)
    starts = jnp.arange(group_rows // block_rows, dtype=jnp.int32) * block_rows

    def block_scores(block_start):
        query_block = lax.dynamic_slice_in_dim(queries, block_start, block_rows, 0)
        allowed = mask_block(block_start, block_rows, slot_ids)
        scores = (
            jnp.einsum("qhd,khd->hqk", query_block, key_rows, preferred_element_type=jnp.float32)
            * score_scale
        )
        return (query_block, jnp.where(allowed[None], scores, MASKED_SCORE))

    def forward_block(block_start):
        query_block, scores = block_scores(block_start)
        row_peak = jnp.max(scores, axis=-1, keepdims=True)
        exp_scores = jnp.exp(scores - row_peak)
        row_total = jnp.sum(exp_scores, axis=-1, keepdims=True)
        weights_now = (exp_scores / row_total).astype(jnp.bfloat16)
        attended = jnp.einsum(
            "hqk,khd->qhd", weights_now, value_rows, preferred_element_type=jnp.float32
        )
        return (attended.astype(jnp.bfloat16), (row_peak + jnp.log(row_total))[..., 0])

    attended_blocks, log_totals = lax.map(forward_block, starts)
    mixed_rows = attended_blocks.reshape(group_rows, head_width)
    hidden = jnp.dot(normed, in_all, preferred_element_type=jnp.float32) + bias_in.astype(
        jnp.float32
    )
    gelu_tanh = partial(jax.nn.gelu, approximate=True)
    active_value, gelu_pull = jax.vjp(gelu_tanh, hidden)
    active = active_value.astype(jnp.bfloat16)
    partial_out = jnp.dot(mixed_rows, out_all, preferred_element_type=jnp.float32) + jnp.dot(
        active, back_all, preferred_element_type=jnp.float32
    )
    summed_all = lax.psum(partial_out.astype(jnp.bfloat16), "mp").astype(jnp.float32)
    summed = lax.dynamic_slice_in_dim(summed_all, model_rank * local_rows, local_rows, 0)
    block_out = (x_local + summed + b_back).astype(jnp.bfloat16)
    cot_group = lax.all_gather(cotangent, "mp", axis=0, tiled=True)
    seed_rows = jnp.where(valid_rows[:, None], cot_group, jnp.zeros_like(cot_group))
    qkv_all, out_all, in_all, back_all = (
        lax.all_gather(w_qkv, "dp", axis=1, tiled=True),
        lax.all_gather(w_out, "dp", axis=1, tiled=True),
        lax.all_gather(w_in, "dp", axis=0, tiled=True),
        lax.all_gather(w_back, "dp", axis=1, tiled=True),
    )
    active_grad = against_weight(seed_rows, back_all)
    hidden_grad = gelu_pull(active_grad)[0].astype(jnp.bfloat16)
    grad_in_local = over_rows(normed, hidden_grad)
    grad_bias_in = jnp.sum(hidden_grad.astype(jnp.float32), axis=0)
    grad_back_local = over_rows(active, seed_rows)
    grad_out_local = over_rows(mixed_rows, seed_rows)
    normed_grad = against_weight(hidden_grad, in_all)
    mixed_grad = (
        against_weight(seed_rows, out_all).astype(jnp.bfloat16).reshape(group_rows, head_count, HD)
    )

    def backward_block(carry, inputs_now):
        key_acc, value_acc = carry
        block_start, log_total = inputs_now
        query_block, scores = block_scores(block_start)
        grad_block = lax.dynamic_slice_in_dim(mixed_grad, block_start, block_rows, 0)
        probs = jnp.exp(scores - log_total[..., None])
        probs_low = probs.astype(jnp.bfloat16)
        value_acc = value_acc + jnp.einsum(
            "hqk,qhd->khd", probs_low, grad_block, preferred_element_type=jnp.float32
        )
        probs_grad = jnp.einsum(
            "qhd,khd->hqk", grad_block, value_rows, preferred_element_type=jnp.float32
        )
        score_grad = probs * (probs_grad - jnp.sum(probs * probs_grad, axis=-1, keepdims=True))
        score_low = score_grad.astype(jnp.bfloat16)
        query_grad = (
            jnp.einsum("hqk,khd->qhd", score_low, key_rows, preferred_element_type=jnp.float32)
            * score_scale
        )
        key_acc = (
            key_acc
            + jnp.einsum("hqk,qhd->khd", score_low, query_block, preferred_element_type=jnp.float32)
            * score_scale
        )
        return ((key_acc, value_acc), query_grad)

    empty_heads = jnp.zeros((group_rows, head_count, HD), jnp.float32)
    (key_acc, value_acc), query_blocks = lax.scan(
        backward_block, (empty_heads, empty_heads), (starts, log_totals)
    )
    turn_back = partial(rotate, cosine_table=cosine_table, sine_table=sine_table)
    unturn = jax.vjp(turn_back, empty_heads)[1]
    query_pre_grad = (
        unturn(query_blocks.reshape(group_rows, head_count, HD))[0]
        .astype(jnp.bfloat16)
        .reshape(group_rows, head_width)
    )
    key_pre_grad = unturn(key_acc)[0].astype(jnp.bfloat16).reshape(group_rows, head_width)
    value_grad = value_acc.astype(jnp.bfloat16).reshape(group_rows, head_width)
    grad_qkv_local = jnp.stack(
        [
            over_rows(normed, query_pre_grad),
            over_rows(normed, key_pre_grad),
            over_rows(normed, value_grad),
        ],
        axis=0,
    )
    normed_grad = (
        normed_grad
        + against_weight(query_pre_grad, qkv_all[0])
        + against_weight(key_pre_grad, qkv_all[1])
        + against_weight(value_grad, qkv_all[2])
    )
    share_grad = lax.psum(normed_grad.astype(jnp.bfloat16), "mp").astype(jnp.float32)
    seed_group = seed_rows.astype(jnp.float32)
    norm_pull = jax.vjp(norm_rows, x_group, ln_gain, ln_bias)[1]
    input_part, gain_part, shift_part = norm_pull(share_grad)
    input_group = seed_group + input_part
    grad_input = lax.dynamic_slice_in_dim(
        input_group, model_rank * local_rows, local_rows, 0
    ).astype(jnp.bfloat16)
    back_part = jnp.sum(seed_group, axis=0)
    grad_w_qkv, grad_w_out, grad_w_in, grad_b_in, grad_w_back, gain_rows, shift_rows, back_rows = (
        lax.psum_scatter(
            grad_qkv_local.astype(jnp.bfloat16), "dp", scatter_dimension=1, tiled=True
        ).astype(jnp.float32),
        lax.psum_scatter(
            grad_out_local.astype(jnp.bfloat16), "dp", scatter_dimension=1, tiled=True
        ).astype(jnp.float32),
        lax.psum_scatter(
            grad_in_local.astype(jnp.bfloat16), "dp", scatter_dimension=0, tiled=True
        ).astype(jnp.float32),
        lax.psum_scatter(
            grad_bias_in.astype(jnp.bfloat16), "dp", scatter_dimension=0, tiled=True
        ).astype(jnp.float32),
        lax.psum_scatter(
            grad_back_local.astype(jnp.bfloat16), "dp", scatter_dimension=1, tiled=True
        ).astype(jnp.float32),
        lax.psum_scatter(
            gain_part.astype(jnp.bfloat16), "dp", scatter_dimension=0, tiled=True
        ).astype(jnp.float32),
        lax.psum_scatter(
            shift_part.astype(jnp.bfloat16), "dp", scatter_dimension=0, tiled=True
        ).astype(jnp.float32),
        lax.psum_scatter(
            back_part.astype(jnp.bfloat16), "dp", scatter_dimension=0, tiled=True
        ).astype(jnp.float32),
    )
    piece_width = gain_rows.shape[0] // model_count
    grad_ln_gain = lax.dynamic_slice_in_dim(gain_rows, model_rank * piece_width, piece_width, 0)
    grad_ln_bias = lax.dynamic_slice_in_dim(shift_rows, model_rank * piece_width, piece_width, 0)
    grad_b_back = lax.dynamic_slice_in_dim(back_rows, model_rank * piece_width, piece_width, 0)
    return (
        block_out,
        grad_input,
        grad_ln_gain,
        grad_ln_bias,
        grad_w_qkv,
        grad_w_out,
        grad_w_in,
        grad_b_in,
        grad_w_back,
        grad_b_back,
    )


MESH = pl.DeviceIdType.MESH
NZ = 4
TILE = 256
N_HEADS = TILE // HD
NQ = 4
NJ = 4
NK = NQ + 2 * NJ
VROWS = 56


def fits_quad(mesh):
    return mesh.shape["mp"] == 2 and mesh.shape["dp"] == 4 * NZ


def dot_nn(a, b):
    return lax.dot_general(a, b, (((1,), (0,)), ((), ())), preferred_element_type=jnp.float32)


def dot_nt(a, b):
    return lax.dot_general(a, b, (((1,), (1,)), ((), ())), preferred_element_type=jnp.float32)


def dot_tn(a, b):
    return lax.dot_general(a, b, (((0,), (0,)), ((), ())), preferred_element_type=jnp.float32)


def layer_kernel(
    bucket_ref,
    counts_ref,
    x_ref,
    cot_ref,
    gain_ref,
    bias_ref,
    bback_ref,
    cos_ref,
    sin_ref,
    bin_ref,
    wqkv_ref,
    wot_ref,
    win_ref,
    wbt_ref,
    block_ref,
    gin_ref,
    gqkv_ref,
    got_ref,
    gi_ref,
    gbt_ref,
    lng_ref,
    lnb_ref,
    bbk_ref,
    gbin_ref,
    B,
    W,
    NA,
    SA,
    NT,
    ST,
    CT,
    SN,
    BM,
    QR,
    KR,
    VR,
    DQ,
    DK,
    DV,
    ATT,
    ACT,
    HG,
    OUT,
    DN,
    GP,
    GC,
    RZ,
    FS,
    YS,
    YR,
    XH,
    RSTD,
    EXS,
    EYS,
    EXR,
    EYR,
    EXS2,
    EYS2,
    EXR2,
    EYR2,
    V,
    VS,
    VRV,
    loc_sem,
    ays,
    ayr,
    azs,
    azr,
    acs,
    acr,
    gs,
    gr,
    rcs,
    rcr,
    rzs,
    rzr,
    rys,
    ryr,
    exs,
    exr,
    vs,
    vr,
):
    f32, bf16 = jnp.float32, jnp.bfloat16
    dp, x = lax.axis_index("dp"), lax.axis_index("mp")
    z = dp // 4
    y = lax.rem(dp // 2, 2)
    c = lax.rem(dp, 2)
    rows = x_ref.shape[0]
    width = x_ref.shape[1]
    dev_x = (dp, 1 - x)
    dev_y = (dp + 2 - 4 * y, x)
    dev_c = (dp + 1 - 2 * c, x)
    dev_r = (lax.rem(dp + 4, 4 * NZ), x)
    dev_l = (lax.rem(dp + 4 * NZ - 4, 4 * NZ), x)
    dev_z = [(lax.rem(dp + 4 * i, 4 * NZ), x) for i in (1, 2, 3)]
    m_own = 2 * y + x
    m_x = 2 * y + 1 - x
    m_y = 2 - 2 * y + x
    m_d = 3 - m_own

    def rcp(src, dst, ss, rs, dev):
        return pltpu.make_async_remote_copy(
            src_ref=src, dst_ref=dst, send_sem=ss, recv_sem=rs, device_id=dev, device_id_type=MESH
        )

    barrier = pltpu.get_barrier_semaphore()
    peers = [dev_x, dev_y, dev_c] + dev_z
    for peer in peers:
        pl.semaphore_signal(barrier, inc=1, device_id=peer, device_id_type=MESH)

    def wsrc(k, q):
        if k == NK:
            return None
        if k < 3:
            return wqkv_ref.at[k, :, pl.ds(pl.multiple_of(q * TILE, TILE), TILE)]
        if k == 3:
            return wot_ref.at[:, pl.ds(pl.multiple_of(q * TILE, TILE), TILE)]
        ref = win_ref if k % 2 == 0 else wbt_ref
        j = (k - NQ) // 2
        return ref.at[:, pl.ds(pl.multiple_of(q * (NJ * TILE) + j * TILE, TILE), TILE)]

    def wv(k):
        return B if isinstance(k, int) and k == NK else W.at[k]

    def own_copy(k):
        return pltpu.make_async_copy(wsrc(k, y), W.at[k, z, y, c], loc_sem.at[k])

    def y_copy(k):
        if k == NK:
            return rcp(B.at[z, y, c], B.at[z, y, c], ays.at[k], ayr.at[k], dev_y)
        return rcp(wsrc(k, 1 - y), W.at[k, z, y, c], ays.at[k], ayr.at[k], dev_y)

    def y_arrived(k):
        here = wv(k).at[z, 1 - y, c]
        rcp(here, here, ays.at[k], ayr.at[k], dev_y).wait_recv()

    def z_copy(k, way, s, e):
        block = wv(k).at[e, :, c]
        return rcp(
            block, block, azs.at[k, way, s], azr.at[k, way, s], dev_r if way == 0 else dev_l
        )

    def c_copy(k, e):
        block = wv(k).at[e, :, c]
        return rcp(block, block, acs.at[k, e], acr.at[k, e], dev_c)

    def ag_own(k, copied=True):
        if copied:
            pltpu.make_async_copy(
                W.at[k, z, y, c], W.at[k, z, y, c], loc_sem.at[k]
            ).wait()
        y_arrived(k)

        @pl.when(z < NZ - 1)
        def _():
            z_copy(k, 0, 0, z).start()

        @pl.when(z > 0)
        def _():
            z_copy(k, 1, 0, z).start()

        c_copy(k, z).start()

    def ag_step(k, s):
        @pl.when(z - 1 - s >= 0)
        def _():
            e = z - 1 - s
            z_copy(k, 0, s, e).wait_recv()
            if s < NZ - 2:

                @pl.when(z < NZ - 1)
                def _():
                    z_copy(k, 0, s + 1, e).start()

            c_copy(k, e).start()

        @pl.when(z + 1 + s <= NZ - 1)
        def _():
            e = z + 1 + s
            z_copy(k, 1, s, e).wait_recv()
            if s < NZ - 2:

                @pl.when(z > 0)
                def _():
                    z_copy(k, 1, s + 1, e).start()

            c_copy(k, e).start()

    def ag_done(k):
        for e in range(NZ):
            block = wv(k).at[e, :, 1 - c]
            rcp(block, block, acs.at[k, e], acr.at[k, e], dev_c).wait_recv()

    def ag_sent(k, copied=True):
        y_copy(k).wait_send() if isinstance(k, int) else None
        for s in range(NZ - 1):

            @pl.when((z < NZ - 1) & (z - s >= 0))
            def _():
                z_copy(k, 0, s, z - s).wait_send()

            @pl.when((z > 0) & (z + s <= NZ - 1))
            def _():
                z_copy(k, 1, s, z + s).wait_send()

        for e in range(NZ):
            c_copy(k, e).wait_send()

    order = [0, NK] + list(range(1, NK))
    turns = iter(range(NK + NZ))

    def ag_turn():
        t = next(turns, None)
        if t is None:
            return
        ahead = range(t, t + 1) if t < 8 else range(2 * t - 8, 2 * t - 6)
        for n in ahead:
            if n <= NK:
                ag_own(order[n], copied=order[n] != NK)
        for s in range(NZ - 1):
            if 0 <= t - 1 - s <= NK:
                ag_step(order[t - 1 - s], s)

    P0 = 64
    parts = (pl.ds(0, P0), pl.ds(P0, rows - P0))
    BUF = (NA, SA)

    def g_copy(t, p, way, m):
        block = BUF[t].at[m, parts[p]]
        i = (t * 2 + p) * 3 + way
        dev = (dev_x, dev_y)[way] if way < 2 else (dev_y, dev_x)[p]
        return rcp(block, block, gs.at[i], gr.at[i], dev)

    def g_send(t):
        g_copy(t, 0, 0, m_own).start()
        g_copy(t, 1, 1, m_own).start()
        g_copy(t, 1, 0, m_own).start()
        g_copy(t, 0, 1, m_own).start()

    def g_near(t):
        g_copy(t, 0, 0, m_x).wait_recv()
        g_copy(t, 1, 1, m_y).wait_recv()

    def g_forward(t):
        g_copy(t, 0, 2, m_x).start()
        g_copy(t, 1, 2, m_y).start()

    def g_rest(t):
        g_copy(t, 1, 0, m_x).wait_recv()
        g_copy(t, 0, 1, m_y).wait_recv()

    def g_far(t):
        g_copy(t, 0, 2, m_d).wait_recv()
        g_copy(t, 1, 2, m_d).wait_recv()

    def g_sent(t):
        for p in (0, 1):
            for way in (0, 1):
                g_copy(t, p, way, m_own).wait_send()
        g_copy(t, 0, 2, m_x).wait_send()
        g_copy(t, 1, 2, m_y).wait_send()

    def rs_c(k):
        return rcp(GP.at[k, :, :, 1 - c], GC.at[k], rcs.at[k], rcr.at[k], dev_c)

    def rs_z(k, way, e, slot):
        return rcp(
            GP.at[k, e, :, c],
            RZ.at[k, slot],
            rzs.at[k, e],
            rzr.at[k, slot],
            dev_r if way == 0 else dev_l,
        )

    def rs_begin(k):
        rs_c(k).wait_recv()
        for e in range(NZ):
            GP[k, e, :, c] = (GP[k, e, :, c].astype(f32) + GC[k, e].astype(f32)).astype(bf16)

        @pl.when(z == 0)
        def _():
            for e in range(NZ - 1, 0, -1):
                rs_z(k, 0, e, e).start()

        @pl.when(z == NZ - 1)
        def _():
            for e in range(NZ - 1):
                rs_z(k, 1, e, e if e < NZ - 2 else 4).start()

    def pass_on(k, way, e, slot):
        rs_z(k, way, e, e).wait_recv()
        GP[k, e, :, c] = (GP[k, e, :, c].astype(f32) + RZ[k, e].astype(f32)).astype(bf16)
        rs_z(k, way, e, slot).start()

    def rs_hop1(k):
        @pl.when(z == 1)
        def _():
            pass_on(k, 0, 3, 3)
            pass_on(k, 0, 2, 2)

        @pl.when(z == 2)
        def _():
            pass_on(k, 1, 0, 0)
            pass_on(k, 1, 1, 4)

    def rs_hop2(k):
        @pl.when(z == 2)
        def _():
            pass_on(k, 0, 3, 3)

        @pl.when(z == 1)
        def _():
            pass_on(k, 1, 0, 4)

    def rs_y(k):
        return rcp(YS.at[k], YR.at[k], rys.at[k], ryr.at[k], dev_y)

    def put(k, q, value):
        if k < 3:
            gqkv_ref[k, :, pl.ds(pl.multiple_of(q * TILE, TILE), TILE)] = value
        elif k == 3:
            got_ref[:, pl.ds(pl.multiple_of(q * TILE, TILE), TILE)] = value
        else:
            ref = gi_ref if k % 2 == 0 else gbt_ref
            j = (k - NQ) // 2
            ref[:, pl.ds(pl.multiple_of(q * (NJ * TILE) + j * TILE, TILE), TILE)] = value

    def rs_final(k):
        FS[...] = GP[k, z, :, c].astype(f32)

        @pl.when(z > 0)
        def _():
            rs_z(k, 0, z, z).wait_recv()
            FS[...] += RZ[k, z].astype(f32)

        @pl.when(z < NZ - 1)
        def _():
            rs_z(k, 1, z, 4).wait_recv()
            FS[...] += RZ[k, 4].astype(f32)

        YS[k] = FS[1 - y].astype(bf16)
        rs_y(k).start()
        put(k, y, FS[y])

    def rs_out(k):
        rs_y(k).wait_recv()
        put(k, 1 - y, YR[k].astype(f32))

    rturns = iter(range(NK + 2))

    def rs_turn():
        r = next(rturns, None)
        if r is None:
            return
        for s, f in enumerate((rs_hop1, rs_hop2, rs_final)):
            if 0 <= r - s < NK:
                f(r - s)

    def rs_sent(k):
        rs_c(k).wait_send()
        for e in range(NZ):

            @pl.when(z != e)
            def _():
                rs_z(k, 0, e, e).wait_send()

        rs_y(k).wait_send()

    def e_copy(t, u, i):
        src, dst, dev = (
            (EXS, EXR, dev_x),
            (EYS, EYR, dev_y),
            (EXS2, EXR2, dev_x),
            (EYS2, EYR2, dev_y),
        )[i]
        return rcp(src.at[t, u], dst.at[t, u], exs.at[t, u, i], exr.at[t, u, i], dev)

    def cols(u, half):
        return pl.ds(half * (width // 2) + u * TILE, TILE)

    def e_first(t, u, P):
        for i in range(2):
            EXS[t, u, i] = P[2 * i + 1 - x, :, cols(u, 0)].astype(bf16)
        e_copy(t, u, 0).start()
        for i in range(2):
            EYS[t, u, i] = P[2 - 2 * y + i, :, cols(u, 1)].astype(bf16)
        e_copy(t, u, 1).start()

    def e_second(t, u, P):
        e_copy(t, u, 0).wait_recv()
        EYS2[t, u] = (P[m_y, :, cols(u, 0)] + EXR[t, u, 1 - y].astype(f32)).astype(bf16)
        e_copy(t, u, 3).start()
        e_copy(t, u, 1).wait_recv()
        EXS2[t, u] = (P[m_x, :, cols(u, 1)] + EYR[t, u, 1 - x].astype(f32)).astype(bf16)
        e_copy(t, u, 2).start()

    def e_last(t, u, P):
        e_copy(t, u, 3).wait_recv()
        P[m_own, :, cols(u, 0)] += EXR[t, u, y].astype(f32) + EYR2[t, u].astype(f32)
        e_copy(t, u, 2).wait_recv()
        P[m_own, :, cols(u, 1)] += EYR[t, u, x].astype(f32) + EXR2[t, u].astype(f32)

    def e_sent(t):
        for u in range(2):
            for i in range(4):
                e_copy(t, u, i).wait_send()

    for k in range(NK):
        own_copy(k).start()
    xf = x_ref[...].astype(f32)
    centred = xf - jnp.mean(xf, axis=-1, keepdims=True)
    rstd = lax.rsqrt(jnp.mean(centred * centred, axis=-1, keepdims=True) + NORM_EPS)
    xhat = centred * rstd
    XH[...] = xhat
    RSTD[...] = jnp.broadcast_to(rstd, RSTD.shape)
    NA[m_own] = (xhat * gain_ref[...] + bias_ref[...]).astype(bf16)

    bucket = bucket_ref[0]
    B[z, y, c, 0:8] = jnp.broadcast_to(bin_ref[...].astype(f32), (8, 128)).astype(bf16)
    B[z, y, c, 8:16] = jnp.full((8, 128), bucket.astype(f32), f32).astype(bf16)

    pl.semaphore_wait(barrier, len(peers))
    for k in order[:5]:
        y_copy(k).start()
    g_send(0)
    for k in order[5:8]:
        y_copy(k).start()

    slot = lax.shift_right_logical(jnp.int32(rows), bucket)
    shift_of = (rows.bit_length() - 1) - bucket
    row = x * rows + lax.broadcasted_iota(jnp.int32, (rows, 128), 0)
    slot_of = lax.shift_right_logical(row, jnp.full(row.shape, shift_of, jnp.int32))
    place = row & jnp.full(row.shape, slot - 1, jnp.int32)
    limit = jnp.zeros((rows, 128), jnp.int32)
    for s in range(SLOTS):
        limit = jnp.where(slot_of == s, counts_ref[s], limit)
    valid = jnp.where(place < limit, 1.0, 0.0)[:, 0:1]
    seeds = cot_ref[...].astype(f32) * valid
    SA[m_own] = seeds.astype(bf16)
    back_sum = jnp.sum(seeds, axis=0, keepdims=True)
    V[...] = jnp.zeros_like(V)
    for i in range(8):
        V[16 + i : 17 + i, :] = back_sum[:, i * 128 : (i + 1) * 128]
    ag_turn()
    ag_turn()

    lane = lax.broadcasted_iota(jnp.int32, (rows, TILE), 1)
    even = (lane & 1) == 0

    def table(g):
        brow = B[z, g, c].astype(f32)[8:9, :]
        ba = jnp.broadcast_to(brow, (rows, 128))

        def pick(ref):
            full = ref[...]
            out = full
            for b in range(1, 4):
                n = rows >> b
                out = jnp.where(ba == float(b), jnp.concatenate([full[:n]] * (1 << b), axis=0), out)
            return out

        cg, sg = pick(cos_ref), pick(sin_ref)
        CT[g] = jnp.concatenate([cg, cg], axis=1)
        SN[g] = jnp.concatenate([sg, sg], axis=1)
        size = jnp.full((rows, 128), rows, jnp.int32)
        for b in range(1, 4):
            size = jnp.where(ba == float(b), rows >> b, size)
        size = jnp.concatenate([size, size], axis=1)
        qi = lax.broadcasted_iota(jnp.int32, (rows, rows), 0)
        ki = lax.broadcasted_iota(jnp.int32, (rows, rows), 1)
        BM[g] = jnp.where((ki <= qi) & ((qi ^ ki) < size), 0.0, MASKED_SCORE)

    def tables():
        for g in range(2):
            table(g)

    def turn(v, g, sign):
        other = jnp.where(even, -pltpu.roll(v, TILE - 1, 1), pltpu.roll(v, 1, 1))
        return v * CT[g] + (sign * other) * SN[g]

    def flip(src, dst, m):
        cs = pl.ds(pl.multiple_of(m * rows, rows), rows)
        for d in range(4):
            dst[d, :, cs] = src[m, :, d * TILE : (d + 1) * TILE].T

    def weight(k):
        return W[k].reshape(width, TILE)

    scale = HD ** (-0.5)

    def project(m):
        g = m // 2
        nb = NA[m]
        QR[m] = turn(dot_nn(nb, weight(0)), g, 1.0).astype(bf16)
        KR[m] = turn(dot_nn(nb, weight(1)), g, 1.0).astype(bf16)
        VR[m] = dot_nn(nb, weight(2)).astype(bf16)

    def attend(m):
        g = m // 2
        q, kk, v = QR[m], KR[m], VR[m]
        da = dot_nn(SA[m], weight(3)).astype(bf16)
        zero = jnp.zeros((rows, TILE), bf16)
        att = dq = dk = dv = None
        for h in range(N_HEADS):
            mine = (lane // HD) == h
            qh = jnp.where(mine, q, zero)
            kh = jnp.where(mine, kk, zero)
            vh = jnp.where(mine, v, zero)
            dh = jnp.where(mine, da, zero)
            s = dot_nt(qh, kk) * scale + BM[g]
            e = jnp.exp(s - jnp.max(s, axis=-1, keepdims=True))
            p = e * (1.0 / jnp.sum(e, axis=-1, keepdims=True))
            pb = p.astype(bf16)
            pg = dot_nt(dh, v)
            sg = p * (pg - jnp.sum(p * pg, axis=-1, keepdims=True))
            sb = sg.astype(bf16)
            now = (dot_nn(pb, vh), dot_nn(sb, kh), dot_tn(sb, qh), dot_tn(pb, dh))
            if h == 0:
                att, dq, dk, dv = now
            else:
                att, dq, dk, dv = (a + b for a, b in zip((att, dq, dk, dv), now))
        at = att.astype(bf16)
        dqb = turn(dq * scale, g, -1.0).astype(bf16)
        dkb = turn(dk * scale, g, -1.0).astype(bf16)
        dvb = dv.astype(bf16)
        rs = pl.ds(pl.multiple_of(m * rows, rows), rows)
        ATT[rs, :] = at
        DQ[rs, :] = dqb
        DK[rs, :] = dkb
        DV[rs, :] = dvb
        OUT[m] = dot_nt(at, weight(3))
        DN[m] = dot_nt(dqb, weight(0)) + dot_nt(dkb, weight(1)) + dot_nt(dvb, weight(2))

    def grad_of(k, left, right):
        total = dot_nn(left[...].reshape(4 * TILE, 4 * rows), right)
        GP[k] = total.astype(bf16).reshape(NZ, 2, 2, 64, TILE)
        rs_c(k).start()

    def slice_of(j):
        return NQ + 2 * j, NQ + 1 + 2 * j

    def feed(j, m):
        ki, kb = slice_of(j)
        b0 = B[2 * y + j // 2, j % 2, 0].astype(f32)[0:1, :]
        b1 = B[2 * y + j // 2, j % 2, 1].astype(f32)[0:1, :]
        u = dot_nn(NA[m], weight(ki)) + jnp.concatenate([b0, b1], axis=1)
        u2 = u * u
        k0 = float(np.sqrt(2.0 / np.pi))
        t = jnp.tanh(k0 * u * (1.0 + 0.044715 * u2))
        act = (0.5 * u * (1.0 + t)).astype(bf16)
        slope = 0.5 * (1.0 + t) + (0.5 * k0) * u * (1.0 - t * t) * (1.0 + 0.134145 * u2)
        hg = (dot_nn(SA[m], weight(kb)) * slope).astype(bf16)
        rs = pl.ds(pl.multiple_of(m * rows, rows), rows)
        ACT[j, rs, :] = act
        HG[j, rs, :] = hg
        OUT[m] += dot_nt(act, weight(kb))
        DN[m] += dot_nt(hg, weight(ki))
        at = 24 + x * 16 + y * 8 + 2 * j
        total = jnp.sum(hg.astype(f32), axis=0, keepdims=True)
        V[pl.ds(at, 1), :] += total[:, :128]
        V[pl.ds(at + 1, 1), :] += total[:, 128:]

    def feed_grads(j):
        ki, kb = slice_of(j)
        grad_of(ki, NT, HG[j])
        grad_of(kb, ST, ACT[j])

    def feed_rows(j, *between):
        for i in (0, 1):
            feed(j, 2 * i)
            feed(j, 2 * i + 1)
            if i < len(between):
                between[i]()

    def v_copy(i, dev):
        return rcp(VS.at[min(i, 3)], VRV.at[i], vs.at[i], vr.at[i], dev)

    v_devs = (dev_c, dev_x, dev_y)

    def v_step(i):
        v_copy(i, v_devs[i]).wait_recv()
        VS[i + 1] = VS[i] + VRV[i]
        if i < 2:
            v_copy(i + 1, v_devs[i + 1]).start()
        else:
            for n, dev in enumerate(dev_z):
                v_copy(3 + n, dev).start()

    def arrived(*chunks):
        for k in chunks:
            ag_done(k)

    flip(NA, NT, m_own)
    flip(SA, ST, m_own)
    ag_turn()
    g_near(0)
    for k in order[8:]:
        y_copy(k).start()
    g_send(1)
    g_forward(0)
    tables()
    ag_turn()
    g_rest(0)
    flip(NA, NT, m_x)
    flip(NA, NT, m_y)
    ag_turn()
    ag_turn()
    ag_turn()
    arrived(0, NK, 1, 2)
    project(m_own)
    project(m_x)
    project(m_y)
    ag_turn()
    arrived(3)
    attend(m_own)
    g_near(1)
    g_forward(1)
    ag_turn()
    g_rest(1)
    attend(m_x)
    flip(SA, ST, m_x)
    flip(SA, ST, m_y)
    ag_turn()
    attend(m_y)
    g_far(0)
    flip(NA, NT, m_d)
    project(m_d)
    ag_turn()
    g_far(1)
    flip(SA, ST, m_d)
    attend(m_d)
    grad_of(0, NT, DQ[...])
    ag_turn()
    grad_of(1, NT, DK[...])
    rs_begin(0)
    grad_of(2, NT, DV[...])
    rs_begin(1)
    grad_of(3, ST, ATT[...])
    rs_begin(2)
    ag_turn()
    arrived(4, 5)
    feed_rows(0, lambda: rs_begin(3))
    rs_turn()
    ag_turn()
    arrived(6, 7)
    feed_rows(1)
    rs_turn()
    ag_turn()
    feed_grads(0)
    arrived(8, 9)
    feed_rows(2, lambda: rs_begin(4))
    rs_begin(5)
    rs_turn()
    ag_turn()
    arrived(10, 11)
    feed_rows(3)

    for u in range(2):
        e_first(1, u, DN)
    rs_turn()
    feed_grads(1)
    rs_begin(6)
    rs_begin(7)
    rs_turn()
    feed_grads(2)
    rs_begin(8)
    rs_begin(9)
    e_second(1, 0, DN)
    rs_turn()
    feed_grads(3)
    rs_begin(10)
    rs_begin(11)
    rs_turn()
    e_second(1, 1, DN)
    for u in range(2):
        e_first(0, u, OUT)
    rs_turn()
    for u in range(2):
        e_last(1, u, DN)
    dn = DN[m_own]
    xhat = XH[...]
    gsum = jnp.sum(dn * xhat, axis=0, keepdims=True)
    bsum = jnp.sum(dn, axis=0, keepdims=True)
    for i in range(8):
        V[i : i + 1, :] = gsum[:, i * 128 : (i + 1) * 128]
        V[8 + i : 9 + i, :] = bsum[:, i * 128 : (i + 1) * 128]
    VS[0] = V[...]
    v_copy(0, dev_c).start()
    e = dn * gain_ref[...]
    me = jnp.mean(e, axis=-1, keepdims=True)
    mex = jnp.mean(e * xhat, axis=-1, keepdims=True)
    gin_ref[...] = (SA[m_own].astype(f32) + RSTD[:, 0:1] * (e - me - xhat * mex)).astype(bf16)
    v_step(0)
    rs_turn()
    rs_turn()
    e_second(0, 0, OUT)
    rs_turn()
    v_step(1)
    e_second(0, 1, OUT)
    rs_turn()
    v_step(2)
    for _ in range(NK + 4):
        rs_turn()
    for k in range(NK):
        rs_out(k)
    for i in range(3):
        v_copy(3 + i, dev_z[i]).wait_recv()
    V[...] = VS[3] + VRV[3] + VRV[4] + VRV[5]
    index = 2 * dp + x
    lane4 = lax.rem(index, 4)
    for base, ref in ((0, lng_ref), (8, lnb_ref), (16, bbk_ref)):
        line = V[pl.ds(base + index // 4, 1), :]
        out = line[:, 0:32]
        for n in range(1, 4):
            out = jnp.where(lane4 == n, line[:, 32 * n : 32 * n + 32], out)
        ref[...] = out
    gbin_ref[...] = V[pl.ds(24 + 16 * x + dp, 1), :]
    for u in range(2):
        e_last(0, u, OUT)
    block_ref[...] = (x_ref[...].astype(f32) + OUT[m_own] + bback_ref[...]).astype(bf16)

    def later(f):
        lax.fori_loop(0, NK, lambda k, _: (f(k), 0)[1], 0)

    for k in range(NK + 1):
        ag_sent(k)
    for t in range(2):
        g_sent(t)
        e_sent(t)
    later(rs_sent)
    for i, dev in enumerate([dev_c, dev_x, dev_y] + dev_z):
        v_copy(i, dev).wait_send()


def write_kernel(*refs):
    srcs, dsts, sems = refs[:10], refs[10:20], refs[20]
    copies = [pltpu.make_async_copy(a, b, sems.at[i]) for i, (a, b) in enumerate(zip(srcs, dsts))]
    for copy in copies:
        copy.start()
    for copy in copies:
        copy.wait()


def rope_constants(rows):
    half = np.arange(ROT // 2, dtype=np.float32)
    rates = (10000.0 ** (-2.0 * half / ROT)).astype(np.float32)
    angle = np.arange(rows, dtype=np.float32)[:, None] * rates[None, :]
    angle = np.repeat(angle, 2, axis=1)
    cos = np.concatenate([np.cos(angle), np.ones((rows, HD - ROT))], axis=1)
    sin = np.concatenate([np.sin(angle), np.zeros((rows, HD - ROT))], axis=1)
    two = lambda t: np.concatenate([t, t], axis=1).astype(np.float32)
    return two(cos), two(sin)


def on_quad(
    residual_in,
    cotangent,
    ln_gain,
    ln_bias,
    w_qkv,
    w_out,
    w_in,
    b_in,
    w_back,
    b_back,
    bucket_ids,
    residue_counts,
):
    rows, width = residual_in.shape
    cos, sin = rope_constants(rows)
    f32, bf16 = jnp.float32, jnp.bfloat16
    vm = pl.BlockSpec(memory_space=pltpu.VMEM)
    sm = pl.BlockSpec(memory_space=pltpu.SMEM)
    anyspace = pl.BlockSpec(memory_space=pl.ANY)
    shard = width // (4 * NZ)
    sem = pltpu.SemaphoreType.DMA
    block = (2, 2, rows, TILE)
    shapes = (
        jax.ShapeDtypeStruct((rows, width), bf16),
        jax.ShapeDtypeStruct((rows, width), bf16),
        jax.ShapeDtypeStruct((3, shard, 2 * TILE), f32),
        jax.ShapeDtypeStruct((shard, 2 * TILE), f32),
        jax.ShapeDtypeStruct((shard, 2 * NJ * TILE), f32),
        jax.ShapeDtypeStruct((shard, 2 * NJ * TILE), f32),
        jax.ShapeDtypeStruct((1, 32), f32),
        jax.ShapeDtypeStruct((1, 32), f32),
        jax.ShapeDtypeStruct((1, 32), f32),
        jax.ShapeDtypeStruct((1, 128), f32),
    )
    held = pl.pallas_call(
        layer_kernel,
        out_shape=tuple(pltpu.VMEM(v.shape, v.dtype) for v in shapes),
        in_specs=[sm, sm] + [vm] * 8 + [anyspace] * 4,
        out_specs=(vm,) * 10,
        scratch_shapes=[
            pltpu.VMEM((NZ, 2, 2, 16, 128), bf16),
            pltpu.VMEM((NK, NZ, 2, 2, shard, TILE), bf16),
            pltpu.VMEM((4, rows, width), bf16),
            pltpu.VMEM((4, rows, width), bf16),
            pltpu.VMEM((4, TILE, 4 * rows), bf16),
            pltpu.VMEM((4, TILE, 4 * rows), bf16),
            pltpu.VMEM((2, rows, TILE), f32),
            pltpu.VMEM((2, rows, TILE), f32),
            pltpu.VMEM((2, rows, rows), f32),
            pltpu.VMEM((4, rows, TILE), bf16),
            pltpu.VMEM((4, rows, TILE), bf16),
            pltpu.VMEM((4, rows, TILE), bf16),
            pltpu.VMEM((4 * rows, TILE), bf16),
            pltpu.VMEM((4 * rows, TILE), bf16),
            pltpu.VMEM((4 * rows, TILE), bf16),
            pltpu.VMEM((4 * rows, TILE), bf16),
            pltpu.VMEM((NJ, 4 * rows, TILE), bf16),
            pltpu.VMEM((NJ, 4 * rows, TILE), bf16),
            pltpu.VMEM((4, rows, width), f32),
            pltpu.VMEM((4, rows, width), f32),
            pltpu.VMEM((NK, NZ, 2, 2, shard, TILE), bf16),
            pltpu.VMEM((NK, NZ, 2, shard, TILE), bf16),
            pltpu.VMEM((NK, 5, 2, shard, TILE), bf16),
            pltpu.VMEM((2, shard, TILE), f32),
            pltpu.VMEM((NK, shard, TILE), bf16),
            pltpu.VMEM((NK, shard, TILE), bf16),
            pltpu.VMEM((rows, width), f32),
            pltpu.VMEM((rows, 128), f32),
            pltpu.VMEM((2,) + block, bf16),
            pltpu.VMEM((2,) + block, bf16),
            pltpu.VMEM((2,) + block, bf16),
            pltpu.VMEM((2,) + block, bf16),
            pltpu.VMEM((2, 2, rows, TILE), bf16),
            pltpu.VMEM((2, 2, rows, TILE), bf16),
            pltpu.VMEM((2, 2, rows, TILE), bf16),
            pltpu.VMEM((2, 2, rows, TILE), bf16),
            pltpu.VMEM((VROWS, 128), f32),
            pltpu.VMEM((4, VROWS, 128), f32),
            pltpu.VMEM((6, VROWS, 128), f32),
            sem((NK,)),
            sem((NK + 1,)),
            sem((NK + 1,)),
            sem((NK + 1, 2, 3)),
            sem((NK + 1, 2, 3)),
            sem((NK + 1, NZ)),
            sem((NK + 1, NZ)),
            sem((12,)),
            sem((12,)),
            sem((NK,)),
            sem((NK,)),
            sem((NK, NZ)),
            sem((NK, 5)),
            sem((NK,)),
            sem((NK,)),
            sem((2, 2, 4)),
            sem((2, 2, 4)),
            sem((6,)),
            sem((6,)),
        ],
        compiler_params=pltpu.CompilerParams(
            collective_id=0, has_side_effects=True, vmem_limit_bytes=58 << 20
        ),
        cost_estimate=pl.CostEstimate(
            flops=20 * 2**30, bytes_accessed=8 * 2**20, transcendentals=2**21
        ),
    )(
        bucket_ids,
        residue_counts.reshape(SLOTS),
        residual_in,
        cotangent,
        ln_gain.reshape(1, width),
        ln_bias.reshape(1, width),
        b_back.reshape(1, width),
        jnp.asarray(cos),
        jnp.asarray(sin),
        b_in.reshape(1, 128),
        w_qkv,
        w_out.T,
        w_in,
        w_back.T,
    )
    held = [pltpu.with_memory_space_constraint(v, pltpu.VMEM) for v in held]
    outs = pl.pallas_call(
        write_kernel,
        out_shape=shapes,
        in_specs=[vm] * 10,
        out_specs=(anyspace,) * 10,
        scratch_shapes=[sem((10,))],
    )(*held)
    block_out, grad_input, grad_w_qkv, gwo, grad_w_in, gwb, lng, lnb, bbk, gbin = outs
    return (
        block_out,
        grad_input,
        lng.reshape(32),
        lnb.reshape(32),
        grad_w_qkv,
        gwo.T,
        grad_w_in,
        gbin.reshape(128),
        gwb.T,
        bbk.reshape(32),
    )


def solution(mesh):
    placed = (
        P(("dp", "mp"), None),
        P(("dp", "mp"), None),
        P(),
        P(),
        P(None, "dp", "mp"),
        P("mp", "dp"),
        P("dp", "mp"),
        P(("mp", "dp")),
        P("mp", "dp"),
        P(),
        P("dp"),
        P("dp", None),
    )
    return jax.shard_map(
        on_quad if fits_quad(mesh) else on_device,
        mesh=mesh,
        in_specs=placed,
        out_specs=(
            P(("dp", "mp"), None),
            P(("dp", "mp"), None),
            P(("dp", "mp")),
            P(("dp", "mp")),
            P(None, "dp", "mp"),
            P("mp", "dp"),
            P("dp", "mp"),
            P(("mp", "dp")),
            P("mp", "dp"),
            P(("dp", "mp")),
        ),
        check_vma=False,
    )
```

```python
from functools import partial

import jax
import jax.numpy as jnp
import numpy as np
from jax import lax
from jax.experimental import pallas as pl
from jax.experimental.pallas import tpu as pltpu
from jax.sharding import PartitionSpec as P

HD = 64
ROT = 32
SLOTS = 16


NORM_EPS = 1e-05
MASKED_SCORE = -1e30


def norm_rows(inputs_now, norm_gain, norm_shift):
    centred = inputs_now - jnp.mean(inputs_now, axis=-1, keepdims=True)
    spread = jnp.mean(centred * centred, axis=-1, keepdims=True)
    return centred * lax.rsqrt(spread + NORM_EPS) * norm_gain + norm_shift


def slot_tables(bucket_one, residue_row, group_rows):
    slot_length = jnp.right_shift(jnp.int32(group_rows // 2), bucket_one)
    places = jnp.arange(group_rows, dtype=jnp.int32)
    slot_ids = places // slot_length
    inside = places - slot_ids * slot_length
    match_table = slot_ids[:, None] == jnp.arange(SLOTS, dtype=jnp.int32)[None, :]
    picked = jnp.sum(jnp.where(match_table, residue_row[None, :], 0), axis=1)
    live_rows = jnp.minimum(picked, slot_length)
    return (slot_ids, inside, inside < live_rows)


def rope_tables(inside):
    half_steps = jnp.arange(ROT // 2, dtype=jnp.float32)
    inverse_rates = 10000.0 ** (-2.0 * half_steps / ROT)
    angles = inside.astype(jnp.float32)[:, None] * inverse_rates[None, :]
    return (jnp.cos(angles), jnp.sin(angles))


def rotate(values, cosine_table, sine_table):
    row_count = values.shape[0]
    head_count = values.shape[1]
    paired = values[..., :ROT].reshape(row_count, head_count, ROT // 2, 2)
    even_part = paired[..., 0]
    odd_part = paired[..., 1]
    cosine_now = cosine_table[:, None, :]
    sine_now = sine_table[:, None, :]
    turned = jnp.stack(
        [
            even_part * cosine_now - odd_part * sine_now,
            odd_part * cosine_now + even_part * sine_now,
        ],
        axis=-1,
    )
    return jnp.concatenate([turned.reshape(row_count, head_count, ROT), values[..., ROT:]], axis=-1)


def mask_block(block_start, block_rows, slot_ids):
    query_places = block_start + jnp.arange(block_rows, dtype=jnp.int32)
    query_slots = lax.dynamic_slice_in_dim(slot_ids, block_start, block_rows, 0)
    key_places = jnp.arange(slot_ids.shape[0], dtype=jnp.int32)
    return (query_slots[:, None] == slot_ids[None, :]) & (
        key_places[None, :] <= query_places[:, None]
    )


def over_rows(first_op, second_op):
    return lax.dot_general(
        first_op, second_op, (((0,), (0,)), ((), ())), preferred_element_type=jnp.float32
    )


def against_weight(first_op, second_op):
    return lax.dot_general(
        first_op, second_op, (((1,), (1,)), ((), ())), preferred_element_type=jnp.float32
    )


def on_device(
    residual_in,
    cotangent,
    ln_gain,
    ln_bias,
    w_qkv,
    w_out,
    w_in,
    b_in,
    w_back,
    b_back,
    bucket_ids,
    residue_counts,
):
    model_count = lax.axis_size("mp")
    model_rank = lax.axis_index("mp")
    local_rows = residual_in.shape[0]
    group_rows = local_rows * model_count
    slot_ids, inside, valid_rows = slot_tables(bucket_ids[0], residue_counts[0], group_rows)
    cosine_table, sine_table = rope_tables(inside)
    qkv_all, out_all, in_all, bias_in, back_all = (
        lax.all_gather(w_qkv, "dp", axis=1, tiled=True),
        lax.all_gather(w_out, "dp", axis=1, tiled=True),
        lax.all_gather(w_in, "dp", axis=0, tiled=True),
        lax.all_gather(b_in, "dp", axis=0, tiled=True),
        lax.all_gather(w_back, "dp", axis=1, tiled=True),
    )
    x_local = residual_in.astype(jnp.float32)
    x_group = lax.all_gather(residual_in, "mp", axis=0, tiled=True).astype(jnp.float32)
    normed = norm_rows(x_group, ln_gain, ln_bias).astype(jnp.bfloat16)
    head_width = qkv_all.shape[2]
    head_count = head_width // HD
    score_scale = HD ** (-0.5)

    def project(member_index):
        return jnp.dot(normed, qkv_all[member_index], preferred_element_type=jnp.float32).reshape(
            group_rows, head_count, HD
        )

    queries = rotate(project(0), cosine_table, sine_table).astype(jnp.bfloat16)
    key_rows = rotate(project(1), cosine_table, sine_table).astype(jnp.bfloat16)
    value_rows = project(2).astype(jnp.bfloat16)
    block_rows = min(512, group_rows)
    starts = jnp.arange(group_rows // block_rows, dtype=jnp.int32) * block_rows

    def block_scores(block_start):
        query_block = lax.dynamic_slice_in_dim(queries, block_start, block_rows, 0)
        allowed = mask_block(block_start, block_rows, slot_ids)
        scores = (
            jnp.einsum("qhd,khd->hqk", query_block, key_rows, preferred_element_type=jnp.float32)
            * score_scale
        )
        return (query_block, jnp.where(allowed[None], scores, MASKED_SCORE))

    def forward_block(block_start):
        query_block, scores = block_scores(block_start)
        row_peak = jnp.max(scores, axis=-1, keepdims=True)
        exp_scores = jnp.exp(scores - row_peak)
        row_total = jnp.sum(exp_scores, axis=-1, keepdims=True)
        weights_now = (exp_scores / row_total).astype(jnp.bfloat16)
        attended = jnp.einsum(
            "hqk,khd->qhd", weights_now, value_rows, preferred_element_type=jnp.float32
        )
        return (attended.astype(jnp.bfloat16), (row_peak + jnp.log(row_total))[..., 0])

    attended_blocks, log_totals = lax.map(forward_block, starts)
    mixed_rows = attended_blocks.reshape(group_rows, head_width)
    hidden = jnp.dot(normed, in_all, preferred_element_type=jnp.float32) + bias_in.astype(
        jnp.float32
    )
    gelu_tanh = partial(jax.nn.gelu, approximate=True)
    active_value, gelu_pull = jax.vjp(gelu_tanh, hidden)
    active = active_value.astype(jnp.bfloat16)
    partial_out = jnp.dot(mixed_rows, out_all, preferred_element_type=jnp.float32) + jnp.dot(
        active, back_all, preferred_element_type=jnp.float32
    )
    summed_all = lax.psum(partial_out.astype(jnp.bfloat16), "mp").astype(jnp.float32)
    summed = lax.dynamic_slice_in_dim(summed_all, model_rank * local_rows, local_rows, 0)
    block_out = (x_local + summed + b_back).astype(jnp.bfloat16)
    cot_group = lax.all_gather(cotangent, "mp", axis=0, tiled=True)
    seed_rows = jnp.where(valid_rows[:, None], cot_group, jnp.zeros_like(cot_group))
    qkv_all, out_all, in_all, back_all = (
        lax.all_gather(w_qkv, "dp", axis=1, tiled=True),
        lax.all_gather(w_out, "dp", axis=1, tiled=True),
        lax.all_gather(w_in, "dp", axis=0, tiled=True),
        lax.all_gather(w_back, "dp", axis=1, tiled=True),
    )
    active_grad = against_weight(seed_rows, back_all)
    hidden_grad = gelu_pull(active_grad)[0].astype(jnp.bfloat16)
    grad_in_local = over_rows(normed, hidden_grad)
    grad_bias_in = jnp.sum(hidden_grad.astype(jnp.float32), axis=0)
    grad_back_local = over_rows(active, seed_rows)
    grad_out_local = over_rows(mixed_rows, seed_rows)
    normed_grad = against_weight(hidden_grad, in_all)
    mixed_grad = (
        against_weight(seed_rows, out_all).astype(jnp.bfloat16).reshape(group_rows, head_count, HD)
    )

    def backward_block(carry, inputs_now):
        key_acc, value_acc = carry
        block_start, log_total = inputs_now
        query_block, scores = block_scores(block_start)
        grad_block = lax.dynamic_slice_in_dim(mixed_grad, block_start, block_rows, 0)
        probs = jnp.exp(scores - log_total[..., None])
        probs_low = probs.astype(jnp.bfloat16)
        value_acc = value_acc + jnp.einsum(
            "hqk,qhd->khd", probs_low, grad_block, preferred_element_type=jnp.float32
        )
        probs_grad = jnp.einsum(
            "qhd,khd->hqk", grad_block, value_rows, preferred_element_type=jnp.float32
        )
        score_grad = probs * (probs_grad - jnp.sum(probs * probs_grad, axis=-1, keepdims=True))
        score_low = score_grad.astype(jnp.bfloat16)
        query_grad = (
            jnp.einsum("hqk,khd->qhd", score_low, key_rows, preferred_element_type=jnp.float32)
            * score_scale
        )
        key_acc = (
            key_acc
            + jnp.einsum("hqk,qhd->khd", score_low, query_block, preferred_element_type=jnp.float32)
            * score_scale
        )
        return ((key_acc, value_acc), query_grad)

    empty_heads = jnp.zeros((group_rows, head_count, HD), jnp.float32)
    (key_acc, value_acc), query_blocks = lax.scan(
        backward_block, (empty_heads, empty_heads), (starts, log_totals)
    )
    turn_back = partial(rotate, cosine_table=cosine_table, sine_table=sine_table)
    unturn = jax.vjp(turn_back, empty_heads)[1]
    query_pre_grad = (
        unturn(query_blocks.reshape(group_rows, head_count, HD))[0]
        .astype(jnp.bfloat16)
        .reshape(group_rows, head_width)
    )
    key_pre_grad = unturn(key_acc)[0].astype(jnp.bfloat16).reshape(group_rows, head_width)
    value_grad = value_acc.astype(jnp.bfloat16).reshape(group_rows, head_width)
    grad_qkv_local = jnp.stack(
        [
            over_rows(normed, query_pre_grad),
            over_rows(normed, key_pre_grad),
            over_rows(normed, value_grad),
        ],
        axis=0,
    )
    normed_grad = (
        normed_grad
        + against_weight(query_pre_grad, qkv_all[0])
        + against_weight(key_pre_grad, qkv_all[1])
        + against_weight(value_grad, qkv_all[2])
    )
    share_grad = lax.psum(normed_grad.astype(jnp.bfloat16), "mp").astype(jnp.float32)
    seed_group = seed_rows.astype(jnp.float32)
    norm_pull = jax.vjp(norm_rows, x_group, ln_gain, ln_bias)[1]
    input_part, gain_part, shift_part = norm_pull(share_grad)
    input_group = seed_group + input_part
    grad_input = lax.dynamic_slice_in_dim(
        input_group, model_rank * local_rows, local_rows, 0
    ).astype(jnp.bfloat16)
    back_part = jnp.sum(seed_group, axis=0)
    grad_w_qkv, grad_w_out, grad_w_in, grad_b_in, grad_w_back, gain_rows, shift_rows, back_rows = (
        lax.psum_scatter(
            grad_qkv_local.astype(jnp.bfloat16), "dp", scatter_dimension=1, tiled=True
        ).astype(jnp.float32),
        lax.psum_scatter(
            grad_out_local.astype(jnp.bfloat16), "dp", scatter_dimension=1, tiled=True
        ).astype(jnp.float32),
        lax.psum_scatter(
            grad_in_local.astype(jnp.bfloat16), "dp", scatter_dimension=0, tiled=True
        ).astype(jnp.float32),
        lax.psum_scatter(
            grad_bias_in.astype(jnp.bfloat16), "dp", scatter_dimension=0, tiled=True
        ).astype(jnp.float32),
        lax.psum_scatter(
            grad_back_local.astype(jnp.bfloat16), "dp", scatter_dimension=1, tiled=True
        ).astype(jnp.float32),
        lax.psum_scatter(
            gain_part.astype(jnp.bfloat16), "dp", scatter_dimension=0, tiled=True
        ).astype(jnp.float32),
        lax.psum_scatter(
            shift_part.astype(jnp.bfloat16), "dp", scatter_dimension=0, tiled=True
        ).astype(jnp.float32),
        lax.psum_scatter(
            back_part.astype(jnp.bfloat16), "dp", scatter_dimension=0, tiled=True
        ).astype(jnp.float32),
    )
    piece_width = gain_rows.shape[0] // model_count
    grad_ln_gain = lax.dynamic_slice_in_dim(gain_rows, model_rank * piece_width, piece_width, 0)
    grad_ln_bias = lax.dynamic_slice_in_dim(shift_rows, model_rank * piece_width, piece_width, 0)
    grad_b_back = lax.dynamic_slice_in_dim(back_rows, model_rank * piece_width, piece_width, 0)
    return (
        block_out,
        grad_input,
        grad_ln_gain,
        grad_ln_bias,
        grad_w_qkv,
        grad_w_out,
        grad_w_in,
        grad_b_in,
        grad_w_back,
        grad_b_back,
    )


MESH = pl.DeviceIdType.MESH
NZ = 4
TILE = 256
N_HEADS = TILE // HD
NQ = 4
NJ = 4
NK = NQ + 2 * NJ
VROWS = 56


def fits_quad(mesh):
    return mesh.shape["mp"] == 2 and mesh.shape["dp"] == 4 * NZ


def dot_nn(a, b):
    return lax.dot_general(a, b, (((1,), (0,)), ((), ())), preferred_element_type=jnp.float32)


def dot_nt(a, b):
    return lax.dot_general(a, b, (((1,), (1,)), ((), ())), preferred_element_type=jnp.float32)


def dot_tn(a, b):
    return lax.dot_general(a, b, (((0,), (0,)), ((), ())), preferred_element_type=jnp.float32)


def layer_kernel(
    bucket_ref,
    counts_ref,
    x_ref,
    cot_ref,
    gain_ref,
    bias_ref,
    bback_ref,
    cos_ref,
    sin_ref,
    bin_ref,
    wqkv_ref,
    wot_ref,
    win_ref,
    wbt_ref,
    block_ref,
    gin_ref,
    gqkv_ref,
    got_ref,
    gi_ref,
    gbt_ref,
    lng_ref,
    lnb_ref,
    bbk_ref,
    gbin_ref,
    B,
    W,
    NA,
    SA,
    CT,
    SN,
    BM,
    QR,
    KR,
    VR,
    DQ,
    DK,
    DV,
    ATT,
    ACT,
    HG,
    OUT,
    DN,
    GP,
    GC,
    RZ,
    FS,
    YS,
    YR,
    XH,
    RSTD,
    EXSa,
    EXSb,
    EYSa,
    EYSb,
    EXRa,
    EXRb,
    EYRa,
    EYRb,
    EXS2a,
    EXS2b,
    EYS2a,
    EYS2b,
    EXR2a,
    EXR2b,
    EYR2a,
    EYR2b,
    V,
    VS,
    VRV,
    loc_sem,
    ays,
    ayr,
    azs,
    azr,
    acs,
    acr,
    gs,
    gr,
    rcs,
    rcr,
    rzs,
    rzr,
    rys,
    ryr,
    exs,
    exr,
    vs,
    vr,
):
    EXS = (EXSa, EXSb)
    EYS = (EYSa, EYSb)
    EXR = (EXRa, EXRb)
    EYR = (EYRa, EYRb)
    EXS2 = (EXS2a, EXS2b)
    EYS2 = (EYS2a, EYS2b)
    EXR2 = (EXR2a, EXR2b)
    EYR2 = (EYR2a, EYR2b)
    f32, bf16 = jnp.float32, jnp.bfloat16
    dp, x = lax.axis_index("dp"), lax.axis_index("mp")
    z = dp // 4
    y = lax.rem(dp // 2, 2)
    c = lax.rem(dp, 2)
    rows = x_ref.shape[0]
    width = x_ref.shape[1]
    dev_x = (dp, 1 - x)
    dev_y = (dp + 2 - 4 * y, x)
    dev_c = (dp + 1 - 2 * c, x)
    dev_r = (lax.rem(dp + 4, 4 * NZ), x)
    dev_l = (lax.rem(dp + 4 * NZ - 4, 4 * NZ), x)
    dev_z = [(lax.rem(dp + 4 * i, 4 * NZ), x) for i in (1, 2, 3)]
    m_own = 2 * y + x
    m_x = 2 * y + 1 - x
    m_y = 2 - 2 * y + x
    m_d = 3 - m_own

    def rcp(src, dst, ss, rs, dev):
        return pltpu.make_async_remote_copy(
            src_ref=src, dst_ref=dst, send_sem=ss, recv_sem=rs, device_id=dev, device_id_type=MESH
        )

    barrier = pltpu.get_barrier_semaphore()
    peers = [dev_x, dev_y, dev_c] + dev_z
    for peer in peers:
        pl.semaphore_signal(barrier, inc=1, device_id=peer, device_id_type=MESH)

    def wsrc(k, q):
        if k == NK:
            return None
        if k < 3:
            return wqkv_ref.at[k, :, pl.ds(pl.multiple_of(q * TILE, TILE), TILE)]
        if k == 3:
            return wot_ref.at[:, pl.ds(pl.multiple_of(q * TILE, TILE), TILE)]
        ref = win_ref if k % 2 == 0 else wbt_ref
        j = (k - NQ) // 2
        return ref.at[:, pl.ds(pl.multiple_of(q * (NJ * TILE) + j * TILE, TILE), TILE)]

    def wv(k):
        return B if isinstance(k, int) and k == NK else W.at[k]

    def own_copy(k):
        return pltpu.make_async_copy(wsrc(k, y), W.at[k, z, y, c], loc_sem.at[k])

    def y_copy(k):
        if k == NK:
            return rcp(B.at[z, y, c], B.at[z, y, c], ays.at[k], ayr.at[k], dev_y)
        return rcp(wsrc(k, 1 - y), W.at[k, z, y, c], ays.at[k], ayr.at[k], dev_y)

    def y_arrived(k):
        here = wv(k).at[z, 1 - y, c]
        rcp(here, here, ays.at[k], ayr.at[k], dev_y).wait_recv()

    def z_copy(k, way, s, e):
        block = wv(k).at[e, :, c]
        return rcp(
            block, block, azs.at[k, way, s], azr.at[k, way, s], dev_r if way == 0 else dev_l
        )

    def c_copy(k, e):
        block = wv(k).at[e, :, c]
        return rcp(block, block, acs.at[k, e], acr.at[k, e], dev_c)

    def ag_own(k, copied=True):
        if copied:
            pltpu.make_async_copy(
                W.at[k, z, y, c], W.at[k, z, y, c], loc_sem.at[k]
            ).wait()
        y_arrived(k)

        @pl.when(z < NZ - 1)
        def _():
            z_copy(k, 0, 0, z).start()

        @pl.when(z > 0)
        def _():
            z_copy(k, 1, 0, z).start()

        c_copy(k, z).start()

    def ag_step(k, s):
        @pl.when(z - 1 - s >= 0)
        def _():
            e = z - 1 - s
            z_copy(k, 0, s, e).wait_recv()
            if s < NZ - 2:

                @pl.when(z < NZ - 1)
                def _():
                    z_copy(k, 0, s + 1, e).start()

            c_copy(k, e).start()

        @pl.when(z + 1 + s <= NZ - 1)
        def _():
            e = z + 1 + s
            z_copy(k, 1, s, e).wait_recv()
            if s < NZ - 2:

                @pl.when(z > 0)
                def _():
                    z_copy(k, 1, s + 1, e).start()

            c_copy(k, e).start()

    def ag_done(k):
        for e in range(NZ):
            block = wv(k).at[e, :, 1 - c]
            rcp(block, block, acs.at[k, e], acr.at[k, e], dev_c).wait_recv()

    def ag_sent(k, copied=True):
        y_copy(k).wait_send() if isinstance(k, int) else None
        for s in range(NZ - 1):

            @pl.when((z < NZ - 1) & (z - s >= 0))
            def _():
                z_copy(k, 0, s, z - s).wait_send()

            @pl.when((z > 0) & (z + s <= NZ - 1))
            def _():
                z_copy(k, 1, s, z + s).wait_send()

        for e in range(NZ):
            c_copy(k, e).wait_send()

    order = [0, NK] + list(range(1, NK))
    turns = iter(range(NK + NZ))

    def ag_turn():
        t = next(turns, None)
        if t is None:
            return
        for n in range(2) if t == 0 else (t + 1,):
            if n <= NK:
                ag_own(order[n], copied=order[n] != NK)
        for s in range(NZ - 1):
            if 0 <= t - 1 - s <= NK:
                ag_step(order[t - 1 - s], s)

    P0 = 80
    parts = (pl.ds(0, P0), pl.ds(P0, rows - P0))
    BUF = (NA, SA)

    def g_copy(t, p, way, m):
        block = BUF[t].at[m, parts[p]]
        i = (t * 2 + p) * 3 + way
        dev = (dev_x, dev_y)[way] if way < 2 else (dev_y, dev_x)[p]
        return rcp(block, block, gs.at[i], gr.at[i], dev)

    def g_send(t):
        g_copy(t, 0, 0, m_own).start()
        g_copy(t, 1, 1, m_own).start()
        g_copy(t, 1, 0, m_own).start()
        g_copy(t, 0, 1, m_own).start()

    def g_near(t):
        g_copy(t, 0, 0, m_x).wait_recv()
        g_copy(t, 1, 1, m_y).wait_recv()

    def g_forward(t):
        g_copy(t, 0, 2, m_x).start()
        g_copy(t, 1, 2, m_y).start()

    def g_rest(t):
        g_copy(t, 1, 0, m_x).wait_recv()
        g_copy(t, 0, 1, m_y).wait_recv()

    def g_far(t):
        g_copy(t, 0, 2, m_d).wait_recv()
        g_copy(t, 1, 2, m_d).wait_recv()

    def g_sent(t):
        for p in (0, 1):
            for way in (0, 1):
                g_copy(t, p, way, m_own).wait_send()
        g_copy(t, 0, 2, m_x).wait_send()
        g_copy(t, 1, 2, m_y).wait_send()

    def rs_c(k):
        return rcp(GP.at[k, :, :, 1 - c], GC.at[k], rcs.at[k], rcr.at[k], dev_c)

    def rs_z(k, way, e, slot):
        return rcp(
            GP.at[k, e, :, c],
            RZ.at[k, slot],
            rzs.at[k, e],
            rzr.at[k, slot],
            dev_r if way == 0 else dev_l,
        )

    def rs_begin(k):
        rs_c(k).wait_recv()
        for e in range(NZ):
            GP[k, e, :, c] = (GP[k, e, :, c].astype(f32) + GC[k, e].astype(f32)).astype(bf16)

        @pl.when(z == 0)
        def _():
            for e in range(NZ - 1, 0, -1):
                rs_z(k, 0, e, e).start()

        @pl.when(z == NZ - 1)
        def _():
            for e in range(NZ - 1):
                rs_z(k, 1, e, e if e < NZ - 2 else 4).start()

    def pass_on(k, way, e, slot):
        rs_z(k, way, e, e).wait_recv()
        GP[k, e, :, c] = (GP[k, e, :, c].astype(f32) + RZ[k, e].astype(f32)).astype(bf16)
        rs_z(k, way, e, slot).start()

    def rs_hop1(k):
        @pl.when(z == 1)
        def _():
            pass_on(k, 0, 3, 3)
            pass_on(k, 0, 2, 2)

        @pl.when(z == 2)
        def _():
            pass_on(k, 1, 0, 0)
            pass_on(k, 1, 1, 4)

    def rs_hop2(k):
        @pl.when(z == 2)
        def _():
            pass_on(k, 0, 3, 3)

        @pl.when(z == 1)
        def _():
            pass_on(k, 1, 0, 4)

    def rs_y(k):
        return rcp(YS.at[k], YR.at[k], rys.at[k], ryr.at[k], dev_y)

    def put(k, q, value):
        if k < 3:
            gqkv_ref[k, :, pl.ds(pl.multiple_of(q * TILE, TILE), TILE)] = value
        elif k == 3:
            got_ref[:, pl.ds(pl.multiple_of(q * TILE, TILE), TILE)] = value
        else:
            ref = gi_ref if k % 2 == 0 else gbt_ref
            j = (k - NQ) // 2
            ref[:, pl.ds(pl.multiple_of(q * (NJ * TILE) + j * TILE, TILE), TILE)] = value

    def rs_final(k):
        FS[...] = GP[k, z, :, c].astype(f32)

        @pl.when(z > 0)
        def _():
            rs_z(k, 0, z, z).wait_recv()
            FS[...] += RZ[k, z].astype(f32)

        @pl.when(z < NZ - 1)
        def _():
            rs_z(k, 1, z, 4).wait_recv()
            FS[...] += RZ[k, 4].astype(f32)

        YS[k] = FS[1 - y].astype(bf16)
        rs_y(k).start()
        put(k, y, FS[y])

    def rs_out(k):
        rs_y(k).wait_recv()
        put(k, 1 - y, YR[k].astype(f32))

    rturns = iter(range(NK + 2))

    def rs_turn():
        r = next(rturns, None)
        if r is None:
            return
        for s, f in enumerate((rs_hop1, rs_hop2, rs_final)):
            if 0 <= r - s < NK:
                f(r - s)

    def rs_sent(k):
        rs_c(k).wait_send()
        for e in range(NZ):

            @pl.when(z != e)
            def _():
                rs_z(k, 0, e, e).wait_send()

        rs_y(k).wait_send()

    def e_copy(t, u, i):
        src, dst, dev = (
            (EXS, EXR, dev_x),
            (EYS, EYR, dev_y),
            (EXS2, EXR2, dev_x),
            (EYS2, EYR2, dev_y),
        )[i]
        src, dst = src[u], dst[u]
        return rcp(src.at[t], dst.at[t], exs.at[t, u, i], exr.at[t, u, i], dev)

    wide = (3 * 128, 2 * 128)
    thin = (2 * 128, 128)

    def cols(u, half):
        if half == 0:
            return pl.ds(u * wide[0], wide[u])
        return pl.ds(sum(wide) + u * thin[0], thin[u])

    def e_first(t, u, P):
        for i in range(2):
            EXS[u][t, i] = P[2 * i + 1 - x, :, cols(u, 0)].astype(bf16)
        e_copy(t, u, 0).start()
        for i in range(2):
            EYS[u][t, i] = P[2 - 2 * y + i, :, cols(u, 1)].astype(bf16)
        e_copy(t, u, 1).start()

    def e_second(t, u, P):
        e_copy(t, u, 0).wait_recv()
        EYS2[u][t] = (P[m_y, :, cols(u, 0)] + EXR[u][t, 1 - y].astype(f32)).astype(bf16)
        e_copy(t, u, 3).start()
        e_copy(t, u, 1).wait_recv()
        EXS2[u][t] = (P[m_x, :, cols(u, 1)] + EYR[u][t, 1 - x].astype(f32)).astype(bf16)
        e_copy(t, u, 2).start()

    def e_last(t, u, P):
        e_copy(t, u, 3).wait_recv()
        P[m_own, :, cols(u, 0)] += EXR[u][t, y].astype(f32) + EYR2[u][t].astype(f32)
        e_copy(t, u, 2).wait_recv()
        P[m_own, :, cols(u, 1)] += EYR[u][t, x].astype(f32) + EXR2[u][t].astype(f32)

    def e_sent(t):
        for u in range(2):
            for i in range(4):
                e_copy(t, u, i).wait_send()

    for k in range(NK):
        own_copy(k).start()
    xf = x_ref[...].astype(f32)
    centred = xf - jnp.mean(xf, axis=-1, keepdims=True)
    rstd = lax.rsqrt(jnp.mean(centred * centred, axis=-1, keepdims=True) + NORM_EPS)
    xhat = centred * rstd
    XH[...] = xhat
    RSTD[...] = jnp.broadcast_to(rstd, RSTD.shape)
    NA[m_own] = (xhat * gain_ref[...] + bias_ref[...]).astype(bf16)

    bucket = bucket_ref[0]
    B[z, y, c, 0:8] = jnp.broadcast_to(bin_ref[...].astype(f32), (8, 128)).astype(bf16)
    B[z, y, c, 8:16] = jnp.full((8, 128), bucket.astype(f32), f32).astype(bf16)

    slot = lax.shift_right_logical(jnp.int32(rows), bucket)
    shift_of = (rows.bit_length() - 1) - bucket
    row = x * rows + lax.broadcasted_iota(jnp.int32, (rows, 128), 0)
    slot_of = lax.shift_right_logical(row, jnp.full(row.shape, shift_of, jnp.int32))
    place = row & jnp.full(row.shape, slot - 1, jnp.int32)
    limit = jnp.zeros((rows, 128), jnp.int32)
    for s in range(SLOTS):
        limit = jnp.where(slot_of == s, counts_ref[s], limit)
    valid = jnp.where(place < limit, 1.0, 0.0)[:, 0:1]
    seeds = cot_ref[...].astype(f32) * valid
    SA[m_own] = seeds.astype(bf16)
    back_sum = jnp.sum(seeds, axis=0, keepdims=True)
    V[...] = jnp.zeros_like(V)
    for i in range(8):
        V[16 + i : 17 + i, :] = back_sum[:, i * 128 : (i + 1) * 128]
    pl.semaphore_wait(barrier, len(peers))
    for k in order:
        y_copy(k).start()
    g_send(0)
    g_send(1)
    ag_turn()
    ag_turn()

    lane = lax.broadcasted_iota(jnp.int32, (rows, TILE), 1)
    even = (lane & 1) == 0

    def table(g):
        brow = B[z, g, c].astype(f32)[8:9, :]
        ba = jnp.broadcast_to(brow, (rows, 128))

        def pick(ref):
            full = ref[...]
            out = full
            for b in range(1, 4):
                n = rows >> b
                out = jnp.where(ba == float(b), jnp.concatenate([full[:n]] * (1 << b), axis=0), out)
            return out

        cg, sg = pick(cos_ref), pick(sin_ref)
        CT[g] = jnp.concatenate([cg, cg], axis=1)
        SN[g] = jnp.concatenate([sg, sg], axis=1)
        size = jnp.full((rows, 128), rows, jnp.int32)
        for b in range(1, 4):
            size = jnp.where(ba == float(b), rows >> b, size)
        size = jnp.concatenate([size, size], axis=1)
        qi = lax.broadcasted_iota(jnp.int32, (rows, rows), 0)
        ki = lax.broadcasted_iota(jnp.int32, (rows, rows), 1)
        BM[g] = jnp.where((ki <= qi) & ((qi ^ ki) < size), 0.0, MASKED_SCORE)

    def tables():
        for g in range(2):
            table(g)

    def turn(v, g, sign):
        other = jnp.where(even, -pltpu.roll(v, TILE - 1, 1), pltpu.roll(v, 1, 1))
        return v * CT[g] + (sign * other) * SN[g]

    def weight(k):
        return W[k].reshape(width, TILE)

    scale = HD ** (-0.5)

    def project(m):
        g = m // 2
        nb = NA[m]
        QR[m] = turn(dot_nn(nb, weight(0)), g, 1.0).astype(bf16)
        KR[m] = turn(dot_nn(nb, weight(1)), g, 1.0).astype(bf16)
        VR[m] = dot_nn(nb, weight(2)).astype(bf16)

    def attend(m):
        g = m // 2
        q, kk, v = QR[m], KR[m], VR[m]
        da = dot_nn(SA[m], weight(3)).astype(bf16)
        zero = jnp.zeros((rows, TILE), bf16)
        ps, ss, qs, ks, vs_, ds = [], [], [], [], [], []
        for h in range(N_HEADS):
            mine = (lane // HD) == h
            qh, kh, vh, dh = (jnp.where(mine, t, zero) for t in (q, kk, v, da))
            s = dot_nt(qh, kk) * scale + BM[g]
            e = jnp.exp(s - jnp.max(s, axis=-1, keepdims=True))
            p = e * (1.0 / jnp.sum(e, axis=-1, keepdims=True))
            pg = dot_nt(dh, v)
            sg = p * (pg - jnp.sum(p * pg, axis=-1, keepdims=True))
            for held, t in ((ps, p), (ss, sg), (qs, qh), (ks, kh), (vs_, vh), (ds, dh)):
                held.append(t.astype(bf16))
        wide_p, wide_s = jnp.concatenate(ps, axis=1), jnp.concatenate(ss, axis=1)
        att = dot_nn(wide_p, jnp.concatenate(vs_, axis=0))
        dq = dot_nn(wide_s, jnp.concatenate(ks, axis=0))
        dk = dot_tn(jnp.concatenate(ss, axis=0), jnp.concatenate(qs, axis=0))
        dv = dot_tn(jnp.concatenate(ps, axis=0), jnp.concatenate(ds, axis=0))
        at = att.astype(bf16)
        dqb = turn(dq * scale, g, -1.0).astype(bf16)
        dkb = turn(dk * scale, g, -1.0).astype(bf16)
        dvb = dv.astype(bf16)
        rs = pl.ds(pl.multiple_of(m * rows, rows), rows)
        ATT[rs, :] = at
        DQ[rs, :] = dqb
        DK[rs, :] = dkb
        DV[rs, :] = dvb
        OUT[m] = dot_nt(at, weight(3))
        DN[m] = dot_nt(dqb, weight(0)) + dot_nt(dkb, weight(1)) + dot_nt(dvb, weight(2))

    def grad_of(k, left, right):
        total = dot_tn(left[...].reshape(4 * rows, width), right)
        GP[k] = total.astype(bf16).reshape(NZ, 2, 2, 64, TILE)
        rs_c(k).start()

    def slice_of(j):
        return NQ + 2 * j, NQ + 1 + 2 * j

    def feed(j, m, count=1):
        ki, kb = slice_of(j)
        n = count * rows
        b0 = B[2 * y + j // 2, j % 2, 0].astype(f32)[0:1, :]
        b1 = B[2 * y + j // 2, j % 2, 1].astype(f32)[0:1, :]
        take = lambda ref: ref[pl.ds(m, count)].reshape(n, width)
        u = dot_nn(take(NA), weight(ki)) + jnp.concatenate([b0, b1], axis=1)
        u2 = u * u
        k0 = float(np.sqrt(2.0 / np.pi))
        t = jnp.tanh(k0 * u * (1.0 + 0.044715 * u2))
        act = (0.5 * u * (1.0 + t)).astype(bf16)
        slope = 0.5 * (1.0 + t) + (0.5 * k0) * u * (1.0 - t * t) * (1.0 + 0.134145 * u2)
        hg = (dot_nn(take(SA), weight(kb)) * slope).astype(bf16)
        rs = pl.ds(pl.multiple_of(m * rows, rows), n)
        ACT[j, rs, :] = act
        HG[j, rs, :] = hg
        OUT[pl.ds(m, count)] += dot_nt(act, weight(kb)).reshape(count, rows, width)
        DN[pl.ds(m, count)] += dot_nt(hg, weight(ki)).reshape(count, rows, width)
        at = 24 + x * 16 + y * 8 + 2 * j
        total = jnp.sum(hg.astype(f32), axis=0, keepdims=True)
        V[pl.ds(at, 1), :] += total[:, :128]
        V[pl.ds(at + 1, 1), :] += total[:, 128:]

    def feed_grads(j):
        ki, kb = slice_of(j)
        grad_of(ki, NA, HG[j])
        grad_of(kb, SA, ACT[j])

    def feed_rows(j, *between):
        if not between:
            return feed(j, 0, 4)
        feed(j, 0, 2)
        between[0]()
        feed(j, 2, 2)

    def v_copy(i, dev):
        return rcp(VS.at[min(i, 3)], VRV.at[i], vs.at[i], vr.at[i], dev)

    v_devs = (dev_c, dev_x, dev_y)

    def v_step(i):
        v_copy(i, v_devs[i]).wait_recv()
        VS[i + 1] = VS[i] + VRV[i]
        if i < 2:
            v_copy(i + 1, v_devs[i + 1]).start()
        else:
            for n, dev in enumerate(dev_z):
                v_copy(3 + n, dev).start()

    def arrived(*chunks):
        for k in chunks:
            ag_done(k)

    ag_turn()
    tables()
    ag_turn()
    ag_turn()
    ag_turn()
    g_near(0)
    g_forward(0)
    ag_turn()
    arrived(0, NK, 1, 2)
    g_rest(0)
    project(m_own)
    project(m_x)
    project(m_y)
    ag_turn()
    arrived(3)
    attend(m_own)
    ag_turn()
    g_near(1)
    g_forward(1)
    g_rest(1)
    attend(m_x)
    ag_turn()
    attend(m_y)
    ag_turn()
    g_far(0)
    project(m_d)
    g_far(1)
    attend(m_d)
    grad_of(0, NA, DQ[...])
    ag_turn()
    grad_of(1, NA, DK[...])
    rs_begin(0)
    grad_of(2, NA, DV[...])
    rs_begin(1)
    grad_of(3, SA, ATT[...])
    rs_begin(2)
    ag_turn()
    arrived(4, 5)
    feed_rows(0)
    rs_begin(3)
    ag_turn()
    rs_turn()
    arrived(6, 7)
    feed_rows(1)
    ag_turn()
    feed_grads(0)
    rs_turn()
    arrived(8, 9)
    feed_rows(2, lambda: rs_begin(4))
    rs_begin(5)
    ag_turn()
    rs_turn()
    arrived(10, 11)
    feed_rows(3)

    for u in range(2):
        e_first(1, u, DN)
    rs_turn()
    feed_grads(1)
    rs_begin(6)
    rs_begin(7)
    rs_turn()
    feed_grads(2)
    rs_begin(8)
    rs_begin(9)
    rs_turn()
    e_second(1, 0, DN)
    e_first(0, 0, OUT)
    feed_grads(3)
    rs_begin(10)
    rs_begin(11)
    e_second(1, 1, DN)
    rs_turn()
    rs_turn()
    rs_turn()
    rs_turn()
    for u in range(2):
        e_last(1, u, DN)
    dn = DN[m_own]
    xhat = XH[...]
    gsum = jnp.sum(dn * xhat, axis=0, keepdims=True)
    bsum = jnp.sum(dn, axis=0, keepdims=True)
    for i in range(8):
        V[i : i + 1, :] = gsum[:, i * 128 : (i + 1) * 128]
        V[8 + i : 9 + i, :] = bsum[:, i * 128 : (i + 1) * 128]
    VS[0] = V[...]
    v_copy(0, dev_c).start()
    e = dn * gain_ref[...]
    me = jnp.mean(e, axis=-1, keepdims=True)
    mex = jnp.mean(e * xhat, axis=-1, keepdims=True)
    gin_ref[...] = (SA[m_own].astype(f32) + RSTD[:, 0:1] * (e - me - xhat * mex)).astype(bf16)
    v_step(0)
    e_first(0, 1, OUT)
    rs_turn()
    v_step(1)
    e_second(0, 0, OUT)
    rs_turn()
    v_step(2)
    for k in range(6):
        rs_out(k)
    rs_turn()
    e_second(0, 1, OUT)
    rs_turn()
    for k in range(6, NK):
        rs_out(k)
    for i in range(3):
        v_copy(3 + i, dev_z[i]).wait_recv()
    V[...] = VS[3] + VRV[3] + VRV[4] + VRV[5]
    index = 2 * dp + x
    lane4 = lax.rem(index, 4)
    for base, ref in ((0, lng_ref), (8, lnb_ref), (16, bbk_ref)):
        line = V[pl.ds(base + index // 4, 1), :]
        out = line[:, 0:32]
        for n in range(1, 4):
            out = jnp.where(lane4 == n, line[:, 32 * n : 32 * n + 32], out)
        ref[...] = out
    gbin_ref[...] = V[pl.ds(24 + 16 * x + dp, 1), :]
    for u in range(2):
        e_last(0, u, OUT)
    block_ref[...] = (x_ref[...].astype(f32) + OUT[m_own] + bback_ref[...]).astype(bf16)

    def later(f):
        lax.fori_loop(0, NK, lambda k, _: (f(k), 0)[1], 0)

    for k in range(NK + 1):
        ag_sent(k)
    for t in range(2):
        g_sent(t)
        e_sent(t)
    later(rs_sent)
    for i, dev in enumerate([dev_c, dev_x, dev_y] + dev_z):
        v_copy(i, dev).wait_send()


def write_kernel(*refs):
    srcs, dsts, sems = refs[:10], refs[10:20], refs[20]
    copies = [pltpu.make_async_copy(a, b, sems.at[i]) for i, (a, b) in enumerate(zip(srcs, dsts))]
    for copy in copies:
        copy.start()
    for copy in copies:
        copy.wait()


def rope_constants(rows):
    half = np.arange(ROT // 2, dtype=np.float32)
    rates = (10000.0 ** (-2.0 * half / ROT)).astype(np.float32)
    angle = np.arange(rows, dtype=np.float32)[:, None] * rates[None, :]
    angle = np.repeat(angle, 2, axis=1)
    cos = np.concatenate([np.cos(angle), np.ones((rows, HD - ROT))], axis=1)
    sin = np.concatenate([np.sin(angle), np.zeros((rows, HD - ROT))], axis=1)
    two = lambda t: np.concatenate([t, t], axis=1).astype(np.float32)
    return two(cos), two(sin)


def on_quad(
    residual_in,
    cotangent,
    ln_gain,
    ln_bias,
    w_qkv,
    w_out,
    w_in,
    b_in,
    w_back,
    b_back,
    bucket_ids,
    residue_counts,
):
    rows, width = residual_in.shape
    cos, sin = rope_constants(rows)
    f32, bf16 = jnp.float32, jnp.bfloat16
    vm = pl.BlockSpec(memory_space=pltpu.VMEM)
    sm = pl.BlockSpec(memory_space=pltpu.SMEM)
    anyspace = pl.BlockSpec(memory_space=pl.ANY)
    shard = width // (4 * NZ)
    sem = pltpu.SemaphoreType.DMA
    shapes = (
        jax.ShapeDtypeStruct((rows, width), bf16),
        jax.ShapeDtypeStruct((rows, width), bf16),
        jax.ShapeDtypeStruct((3, shard, 2 * TILE), f32),
        jax.ShapeDtypeStruct((shard, 2 * TILE), f32),
        jax.ShapeDtypeStruct((shard, 2 * NJ * TILE), f32),
        jax.ShapeDtypeStruct((shard, 2 * NJ * TILE), f32),
        jax.ShapeDtypeStruct((1, 32), f32),
        jax.ShapeDtypeStruct((1, 32), f32),
        jax.ShapeDtypeStruct((1, 32), f32),
        jax.ShapeDtypeStruct((1, 128), f32),
    )
    held = pl.pallas_call(
        layer_kernel,
        out_shape=tuple(pltpu.VMEM(v.shape, v.dtype) for v in shapes),
        in_specs=[sm, sm] + [vm] * 8 + [anyspace] * 4,
        out_specs=(vm,) * 10,
        scratch_shapes=[
            pltpu.VMEM((NZ, 2, 2, 16, 128), bf16),
            pltpu.VMEM((NK, NZ, 2, 2, shard, TILE), bf16),
            pltpu.VMEM((4, rows, width), bf16),
            pltpu.VMEM((4, rows, width), bf16),
            pltpu.VMEM((2, rows, TILE), f32),
            pltpu.VMEM((2, rows, TILE), f32),
            pltpu.VMEM((2, rows, rows), f32),
            pltpu.VMEM((4, rows, TILE), bf16),
            pltpu.VMEM((4, rows, TILE), bf16),
            pltpu.VMEM((4, rows, TILE), bf16),
            pltpu.VMEM((4 * rows, TILE), bf16),
            pltpu.VMEM((4 * rows, TILE), bf16),
            pltpu.VMEM((4 * rows, TILE), bf16),
            pltpu.VMEM((4 * rows, TILE), bf16),
            pltpu.VMEM((NJ, 4 * rows, TILE), bf16),
            pltpu.VMEM((NJ, 4 * rows, TILE), bf16),
            pltpu.VMEM((4, rows, width), f32),
            pltpu.VMEM((4, rows, width), f32),
            pltpu.VMEM((NK, NZ, 2, 2, shard, TILE), bf16),
            pltpu.VMEM((NK, NZ, 2, shard, TILE), bf16),
            pltpu.VMEM((NK, 5, 2, shard, TILE), bf16),
            pltpu.VMEM((2, shard, TILE), f32),
            pltpu.VMEM((NK, shard, TILE), bf16),
            pltpu.VMEM((NK, shard, TILE), bf16),
            pltpu.VMEM((rows, width), f32),
            pltpu.VMEM((rows, 128), f32),
            pltpu.VMEM((2, 2, rows, 384), bf16),
            pltpu.VMEM((2, 2, rows, 256), bf16),
            pltpu.VMEM((2, 2, rows, 256), bf16),
            pltpu.VMEM((2, 2, rows, 128), bf16),
            pltpu.VMEM((2, 2, rows, 384), bf16),
            pltpu.VMEM((2, 2, rows, 256), bf16),
            pltpu.VMEM((2, 2, rows, 256), bf16),
            pltpu.VMEM((2, 2, rows, 128), bf16),
            pltpu.VMEM((2, rows, 256), bf16),
            pltpu.VMEM((2, rows, 128), bf16),
            pltpu.VMEM((2, rows, 384), bf16),
            pltpu.VMEM((2, rows, 256), bf16),
            pltpu.VMEM((2, rows, 256), bf16),
            pltpu.VMEM((2, rows, 128), bf16),
            pltpu.VMEM((2, rows, 384), bf16),
            pltpu.VMEM((2, rows, 256), bf16),
            pltpu.VMEM((VROWS, 128), f32),
            pltpu.VMEM((4, VROWS, 128), f32),
            pltpu.VMEM((6, VROWS, 128), f32),
            sem((NK,)),
            sem((NK + 1,)),
            sem((NK + 1,)),
            sem((NK + 1, 2, 3)),
            sem((NK + 1, 2, 3)),
            sem((NK + 1, NZ)),
            sem((NK + 1, NZ)),
            sem((12,)),
            sem((12,)),
            sem((NK,)),
            sem((NK,)),
            sem((NK, NZ)),
            sem((NK, 5)),
            sem((NK,)),
            sem((NK,)),
            sem((2, 2, 4)),
            sem((2, 2, 4)),
            sem((6,)),
            sem((6,)),
        ],
        compiler_params=pltpu.CompilerParams(
            collective_id=0, has_side_effects=True, vmem_limit_bytes=58 << 20
        ),
        cost_estimate=pl.CostEstimate(
            flops=20 * 2**30, bytes_accessed=8 * 2**20, transcendentals=2**21
        ),
    )(
        bucket_ids,
        residue_counts.reshape(SLOTS),
        residual_in,
        cotangent,
        ln_gain.reshape(1, width),
        ln_bias.reshape(1, width),
        b_back.reshape(1, width),
        jnp.asarray(cos),
        jnp.asarray(sin),
        b_in.reshape(1, 128),
        w_qkv,
        w_out.T,
        w_in,
        w_back.T,
    )
    held = [pltpu.with_memory_space_constraint(v, pltpu.VMEM) for v in held]
    outs = pl.pallas_call(
        write_kernel,
        out_shape=shapes,
        in_specs=[vm] * 10,
        out_specs=(anyspace,) * 10,
        scratch_shapes=[sem((10,))],
    )(*held)
    block_out, grad_input, grad_w_qkv, gwo, grad_w_in, gwb, lng, lnb, bbk, gbin = outs
    return (
        block_out,
        grad_input,
        lng.reshape(32),
        lnb.reshape(32),
        grad_w_qkv,
        gwo.T,
        grad_w_in,
        gbin.reshape(128),
        gwb.T,
        bbk.reshape(32),
    )


def solution(mesh):
    placed = (
        P(("dp", "mp"), None),
        P(("dp", "mp"), None),
        P(),
        P(),
        P(None, "dp", "mp"),
        P("mp", "dp"),
        P("dp", "mp"),
        P(("mp", "dp")),
        P("mp", "dp"),
        P(),
        P("dp"),
        P("dp", None),
    )
    return jax.shard_map(
        on_quad if fits_quad(mesh) else on_device,
        mesh=mesh,
        in_specs=placed,
        out_specs=(
            P(("dp", "mp"), None),
            P(("dp", "mp"), None),
            P(("dp", "mp")),
            P(("dp", "mp")),
            P(None, "dp", "mp"),
            P("mp", "dp"),
            P("dp", "mp"),
            P(("mp", "dp")),
            P("mp", "dp"),
            P(("dp", "mp")),
        ),
        check_vma=False,
    )
```

```python
from functools import partial

import jax
import jax.numpy as jnp
import numpy as np
from jax import lax
from jax.experimental import pallas as pl
from jax.experimental.pallas import tpu as pltpu
from jax.sharding import PartitionSpec as P

HD = 64
ROT = 32
SLOTS = 16


NORM_EPS = 1e-05
MASKED_SCORE = -1e30


def norm_rows(inputs_now, norm_gain, norm_shift):
    centred = inputs_now - jnp.mean(inputs_now, axis=-1, keepdims=True)
    spread = jnp.mean(centred * centred, axis=-1, keepdims=True)
    return centred * lax.rsqrt(spread + NORM_EPS) * norm_gain + norm_shift


def slot_tables(bucket_one, residue_row, group_rows):
    slot_length = jnp.right_shift(jnp.int32(group_rows // 2), bucket_one)
    places = jnp.arange(group_rows, dtype=jnp.int32)
    slot_ids = places // slot_length
    inside = places - slot_ids * slot_length
    match_table = slot_ids[:, None] == jnp.arange(SLOTS, dtype=jnp.int32)[None, :]
    picked = jnp.sum(jnp.where(match_table, residue_row[None, :], 0), axis=1)
    live_rows = jnp.minimum(picked, slot_length)
    return (slot_ids, inside, inside < live_rows)


def rope_tables(inside):
    half_steps = jnp.arange(ROT // 2, dtype=jnp.float32)
    inverse_rates = 10000.0 ** (-2.0 * half_steps / ROT)
    angles = inside.astype(jnp.float32)[:, None] * inverse_rates[None, :]
    return (jnp.cos(angles), jnp.sin(angles))


def rotate(values, cosine_table, sine_table):
    row_count = values.shape[0]
    head_count = values.shape[1]
    paired = values[..., :ROT].reshape(row_count, head_count, ROT // 2, 2)
    even_part = paired[..., 0]
    odd_part = paired[..., 1]
    cosine_now = cosine_table[:, None, :]
    sine_now = sine_table[:, None, :]
    turned = jnp.stack(
        [
            even_part * cosine_now - odd_part * sine_now,
            odd_part * cosine_now + even_part * sine_now,
        ],
        axis=-1,
    )
    return jnp.concatenate([turned.reshape(row_count, head_count, ROT), values[..., ROT:]], axis=-1)


def mask_block(block_start, block_rows, slot_ids):
    query_places = block_start + jnp.arange(block_rows, dtype=jnp.int32)
    query_slots = lax.dynamic_slice_in_dim(slot_ids, block_start, block_rows, 0)
    key_places = jnp.arange(slot_ids.shape[0], dtype=jnp.int32)
    return (query_slots[:, None] == slot_ids[None, :]) & (
        key_places[None, :] <= query_places[:, None]
    )


def over_rows(first_op, second_op):
    return lax.dot_general(
        first_op, second_op, (((0,), (0,)), ((), ())), preferred_element_type=jnp.float32
    )


def against_weight(first_op, second_op):
    return lax.dot_general(
        first_op, second_op, (((1,), (1,)), ((), ())), preferred_element_type=jnp.float32
    )


def on_device(
    residual_in,
    cotangent,
    ln_gain,
    ln_bias,
    w_qkv,
    w_out,
    w_in,
    b_in,
    w_back,
    b_back,
    bucket_ids,
    residue_counts,
):
    model_count = lax.axis_size("mp")
    model_rank = lax.axis_index("mp")
    local_rows = residual_in.shape[0]
    group_rows = local_rows * model_count
    slot_ids, inside, valid_rows = slot_tables(bucket_ids[0], residue_counts[0], group_rows)
    cosine_table, sine_table = rope_tables(inside)
    qkv_all, out_all, in_all, bias_in, back_all = (
        lax.all_gather(w_qkv, "dp", axis=1, tiled=True),
        lax.all_gather(w_out, "dp", axis=1, tiled=True),
        lax.all_gather(w_in, "dp", axis=0, tiled=True),
        lax.all_gather(b_in, "dp", axis=0, tiled=True),
        lax.all_gather(w_back, "dp", axis=1, tiled=True),
    )
    x_local = residual_in.astype(jnp.float32)
    x_group = lax.all_gather(residual_in, "mp", axis=0, tiled=True).astype(jnp.float32)
    normed = norm_rows(x_group, ln_gain, ln_bias).astype(jnp.bfloat16)
    head_width = qkv_all.shape[2]
    head_count = head_width // HD
    score_scale = HD ** (-0.5)

    def project(member_index):
        return jnp.dot(normed, qkv_all[member_index], preferred_element_type=jnp.float32).reshape(
            group_rows, head_count, HD
        )

    queries = rotate(project(0), cosine_table, sine_table).astype(jnp.bfloat16)
    key_rows = rotate(project(1), cosine_table, sine_table).astype(jnp.bfloat16)
    value_rows = project(2).astype(jnp.bfloat16)
    block_rows = min(512, group_rows)
    starts = jnp.arange(group_rows // block_rows, dtype=jnp.int32) * block_rows

    def block_scores(block_start):
        query_block = lax.dynamic_slice_in_dim(queries, block_start, block_rows, 0)
        allowed = mask_block(block_start, block_rows, slot_ids)
        scores = (
            jnp.einsum("qhd,khd->hqk", query_block, key_rows, preferred_element_type=jnp.float32)
            * score_scale
        )
        return (query_block, jnp.where(allowed[None], scores, MASKED_SCORE))

    def forward_block(block_start):
        query_block, scores = block_scores(block_start)
        row_peak = jnp.max(scores, axis=-1, keepdims=True)
        exp_scores = jnp.exp(scores - row_peak)
        row_total = jnp.sum(exp_scores, axis=-1, keepdims=True)
        weights_now = (exp_scores / row_total).astype(jnp.bfloat16)
        attended = jnp.einsum(
            "hqk,khd->qhd", weights_now, value_rows, preferred_element_type=jnp.float32
        )
        return (attended.astype(jnp.bfloat16), (row_peak + jnp.log(row_total))[..., 0])

    attended_blocks, log_totals = lax.map(forward_block, starts)
    mixed_rows = attended_blocks.reshape(group_rows, head_width)
    hidden = jnp.dot(normed, in_all, preferred_element_type=jnp.float32) + bias_in.astype(
        jnp.float32
    )
    gelu_tanh = partial(jax.nn.gelu, approximate=True)
    active_value, gelu_pull = jax.vjp(gelu_tanh, hidden)
    active = active_value.astype(jnp.bfloat16)
    partial_out = jnp.dot(mixed_rows, out_all, preferred_element_type=jnp.float32) + jnp.dot(
        active, back_all, preferred_element_type=jnp.float32
    )
    summed_all = lax.psum(partial_out.astype(jnp.bfloat16), "mp").astype(jnp.float32)
    summed = lax.dynamic_slice_in_dim(summed_all, model_rank * local_rows, local_rows, 0)
    block_out = (x_local + summed + b_back).astype(jnp.bfloat16)
    cot_group = lax.all_gather(cotangent, "mp", axis=0, tiled=True)
    seed_rows = jnp.where(valid_rows[:, None], cot_group, jnp.zeros_like(cot_group))
    qkv_all, out_all, in_all, back_all = (
        lax.all_gather(w_qkv, "dp", axis=1, tiled=True),
        lax.all_gather(w_out, "dp", axis=1, tiled=True),
        lax.all_gather(w_in, "dp", axis=0, tiled=True),
        lax.all_gather(w_back, "dp", axis=1, tiled=True),
    )
    active_grad = against_weight(seed_rows, back_all)
    hidden_grad = gelu_pull(active_grad)[0].astype(jnp.bfloat16)
    grad_in_local = over_rows(normed, hidden_grad)
    grad_bias_in = jnp.sum(hidden_grad.astype(jnp.float32), axis=0)
    grad_back_local = over_rows(active, seed_rows)
    grad_out_local = over_rows(mixed_rows, seed_rows)
    normed_grad = against_weight(hidden_grad, in_all)
    mixed_grad = (
        against_weight(seed_rows, out_all).astype(jnp.bfloat16).reshape(group_rows, head_count, HD)
    )

    def backward_block(carry, inputs_now):
        key_acc, value_acc = carry
        block_start, log_total = inputs_now
        query_block, scores = block_scores(block_start)
        grad_block = lax.dynamic_slice_in_dim(mixed_grad, block_start, block_rows, 0)
        probs = jnp.exp(scores - log_total[..., None])
        probs_low = probs.astype(jnp.bfloat16)
        value_acc = value_acc + jnp.einsum(
            "hqk,qhd->khd", probs_low, grad_block, preferred_element_type=jnp.float32
        )
        probs_grad = jnp.einsum(
            "qhd,khd->hqk", grad_block, value_rows, preferred_element_type=jnp.float32
        )
        score_grad = probs * (probs_grad - jnp.sum(probs * probs_grad, axis=-1, keepdims=True))
        score_low = score_grad.astype(jnp.bfloat16)
        query_grad = (
            jnp.einsum("hqk,khd->qhd", score_low, key_rows, preferred_element_type=jnp.float32)
            * score_scale
        )
        key_acc = (
            key_acc
            + jnp.einsum("hqk,qhd->khd", score_low, query_block, preferred_element_type=jnp.float32)
            * score_scale
        )
        return ((key_acc, value_acc), query_grad)

    empty_heads = jnp.zeros((group_rows, head_count, HD), jnp.float32)
    (key_acc, value_acc), query_blocks = lax.scan(
        backward_block, (empty_heads, empty_heads), (starts, log_totals)
    )
    turn_back = partial(rotate, cosine_table=cosine_table, sine_table=sine_table)
    unturn = jax.vjp(turn_back, empty_heads)[1]
    query_pre_grad = (
        unturn(query_blocks.reshape(group_rows, head_count, HD))[0]
        .astype(jnp.bfloat16)
        .reshape(group_rows, head_width)
    )
    key_pre_grad = unturn(key_acc)[0].astype(jnp.bfloat16).reshape(group_rows, head_width)
    value_grad = value_acc.astype(jnp.bfloat16).reshape(group_rows, head_width)
    grad_qkv_local = jnp.stack(
        [
            over_rows(normed, query_pre_grad),
            over_rows(normed, key_pre_grad),
            over_rows(normed, value_grad),
        ],
        axis=0,
    )
    normed_grad = (
        normed_grad
        + against_weight(query_pre_grad, qkv_all[0])
        + against_weight(key_pre_grad, qkv_all[1])
        + against_weight(value_grad, qkv_all[2])
    )
    share_grad = lax.psum(normed_grad.astype(jnp.bfloat16), "mp").astype(jnp.float32)
    seed_group = seed_rows.astype(jnp.float32)
    norm_pull = jax.vjp(norm_rows, x_group, ln_gain, ln_bias)[1]
    input_part, gain_part, shift_part = norm_pull(share_grad)
    input_group = seed_group + input_part
    grad_input = lax.dynamic_slice_in_dim(
        input_group, model_rank * local_rows, local_rows, 0
    ).astype(jnp.bfloat16)
    back_part = jnp.sum(seed_group, axis=0)
    grad_w_qkv, grad_w_out, grad_w_in, grad_b_in, grad_w_back, gain_rows, shift_rows, back_rows = (
        lax.psum_scatter(
            grad_qkv_local.astype(jnp.bfloat16), "dp", scatter_dimension=1, tiled=True
        ).astype(jnp.float32),
        lax.psum_scatter(
            grad_out_local.astype(jnp.bfloat16), "dp", scatter_dimension=1, tiled=True
        ).astype(jnp.float32),
        lax.psum_scatter(
            grad_in_local.astype(jnp.bfloat16), "dp", scatter_dimension=0, tiled=True
        ).astype(jnp.float32),
        lax.psum_scatter(
            grad_bias_in.astype(jnp.bfloat16), "dp", scatter_dimension=0, tiled=True
        ).astype(jnp.float32),
        lax.psum_scatter(
            grad_back_local.astype(jnp.bfloat16), "dp", scatter_dimension=1, tiled=True
        ).astype(jnp.float32),
        lax.psum_scatter(
            gain_part.astype(jnp.bfloat16), "dp", scatter_dimension=0, tiled=True
        ).astype(jnp.float32),
        lax.psum_scatter(
            shift_part.astype(jnp.bfloat16), "dp", scatter_dimension=0, tiled=True
        ).astype(jnp.float32),
        lax.psum_scatter(
            back_part.astype(jnp.bfloat16), "dp", scatter_dimension=0, tiled=True
        ).astype(jnp.float32),
    )
    piece_width = gain_rows.shape[0] // model_count
    grad_ln_gain = lax.dynamic_slice_in_dim(gain_rows, model_rank * piece_width, piece_width, 0)
    grad_ln_bias = lax.dynamic_slice_in_dim(shift_rows, model_rank * piece_width, piece_width, 0)
    grad_b_back = lax.dynamic_slice_in_dim(back_rows, model_rank * piece_width, piece_width, 0)
    return (
        block_out,
        grad_input,
        grad_ln_gain,
        grad_ln_bias,
        grad_w_qkv,
        grad_w_out,
        grad_w_in,
        grad_b_in,
        grad_w_back,
        grad_b_back,
    )


MESH = pl.DeviceIdType.MESH
NZ = 4
TILE = 256
N_HEADS = TILE // HD
NQ = 4
NJ = 4
NK = NQ + 2 * NJ
VROWS = 56


def fits_quad(mesh):
    return mesh.shape["mp"] == 2 and mesh.shape["dp"] == 4 * NZ


def dot_nn(a, b):
    return lax.dot_general(a, b, (((1,), (0,)), ((), ())), preferred_element_type=jnp.float32)


def dot_nt(a, b):
    return lax.dot_general(a, b, (((1,), (1,)), ((), ())), preferred_element_type=jnp.float32)


def dot_tn(a, b):
    return lax.dot_general(a, b, (((0,), (0,)), ((), ())), preferred_element_type=jnp.float32)


def layer_kernel(
    bucket_ref,
    counts_ref,
    x_ref,
    cot_ref,
    gain_ref,
    bias_ref,
    bback_ref,
    cos_ref,
    sin_ref,
    bin_ref,
    wqkv_ref,
    wot_ref,
    win_ref,
    wbt_ref,
    block_ref,
    gin_ref,
    gqkv_ref,
    got_ref,
    gi_ref,
    gbt_ref,
    lng_ref,
    lnb_ref,
    bbk_ref,
    gbin_ref,
    B,
    W,
    NS,
    CT,
    SN,
    BM,
    QR,
    KR,
    VR,
    R,
    XV,
    CV,
    COSV,
    SINV,
    ins,
    OUT,
    DN,
    GP,
    GC,
    RZ,
    FS,
    YS,
    YR,
    XH,
    RSTD,
    EXSa,
    EXSb,
    EYSa,
    EYSb,
    EXRa,
    EXRb,
    EYRa,
    EYRb,
    EXS2a,
    EXS2b,
    EYS2a,
    EYS2b,
    EXR2a,
    EXR2b,
    EYR2a,
    EYR2b,
    V,
    VS,
    VRV,
    loc_sem,
    ays,
    ayr,
    azs,
    azr,
    acs,
    acr,
    gs,
    gr,
    rcs,
    rcr,
    rzs,
    rzr,
    rys,
    ryr,
    exs,
    exr,
    vs,
    vr,
):
    EXS = (EXSa, EXSb)
    EYS = (EYSa, EYSb)
    EXR = (EXRa, EXRb)
    EYR = (EYRa, EYRb)
    EXS2 = (EXS2a, EXS2b)
    EYS2 = (EYS2a, EYS2b)
    EXR2 = (EXR2a, EXR2b)
    EYR2 = (EYR2a, EYR2b)
    f32, bf16 = jnp.float32, jnp.bfloat16
    dp, x = lax.axis_index("dp"), lax.axis_index("mp")
    z = dp // 4
    y = lax.rem(dp // 2, 2)
    c = lax.rem(dp, 2)
    rows = x_ref.shape[0]
    width = x_ref.shape[1]
    dev_x = (dp, 1 - x)
    dev_y = (dp + 2 - 4 * y, x)
    dev_c = (dp + 1 - 2 * c, x)
    dev_r = (lax.rem(dp + 4, 4 * NZ), x)
    dev_l = (lax.rem(dp + 4 * NZ - 4, 4 * NZ), x)
    dev_z = [(lax.rem(dp + 4 * i, 4 * NZ), x) for i in (1, 2, 3)]
    NA, SA = NS.at[0], NS.at[1]
    m_own = 2 * y + x
    m_x = 2 * y + 1 - x
    m_y = 2 - 2 * y + x
    m_d = 3 - m_own

    def rcp(src, dst, ss, rs, dev):
        return pltpu.make_async_remote_copy(
            src_ref=src, dst_ref=dst, send_sem=ss, recv_sem=rs, device_id=dev, device_id_type=MESH
        )

    barrier = pltpu.get_barrier_semaphore()
    peers = [dev_x, dev_y, dev_c] + dev_z
    for peer in peers:
        pl.semaphore_signal(barrier, inc=1, device_id=peer, device_id_type=MESH)

    def wsrc(k, q):
        if k == NK:
            return None
        if k < 3:
            return wqkv_ref.at[k, :, pl.ds(pl.multiple_of(q * TILE, TILE), TILE)]
        if k == 3:
            return wot_ref.at[:, pl.ds(pl.multiple_of(q * TILE, TILE), TILE)]
        ref = win_ref if k % 2 == 0 else wbt_ref
        j = (k - NQ) // 2
        return ref.at[:, pl.ds(pl.multiple_of(q * (NJ * TILE) + j * TILE, TILE), TILE)]

    def wv(k):
        return B if isinstance(k, int) and k == NK else W.at[k]

    def own_copy(k):
        return pltpu.make_async_copy(wsrc(k, y), W.at[k, z, y, c], loc_sem.at[k])

    def y_copy(k):
        if k == NK:
            return rcp(B.at[z, y, c], B.at[z, y, c], ays.at[k], ayr.at[k], dev_y)
        return rcp(wsrc(k, 1 - y), W.at[k, z, y, c], ays.at[k], ayr.at[k], dev_y)

    def y_arrived(k):
        here = wv(k).at[z, 1 - y, c]
        rcp(here, here, ays.at[k], ayr.at[k], dev_y).wait_recv()

    def z_copy(k, way, s, e):
        block = wv(k).at[e, :, c]
        return rcp(
            block, block, azs.at[k, way, s], azr.at[k, way, s], dev_r if way == 0 else dev_l
        )

    def c_copy(k, e):
        block = wv(k).at[e, :, c]
        return rcp(block, block, acs.at[k, e], acr.at[k, e], dev_c)

    def ag_own(k, copied=True):
        if copied:
            pltpu.make_async_copy(
                W.at[k, z, y, c], W.at[k, z, y, c], loc_sem.at[k]
            ).wait()
        y_arrived(k)

        @pl.when(z < NZ - 1)
        def _():
            z_copy(k, 0, 0, z).start()

        @pl.when(z > 0)
        def _():
            z_copy(k, 1, 0, z).start()

        c_copy(k, z).start()

    def ag_step(k, s):
        @pl.when(z - 1 - s >= 0)
        def _():
            e = z - 1 - s
            z_copy(k, 0, s, e).wait_recv()
            if s < NZ - 2:

                @pl.when(z < NZ - 1)
                def _():
                    z_copy(k, 0, s + 1, e).start()

            c_copy(k, e).start()

        @pl.when(z + 1 + s <= NZ - 1)
        def _():
            e = z + 1 + s
            z_copy(k, 1, s, e).wait_recv()
            if s < NZ - 2:

                @pl.when(z > 0)
                def _():
                    z_copy(k, 1, s + 1, e).start()

            c_copy(k, e).start()

    def ag_done(k):
        for e in range(NZ):
            block = wv(k).at[e, :, 1 - c]
            rcp(block, block, acs.at[k, e], acr.at[k, e], dev_c).wait_recv()

    def ag_sent(k, copied=True):
        y_copy(k).wait_send() if isinstance(k, int) else None
        for s in range(NZ - 1):

            @pl.when((z < NZ - 1) & (z - s >= 0))
            def _():
                z_copy(k, 0, s, z - s).wait_send()

            @pl.when((z > 0) & (z + s <= NZ - 1))
            def _():
                z_copy(k, 1, s, z + s).wait_send()

        for e in range(NZ):
            c_copy(k, e).wait_send()

    order = [0, NK] + list(range(1, NK))
    turns = iter([t for t in range(NK + NZ) if not 8 <= t <= 11])

    def ag_turn():
        t = next(turns, None)
        if t is None:
            return
        for n in range(2) if t == 0 else (t + 1,):
            if n <= NK:
                ag_own(order[n], copied=order[n] != NK)
        for s in range(NZ - 1):
            if 0 <= t - 1 - s <= NK:
                ag_step(order[t - 1 - s], s)

    def late_turn(t):
        ag_own(t)
        for s in range(NZ - 1):
            ag_step(t - 2 - s, s)

    P0 = 80
    parts = (pl.ds(0, P0), pl.ds(P0, rows - P0))
    BUF = (NA, SA)

    def g_copy(t, p, way, m):
        block = BUF[t].at[m, parts[p]]
        i = (t * 2 + p) * 3 + way
        dev = (dev_x, dev_y)[way] if way < 2 else (dev_y, dev_x)[p]
        return rcp(block, block, gs.at[i], gr.at[i], dev)

    def g_send(t):
        g_copy(t, 0, 0, m_own).start()
        g_copy(t, 1, 1, m_own).start()
        g_copy(t, 1, 0, m_own).start()
        g_copy(t, 0, 1, m_own).start()

    def g_near(t):
        g_copy(t, 0, 0, m_x).wait_recv()
        g_copy(t, 1, 1, m_y).wait_recv()

    def g_forward(t):
        g_copy(t, 0, 2, m_x).start()
        g_copy(t, 1, 2, m_y).start()

    def g_rest(t):
        g_copy(t, 1, 0, m_x).wait_recv()
        g_copy(t, 0, 1, m_y).wait_recv()

    def g_far(t):
        g_copy(t, 0, 2, m_d).wait_recv()
        g_copy(t, 1, 2, m_d).wait_recv()

    def g_sent(t):
        for p in (0, 1):
            for way in (0, 1):
                g_copy(t, p, way, m_own).wait_send()
        g_copy(t, 0, 2, m_x).wait_send()
        g_copy(t, 1, 2, m_y).wait_send()

    def rs_c(k):
        return rcp(GP.at[k, :, :, 1 - c], GC.at[k], rcs.at[k], rcr.at[k], dev_c)

    def rs_z(k, way, e, slot):
        return rcp(
            GP.at[k, e, :, c],
            RZ.at[k, slot],
            rzs.at[k, e],
            rzr.at[k, slot],
            dev_r if way == 0 else dev_l,
        )

    def rs_begin(k):
        rs_c(k).wait_recv()
        for e in range(NZ):
            GP[k, e, :, c] = (GP[k, e, :, c].astype(f32) + GC[k, e].astype(f32)).astype(bf16)

        @pl.when(z == 0)
        def _():
            for e in range(NZ - 1, 0, -1):
                rs_z(k, 0, e, e).start()

        @pl.when(z == NZ - 1)
        def _():
            for e in range(NZ - 1):
                rs_z(k, 1, e, e if e < NZ - 2 else 4).start()

    def pass_on(k, way, e, slot):
        rs_z(k, way, e, e).wait_recv()
        GP[k, e, :, c] = (GP[k, e, :, c].astype(f32) + RZ[k, e].astype(f32)).astype(bf16)
        rs_z(k, way, e, slot).start()

    def rs_hop1(k):
        @pl.when(z == 1)
        def _():
            pass_on(k, 0, 3, 3)
            pass_on(k, 0, 2, 2)

        @pl.when(z == 2)
        def _():
            pass_on(k, 1, 0, 0)
            pass_on(k, 1, 1, 4)

    def rs_hop2(k):
        @pl.when(z == 2)
        def _():
            pass_on(k, 0, 3, 3)

        @pl.when(z == 1)
        def _():
            pass_on(k, 1, 0, 4)

    def rs_y(k):
        return rcp(YS.at[k], YR.at[k], rys.at[k], ryr.at[k], dev_y)

    def put(k, q, value):
        if k < 3:
            gqkv_ref[k, :, pl.ds(pl.multiple_of(q * TILE, TILE), TILE)] = value
        elif k == 3:
            got_ref[:, pl.ds(pl.multiple_of(q * TILE, TILE), TILE)] = value
        else:
            ref = gi_ref if k % 2 == 0 else gbt_ref
            j = (k - NQ) // 2
            ref[:, pl.ds(pl.multiple_of(q * (NJ * TILE) + j * TILE, TILE), TILE)] = value

    def rs_final(k):
        FS[...] = GP[k, z, :, c].astype(f32)

        @pl.when(z > 0)
        def _():
            rs_z(k, 0, z, z).wait_recv()
            FS[...] += RZ[k, z].astype(f32)

        @pl.when(z < NZ - 1)
        def _():
            rs_z(k, 1, z, 4).wait_recv()
            FS[...] += RZ[k, 4].astype(f32)

        YS[k] = FS[1 - y].astype(bf16)
        rs_y(k).start()
        put(k, y, FS[y])

    def rs_out(k):
        rs_y(k).wait_recv()
        put(k, 1 - y, YR[k].astype(f32))

    rturns = iter(range(NK + 2))

    def rs_turn():
        r = next(rturns, None)
        if r is None:
            return
        for s, f in enumerate((rs_hop1, rs_hop2, rs_final)):
            if 0 <= r - s < NK:
                f(r - s)

    def rs_sent(k):
        rs_c(k).wait_send()
        for e in range(NZ):

            @pl.when(z != e)
            def _():
                rs_z(k, 0, e, e).wait_send()

        rs_y(k).wait_send()

    def e_copy(t, u, i):
        src, dst, dev = (
            (EXS, EXR, dev_x),
            (EYS, EYR, dev_y),
            (EXS2, EXR2, dev_x),
            (EYS2, EYR2, dev_y),
        )[i]
        src, dst = src[u], dst[u]
        return rcp(src.at[t], dst.at[t], exs.at[t, u, i], exr.at[t, u, i], dev)

    wide = (384, 256)
    thin = (2 * 128, 128)

    def cols(u, half):
        if half == 0:
            return pl.ds(u * wide[0], wide[u])
        return pl.ds(sum(wide) + u * thin[0], thin[u])

    def e_first_x(t, u, P):
        for i in range(2):
            EXS[u][t, i] = P[2 * i + 1 - x, :, cols(u, 0)].astype(bf16)
        e_copy(t, u, 0).start()

    def e_first_y(t, u, P):
        for i in range(2):
            EYS[u][t, i] = P[2 - 2 * y + i, :, cols(u, 1)].astype(bf16)
        e_copy(t, u, 1).start()

    def e_first(t, u, P):
        e_first_x(t, u, P)
        e_first_y(t, u, P)

    def e_second(t, u, P):
        e_copy(t, u, 0).wait_recv()
        EYS2[u][t] = (P[m_y, :, cols(u, 0)] + EXR[u][t, 1 - y].astype(f32)).astype(bf16)
        e_copy(t, u, 3).start()
        e_copy(t, u, 1).wait_recv()
        EXS2[u][t] = (P[m_x, :, cols(u, 1)] + EYR[u][t, 1 - x].astype(f32)).astype(bf16)
        e_copy(t, u, 2).start()

    def e_last(t, u, P):
        e_copy(t, u, 3).wait_recv()
        P[m_own, :, cols(u, 0)] += EXR[u][t, y].astype(f32) + EYR2[u][t].astype(f32)
        e_copy(t, u, 2).wait_recv()
        P[m_own, :, cols(u, 1)] += EYR[u][t, x].astype(f32) + EXR2[u][t].astype(f32)

    def e_sent(t):
        for u in range(2):
            for i in range(4):
                e_copy(t, u, i).wait_send()

    inputs = [
        pltpu.make_async_copy(src, dst, ins.at[i])
        for i, (src, dst) in enumerate(
            ((x_ref, XV), (cot_ref, CV), (cos_ref, COSV), (sin_ref, SINV))
        )
    ]
    for copy in inputs:
        copy.start()
    for k in range(NK):
        own_copy(k).start()
    inputs[0].wait()
    xf = XV[...].astype(f32)
    centred = xf - jnp.mean(xf, axis=-1, keepdims=True)
    rstd = lax.rsqrt(jnp.mean(centred * centred, axis=-1, keepdims=True) + NORM_EPS)
    xhat = centred * rstd
    XH[...] = xhat
    RSTD[...] = jnp.broadcast_to(rstd, RSTD.shape)
    NA[m_own] = (xhat * gain_ref[...] + bias_ref[...]).astype(bf16)

    bucket = bucket_ref[0]
    B[z, y, c, 0:8] = jnp.broadcast_to(bin_ref[...].astype(f32), (8, 128)).astype(bf16)
    B[z, y, c, 8:16] = jnp.full((8, 128), bucket.astype(f32), f32).astype(bf16)

    slot = lax.shift_right_logical(jnp.int32(rows), bucket)
    shift_of = (rows.bit_length() - 1) - bucket
    row = x * rows + lax.broadcasted_iota(jnp.int32, (rows, 128), 0)
    slot_of = lax.shift_right_logical(row, jnp.full(row.shape, shift_of, jnp.int32))
    place = row & jnp.full(row.shape, slot - 1, jnp.int32)
    limit = jnp.zeros((rows, 128), jnp.int32)
    for s in range(SLOTS):
        limit = jnp.where(slot_of == s, counts_ref[s], limit)
    valid = jnp.where(place < limit, 1.0, 0.0)[:, 0:1]
    inputs[1].wait()
    seeds = CV[...].astype(f32) * valid
    SA[m_own] = seeds.astype(bf16)
    back_sum = jnp.sum(seeds, axis=0, keepdims=True)
    V[...] = jnp.zeros_like(V)
    for i in range(8):
        V[16 + i : 17 + i, :] = back_sum[:, i * 128 : (i + 1) * 128]
    pl.semaphore_wait(barrier, len(peers))
    for k in order:
        y_copy(k).start()
    g_send(0)
    g_send(1)
    ag_turn()
    ag_turn()

    lane = lax.broadcasted_iota(jnp.int32, (rows, TILE), 1)
    even = (lane & 1) == 0

    def table(g):
        brow = B[z, g, c].astype(f32)[8:9, :]
        ba = jnp.broadcast_to(brow, (rows, 128))

        def pick(ref):
            full = ref[...]
            out = full
            for b in range(1, 4):
                n = rows >> b
                out = jnp.where(ba == float(b), jnp.concatenate([full[:n]] * (1 << b), axis=0), out)
            return out

        cg, sg = pick(COSV), pick(SINV)
        CT[g] = jnp.concatenate([cg, cg], axis=1)
        SN[g] = jnp.concatenate([sg, sg], axis=1)
        size = jnp.full((rows, 128), rows, jnp.int32)
        for b in range(1, 4):
            size = jnp.where(ba == float(b), rows >> b, size)
        size = jnp.concatenate([size, size], axis=1)
        qi = lax.broadcasted_iota(jnp.int32, (rows, rows), 0)
        ki = lax.broadcasted_iota(jnp.int32, (rows, rows), 1)
        BM[g] = jnp.where((ki <= qi) & ((qi ^ ki) < size), 0.0, MASKED_SCORE)

    def tables():
        for g in range(2):
            table(g)

    def turn(v, g, sign):
        other = jnp.where(even, -pltpu.roll(v, TILE - 1, 1), pltpu.roll(v, 1, 1))
        return v * CT[g] + (sign * other) * SN[g]

    def weight(k):
        return W[k].reshape(width, TILE)

    scale = HD ** (-0.5)

    def project(m):
        g = m // 2
        nb = NA[m]
        QR[m] = turn(dot_nn(nb, weight(0)), g, 1.0).astype(bf16)
        KR[m] = turn(dot_nn(nb, weight(1)), g, 1.0).astype(bf16)
        VR[m] = dot_nn(nb, weight(2)).astype(bf16)

    def attend(m):
        g = m // 2
        q, kk, v = QR[m], KR[m], VR[m]
        da = dot_nn(SA[m], weight(3)).astype(bf16)
        zero = jnp.zeros((rows, TILE), bf16)
        ps, ss, qs, ks, vs_, ds = [], [], [], [], [], []
        for h in range(N_HEADS):
            mine = (lane // HD) == h
            qh, kh, vh, dh = (jnp.where(mine, t, zero) for t in (q, kk, v, da))
            s = dot_nt(qh, kk) * scale + BM[g]
            e = jnp.exp(s - jnp.max(s, axis=-1, keepdims=True))
            p = e * (1.0 / jnp.sum(e, axis=-1, keepdims=True))
            pg = dot_nt(dh, v)
            sg = p * (pg - jnp.sum(p * pg, axis=-1, keepdims=True))
            for held, t in ((ps, p), (ss, sg), (qs, qh), (ks, kh), (vs_, vh), (ds, dh)):
                held.append(t.astype(bf16))
        wide_p, wide_s = jnp.concatenate(ps, axis=1), jnp.concatenate(ss, axis=1)
        att = dot_nn(wide_p, jnp.concatenate(vs_, axis=0))
        dq = dot_nn(wide_s, jnp.concatenate(ks, axis=0))
        dk = dot_tn(jnp.concatenate(ss, axis=0), jnp.concatenate(qs, axis=0))
        dv = dot_tn(jnp.concatenate(ps, axis=0), jnp.concatenate(ds, axis=0))
        at = att.astype(bf16)
        dqb = turn(dq * scale, g, -1.0).astype(bf16)
        dkb = turn(dk * scale, g, -1.0).astype(bf16)
        dvb = dv.astype(bf16)
        rs = pl.ds(pl.multiple_of(m * rows, rows), rows)
        R[3, rs, :] = at
        R[0, rs, :] = dqb
        R[1, rs, :] = dkb
        R[2, rs, :] = dvb
        OUT[m] = dot_nt(at, weight(3))
        DN[m] = dot_nt(dqb, weight(0)) + dot_nt(dkb, weight(1)) + dot_nt(dvb, weight(2))

    def grad_of(k, left):
        total = dot_tn(NS[left].reshape(4 * rows, width), R[k])
        GP[k] = total.astype(bf16).reshape(NZ, 2, 2, 64, TILE)
        rs_c(k).start()

    def slice_of(j):
        return NQ + 2 * j, NQ + 1 + 2 * j

    def feed(j, m, count=1):
        ki, kb = slice_of(j)
        n = count * rows
        b0 = B[2 * y + lax.div(j, 2), lax.rem(j, 2), 0].astype(f32)[0:1, :]
        b1 = B[2 * y + lax.div(j, 2), lax.rem(j, 2), 1].astype(f32)[0:1, :]
        take = lambda ref: ref[pl.ds(m, count)].reshape(n, width)
        u = dot_nn(take(NA), weight(ki)) + jnp.concatenate([b0, b1], axis=1)
        u2 = u * u
        k0 = float(np.sqrt(2.0 / np.pi))
        t = jnp.tanh(k0 * u * (1.0 + 0.044715 * u2))
        act = (0.5 * u * (1.0 + t)).astype(bf16)
        slope = 0.5 * (1.0 + t) + (0.5 * k0) * u * (1.0 - t * t) * (1.0 + 0.134145 * u2)
        hg = (dot_nn(take(SA), weight(kb)) * slope).astype(bf16)
        rs = pl.ds(pl.multiple_of(m * rows, rows), n)
        R[kb, rs, :] = act
        R[ki, rs, :] = hg
        OUT[pl.ds(m, count)] += dot_nt(act, weight(kb)).reshape(count, rows, width)
        DN[pl.ds(m, count)] += dot_nt(hg, weight(ki)).reshape(count, rows, width)
        at = 24 + x * 16 + y * 8 + 2 * j
        total = jnp.sum(hg.astype(f32), axis=0, keepdims=True)
        V[pl.ds(at, 1), :] += total[:, :128]
        V[pl.ds(at + 1, 1), :] += total[:, 128:]

    def feed_grads(j):
        lax.fori_loop(0, 2, lambda i, _: (grad_of(NQ + 2 * j + i, i), 0)[1], 0)

    def v_copy(i, dev):
        return rcp(VS.at[min(i, 3)], VRV.at[i], vs.at[i], vr.at[i], dev)

    v_devs = (dev_c, dev_x, dev_y)

    def v_step(i):
        v_copy(i, v_devs[i]).wait_recv()
        VS[i + 1] = VS[i] + VRV[i]
        if i < 2:
            v_copy(i + 1, v_devs[i + 1]).start()
        else:
            for n, dev in enumerate(dev_z):
                v_copy(3 + n, dev).start()

    def arrived(*chunks):
        for k in chunks:
            ag_done(k)

    ag_turn()
    inputs[2].wait()
    inputs[3].wait()
    tables()
    ag_turn()
    ag_turn()
    ag_turn()
    g_near(0)
    g_forward(0)
    ag_turn()
    arrived(0, NK, 1, 2)
    g_rest(0)
    def near(i):
        ix, iy = lax.rem(i, 2), lax.div(i, 2)
        return 2 * (y + iy - 2 * y * iy) + x + ix - 2 * x * ix

    lax.fori_loop(0, 3, lambda i, _: (project(near(i)), 0)[1], 0)
    ag_turn()
    arrived(3)

    def rows_turn(i, _):
        @pl.when(i == 1)
        def _():
            g_near(1)
            g_forward(1)
            g_rest(1)

        @pl.when(i == 3)
        def _():
            g_far(0)
            project(m_d)
            g_far(1)

        attend(near(i))
        late_turn(8 + i)
        return 0

    lax.fori_loop(0, 4, rows_turn, 0)

    def head_grads(k, _):
        grad_of(k, lax.div(k, 3))

        @pl.when(k > 0)
        def _():
            rs_begin(k - 1)

        return 0

    lax.fori_loop(0, NQ, head_grads, 0)
    ag_turn()

    def slices(j, _):
        arrived(NQ + 2 * j, NQ + 1 + 2 * j)
        feed(j, 0, 4)

        @pl.when(j == 0)
        def _():
            rs_begin(3)
            ag_turn()
            rs_turn()

        @pl.when(j == 1)
        def _():
            ag_turn()
            feed_grads(0)
            rs_turn()
            rs_begin(4)

        @pl.when(j == 2)
        def _():
            rs_begin(5)
            ag_turn()
            rs_turn()

        return 0

    lax.fori_loop(0, NJ, slices, 0)

    for u in range(2):
        e_first(1, u, DN)
    rs_turn()
    feed_grads(1)
    rs_begin(6)
    rs_begin(7)
    rs_turn()
    feed_grads(2)
    rs_begin(8)
    rs_begin(9)
    rs_turn()
    e_second(1, 0, DN)
    e_first(0, 0, OUT)
    feed_grads(3)
    rs_begin(10)
    rs_begin(11)
    e_second(1, 1, DN)
    e_first_y(0, 1, OUT)
    rs_turn()
    rs_turn()
    rs_turn()
    rs_turn()
    for u in range(2):
        e_last(1, u, DN)
    dn = DN[m_own]
    xhat = XH[...]
    gsum = jnp.sum(dn * xhat, axis=0, keepdims=True)
    bsum = jnp.sum(dn, axis=0, keepdims=True)
    for i in range(8):
        V[i : i + 1, :] = gsum[:, i * 128 : (i + 1) * 128]
        V[8 + i : 9 + i, :] = bsum[:, i * 128 : (i + 1) * 128]
    VS[0] = V[...]
    v_copy(0, dev_c).start()
    e = dn * gain_ref[...]
    me = jnp.mean(e, axis=-1, keepdims=True)
    mex = jnp.mean(e * xhat, axis=-1, keepdims=True)
    gin_ref[...] = (SA[m_own].astype(f32) + RSTD[:, 0:1] * (e - me - xhat * mex)).astype(bf16)
    v_step(0)
    e_first_x(0, 1, OUT)
    e_second(0, 0, OUT)
    rs_turn()
    v_step(1)
    rs_turn()
    v_step(2)
    for k in range(6):
        rs_out(k)
    rs_turn()
    e_second(0, 1, OUT)
    rs_turn()
    for k in range(6, 9):
        rs_out(k)
    for k in range(9, NK):
        rs_out(k)
    for i in range(3):
        v_copy(3 + i, dev_z[i]).wait_recv()
    V[...] = VS[3] + VRV[3] + VRV[4] + VRV[5]
    index = 2 * dp + x
    lane4 = lax.rem(index, 4)
    for base, ref in ((0, lng_ref), (8, lnb_ref), (16, bbk_ref)):
        line = V[pl.ds(base + index // 4, 1), :]
        out = line[:, 0:32]
        for n in range(1, 4):
            out = jnp.where(lane4 == n, line[:, 32 * n : 32 * n + 32], out)
        ref[...] = out
    gbin_ref[...] = V[pl.ds(24 + 16 * x + dp, 1), :]
    for u in range(2):
        e_last(0, u, OUT)
    block_ref[...] = (XV[...].astype(f32) + OUT[m_own] + bback_ref[...]).astype(bf16)

    def later(f):
        lax.fori_loop(0, NK, lambda k, _: (f(k), 0)[1], 0)

    for k in range(NK + 1):
        ag_sent(k)
    for t in range(2):
        g_sent(t)
        e_sent(t)
    later(rs_sent)
    for i, dev in enumerate([dev_c, dev_x, dev_y] + dev_z):
        v_copy(i, dev).wait_send()


def write_kernel(*refs):
    srcs, dsts, sems = refs[:10], refs[10:20], refs[20]
    copies = [pltpu.make_async_copy(a, b, sems.at[i]) for i, (a, b) in enumerate(zip(srcs, dsts))]
    for copy in copies:
        copy.start()
    for copy in copies:
        copy.wait()


def rope_constants(rows):
    half = np.arange(ROT // 2, dtype=np.float32)
    rates = (10000.0 ** (-2.0 * half / ROT)).astype(np.float32)
    angle = np.arange(rows, dtype=np.float32)[:, None] * rates[None, :]
    angle = np.repeat(angle, 2, axis=1)
    cos = np.concatenate([np.cos(angle), np.ones((rows, HD - ROT))], axis=1)
    sin = np.concatenate([np.sin(angle), np.zeros((rows, HD - ROT))], axis=1)
    two = lambda t: np.concatenate([t, t], axis=1).astype(np.float32)
    return two(cos), two(sin)


def on_quad(
    residual_in,
    cotangent,
    ln_gain,
    ln_bias,
    w_qkv,
    w_out,
    w_in,
    b_in,
    w_back,
    b_back,
    bucket_ids,
    residue_counts,
):
    rows, width = residual_in.shape
    cos, sin = rope_constants(rows)
    f32, bf16 = jnp.float32, jnp.bfloat16
    vm = pl.BlockSpec(memory_space=pltpu.VMEM)
    sm = pl.BlockSpec(memory_space=pltpu.SMEM)
    anyspace = pl.BlockSpec(memory_space=pl.ANY)
    shard = width // (4 * NZ)
    sem = pltpu.SemaphoreType.DMA
    shapes = (
        jax.ShapeDtypeStruct((rows, width), bf16),
        jax.ShapeDtypeStruct((rows, width), bf16),
        jax.ShapeDtypeStruct((3, shard, 2 * TILE), f32),
        jax.ShapeDtypeStruct((shard, 2 * TILE), f32),
        jax.ShapeDtypeStruct((shard, 2 * NJ * TILE), f32),
        jax.ShapeDtypeStruct((shard, 2 * NJ * TILE), f32),
        jax.ShapeDtypeStruct((1, 32), f32),
        jax.ShapeDtypeStruct((1, 32), f32),
        jax.ShapeDtypeStruct((1, 32), f32),
        jax.ShapeDtypeStruct((1, 128), f32),
    )
    held = pl.pallas_call(
        layer_kernel,
        out_shape=tuple(pltpu.VMEM(v.shape, v.dtype) for v in shapes),
        in_specs=[sm, sm, anyspace, anyspace] + [vm] * 3 + [anyspace] * 2 + [vm] + [anyspace] * 4,
        out_specs=(vm,) * 10,
        scratch_shapes=[
            pltpu.VMEM((NZ, 2, 2, 16, 128), bf16),
            pltpu.VMEM((NK, NZ, 2, 2, shard, TILE), bf16),
            pltpu.VMEM((2, 4, rows, width), bf16),
            pltpu.VMEM((2, rows, TILE), f32),
            pltpu.VMEM((2, rows, TILE), f32),
            pltpu.VMEM((2, rows, rows), f32),
            pltpu.VMEM((4, rows, TILE), bf16),
            pltpu.VMEM((4, rows, TILE), bf16),
            pltpu.VMEM((4, rows, TILE), bf16),
            pltpu.VMEM((NK, 4 * rows, TILE), bf16),
            pltpu.VMEM((rows, width), bf16),
            pltpu.VMEM((rows, width), bf16),
            pltpu.VMEM((rows, 128), f32),
            pltpu.VMEM((rows, 128), f32),
            sem((4,)),
            pltpu.VMEM((4, rows, width), f32),
            pltpu.VMEM((4, rows, width), f32),
            pltpu.VMEM((NK, NZ, 2, 2, shard, TILE), bf16),
            pltpu.VMEM((NK, NZ, 2, shard, TILE), bf16),
            pltpu.VMEM((NK, 5, 2, shard, TILE), bf16),
            pltpu.VMEM((2, shard, TILE), f32),
            pltpu.VMEM((NK, shard, TILE), bf16),
            pltpu.VMEM((NK, shard, TILE), bf16),
            pltpu.VMEM((rows, width), f32),
            pltpu.VMEM((rows, 128), f32),
            pltpu.VMEM((2, 2, rows, 384), bf16),
            pltpu.VMEM((2, 2, rows, 256), bf16),
            pltpu.VMEM((2, 2, rows, 256), bf16),
            pltpu.VMEM((2, 2, rows, 128), bf16),
            pltpu.VMEM((2, 2, rows, 384), bf16),
            pltpu.VMEM((2, 2, rows, 256), bf16),
            pltpu.VMEM((2, 2, rows, 256), bf16),
            pltpu.VMEM((2, 2, rows, 128), bf16),
            pltpu.VMEM((2, rows, 256), bf16),
            pltpu.VMEM((2, rows, 128), bf16),
            pltpu.VMEM((2, rows, 384), bf16),
            pltpu.VMEM((2, rows, 256), bf16),
            pltpu.VMEM((2, rows, 256), bf16),
            pltpu.VMEM((2, rows, 128), bf16),
            pltpu.VMEM((2, rows, 384), bf16),
            pltpu.VMEM((2, rows, 256), bf16),
            pltpu.VMEM((VROWS, 128), f32),
            pltpu.VMEM((4, VROWS, 128), f32),
            pltpu.VMEM((6, VROWS, 128), f32),
            sem((NK,)),
            sem((NK + 1,)),
            sem((NK + 1,)),
            sem((NK + 1, 2, 3)),
            sem((NK + 1, 2, 3)),
            sem((NK + 1, NZ)),
            sem((NK + 1, NZ)),
            sem((12,)),
            sem((12,)),
            sem((NK,)),
            sem((NK,)),
            sem((NK, NZ)),
            sem((NK, 5)),
            sem((NK,)),
            sem((NK,)),
            sem((2, 2, 4)),
            sem((2, 2, 4)),
            sem((6,)),
            sem((6,)),
        ],
        compiler_params=pltpu.CompilerParams(
            collective_id=0, has_side_effects=True, vmem_limit_bytes=58 << 20
        ),
        cost_estimate=pl.CostEstimate(
            flops=20 * 2**30, bytes_accessed=8 * 2**20, transcendentals=2**21
        ),
    )(
        bucket_ids,
        residue_counts.reshape(SLOTS),
        residual_in,
        cotangent,
        ln_gain.reshape(1, width),
        ln_bias.reshape(1, width),
        b_back.reshape(1, width),
        jnp.asarray(cos),
        jnp.asarray(sin),
        b_in.reshape(1, 128),
        w_qkv,
        w_out.T,
        w_in,
        w_back.T,
    )
    held = [pltpu.with_memory_space_constraint(v, pltpu.VMEM) for v in held]
    outs = pl.pallas_call(
        write_kernel,
        out_shape=shapes,
        in_specs=[vm] * 10,
        out_specs=(anyspace,) * 10,
        scratch_shapes=[sem((10,))],
    )(*held)
    block_out, grad_input, grad_w_qkv, gwo, grad_w_in, gwb, lng, lnb, bbk, gbin = outs
    return (
        block_out,
        grad_input,
        lng.reshape(32),
        lnb.reshape(32),
        grad_w_qkv,
        gwo.T,
        grad_w_in,
        gbin.reshape(128),
        gwb.T,
        bbk.reshape(32),
    )


def solution(mesh):
    placed = (
        P(("dp", "mp"), None),
        P(("dp", "mp"), None),
        P(),
        P(),
        P(None, "dp", "mp"),
        P("mp", "dp"),
        P("dp", "mp"),
        P(("mp", "dp")),
        P("mp", "dp"),
        P(),
        P("dp"),
        P("dp", None),
    )
    return jax.shard_map(
        on_quad if fits_quad(mesh) else on_device,
        mesh=mesh,
        in_specs=placed,
        out_specs=(
            P(("dp", "mp"), None),
            P(("dp", "mp"), None),
            P(("dp", "mp")),
            P(("dp", "mp")),
            P(None, "dp", "mp"),
            P("mp", "dp"),
            P("dp", "mp"),
            P(("mp", "dp")),
            P("mp", "dp"),
            P(("dp", "mp")),
        ),
        check_vma=False,
    )
```

```python
from functools import partial

import jax
import jax.numpy as jnp
import numpy as np
from jax import lax
from jax.experimental import pallas as pl
from jax.experimental.pallas import tpu as pltpu
from jax.sharding import PartitionSpec as P

HD = 64
ROT = 32
SLOTS = 16


NORM_EPS = 1e-05
MASKED_SCORE = -1e30


def norm_rows(inputs_now, norm_gain, norm_shift):
    centred = inputs_now - jnp.mean(inputs_now, axis=-1, keepdims=True)
    spread = jnp.mean(centred * centred, axis=-1, keepdims=True)
    return centred * lax.rsqrt(spread + NORM_EPS) * norm_gain + norm_shift


def slot_tables(bucket_one, residue_row, group_rows):
    slot_length = jnp.right_shift(jnp.int32(group_rows // 2), bucket_one)
    places = jnp.arange(group_rows, dtype=jnp.int32)
    slot_ids = places // slot_length
    inside = places - slot_ids * slot_length
    match_table = slot_ids[:, None] == jnp.arange(SLOTS, dtype=jnp.int32)[None, :]
    picked = jnp.sum(jnp.where(match_table, residue_row[None, :], 0), axis=1)
    live_rows = jnp.minimum(picked, slot_length)
    return (slot_ids, inside, inside < live_rows)


def rope_tables(inside):
    half_steps = jnp.arange(ROT // 2, dtype=jnp.float32)
    inverse_rates = 10000.0 ** (-2.0 * half_steps / ROT)
    angles = inside.astype(jnp.float32)[:, None] * inverse_rates[None, :]
    return (jnp.cos(angles), jnp.sin(angles))


def rotate(values, cosine_table, sine_table):
    row_count = values.shape[0]
    head_count = values.shape[1]
    paired = values[..., :ROT].reshape(row_count, head_count, ROT // 2, 2)
    even_part = paired[..., 0]
    odd_part = paired[..., 1]
    cosine_now = cosine_table[:, None, :]
    sine_now = sine_table[:, None, :]
    turned = jnp.stack(
        [
            even_part * cosine_now - odd_part * sine_now,
            odd_part * cosine_now + even_part * sine_now,
        ],
        axis=-1,
    )
    return jnp.concatenate([turned.reshape(row_count, head_count, ROT), values[..., ROT:]], axis=-1)


def mask_block(block_start, block_rows, slot_ids):
    query_places = block_start + jnp.arange(block_rows, dtype=jnp.int32)
    query_slots = lax.dynamic_slice_in_dim(slot_ids, block_start, block_rows, 0)
    key_places = jnp.arange(slot_ids.shape[0], dtype=jnp.int32)
    return (query_slots[:, None] == slot_ids[None, :]) & (
        key_places[None, :] <= query_places[:, None]
    )


def over_rows(first_op, second_op):
    return lax.dot_general(
        first_op, second_op, (((0,), (0,)), ((), ())), preferred_element_type=jnp.float32
    )


def against_weight(first_op, second_op):
    return lax.dot_general(
        first_op, second_op, (((1,), (1,)), ((), ())), preferred_element_type=jnp.float32
    )


def on_device(
    residual_in,
    cotangent,
    ln_gain,
    ln_bias,
    w_qkv,
    w_out,
    w_in,
    b_in,
    w_back,
    b_back,
    bucket_ids,
    residue_counts,
):
    model_count = lax.axis_size("mp")
    model_rank = lax.axis_index("mp")
    local_rows = residual_in.shape[0]
    group_rows = local_rows * model_count
    slot_ids, inside, valid_rows = slot_tables(bucket_ids[0], residue_counts[0], group_rows)
    cosine_table, sine_table = rope_tables(inside)
    qkv_all, out_all, in_all, bias_in, back_all = (
        lax.all_gather(w_qkv, "dp", axis=1, tiled=True),
        lax.all_gather(w_out, "dp", axis=1, tiled=True),
        lax.all_gather(w_in, "dp", axis=0, tiled=True),
        lax.all_gather(b_in, "dp", axis=0, tiled=True),
        lax.all_gather(w_back, "dp", axis=1, tiled=True),
    )
    x_local = residual_in.astype(jnp.float32)
    x_group = lax.all_gather(residual_in, "mp", axis=0, tiled=True).astype(jnp.float32)
    normed = norm_rows(x_group, ln_gain, ln_bias).astype(jnp.bfloat16)
    head_width = qkv_all.shape[2]
    head_count = head_width // HD
    score_scale = HD ** (-0.5)

    def project(member_index):
        return jnp.dot(normed, qkv_all[member_index], preferred_element_type=jnp.float32).reshape(
            group_rows, head_count, HD
        )

    queries = rotate(project(0), cosine_table, sine_table).astype(jnp.bfloat16)
    key_rows = rotate(project(1), cosine_table, sine_table).astype(jnp.bfloat16)
    value_rows = project(2).astype(jnp.bfloat16)
    block_rows = min(512, group_rows)
    starts = jnp.arange(group_rows // block_rows, dtype=jnp.int32) * block_rows

    def block_scores(block_start):
        query_block = lax.dynamic_slice_in_dim(queries, block_start, block_rows, 0)
        allowed = mask_block(block_start, block_rows, slot_ids)
        scores = (
            jnp.einsum("qhd,khd->hqk", query_block, key_rows, preferred_element_type=jnp.float32)
            * score_scale
        )
        return (query_block, jnp.where(allowed[None], scores, MASKED_SCORE))

    def forward_block(block_start):
        query_block, scores = block_scores(block_start)
        row_peak = jnp.max(scores, axis=-1, keepdims=True)
        exp_scores = jnp.exp(scores - row_peak)
        row_total = jnp.sum(exp_scores, axis=-1, keepdims=True)
        weights_now = (exp_scores / row_total).astype(jnp.bfloat16)
        attended = jnp.einsum(
            "hqk,khd->qhd", weights_now, value_rows, preferred_element_type=jnp.float32
        )
        return (attended.astype(jnp.bfloat16), (row_peak + jnp.log(row_total))[..., 0])

    attended_blocks, log_totals = lax.map(forward_block, starts)
    mixed_rows = attended_blocks.reshape(group_rows, head_width)
    hidden = jnp.dot(normed, in_all, preferred_element_type=jnp.float32) + bias_in.astype(
        jnp.float32
    )
    gelu_tanh = partial(jax.nn.gelu, approximate=True)
    active_value, gelu_pull = jax.vjp(gelu_tanh, hidden)
    active = active_value.astype(jnp.bfloat16)
    partial_out = jnp.dot(mixed_rows, out_all, preferred_element_type=jnp.float32) + jnp.dot(
        active, back_all, preferred_element_type=jnp.float32
    )
    summed_all = lax.psum(partial_out.astype(jnp.bfloat16), "mp").astype(jnp.float32)
    summed = lax.dynamic_slice_in_dim(summed_all, model_rank * local_rows, local_rows, 0)
    block_out = (x_local + summed + b_back).astype(jnp.bfloat16)
    cot_group = lax.all_gather(cotangent, "mp", axis=0, tiled=True)
    seed_rows = jnp.where(valid_rows[:, None], cot_group, jnp.zeros_like(cot_group))
    qkv_all, out_all, in_all, back_all = (
        lax.all_gather(w_qkv, "dp", axis=1, tiled=True),
        lax.all_gather(w_out, "dp", axis=1, tiled=True),
        lax.all_gather(w_in, "dp", axis=0, tiled=True),
        lax.all_gather(w_back, "dp", axis=1, tiled=True),
    )
    active_grad = against_weight(seed_rows, back_all)
    hidden_grad = gelu_pull(active_grad)[0].astype(jnp.bfloat16)
    grad_in_local = over_rows(normed, hidden_grad)
    grad_bias_in = jnp.sum(hidden_grad.astype(jnp.float32), axis=0)
    grad_back_local = over_rows(active, seed_rows)
    grad_out_local = over_rows(mixed_rows, seed_rows)
    normed_grad = against_weight(hidden_grad, in_all)
    mixed_grad = (
        against_weight(seed_rows, out_all).astype(jnp.bfloat16).reshape(group_rows, head_count, HD)
    )

    def backward_block(carry, inputs_now):
        key_acc, value_acc = carry
        block_start, log_total = inputs_now
        query_block, scores = block_scores(block_start)
        grad_block = lax.dynamic_slice_in_dim(mixed_grad, block_start, block_rows, 0)
        probs = jnp.exp(scores - log_total[..., None])
        probs_low = probs.astype(jnp.bfloat16)
        value_acc = value_acc + jnp.einsum(
            "hqk,qhd->khd", probs_low, grad_block, preferred_element_type=jnp.float32
        )
        probs_grad = jnp.einsum(
            "qhd,khd->hqk", grad_block, value_rows, preferred_element_type=jnp.float32
        )
        score_grad = probs * (probs_grad - jnp.sum(probs * probs_grad, axis=-1, keepdims=True))
        score_low = score_grad.astype(jnp.bfloat16)
        query_grad = (
            jnp.einsum("hqk,khd->qhd", score_low, key_rows, preferred_element_type=jnp.float32)
            * score_scale
        )
        key_acc = (
            key_acc
            + jnp.einsum("hqk,qhd->khd", score_low, query_block, preferred_element_type=jnp.float32)
            * score_scale
        )
        return ((key_acc, value_acc), query_grad)

    empty_heads = jnp.zeros((group_rows, head_count, HD), jnp.float32)
    (key_acc, value_acc), query_blocks = lax.scan(
        backward_block, (empty_heads, empty_heads), (starts, log_totals)
    )
    turn_back = partial(rotate, cosine_table=cosine_table, sine_table=sine_table)
    unturn = jax.vjp(turn_back, empty_heads)[1]
    query_pre_grad = (
        unturn(query_blocks.reshape(group_rows, head_count, HD))[0]
        .astype(jnp.bfloat16)
        .reshape(group_rows, head_width)
    )
    key_pre_grad = unturn(key_acc)[0].astype(jnp.bfloat16).reshape(group_rows, head_width)
    value_grad = value_acc.astype(jnp.bfloat16).reshape(group_rows, head_width)
    grad_qkv_local = jnp.stack(
        [
            over_rows(normed, query_pre_grad),
            over_rows(normed, key_pre_grad),
            over_rows(normed, value_grad),
        ],
        axis=0,
    )
    normed_grad = (
        normed_grad
        + against_weight(query_pre_grad, qkv_all[0])
        + against_weight(key_pre_grad, qkv_all[1])
        + against_weight(value_grad, qkv_all[2])
    )
    share_grad = lax.psum(normed_grad.astype(jnp.bfloat16), "mp").astype(jnp.float32)
    seed_group = seed_rows.astype(jnp.float32)
    norm_pull = jax.vjp(norm_rows, x_group, ln_gain, ln_bias)[1]
    input_part, gain_part, shift_part = norm_pull(share_grad)
    input_group = seed_group + input_part
    grad_input = lax.dynamic_slice_in_dim(
        input_group, model_rank * local_rows, local_rows, 0
    ).astype(jnp.bfloat16)
    back_part = jnp.sum(seed_group, axis=0)
    grad_w_qkv, grad_w_out, grad_w_in, grad_b_in, grad_w_back, gain_rows, shift_rows, back_rows = (
        lax.psum_scatter(
            grad_qkv_local.astype(jnp.bfloat16), "dp", scatter_dimension=1, tiled=True
        ).astype(jnp.float32),
        lax.psum_scatter(
            grad_out_local.astype(jnp.bfloat16), "dp", scatter_dimension=1, tiled=True
        ).astype(jnp.float32),
        lax.psum_scatter(
            grad_in_local.astype(jnp.bfloat16), "dp", scatter_dimension=0, tiled=True
        ).astype(jnp.float32),
        lax.psum_scatter(
            grad_bias_in.astype(jnp.bfloat16), "dp", scatter_dimension=0, tiled=True
        ).astype(jnp.float32),
        lax.psum_scatter(
            grad_back_local.astype(jnp.bfloat16), "dp", scatter_dimension=1, tiled=True
        ).astype(jnp.float32),
        lax.psum_scatter(
            gain_part.astype(jnp.bfloat16), "dp", scatter_dimension=0, tiled=True
        ).astype(jnp.float32),
        lax.psum_scatter(
            shift_part.astype(jnp.bfloat16), "dp", scatter_dimension=0, tiled=True
        ).astype(jnp.float32),
        lax.psum_scatter(
            back_part.astype(jnp.bfloat16), "dp", scatter_dimension=0, tiled=True
        ).astype(jnp.float32),
    )
    piece_width = gain_rows.shape[0] // model_count
    grad_ln_gain = lax.dynamic_slice_in_dim(gain_rows, model_rank * piece_width, piece_width, 0)
    grad_ln_bias = lax.dynamic_slice_in_dim(shift_rows, model_rank * piece_width, piece_width, 0)
    grad_b_back = lax.dynamic_slice_in_dim(back_rows, model_rank * piece_width, piece_width, 0)
    return (
        block_out,
        grad_input,
        grad_ln_gain,
        grad_ln_bias,
        grad_w_qkv,
        grad_w_out,
        grad_w_in,
        grad_b_in,
        grad_w_back,
        grad_b_back,
    )


MESH = pl.DeviceIdType.MESH
NZ = 4
TILE = 256
N_HEADS = TILE // HD
NQ = 4
NJ = 4
NK = NQ + 2 * NJ
VROWS = 56


def fits_quad(mesh):
    return mesh.shape["mp"] == 2 and mesh.shape["dp"] == 4 * NZ


def dot_nn(a, b):
    return lax.dot_general(a, b, (((1,), (0,)), ((), ())), preferred_element_type=jnp.float32)


def dot_nt(a, b):
    return lax.dot_general(a, b, (((1,), (1,)), ((), ())), preferred_element_type=jnp.float32)


def dot_tn(a, b):
    return lax.dot_general(a, b, (((0,), (0,)), ((), ())), preferred_element_type=jnp.float32)


def layer_kernel(
    bucket_ref,
    counts_ref,
    x_ref,
    cot_ref,
    gain_ref,
    bias_ref,
    bback_ref,
    cos_ref,
    sin_ref,
    bin_ref,
    wqkv_ref,
    wot_ref,
    win_ref,
    wbt_ref,
    block_ref,
    gin_ref,
    gqkv_ref,
    got_ref,
    gi_ref,
    gbt_ref,
    lng_ref,
    lnb_ref,
    bbk_ref,
    gbin_ref,
    B,
    W,
    NS,
    CT,
    SN,
    BM,
    QR,
    KR,
    VR,
    R,
    SL,
    XV,
    CV,
    COSV,
    SINV,
    ins,
    OUT,
    DN,
    GP,
    GC,
    RZ,
    FS,
    YS,
    YR,
    XH,
    RSTD,
    EXSa,
    EXSb,
    EYSa,
    EYSb,
    EXRa,
    EXRb,
    EYRa,
    EYRb,
    EXS2a,
    EXS2b,
    EYS2a,
    EYS2b,
    EXR2a,
    EXR2b,
    EYR2a,
    EYR2b,
    V,
    VS,
    VRV,
    loc_sem,
    ays,
    ayr,
    azs,
    azr,
    acs,
    acr,
    gs,
    gr,
    rcs,
    rcr,
    rzs,
    rzr,
    rys,
    ryr,
    exs,
    exr,
    vs,
    vr,
):
    EXS = (EXSa, EXSb)
    EYS = (EYSa, EYSb)
    EXR = (EXRa, EXRb)
    EYR = (EYRa, EYRb)
    EXS2 = (EXS2a, EXS2b)
    EYS2 = (EYS2a, EYS2b)
    EXR2 = (EXR2a, EXR2b)
    EYR2 = (EYR2a, EYR2b)
    f32, bf16 = jnp.float32, jnp.bfloat16
    dp, x = lax.axis_index("dp"), lax.axis_index("mp")
    z = dp // 4
    y = lax.rem(dp // 2, 2)
    c = lax.rem(dp, 2)
    rows = x_ref.shape[0]
    width = x_ref.shape[1]
    dev_x = (dp, 1 - x)
    dev_y = (dp + 2 - 4 * y, x)
    dev_c = (dp + 1 - 2 * c, x)
    dev_r = (lax.rem(dp + 4, 4 * NZ), x)
    dev_l = (lax.rem(dp + 4 * NZ - 4, 4 * NZ), x)
    dev_z = [(lax.rem(dp + 4 * i, 4 * NZ), x) for i in (1, 2, 3)]
    NA, SA = NS.at[0], NS.at[1]
    m_own = 2 * y + x
    m_x = 2 * y + 1 - x
    m_y = 2 - 2 * y + x
    m_d = 3 - m_own

    def rcp(src, dst, ss, rs, dev):
        return pltpu.make_async_remote_copy(
            src_ref=src, dst_ref=dst, send_sem=ss, recv_sem=rs, device_id=dev, device_id_type=MESH
        )

    barrier = pltpu.get_barrier_semaphore()
    peers = [dev_x, dev_y, dev_c] + dev_z
    for peer in peers:
        pl.semaphore_signal(barrier, inc=1, device_id=peer, device_id_type=MESH)

    def wsrc(k, q):
        if k == NK:
            return None
        if k < 3:
            return wqkv_ref.at[k, :, pl.ds(pl.multiple_of(q * TILE, TILE), TILE)]
        if k == 3:
            return wot_ref.at[:, pl.ds(pl.multiple_of(q * TILE, TILE), TILE)]
        ref = win_ref if k % 2 == 0 else wbt_ref
        j = (k - NQ) // 2
        return ref.at[:, pl.ds(pl.multiple_of(q * (NJ * TILE) + j * TILE, TILE), TILE)]

    def wv(k):
        return B if isinstance(k, int) and k == NK else W.at[k]

    def own_copy(k):
        return pltpu.make_async_copy(wsrc(k, y), W.at[k, z, y, c], loc_sem.at[k])

    def y_copy(k):
        if k == NK:
            return rcp(B.at[z, y, c], B.at[z, y, c], ays.at[k], ayr.at[k], dev_y)
        return rcp(wsrc(k, 1 - y), W.at[k, z, y, c], ays.at[k], ayr.at[k], dev_y)

    def y_arrived(k):
        here = wv(k).at[z, 1 - y, c]
        rcp(here, here, ays.at[k], ayr.at[k], dev_y).wait_recv()

    def z_copy(k, way, s, e):
        block = wv(k).at[e, :, c]
        return rcp(
            block, block, azs.at[k, way, s], azr.at[k, way, s], dev_r if way == 0 else dev_l
        )

    def c_copy(k, e):
        block = wv(k).at[e, :, c]
        return rcp(block, block, acs.at[k, e], acr.at[k, e], dev_c)

    def ag_own(k, copied=True):
        if copied:
            pltpu.make_async_copy(
                W.at[k, z, y, c], W.at[k, z, y, c], loc_sem.at[k]
            ).wait()
        y_arrived(k)

        @pl.when(z < NZ - 1)
        def _():
            z_copy(k, 0, 0, z).start()

        @pl.when(z > 0)
        def _():
            z_copy(k, 1, 0, z).start()

        c_copy(k, z).start()

    def ag_step(k, s):
        @pl.when(z - 1 - s >= 0)
        def _():
            e = z - 1 - s
            z_copy(k, 0, s, e).wait_recv()
            if s < NZ - 2:

                @pl.when(z < NZ - 1)
                def _():
                    z_copy(k, 0, s + 1, e).start()

            c_copy(k, e).start()

        @pl.when(z + 1 + s <= NZ - 1)
        def _():
            e = z + 1 + s
            z_copy(k, 1, s, e).wait_recv()
            if s < NZ - 2:

                @pl.when(z > 0)
                def _():
                    z_copy(k, 1, s + 1, e).start()

            c_copy(k, e).start()

    def ag_done(k):
        for e in range(NZ):
            block = wv(k).at[e, :, 1 - c]
            rcp(block, block, acs.at[k, e], acr.at[k, e], dev_c).wait_recv()

    def ag_sent(k, copied=True):
        y_copy(k).wait_send() if isinstance(k, int) else None
        for s in range(NZ - 1):

            @pl.when((z < NZ - 1) & (z - s >= 0))
            def _():
                z_copy(k, 0, s, z - s).wait_send()

            @pl.when((z > 0) & (z + s <= NZ - 1))
            def _():
                z_copy(k, 1, s, z + s).wait_send()

        for e in range(NZ):
            c_copy(k, e).wait_send()

    order = [0, NK] + list(range(1, NK))
    turns = iter([t for t in range(NK + NZ) if not 8 <= t <= 11])

    def ag_turn():
        t = next(turns, None)
        if t is None:
            return
        for n in range(2) if t == 0 else (t + 1,):
            if n <= NK:
                ag_own(order[n], copied=order[n] != NK)
        for s in range(NZ - 1):
            if 0 <= t - 1 - s <= NK:
                ag_step(order[t - 1 - s], s)

    def late_turn(t):
        ag_own(t)
        for s in range(NZ - 1):
            ag_step(t - 2 - s, s)

    P0 = 80
    parts = (pl.ds(0, P0), pl.ds(P0, rows - P0))
    BUF = (NA, SA)

    def g_copy(t, p, way, m):
        block = BUF[t].at[m, parts[p]]
        i = (t * 2 + p) * 3 + way
        dev = (dev_x, dev_y)[way] if way < 2 else (dev_y, dev_x)[p]
        return rcp(block, block, gs.at[i], gr.at[i], dev)

    def g_send(t):
        g_copy(t, 0, 0, m_own).start()
        g_copy(t, 1, 1, m_own).start()
        g_copy(t, 1, 0, m_own).start()
        g_copy(t, 0, 1, m_own).start()

    def g_near(t):
        g_copy(t, 0, 0, m_x).wait_recv()
        g_copy(t, 1, 1, m_y).wait_recv()

    def g_forward(t):
        g_copy(t, 0, 2, m_x).start()
        g_copy(t, 1, 2, m_y).start()

    def g_rest(t):
        g_copy(t, 1, 0, m_x).wait_recv()
        g_copy(t, 0, 1, m_y).wait_recv()

    def g_far(t):
        g_copy(t, 0, 2, m_d).wait_recv()
        g_copy(t, 1, 2, m_d).wait_recv()

    def g_sent(t):
        for p in (0, 1):
            for way in (0, 1):
                g_copy(t, p, way, m_own).wait_send()
        g_copy(t, 0, 2, m_x).wait_send()
        g_copy(t, 1, 2, m_y).wait_send()

    def rs_c(k):
        return rcp(GP.at[k, :, :, 1 - c], GC.at[k], rcs.at[k], rcr.at[k], dev_c)

    def rs_z(k, way, e, slot):
        return rcp(
            GP.at[k, e, :, c],
            RZ.at[k, slot],
            rzs.at[k, e],
            rzr.at[k, slot],
            dev_r if way == 0 else dev_l,
        )

    def rs_begin(k):
        rs_c(k).wait_recv()
        for e in range(NZ):
            GP[k, e, :, c] = (GP[k, e, :, c].astype(f32) + GC[k, e].astype(f32)).astype(bf16)

        @pl.when(z == 0)
        def _():
            for e in range(NZ - 1, 0, -1):
                rs_z(k, 0, e, e).start()

        @pl.when(z == NZ - 1)
        def _():
            for e in range(NZ - 1):
                rs_z(k, 1, e, e if e < NZ - 2 else 4).start()

    def pass_on(k, way, e, slot):
        rs_z(k, way, e, e).wait_recv()
        GP[k, e, :, c] = (GP[k, e, :, c].astype(f32) + RZ[k, e].astype(f32)).astype(bf16)
        rs_z(k, way, e, slot).start()

    def rs_hop1(k):
        @pl.when(z == 1)
        def _():
            pass_on(k, 0, 3, 3)
            pass_on(k, 0, 2, 2)

        @pl.when(z == 2)
        def _():
            pass_on(k, 1, 0, 0)
            pass_on(k, 1, 1, 4)

    def rs_hop2(k):
        @pl.when(z == 2)
        def _():
            pass_on(k, 0, 3, 3)

        @pl.when(z == 1)
        def _():
            pass_on(k, 1, 0, 4)

    def rs_y(k):
        return rcp(YS.at[k], YR.at[k], rys.at[k], ryr.at[k], dev_y)

    def put(k, q, value):
        if k < 3:
            gqkv_ref[k, :, pl.ds(pl.multiple_of(q * TILE, TILE), TILE)] = value
        elif k == 3:
            got_ref[:, pl.ds(pl.multiple_of(q * TILE, TILE), TILE)] = value
        else:
            ref = gi_ref if k % 2 == 0 else gbt_ref
            j = (k - NQ) // 2
            ref[:, pl.ds(pl.multiple_of(q * (NJ * TILE) + j * TILE, TILE), TILE)] = value

    def rs_final(k):
        FS[...] = GP[k, z, :, c].astype(f32)

        @pl.when(z > 0)
        def _():
            rs_z(k, 0, z, z).wait_recv()
            FS[...] += RZ[k, z].astype(f32)

        @pl.when(z < NZ - 1)
        def _():
            rs_z(k, 1, z, 4).wait_recv()
            FS[...] += RZ[k, 4].astype(f32)

        YS[k] = FS[1 - y].astype(bf16)
        rs_y(k).start()
        put(k, y, FS[y])

    def rs_out(k):
        rs_y(k).wait_recv()
        put(k, 1 - y, YR[k].astype(f32))

    rturns = iter(range(NK + 2))
    rorder = [NQ + 1] + [k for k in range(NK) if k != NQ + 1]

    def rs_turn():
        r = next(rturns, None)
        if r is None:
            return
        for s, f in enumerate((rs_hop1, rs_hop2, rs_final)):
            if 0 <= r - s < NK:
                f(rorder[r - s])

    def rs_sent(k):
        rs_c(k).wait_send()
        for e in range(NZ):

            @pl.when(z != e)
            def _():
                rs_z(k, 0, e, e).wait_send()

        rs_y(k).wait_send()

    def e_copy(t, u, i):
        src, dst, dev = (
            (EXS, EXR, dev_x),
            (EYS, EYR, dev_y),
            (EXS2, EXR2, dev_x),
            (EYS2, EYR2, dev_y),
        )[i]
        src, dst = src[u], dst[u]
        return rcp(src.at[t], dst.at[t], exs.at[t, u, i], exr.at[t, u, i], dev)

    wide = (384, 256)
    thin = (2 * 128, 128)

    def cols(u, half):
        if half == 0:
            return pl.ds(u * wide[0], wide[u])
        return pl.ds(sum(wide) + u * thin[0], thin[u])

    def e_first_x(t, u, P):
        for i in range(2):
            EXS[u][t, i] = P[2 * i + 1 - x, :, cols(u, 0)].astype(bf16)
        e_copy(t, u, 0).start()

    def e_first_y(t, u, P):
        for i in range(2):
            EYS[u][t, i] = P[2 - 2 * y + i, :, cols(u, 1)].astype(bf16)
        e_copy(t, u, 1).start()

    def e_first(t, u, P):
        e_first_x(t, u, P)
        e_first_y(t, u, P)

    def e_second(t, u, P):
        e_copy(t, u, 0).wait_recv()
        EYS2[u][t] = (P[m_y, :, cols(u, 0)] + EXR[u][t, 1 - y].astype(f32)).astype(bf16)
        e_copy(t, u, 3).start()
        e_copy(t, u, 1).wait_recv()
        EXS2[u][t] = (P[m_x, :, cols(u, 1)] + EYR[u][t, 1 - x].astype(f32)).astype(bf16)
        e_copy(t, u, 2).start()

    def e_last(t, u, P):
        e_copy(t, u, 3).wait_recv()
        P[m_own, :, cols(u, 0)] += EXR[u][t, y].astype(f32) + EYR2[u][t].astype(f32)
        e_copy(t, u, 2).wait_recv()
        P[m_own, :, cols(u, 1)] += EYR[u][t, x].astype(f32) + EXR2[u][t].astype(f32)

    def e_sent(t):
        for u in range(2):
            for i in range(4):
                e_copy(t, u, i).wait_send()

    inputs = [
        pltpu.make_async_copy(src, dst, ins.at[i])
        for i, (src, dst) in enumerate(
            ((x_ref, XV), (cot_ref, CV), (cos_ref, COSV), (sin_ref, SINV))
        )
    ]
    for copy in inputs:
        copy.start()
    for k in range(NK):
        own_copy(k).start()
    inputs[0].wait()
    xf = XV[...].astype(f32)
    centred = xf - jnp.mean(xf, axis=-1, keepdims=True)
    rstd = lax.rsqrt(jnp.mean(centred * centred, axis=-1, keepdims=True) + NORM_EPS)
    xhat = centred * rstd
    XH[...] = xhat
    RSTD[...] = jnp.broadcast_to(rstd, RSTD.shape)
    NA[m_own] = (xhat * gain_ref[...] + bias_ref[...]).astype(bf16)

    bucket = bucket_ref[0]
    B[z, y, c, 0:8] = jnp.broadcast_to(bin_ref[...].astype(f32), (8, 128)).astype(bf16)
    B[z, y, c, 8:16] = jnp.full((8, 128), bucket.astype(f32), f32).astype(bf16)

    slot = lax.shift_right_logical(jnp.int32(rows), bucket)
    shift_of = (rows.bit_length() - 1) - bucket
    row = x * rows + lax.broadcasted_iota(jnp.int32, (rows, 128), 0)
    slot_of = lax.shift_right_logical(row, jnp.full(row.shape, shift_of, jnp.int32))
    place = row & jnp.full(row.shape, slot - 1, jnp.int32)
    limit = jnp.zeros((rows, 128), jnp.int32)
    for s in range(SLOTS):
        limit = jnp.where(slot_of == s, counts_ref[s], limit)
    valid = jnp.where(place < limit, 1.0, 0.0)[:, 0:1]
    inputs[1].wait()
    seeds = CV[...].astype(f32) * valid
    SA[m_own] = seeds.astype(bf16)
    back_sum = jnp.sum(seeds, axis=0, keepdims=True)
    V[...] = jnp.zeros_like(V)
    for i in range(8):
        V[16 + i : 17 + i, :] = back_sum[:, i * 128 : (i + 1) * 128]
    pl.semaphore_wait(barrier, len(peers))
    for k in order:
        y_copy(k).start()
    g_send(0)
    g_send(1)
    ag_turn()
    ag_turn()

    lane = lax.broadcasted_iota(jnp.int32, (rows, TILE), 1)
    even = (lane & 1) == 0

    def table(g):
        brow = B[z, g, c].astype(f32)[8:9, :]
        ba = jnp.broadcast_to(brow, (rows, 128))

        def pick(ref):
            full = ref[...]
            out = full
            for b in range(1, 4):
                n = rows >> b
                out = jnp.where(ba == float(b), jnp.concatenate([full[:n]] * (1 << b), axis=0), out)
            return out

        cg, sg = pick(COSV), pick(SINV)
        CT[g] = jnp.concatenate([cg, cg], axis=1)
        SN[g] = jnp.concatenate([sg, sg], axis=1)
        size = jnp.full((rows, 128), rows, jnp.int32)
        for b in range(1, 4):
            size = jnp.where(ba == float(b), rows >> b, size)
        size = jnp.concatenate([size, size], axis=1)
        qi = lax.broadcasted_iota(jnp.int32, (rows, rows), 0)
        ki = lax.broadcasted_iota(jnp.int32, (rows, rows), 1)
        BM[g] = jnp.where((ki <= qi) & ((qi ^ ki) < size), 0.0, MASKED_SCORE)

    def tables():
        for g in range(2):
            table(g)

    def turn(v, g, sign):
        other = jnp.where(even, -pltpu.roll(v, TILE - 1, 1), pltpu.roll(v, 1, 1))
        return v * CT[g] + (sign * other) * SN[g]

    def weight(k):
        return W[k].reshape(width, TILE)

    scale = HD ** (-0.5)

    def project(m):
        g = m // 2
        nb = NA[m]
        QR[m] = turn(dot_nn(nb, weight(0)), g, 1.0).astype(bf16)
        KR[m] = turn(dot_nn(nb, weight(1)), g, 1.0).astype(bf16)
        VR[m] = dot_nn(nb, weight(2)).astype(bf16)

    def attend(m):
        g = m // 2
        q, kk, v = QR[m], KR[m], VR[m]
        da = dot_nn(SA[m], weight(3)).astype(bf16)
        zero = jnp.zeros((rows, TILE), bf16)
        ps, ss, qs, ks, vs_, ds = [], [], [], [], [], []
        for h in range(N_HEADS):
            mine = (lane // HD) == h
            qh, kh, vh, dh = (jnp.where(mine, t, zero) for t in (q, kk, v, da))
            s = dot_nt(qh, kk) * scale + BM[g]
            e = jnp.exp(s - jnp.max(s, axis=-1, keepdims=True))
            p = e * (1.0 / jnp.sum(e, axis=-1, keepdims=True))
            pg = dot_nt(dh, v)
            sg = p * (pg - jnp.sum(p * pg, axis=-1, keepdims=True))
            for held, t in ((ps, p), (ss, sg), (qs, qh), (ks, kh), (vs_, vh), (ds, dh)):
                held.append(t.astype(bf16))
        wide_p, wide_s = jnp.concatenate(ps, axis=1), jnp.concatenate(ss, axis=1)
        att = dot_nn(wide_p, jnp.concatenate(vs_, axis=0))
        dq = dot_nn(wide_s, jnp.concatenate(ks, axis=0))
        dk = dot_tn(jnp.concatenate(ss, axis=0), jnp.concatenate(qs, axis=0))
        dv = dot_tn(jnp.concatenate(ps, axis=0), jnp.concatenate(ds, axis=0))
        at = att.astype(bf16)
        dqb = turn(dq * scale, g, -1.0).astype(bf16)
        dkb = turn(dk * scale, g, -1.0).astype(bf16)
        dvb = dv.astype(bf16)
        rs = pl.ds(pl.multiple_of(m * rows, rows), rows)
        R[3, rs, :] = at
        R[0, rs, :] = dqb
        R[1, rs, :] = dkb
        R[2, rs, :] = dvb
        OUT[m] = dot_nt(at, weight(3))
        DN[m] = dot_nt(dqb, weight(0)) + dot_nt(dkb, weight(1)) + dot_nt(dvb, weight(2))

    def grad_of(k, left):
        total = dot_tn(NS[left].reshape(4 * rows, width), R[k])
        GP[k] = total.astype(bf16).reshape(NZ, 2, 2, 64, TILE)
        rs_c(k).start()

    def slice_of(j):
        return NQ + 2 * j, NQ + 1 + 2 * j

    def all_rows(ref):
        return ref[...].reshape(4 * rows, width)

    def feed(j):
        ki, kb = slice_of(j)
        b0 = B[2 * y + lax.div(j, 2), lax.rem(j, 2), 0].astype(f32)[0:1, :]
        b1 = B[2 * y + lax.div(j, 2), lax.rem(j, 2), 1].astype(f32)[0:1, :]
        u = dot_nn(all_rows(NA), weight(ki)) + jnp.concatenate([b0, b1], axis=1)
        u2 = u * u
        k0 = float(np.sqrt(2.0 / np.pi))
        t = jnp.tanh(k0 * u * (1.0 + 0.044715 * u2))
        R[kb] = (0.5 * u * (1.0 + t)).astype(bf16)
        SL[...] = 0.5 * (1.0 + t) + (0.5 * k0) * u * (1.0 - t * t) * (1.0 + 0.134145 * u2)

    def feed_back(j):
        ki, kb = slice_of(j)
        hg = (dot_nn(all_rows(SA), weight(kb)) * SL[...]).astype(bf16)
        R[ki] = hg
        OUT[...] += dot_nt(R[kb], weight(kb)).reshape(4, rows, width)
        DN[...] += dot_nt(hg, weight(ki)).reshape(4, rows, width)
        at = 24 + x * 16 + y * 8 + 2 * j
        total = jnp.sum(hg.astype(f32), axis=0, keepdims=True)
        V[pl.ds(at, 1), :] = total[:, :128]
        V[pl.ds(at + 1, 1), :] = total[:, 128:]

    def feed_grads(j):
        lax.fori_loop(0, 2, lambda i, _: (grad_of(NQ + 2 * j + i, i), 0)[1], 0)

    def v_copy(i, dev):
        return rcp(VS.at[min(i, 3)], VRV.at[i], vs.at[i], vr.at[i], dev)

    v_devs = (dev_c, dev_x, dev_y)

    def v_step(i):
        v_copy(i, v_devs[i]).wait_recv()
        VS[i + 1] = VS[i] + VRV[i]
        if i < 2:
            v_copy(i + 1, v_devs[i + 1]).start()
        else:
            for n, dev in enumerate(dev_z):
                v_copy(3 + n, dev).start()

    def arrived(*chunks):
        for k in chunks:
            ag_done(k)

    ag_turn()
    inputs[2].wait()
    inputs[3].wait()
    tables()
    ag_turn()
    ag_turn()
    ag_turn()
    g_near(0)
    g_forward(0)
    ag_turn()
    arrived(0, NK, 1, 2)
    g_rest(0)
    def near(i):
        ix, iy = lax.rem(i, 2), lax.div(i, 2)
        return 2 * (y + iy - 2 * y * iy) + x + ix - 2 * x * ix

    lax.fori_loop(0, 3, lambda i, _: (project(near(i)), 0)[1], 0)
    ag_turn()
    arrived(3)

    def rows_turn(i, _):
        @pl.when(i == 1)
        def _():
            g_near(1)
            g_forward(1)
            g_rest(1)

        @pl.when(i == 3)
        def _():
            g_far(1)
            grad_of(NQ + 1, 1)

        attend(near(i))

        @pl.when(i == 2)
        def _():
            g_far(0)
            project(m_d)
            arrived(NQ)
            feed(0)

        @pl.when(i < 3)
        def _():
            late_turn(8 + i)

        return 0

    lax.fori_loop(0, 4, rows_turn, 0)

    def head_grads(k, _):
        grad_of(k, lax.div(k, 3))

        @pl.when(k == 1)
        def _():
            late_turn(11)

        @pl.when(k > 0)
        def _():
            rs_begin(k - 1)

        return 0

    rs_begin(NQ + 1)
    lax.fori_loop(0, NQ, head_grads, 0)
    ag_turn()

    def slices(j, _):
        @pl.when(j > 0)
        def _():
            arrived(NQ + 2 * j)
            feed(j)

        arrived(NQ + 1 + 2 * j)
        feed_back(j)

        @pl.when(j == 0)
        def _():
            rs_begin(3)
            ag_turn()
            rs_turn()

        @pl.when(j == 1)
        def _():
            ag_turn()
            grad_of(NQ, 0)
            rs_turn()
            rs_begin(NQ)

        @pl.when(j == 2)
        def _():
            ag_turn()
            rs_turn()

        return 0

    lax.fori_loop(0, NJ, slices, 0)

    for u in range(2):
        e_first(1, u, DN)
    rs_turn()
    feed_grads(1)
    rs_begin(6)
    rs_begin(7)
    rs_turn()
    feed_grads(2)
    rs_begin(8)
    rs_begin(9)
    rs_turn()
    e_second(1, 0, DN)
    feed_grads(3)
    rs_begin(10)
    rs_begin(11)
    rs_turn()
    e_second(1, 1, DN)
    e_first(0, 0, OUT)
    e_first_y(0, 1, OUT)
    rs_turn()
    rs_turn()
    for u in range(2):
        e_last(1, u, DN)
    dn = DN[m_own]
    xhat = XH[...]
    gsum = jnp.sum(dn * xhat, axis=0, keepdims=True)
    bsum = jnp.sum(dn, axis=0, keepdims=True)
    for i in range(8):
        V[i : i + 1, :] = gsum[:, i * 128 : (i + 1) * 128]
        V[8 + i : 9 + i, :] = bsum[:, i * 128 : (i + 1) * 128]
    VS[0] = V[...]
    v_copy(0, dev_c).start()
    e = dn * gain_ref[...]
    me = jnp.mean(e, axis=-1, keepdims=True)
    mex = jnp.mean(e * xhat, axis=-1, keepdims=True)
    gin_ref[...] = (SA[m_own].astype(f32) + RSTD[:, 0:1] * (e - me - xhat * mex)).astype(bf16)
    v_step(0)
    rs_turn()
    e_first_x(0, 1, OUT)
    rs_turn()
    v_step(1)
    e_second(0, 0, OUT)
    rs_turn()
    v_step(2)
    rs_turn()
    e_second(0, 1, OUT)
    for k in rorder[:9]:
        rs_out(k)
    rs_turn()
    rs_out(rorder[9])
    for k in rorder[10:]:
        rs_out(k)
    for i in range(3):
        v_copy(3 + i, dev_z[i]).wait_recv()
    V[...] = VS[3] + VRV[3] + VRV[4] + VRV[5]
    index = 2 * dp + x
    lane4 = lax.rem(index, 4)
    for base, ref in ((0, lng_ref), (8, lnb_ref), (16, bbk_ref)):
        line = V[pl.ds(base + index // 4, 1), :]
        out = line[:, 0:32]
        for n in range(1, 4):
            out = jnp.where(lane4 == n, line[:, 32 * n : 32 * n + 32], out)
        ref[...] = out
    gbin_ref[...] = V[pl.ds(24 + 16 * x + dp, 1), :]
    for u in range(2):
        e_last(0, u, OUT)
    block_ref[...] = (XV[...].astype(f32) + OUT[m_own] + bback_ref[...]).astype(bf16)

    def later(f):
        lax.fori_loop(0, NK, lambda k, _: (f(k), 0)[1], 0)

    for k in range(NK + 1):
        ag_sent(k)
    for t in range(2):
        g_sent(t)
        e_sent(t)
    later(rs_sent)
    for i, dev in enumerate([dev_c, dev_x, dev_y] + dev_z):
        v_copy(i, dev).wait_send()


def write_kernel(*refs):
    srcs, dsts, sems = refs[:10], refs[10:20], refs[20]
    copies = [pltpu.make_async_copy(a, b, sems.at[i]) for i, (a, b) in enumerate(zip(srcs, dsts))]
    for copy in copies:
        copy.start()
    for copy in copies:
        copy.wait()


def rope_constants(rows):
    half = np.arange(ROT // 2, dtype=np.float32)
    rates = (10000.0 ** (-2.0 * half / ROT)).astype(np.float32)
    angle = np.arange(rows, dtype=np.float32)[:, None] * rates[None, :]
    angle = np.repeat(angle, 2, axis=1)
    cos = np.concatenate([np.cos(angle), np.ones((rows, HD - ROT))], axis=1)
    sin = np.concatenate([np.sin(angle), np.zeros((rows, HD - ROT))], axis=1)
    two = lambda t: np.concatenate([t, t], axis=1).astype(np.float32)
    return two(cos), two(sin)


def on_quad(
    residual_in,
    cotangent,
    ln_gain,
    ln_bias,
    w_qkv,
    w_out,
    w_in,
    b_in,
    w_back,
    b_back,
    bucket_ids,
    residue_counts,
):
    rows, width = residual_in.shape
    cos, sin = rope_constants(rows)
    f32, bf16 = jnp.float32, jnp.bfloat16
    vm = pl.BlockSpec(memory_space=pltpu.VMEM)
    sm = pl.BlockSpec(memory_space=pltpu.SMEM)
    anyspace = pl.BlockSpec(memory_space=pl.ANY)
    shard = width // (4 * NZ)
    sem = pltpu.SemaphoreType.DMA
    shapes = (
        jax.ShapeDtypeStruct((rows, width), bf16),
        jax.ShapeDtypeStruct((rows, width), bf16),
        jax.ShapeDtypeStruct((3, shard, 2 * TILE), f32),
        jax.ShapeDtypeStruct((shard, 2 * TILE), f32),
        jax.ShapeDtypeStruct((shard, 2 * NJ * TILE), f32),
        jax.ShapeDtypeStruct((shard, 2 * NJ * TILE), f32),
        jax.ShapeDtypeStruct((1, 32), f32),
        jax.ShapeDtypeStruct((1, 32), f32),
        jax.ShapeDtypeStruct((1, 32), f32),
        jax.ShapeDtypeStruct((1, 128), f32),
    )
    held = pl.pallas_call(
        layer_kernel,
        out_shape=tuple(pltpu.VMEM(v.shape, v.dtype) for v in shapes),
        in_specs=[sm, sm, anyspace, anyspace] + [vm] * 3 + [anyspace] * 2 + [vm] + [anyspace] * 4,
        out_specs=(vm,) * 10,
        scratch_shapes=[
            pltpu.VMEM((NZ, 2, 2, 16, 128), bf16),
            pltpu.VMEM((NK, NZ, 2, 2, shard, TILE), bf16),
            pltpu.VMEM((2, 4, rows, width), bf16),
            pltpu.VMEM((2, rows, TILE), f32),
            pltpu.VMEM((2, rows, TILE), f32),
            pltpu.VMEM((2, rows, rows), f32),
            pltpu.VMEM((4, rows, TILE), bf16),
            pltpu.VMEM((4, rows, TILE), bf16),
            pltpu.VMEM((4, rows, TILE), bf16),
            pltpu.VMEM((NK, 4 * rows, TILE), bf16),
            pltpu.VMEM((4 * rows, TILE), f32),
            pltpu.VMEM((rows, width), bf16),
            pltpu.VMEM((rows, width), bf16),
            pltpu.VMEM((rows, 128), f32),
            pltpu.VMEM((rows, 128), f32),
            sem((4,)),
            pltpu.VMEM((4, rows, width), f32),
            pltpu.VMEM((4, rows, width), f32),
            pltpu.VMEM((NK, NZ, 2, 2, shard, TILE), bf16),
            pltpu.VMEM((NK, NZ, 2, shard, TILE), bf16),
            pltpu.VMEM((NK, 5, 2, shard, TILE), bf16),
            pltpu.VMEM((2, shard, TILE), f32),
            pltpu.VMEM((NK, shard, TILE), bf16),
            pltpu.VMEM((NK, shard, TILE), bf16),
            pltpu.VMEM((rows, width), f32),
            pltpu.VMEM((rows, 128), f32),
            pltpu.VMEM((2, 2, rows, 384), bf16),
            pltpu.VMEM((2, 2, rows, 256), bf16),
            pltpu.VMEM((2, 2, rows, 256), bf16),
            pltpu.VMEM((2, 2, rows, 128), bf16),
            pltpu.VMEM((2, 2, rows, 384), bf16),
            pltpu.VMEM((2, 2, rows, 256), bf16),
            pltpu.VMEM((2, 2, rows, 256), bf16),
            pltpu.VMEM((2, 2, rows, 128), bf16),
            pltpu.VMEM((2, rows, 256), bf16),
            pltpu.VMEM((2, rows, 128), bf16),
            pltpu.VMEM((2, rows, 384), bf16),
            pltpu.VMEM((2, rows, 256), bf16),
            pltpu.VMEM((2, rows, 256), bf16),
            pltpu.VMEM((2, rows, 128), bf16),
            pltpu.VMEM((2, rows, 384), bf16),
            pltpu.VMEM((2, rows, 256), bf16),
            pltpu.VMEM((VROWS, 128), f32),
            pltpu.VMEM((4, VROWS, 128), f32),
            pltpu.VMEM((6, VROWS, 128), f32),
            sem((NK,)),
            sem((NK + 1,)),
            sem((NK + 1,)),
            sem((NK + 1, 2, 3)),
            sem((NK + 1, 2, 3)),
            sem((NK + 1, NZ)),
            sem((NK + 1, NZ)),
            sem((12,)),
            sem((12,)),
            sem((NK,)),
            sem((NK,)),
            sem((NK, NZ)),
            sem((NK, 5)),
            sem((NK,)),
            sem((NK,)),
            sem((2, 2, 4)),
            sem((2, 2, 4)),
            sem((6,)),
            sem((6,)),
        ],
        compiler_params=pltpu.CompilerParams(
            collective_id=0, has_side_effects=True, vmem_limit_bytes=58 << 20
        ),
        cost_estimate=pl.CostEstimate(
            flops=20 * 2**30, bytes_accessed=8 * 2**20, transcendentals=2**21
        ),
    )(
        bucket_ids,
        residue_counts.reshape(SLOTS),
        residual_in,
        cotangent,
        ln_gain.reshape(1, width),
        ln_bias.reshape(1, width),
        b_back.reshape(1, width),
        jnp.asarray(cos),
        jnp.asarray(sin),
        b_in.reshape(1, 128),
        w_qkv,
        w_out.T,
        w_in,
        w_back.T,
    )
    held = [pltpu.with_memory_space_constraint(v, pltpu.VMEM) for v in held]
    outs = pl.pallas_call(
        write_kernel,
        out_shape=shapes,
        in_specs=[vm] * 10,
        out_specs=(anyspace,) * 10,
        scratch_shapes=[sem((10,))],
    )(*held)
    block_out, grad_input, grad_w_qkv, gwo, grad_w_in, gwb, lng, lnb, bbk, gbin = outs
    return (
        block_out,
        grad_input,
        lng.reshape(32),
        lnb.reshape(32),
        grad_w_qkv,
        gwo.T,
        grad_w_in,
        gbin.reshape(128),
        gwb.T,
        bbk.reshape(32),
    )


def solution(mesh):
    placed = (
        P(("dp", "mp"), None),
        P(("dp", "mp"), None),
        P(),
        P(),
        P(None, "dp", "mp"),
        P("mp", "dp"),
        P("dp", "mp"),
        P(("mp", "dp")),
        P("mp", "dp"),
        P(),
        P("dp"),
        P("dp", None),
    )
    return jax.shard_map(
        on_quad if fits_quad(mesh) else on_device,
        mesh=mesh,
        in_specs=placed,
        out_specs=(
            P(("dp", "mp"), None),
            P(("dp", "mp"), None),
            P(("dp", "mp")),
            P(("dp", "mp")),
            P(None, "dp", "mp"),
            P("mp", "dp"),
            P("dp", "mp"),
            P(("mp", "dp")),
            P("mp", "dp"),
            P(("dp", "mp")),
        ),
        check_vma=False,
    )
```

```python
from functools import partial

import jax
import jax.numpy as jnp
import numpy as np
from jax import lax
from jax.experimental import pallas as pl
from jax.experimental.pallas import tpu as pltpu
from jax.sharding import PartitionSpec as P

HD = 64
ROT = 32
SLOTS = 16


NORM_EPS = 1e-05
MASKED_SCORE = -1e30


def norm_rows(inputs_now, norm_gain, norm_shift):
    centred = inputs_now - jnp.mean(inputs_now, axis=-1, keepdims=True)
    spread = jnp.mean(centred * centred, axis=-1, keepdims=True)
    return centred * lax.rsqrt(spread + NORM_EPS) * norm_gain + norm_shift


def slot_tables(bucket_one, residue_row, group_rows):
    slot_length = jnp.right_shift(jnp.int32(group_rows // 2), bucket_one)
    places = jnp.arange(group_rows, dtype=jnp.int32)
    slot_ids = places // slot_length
    inside = places - slot_ids * slot_length
    match_table = slot_ids[:, None] == jnp.arange(SLOTS, dtype=jnp.int32)[None, :]
    picked = jnp.sum(jnp.where(match_table, residue_row[None, :], 0), axis=1)
    live_rows = jnp.minimum(picked, slot_length)
    return (slot_ids, inside, inside < live_rows)


def rope_tables(inside):
    half_steps = jnp.arange(ROT // 2, dtype=jnp.float32)
    inverse_rates = 10000.0 ** (-2.0 * half_steps / ROT)
    angles = inside.astype(jnp.float32)[:, None] * inverse_rates[None, :]
    return (jnp.cos(angles), jnp.sin(angles))


def rotate(values, cosine_table, sine_table):
    row_count = values.shape[0]
    head_count = values.shape[1]
    paired = values[..., :ROT].reshape(row_count, head_count, ROT // 2, 2)
    even_part = paired[..., 0]
    odd_part = paired[..., 1]
    cosine_now = cosine_table[:, None, :]
    sine_now = sine_table[:, None, :]
    turned = jnp.stack(
        [
            even_part * cosine_now - odd_part * sine_now,
            odd_part * cosine_now + even_part * sine_now,
        ],
        axis=-1,
    )
    return jnp.concatenate([turned.reshape(row_count, head_count, ROT), values[..., ROT:]], axis=-1)


def mask_block(block_start, block_rows, slot_ids):
    query_places = block_start + jnp.arange(block_rows, dtype=jnp.int32)
    query_slots = lax.dynamic_slice_in_dim(slot_ids, block_start, block_rows, 0)
    key_places = jnp.arange(slot_ids.shape[0], dtype=jnp.int32)
    return (query_slots[:, None] == slot_ids[None, :]) & (
        key_places[None, :] <= query_places[:, None]
    )


def over_rows(first_op, second_op):
    return lax.dot_general(
        first_op, second_op, (((0,), (0,)), ((), ())), preferred_element_type=jnp.float32
    )


def against_weight(first_op, second_op):
    return lax.dot_general(
        first_op, second_op, (((1,), (1,)), ((), ())), preferred_element_type=jnp.float32
    )


def on_device(
    residual_in,
    cotangent,
    ln_gain,
    ln_bias,
    w_qkv,
    w_out,
    w_in,
    b_in,
    w_back,
    b_back,
    bucket_ids,
    residue_counts,
):
    model_count = lax.axis_size("mp")
    model_rank = lax.axis_index("mp")
    local_rows = residual_in.shape[0]
    group_rows = local_rows * model_count
    slot_ids, inside, valid_rows = slot_tables(bucket_ids[0], residue_counts[0], group_rows)
    cosine_table, sine_table = rope_tables(inside)
    qkv_all, out_all, in_all, bias_in, back_all = (
        lax.all_gather(w_qkv, "dp", axis=1, tiled=True),
        lax.all_gather(w_out, "dp", axis=1, tiled=True),
        lax.all_gather(w_in, "dp", axis=0, tiled=True),
        lax.all_gather(b_in, "dp", axis=0, tiled=True),
        lax.all_gather(w_back, "dp", axis=1, tiled=True),
    )
    x_local = residual_in.astype(jnp.float32)
    x_group = lax.all_gather(residual_in, "mp", axis=0, tiled=True).astype(jnp.float32)
    normed = norm_rows(x_group, ln_gain, ln_bias).astype(jnp.bfloat16)
    head_width = qkv_all.shape[2]
    head_count = head_width // HD
    score_scale = HD ** (-0.5)

    def project(member_index):
        return jnp.dot(normed, qkv_all[member_index], preferred_element_type=jnp.float32).reshape(
            group_rows, head_count, HD
        )

    queries = rotate(project(0), cosine_table, sine_table).astype(jnp.bfloat16)
    key_rows = rotate(project(1), cosine_table, sine_table).astype(jnp.bfloat16)
    value_rows = project(2).astype(jnp.bfloat16)
    block_rows = min(512, group_rows)
    starts = jnp.arange(group_rows // block_rows, dtype=jnp.int32) * block_rows

    def block_scores(block_start):
        query_block = lax.dynamic_slice_in_dim(queries, block_start, block_rows, 0)
        allowed = mask_block(block_start, block_rows, slot_ids)
        scores = (
            jnp.einsum("qhd,khd->hqk", query_block, key_rows, preferred_element_type=jnp.float32)
            * score_scale
        )
        return (query_block, jnp.where(allowed[None], scores, MASKED_SCORE))

    def forward_block(block_start):
        query_block, scores = block_scores(block_start)
        row_peak = jnp.max(scores, axis=-1, keepdims=True)
        exp_scores = jnp.exp(scores - row_peak)
        row_total = jnp.sum(exp_scores, axis=-1, keepdims=True)
        weights_now = (exp_scores / row_total).astype(jnp.bfloat16)
        attended = jnp.einsum(
            "hqk,khd->qhd", weights_now, value_rows, preferred_element_type=jnp.float32
        )
        return (attended.astype(jnp.bfloat16), (row_peak + jnp.log(row_total))[..., 0])

    attended_blocks, log_totals = lax.map(forward_block, starts)
    mixed_rows = attended_blocks.reshape(group_rows, head_width)
    hidden = jnp.dot(normed, in_all, preferred_element_type=jnp.float32) + bias_in.astype(
        jnp.float32
    )
    gelu_tanh = partial(jax.nn.gelu, approximate=True)
    active_value, gelu_pull = jax.vjp(gelu_tanh, hidden)
    active = active_value.astype(jnp.bfloat16)
    partial_out = jnp.dot(mixed_rows, out_all, preferred_element_type=jnp.float32) + jnp.dot(
        active, back_all, preferred_element_type=jnp.float32
    )
    summed_all = lax.psum(partial_out.astype(jnp.bfloat16), "mp").astype(jnp.float32)
    summed = lax.dynamic_slice_in_dim(summed_all, model_rank * local_rows, local_rows, 0)
    block_out = (x_local + summed + b_back).astype(jnp.bfloat16)
    cot_group = lax.all_gather(cotangent, "mp", axis=0, tiled=True)
    seed_rows = jnp.where(valid_rows[:, None], cot_group, jnp.zeros_like(cot_group))
    qkv_all, out_all, in_all, back_all = (
        lax.all_gather(w_qkv, "dp", axis=1, tiled=True),
        lax.all_gather(w_out, "dp", axis=1, tiled=True),
        lax.all_gather(w_in, "dp", axis=0, tiled=True),
        lax.all_gather(w_back, "dp", axis=1, tiled=True),
    )
    active_grad = against_weight(seed_rows, back_all)
    hidden_grad = gelu_pull(active_grad)[0].astype(jnp.bfloat16)
    grad_in_local = over_rows(normed, hidden_grad)
    grad_bias_in = jnp.sum(hidden_grad.astype(jnp.float32), axis=0)
    grad_back_local = over_rows(active, seed_rows)
    grad_out_local = over_rows(mixed_rows, seed_rows)
    normed_grad = against_weight(hidden_grad, in_all)
    mixed_grad = (
        against_weight(seed_rows, out_all).astype(jnp.bfloat16).reshape(group_rows, head_count, HD)
    )

    def backward_block(carry, inputs_now):
        key_acc, value_acc = carry
        block_start, log_total = inputs_now
        query_block, scores = block_scores(block_start)
        grad_block = lax.dynamic_slice_in_dim(mixed_grad, block_start, block_rows, 0)
        probs = jnp.exp(scores - log_total[..., None])
        probs_low = probs.astype(jnp.bfloat16)
        value_acc = value_acc + jnp.einsum(
            "hqk,qhd->khd", probs_low, grad_block, preferred_element_type=jnp.float32
        )
        probs_grad = jnp.einsum(
            "qhd,khd->hqk", grad_block, value_rows, preferred_element_type=jnp.float32
        )
        score_grad = probs * (probs_grad - jnp.sum(probs * probs_grad, axis=-1, keepdims=True))
        score_low = score_grad.astype(jnp.bfloat16)
        query_grad = (
            jnp.einsum("hqk,khd->qhd", score_low, key_rows, preferred_element_type=jnp.float32)
            * score_scale
        )
        key_acc = (
            key_acc
            + jnp.einsum("hqk,qhd->khd", score_low, query_block, preferred_element_type=jnp.float32)
            * score_scale
        )
        return ((key_acc, value_acc), query_grad)

    empty_heads = jnp.zeros((group_rows, head_count, HD), jnp.float32)
    (key_acc, value_acc), query_blocks = lax.scan(
        backward_block, (empty_heads, empty_heads), (starts, log_totals)
    )
    turn_back = partial(rotate, cosine_table=cosine_table, sine_table=sine_table)
    unturn = jax.vjp(turn_back, empty_heads)[1]
    query_pre_grad = (
        unturn(query_blocks.reshape(group_rows, head_count, HD))[0]
        .astype(jnp.bfloat16)
        .reshape(group_rows, head_width)
    )
    key_pre_grad = unturn(key_acc)[0].astype(jnp.bfloat16).reshape(group_rows, head_width)
    value_grad = value_acc.astype(jnp.bfloat16).reshape(group_rows, head_width)
    grad_qkv_local = jnp.stack(
        [
            over_rows(normed, query_pre_grad),
            over_rows(normed, key_pre_grad),
            over_rows(normed, value_grad),
        ],
        axis=0,
    )
    normed_grad = (
        normed_grad
        + against_weight(query_pre_grad, qkv_all[0])
        + against_weight(key_pre_grad, qkv_all[1])
        + against_weight(value_grad, qkv_all[2])
    )
    share_grad = lax.psum(normed_grad.astype(jnp.bfloat16), "mp").astype(jnp.float32)
    seed_group = seed_rows.astype(jnp.float32)
    norm_pull = jax.vjp(norm_rows, x_group, ln_gain, ln_bias)[1]
    input_part, gain_part, shift_part = norm_pull(share_grad)
    input_group = seed_group + input_part
    grad_input = lax.dynamic_slice_in_dim(
        input_group, model_rank * local_rows, local_rows, 0
    ).astype(jnp.bfloat16)
    back_part = jnp.sum(seed_group, axis=0)
    grad_w_qkv, grad_w_out, grad_w_in, grad_b_in, grad_w_back, gain_rows, shift_rows, back_rows = (
        lax.psum_scatter(
            grad_qkv_local.astype(jnp.bfloat16), "dp", scatter_dimension=1, tiled=True
        ).astype(jnp.float32),
        lax.psum_scatter(
            grad_out_local.astype(jnp.bfloat16), "dp", scatter_dimension=1, tiled=True
        ).astype(jnp.float32),
        lax.psum_scatter(
            grad_in_local.astype(jnp.bfloat16), "dp", scatter_dimension=0, tiled=True
        ).astype(jnp.float32),
        lax.psum_scatter(
            grad_bias_in.astype(jnp.bfloat16), "dp", scatter_dimension=0, tiled=True
        ).astype(jnp.float32),
        lax.psum_scatter(
            grad_back_local.astype(jnp.bfloat16), "dp", scatter_dimension=1, tiled=True
        ).astype(jnp.float32),
        lax.psum_scatter(
            gain_part.astype(jnp.bfloat16), "dp", scatter_dimension=0, tiled=True
        ).astype(jnp.float32),
        lax.psum_scatter(
            shift_part.astype(jnp.bfloat16), "dp", scatter_dimension=0, tiled=True
        ).astype(jnp.float32),
        lax.psum_scatter(
            back_part.astype(jnp.bfloat16), "dp", scatter_dimension=0, tiled=True
        ).astype(jnp.float32),
    )
    piece_width = gain_rows.shape[0] // model_count
    grad_ln_gain = lax.dynamic_slice_in_dim(gain_rows, model_rank * piece_width, piece_width, 0)
    grad_ln_bias = lax.dynamic_slice_in_dim(shift_rows, model_rank * piece_width, piece_width, 0)
    grad_b_back = lax.dynamic_slice_in_dim(back_rows, model_rank * piece_width, piece_width, 0)
    return (
        block_out,
        grad_input,
        grad_ln_gain,
        grad_ln_bias,
        grad_w_qkv,
        grad_w_out,
        grad_w_in,
        grad_b_in,
        grad_w_back,
        grad_b_back,
    )


MESH = pl.DeviceIdType.MESH
NZ = 4
TILE = 256
N_HEADS = TILE // HD
NQ = 4
NJ = 4
NK = NQ + 2 * NJ
VROWS = 56


def fits_quad(mesh):
    return mesh.shape["mp"] == 2 and mesh.shape["dp"] == 4 * NZ


def dot_nn(a, b):
    return lax.dot_general(a, b, (((1,), (0,)), ((), ())), preferred_element_type=jnp.float32)


def dot_nt(a, b):
    return lax.dot_general(a, b, (((1,), (1,)), ((), ())), preferred_element_type=jnp.float32)


def dot_tn(a, b):
    return lax.dot_general(a, b, (((0,), (0,)), ((), ())), preferred_element_type=jnp.float32)


def layer_kernel(
    bucket_ref,
    counts_ref,
    x_ref,
    cot_ref,
    gain_ref,
    bias_ref,
    bback_ref,
    cos_ref,
    sin_ref,
    bin_ref,
    wqkv_ref,
    wot_ref,
    win_ref,
    wbt_ref,
    block_ref,
    gin_ref,
    gqkv_ref,
    got_ref,
    gi_ref,
    gbt_ref,
    lng_ref,
    lnb_ref,
    bbk_ref,
    gbin_ref,
    B,
    W,
    NS,
    CT,
    SN,
    BM,
    QR,
    KR,
    VR,
    R,
    SL,
    XV,
    CV,
    COSV,
    SINV,
    ins,
    OUT,
    DN,
    GP,
    GC,
    RZ,
    FS,
    YS,
    YR,
    XH,
    RSTD,
    EXSa,
    EXSb,
    EYSa,
    EYSb,
    EXRa,
    EXRb,
    EYRa,
    EYRb,
    EXS2a,
    EXS2b,
    EYS2a,
    EYS2b,
    EXR2a,
    EXR2b,
    EYR2a,
    EYR2b,
    V,
    VS,
    VRV,
    loc_sem,
    ays,
    ayr,
    azs,
    azr,
    acs,
    acr,
    gs,
    gr,
    rcs,
    rcr,
    rzs,
    rzr,
    rys,
    ryr,
    exs,
    exr,
    vs,
    vr,
):
    EXS = (EXSa, EXSb)
    EYS = (EYSa, EYSb)
    EXR = (EXRa, EXRb)
    EYR = (EYRa, EYRb)
    EXS2 = (EXS2a, EXS2b)
    EYS2 = (EYS2a, EYS2b)
    EXR2 = (EXR2a, EXR2b)
    EYR2 = (EYR2a, EYR2b)
    f32, bf16 = jnp.float32, jnp.bfloat16
    dp, x = lax.axis_index("dp"), lax.axis_index("mp")
    z = dp // 4
    y = lax.rem(dp // 2, 2)
    c = lax.rem(dp, 2)
    rows = x_ref.shape[0]
    width = x_ref.shape[1]
    dev_x = (dp, 1 - x)
    dev_y = (dp + 2 - 4 * y, x)
    dev_c = (dp + 1 - 2 * c, x)
    dev_r = (lax.rem(dp + 4, 4 * NZ), x)
    dev_l = (lax.rem(dp + 4 * NZ - 4, 4 * NZ), x)
    dev_z = [(lax.rem(dp + 4 * i, 4 * NZ), x) for i in (1, 2, 3)]
    NA, SA = NS.at[0], NS.at[1]
    m_own = 2 * y + x
    m_x = 2 * y + 1 - x
    m_y = 2 - 2 * y + x
    m_d = 3 - m_own

    def rcp(src, dst, ss, rs, dev):
        return pltpu.make_async_remote_copy(
            src_ref=src, dst_ref=dst, send_sem=ss, recv_sem=rs, device_id=dev, device_id_type=MESH
        )

    barrier = pltpu.get_barrier_semaphore()
    peers = [dev_x, dev_y, dev_c] + dev_z
    for peer in peers:
        pl.semaphore_signal(barrier, inc=1, device_id=peer, device_id_type=MESH)

    def wsrc(k, q):
        if k == NK:
            return None
        if k < 3:
            return wqkv_ref.at[k, :, pl.ds(pl.multiple_of(q * TILE, TILE), TILE)]
        if k == 3:
            return wot_ref.at[:, pl.ds(pl.multiple_of(q * TILE, TILE), TILE)]
        ref = win_ref if k % 2 == 0 else wbt_ref
        j = (k - NQ) // 2
        return ref.at[:, pl.ds(pl.multiple_of(q * (NJ * TILE) + j * TILE, TILE), TILE)]

    def wv(k):
        return B if isinstance(k, int) and k == NK else W.at[k]

    def own_copy(k):
        return pltpu.make_async_copy(wsrc(k, y), W.at[k, z, y, c], loc_sem.at[k])

    def y_copy(k):
        if k == NK:
            return rcp(B.at[z, y, c], B.at[z, y, c], ays.at[k], ayr.at[k], dev_y)
        return rcp(wsrc(k, 1 - y), W.at[k, z, y, c], ays.at[k], ayr.at[k], dev_y)

    def y_arrived(k):
        here = wv(k).at[z, 1 - y, c]
        rcp(here, here, ays.at[k], ayr.at[k], dev_y).wait_recv()

    def z_copy(k, way, s, e):
        block = wv(k).at[e, :, c]
        return rcp(
            block, block, azs.at[k, way, s], azr.at[k, way, s], dev_r if way == 0 else dev_l
        )

    def c_copy(k, e):
        block = wv(k).at[e, :, c]
        return rcp(block, block, acs.at[k, e], acr.at[k, e], dev_c)

    def ag_own(k, copied=True):
        if copied:
            pltpu.make_async_copy(
                W.at[k, z, y, c], W.at[k, z, y, c], loc_sem.at[k]
            ).wait()
        y_arrived(k)

        @pl.when(z < NZ - 1)
        def _():
            z_copy(k, 0, 0, z).start()

        @pl.when(z > 0)
        def _():
            z_copy(k, 1, 0, z).start()

        c_copy(k, z).start()

    def ag_step(k, s):
        @pl.when(z - 1 - s >= 0)
        def _():
            e = z - 1 - s
            z_copy(k, 0, s, e).wait_recv()
            if s < NZ - 2:

                @pl.when(z < NZ - 1)
                def _():
                    z_copy(k, 0, s + 1, e).start()

            c_copy(k, e).start()

        @pl.when(z + 1 + s <= NZ - 1)
        def _():
            e = z + 1 + s
            z_copy(k, 1, s, e).wait_recv()
            if s < NZ - 2:

                @pl.when(z > 0)
                def _():
                    z_copy(k, 1, s + 1, e).start()

            c_copy(k, e).start()

    def ag_done(k):
        for e in range(NZ):
            block = wv(k).at[e, :, 1 - c]
            rcp(block, block, acs.at[k, e], acr.at[k, e], dev_c).wait_recv()

    def ag_sent(k, copied=True):
        y_copy(k).wait_send() if isinstance(k, int) else None
        for s in range(NZ - 1):

            @pl.when((z < NZ - 1) & (z - s >= 0))
            def _():
                z_copy(k, 0, s, z - s).wait_send()

            @pl.when((z > 0) & (z + s <= NZ - 1))
            def _():
                z_copy(k, 1, s, z + s).wait_send()

        for e in range(NZ):
            c_copy(k, e).wait_send()

    order = [0, NK] + list(range(1, NK))
    turns = iter([t for t in range(NK + NZ) if not 8 <= t <= 11])

    def ag_turn():
        t = next(turns, None)
        if t is None:
            return
        for n in range(2) if t == 0 else (t + 1,):
            if n <= NK:
                ag_own(order[n], copied=order[n] != NK)
        for s in range(NZ - 1):
            if 0 <= t - 1 - s <= NK:
                ag_step(order[t - 1 - s], s)

    def late_turn(t):
        ag_own(t)
        for s in range(NZ - 1):
            ag_step(t - 2 - s, s)

    P0 = 80
    parts = (pl.ds(0, P0), pl.ds(P0, rows - P0))
    BUF = (NA, SA)

    def g_copy(t, p, way, m):
        block = BUF[t].at[m, parts[p]]
        i = (t * 2 + p) * 3 + way
        dev = (dev_x, dev_y)[way] if way < 2 else (dev_y, dev_x)[p]
        return rcp(block, block, gs.at[i], gr.at[i], dev)

    def g_send(t):
        g_copy(t, 0, 0, m_own).start()
        g_copy(t, 1, 1, m_own).start()
        g_copy(t, 1, 0, m_own).start()
        g_copy(t, 0, 1, m_own).start()

    def g_near(t):
        g_copy(t, 0, 0, m_x).wait_recv()
        g_copy(t, 1, 1, m_y).wait_recv()

    def g_forward(t):
        g_copy(t, 0, 2, m_x).start()
        g_copy(t, 1, 2, m_y).start()

    def g_rest(t):
        g_copy(t, 1, 0, m_x).wait_recv()
        g_copy(t, 0, 1, m_y).wait_recv()

    def g_far(t):
        g_copy(t, 0, 2, m_d).wait_recv()
        g_copy(t, 1, 2, m_d).wait_recv()

    def g_sent(t):
        for p in (0, 1):
            for way in (0, 1):
                g_copy(t, p, way, m_own).wait_send()
        g_copy(t, 0, 2, m_x).wait_send()
        g_copy(t, 1, 2, m_y).wait_send()

    def rs_c(k):
        return rcp(GP.at[k, :, :, 1 - c], GC.at[k], rcs.at[k], rcr.at[k], dev_c)

    def rs_z(k, way, e, slot):
        return rcp(
            GP.at[k, e, :, c],
            RZ.at[k, slot],
            rzs.at[k, e],
            rzr.at[k, slot],
            dev_r if way == 0 else dev_l,
        )

    def rs_begin(k):
        rs_c(k).wait_recv()
        for e in range(NZ):
            GP[k, e, :, c] = (GP[k, e, :, c].astype(f32) + GC[k, e].astype(f32)).astype(bf16)

        @pl.when(z == 0)
        def _():
            for e in range(NZ - 1, 0, -1):
                rs_z(k, 0, e, e).start()

        @pl.when(z == NZ - 1)
        def _():
            for e in range(NZ - 1):
                rs_z(k, 1, e, e if e < NZ - 2 else 4).start()

    def pass_on(k, way, e, slot):
        rs_z(k, way, e, e).wait_recv()
        GP[k, e, :, c] = (GP[k, e, :, c].astype(f32) + RZ[k, e].astype(f32)).astype(bf16)
        rs_z(k, way, e, slot).start()

    def rs_hop1(k):
        @pl.when(z == 1)
        def _():
            pass_on(k, 0, 3, 3)
            pass_on(k, 0, 2, 2)

        @pl.when(z == 2)
        def _():
            pass_on(k, 1, 0, 0)
            pass_on(k, 1, 1, 4)

    def rs_hop2(k):
        @pl.when(z == 2)
        def _():
            pass_on(k, 0, 3, 3)

        @pl.when(z == 1)
        def _():
            pass_on(k, 1, 0, 4)

    def rs_y(k):
        return rcp(YS.at[k], YR.at[k], rys.at[k], ryr.at[k], dev_y)

    def put(k, q, value):
        if k < 3:
            gqkv_ref[k, :, pl.ds(pl.multiple_of(q * TILE, TILE), TILE)] = value
        elif k == 3:
            got_ref[:, pl.ds(pl.multiple_of(q * TILE, TILE), TILE)] = value
        else:
            ref = gi_ref if k % 2 == 0 else gbt_ref
            j = (k - NQ) // 2
            ref[:, pl.ds(pl.multiple_of(q * (NJ * TILE) + j * TILE, TILE), TILE)] = value

    def rs_final(k):
        FS[...] = GP[k, z, :, c].astype(f32)

        @pl.when(z > 0)
        def _():
            rs_z(k, 0, z, z).wait_recv()
            FS[...] += RZ[k, z].astype(f32)

        @pl.when(z < NZ - 1)
        def _():
            rs_z(k, 1, z, 4).wait_recv()
            FS[...] += RZ[k, 4].astype(f32)

        YS[k] = FS[1 - y].astype(bf16)
        rs_y(k).start()
        put(k, y, FS[y])

    def rs_out(k):
        rs_y(k).wait_recv()
        put(k, 1 - y, YR[k].astype(f32))

    rturns = iter(range(NK + 2))
    rorder = [NQ + 1] + [k for k in range(NK) if k != NQ + 1]

    def rs_turn():
        r = next(rturns, None)
        if r is None:
            return
        for s, f in enumerate((rs_hop1, rs_hop2, rs_final)):
            if 0 <= r - s < NK:
                f(rorder[r - s])

    def rs_sent(k):
        rs_c(k).wait_send()
        for e in range(NZ):

            @pl.when(z != e)
            def _():
                rs_z(k, 0, e, e).wait_send()

        rs_y(k).wait_send()

    def e_copy(t, u, i):
        src, dst, dev = (
            (EXS, EXR, dev_x),
            (EYS, EYR, dev_y),
            (EXS2, EXR2, dev_x),
            (EYS2, EYR2, dev_y),
        )[i]
        src, dst = src[u], dst[u]
        return rcp(src.at[t], dst.at[t], exs.at[t, u, i], exr.at[t, u, i], dev)

    wide = (384, 256)
    thin = (2 * 128, 128)

    def cols(u, half):
        if half == 0:
            return pl.ds(u * wide[0], wide[u])
        return pl.ds(sum(wide) + u * thin[0], thin[u])

    def e_first_x(t, u, P):
        for i in range(2):
            EXS[u][t, i] = P[2 * i + 1 - x, :, cols(u, 0)].astype(bf16)
        e_copy(t, u, 0).start()

    def e_first_y(t, u, P):
        for i in range(2):
            EYS[u][t, i] = P[2 - 2 * y + i, :, cols(u, 1)].astype(bf16)
        e_copy(t, u, 1).start()

    def e_first(t, u, P):
        e_first_x(t, u, P)
        e_first_y(t, u, P)

    def e_second(t, u, P):
        e_copy(t, u, 0).wait_recv()
        EYS2[u][t] = (P[m_y, :, cols(u, 0)] + EXR[u][t, 1 - y].astype(f32)).astype(bf16)
        e_copy(t, u, 3).start()
        e_copy(t, u, 1).wait_recv()
        EXS2[u][t] = (P[m_x, :, cols(u, 1)] + EYR[u][t, 1 - x].astype(f32)).astype(bf16)
        e_copy(t, u, 2).start()

    def e_last(t, u, P):
        e_copy(t, u, 3).wait_recv()
        P[m_own, :, cols(u, 0)] += EXR[u][t, y].astype(f32) + EYR2[u][t].astype(f32)
        e_copy(t, u, 2).wait_recv()
        P[m_own, :, cols(u, 1)] += EYR[u][t, x].astype(f32) + EXR2[u][t].astype(f32)

    def e_sent(t):
        for u in range(2):
            for i in range(4):
                e_copy(t, u, i).wait_send()

    inputs = [
        pltpu.make_async_copy(src, dst, ins.at[i])
        for i, (src, dst) in enumerate(
            ((x_ref, XV), (cot_ref, CV), (cos_ref, COSV), (sin_ref, SINV))
        )
    ]
    for copy in inputs:
        copy.start()
    for k in range(NK):
        own_copy(k).start()
    inputs[0].wait()
    xf = XV[...].astype(f32)
    centred = xf - jnp.mean(xf, axis=-1, keepdims=True)
    rstd = lax.rsqrt(jnp.mean(centred * centred, axis=-1, keepdims=True) + NORM_EPS)
    xhat = centred * rstd
    XH[...] = xhat
    RSTD[...] = jnp.broadcast_to(rstd, RSTD.shape)
    NA[m_own] = (xhat * gain_ref[...] + bias_ref[...]).astype(bf16)

    bucket = bucket_ref[0]
    B[z, y, c, 0:8] = jnp.broadcast_to(bin_ref[...].astype(f32), (8, 128)).astype(bf16)
    B[z, y, c, 8:16] = jnp.full((8, 128), bucket.astype(f32), f32).astype(bf16)

    slot = lax.shift_right_logical(jnp.int32(rows), bucket)
    shift_of = (rows.bit_length() - 1) - bucket
    row = x * rows + lax.broadcasted_iota(jnp.int32, (rows, 128), 0)
    slot_of = lax.shift_right_logical(row, jnp.full(row.shape, shift_of, jnp.int32))
    place = row & jnp.full(row.shape, slot - 1, jnp.int32)
    limit = jnp.zeros((rows, 128), jnp.int32)
    for s in range(SLOTS):
        limit = jnp.where(slot_of == s, counts_ref[s], limit)
    valid = jnp.where(place < limit, 1.0, 0.0)[:, 0:1]
    inputs[1].wait()
    seeds = CV[...].astype(f32) * valid
    SA[m_own] = seeds.astype(bf16)
    back_sum = jnp.sum(seeds, axis=0, keepdims=True)
    V[...] = jnp.zeros_like(V)
    for i in range(8):
        V[16 + i : 17 + i, :] = back_sum[:, i * 128 : (i + 1) * 128]
    pl.semaphore_wait(barrier, len(peers))
    for k in order:
        y_copy(k).start()
    g_send(0)
    g_send(1)
    ag_turn()
    ag_turn()

    lane = lax.broadcasted_iota(jnp.int32, (rows, TILE), 1)
    even = (lane & 1) == 0

    def table(g):
        brow = B[z, g, c].astype(f32)[8:9, :]
        ba = jnp.broadcast_to(brow, (rows, 128))

        def pick(ref):
            full = ref[...]
            out = full
            for b in range(1, 4):
                n = rows >> b
                out = jnp.where(ba == float(b), jnp.concatenate([full[:n]] * (1 << b), axis=0), out)
            return out

        cg, sg = pick(COSV), pick(SINV)
        CT[g] = jnp.concatenate([cg, cg], axis=1)
        SN[g] = jnp.concatenate([sg, sg], axis=1)
        size = jnp.full((rows, 128), rows, jnp.int32)
        for b in range(1, 4):
            size = jnp.where(ba == float(b), rows >> b, size)
        size = jnp.concatenate([size, size], axis=1)
        qi = lax.broadcasted_iota(jnp.int32, (rows, rows), 0)
        ki = lax.broadcasted_iota(jnp.int32, (rows, rows), 1)
        BM[g] = jnp.where((ki <= qi) & ((qi ^ ki) < size), 0.0, MASKED_SCORE)

    def tables():
        for g in range(2):
            table(g)

    def turn(v, g, sign):
        other = jnp.where(even, -pltpu.roll(v, TILE - 1, 1), pltpu.roll(v, 1, 1))
        return v * CT[g] + (sign * other) * SN[g]

    def weight(k):
        return W[k].reshape(width, TILE)

    scale = HD ** (-0.5)

    def project(m):
        g = m // 2
        nb = NA[m]
        QR[m] = turn(dot_nn(nb, weight(0)), g, 1.0).astype(bf16)
        KR[m] = turn(dot_nn(nb, weight(1)), g, 1.0).astype(bf16)
        VR[m] = dot_nn(nb, weight(2)).astype(bf16)

    def attend(m):
        g = m // 2
        q, kk, v = QR[m], KR[m], VR[m]
        da = dot_nn(SA[m], weight(3)).astype(bf16)
        zero = jnp.zeros((rows, TILE), bf16)
        ps, ss, qs, ks, vs_, ds = [], [], [], [], [], []
        for h in range(N_HEADS):
            mine = (lane // HD) == h
            qh, kh, vh, dh = (jnp.where(mine, t, zero) for t in (q, kk, v, da))
            s = dot_nt(qh, kk) * scale + BM[g]
            e = jnp.exp(s - jnp.max(s, axis=-1, keepdims=True))
            p = e * (1.0 / jnp.sum(e, axis=-1, keepdims=True))
            pg = dot_nt(dh, v)
            sg = p * (pg - jnp.sum(p * pg, axis=-1, keepdims=True))
            for held, t in ((ps, p), (ss, sg), (qs, qh), (ks, kh), (vs_, vh), (ds, dh)):
                held.append(t.astype(bf16))
        wide_p, wide_s = jnp.concatenate(ps, axis=1), jnp.concatenate(ss, axis=1)
        att = dot_nn(wide_p, jnp.concatenate(vs_, axis=0))
        dq = dot_nn(wide_s, jnp.concatenate(ks, axis=0))
        dk = dot_tn(jnp.concatenate(ss, axis=0), jnp.concatenate(qs, axis=0))
        dv = dot_tn(jnp.concatenate(ps, axis=0), jnp.concatenate(ds, axis=0))
        at = att.astype(bf16)
        dqb = turn(dq * scale, g, -1.0).astype(bf16)
        dkb = turn(dk * scale, g, -1.0).astype(bf16)
        dvb = dv.astype(bf16)
        rs = pl.ds(pl.multiple_of(m * rows, rows), rows)
        R[3, rs, :] = at
        R[0, rs, :] = dqb
        R[1, rs, :] = dkb
        R[2, rs, :] = dvb
        OUT[m] = dot_nt(at, weight(3))
        DN[m] = dot_nt(dqb, weight(0)) + dot_nt(dkb, weight(1)) + dot_nt(dvb, weight(2))

    def grad_of(k, left):
        total = dot_tn(NS[left].reshape(4 * rows, width), R[k])
        GP[k] = total.astype(bf16).reshape(NZ, 2, 2, 64, TILE)
        rs_c(k).start()

    def slice_of(j):
        return NQ + 2 * j, NQ + 1 + 2 * j

    def all_rows(ref):
        return ref[...].reshape(4 * rows, width)

    def feed(j):
        ki, kb = slice_of(j)
        b0 = B[2 * y + lax.div(j, 2), lax.rem(j, 2), 0].astype(f32)[0:1, :]
        b1 = B[2 * y + lax.div(j, 2), lax.rem(j, 2), 1].astype(f32)[0:1, :]
        u = dot_nn(all_rows(NA), weight(ki)) + jnp.concatenate([b0, b1], axis=1)
        u2 = u * u
        k0 = float(np.sqrt(2.0 / np.pi))
        t = jnp.tanh(k0 * u * (1.0 + 0.044715 * u2))
        R[kb] = (0.5 * u * (1.0 + t)).astype(bf16)
        SL[...] = 0.5 * (1.0 + t) + (0.5 * k0) * u * (1.0 - t * t) * (1.0 + 0.134145 * u2)

    def feed_back(j):
        ki, kb = slice_of(j)
        hg = (dot_nn(all_rows(SA), weight(kb)) * SL[...]).astype(bf16)
        R[ki] = hg
        OUT[...] += dot_nt(R[kb], weight(kb)).reshape(4, rows, width)
        DN[...] += dot_nt(hg, weight(ki)).reshape(4, rows, width)
        at = 24 + x * 16 + y * 8 + 2 * j
        total = jnp.sum(hg.astype(f32), axis=0, keepdims=True)
        V[pl.ds(at, 1), :] = total[:, :128]
        V[pl.ds(at + 1, 1), :] = total[:, 128:]

    def feed_grads(j):
        lax.fori_loop(0, 2, lambda i, _: (grad_of(NQ + 2 * j + i, i), 0)[1], 0)

    def v_copy(i, dev):
        return rcp(VS.at[min(i, 3)], VRV.at[i], vs.at[i], vr.at[i], dev)

    v_devs = (dev_c, dev_x, dev_y)

    def v_step(i):
        v_copy(i, v_devs[i]).wait_recv()
        VS[i + 1] = VS[i] + VRV[i]
        if i < 2:
            v_copy(i + 1, v_devs[i + 1]).start()
        else:
            for n, dev in enumerate(dev_z):
                v_copy(3 + n, dev).start()

    def arrived(*chunks):
        for k in chunks:
            ag_done(k)

    ag_turn()
    inputs[2].wait()
    inputs[3].wait()
    tables()
    ag_turn()
    ag_turn()
    ag_turn()
    g_near(0)
    g_forward(0)
    ag_turn()
    arrived(0, NK, 1, 2)
    g_rest(0)
    def near(i):
        ix, iy = lax.rem(i, 2), lax.div(i, 2)
        return 2 * (y + iy - 2 * y * iy) + x + ix - 2 * x * ix

    lax.fori_loop(0, 3, lambda i, _: (project(near(i)), 0)[1], 0)
    ag_turn()
    arrived(3)

    def rows_turn(i, _):
        @pl.when(i == 1)
        def _():
            g_near(1)
            g_forward(1)
            g_rest(1)

        @pl.when(i == 3)
        def _():
            g_far(1)
            grad_of(NQ + 1, 1)
            project(m_d)
            rs_begin(NQ + 1)

        attend(near(i))

        @pl.when(i == 2)
        def _():
            g_far(0)
            arrived(NQ)
            feed(0)

        @pl.when(i < 3)
        def _():
            late_turn(8 + i)

        return 0

    lax.fori_loop(0, 4, rows_turn, 0)

    def head_grads(k, _):
        grad_of(k, lax.div(k, 3))

        @pl.when(k == 1)
        def _():
            late_turn(11)

        @pl.when(k > 0)
        def _():
            rs_begin(k - 1)

        return 0

    lax.fori_loop(0, NQ, head_grads, 0)
    ag_turn()

    def slices(j, _):
        @pl.when(j > 0)
        def _():
            arrived(NQ + 2 * j)
            feed(j)

        arrived(NQ + 1 + 2 * j)
        feed_back(j)

        @pl.when(j == 0)
        def _():
            rs_begin(3)
            ag_turn()
            rs_turn()

        @pl.when(j == 1)
        def _():
            ag_turn()
            rs_turn()

        @pl.when(j == 2)
        def _():
            ag_turn()
            rs_turn()

        return 0

    lax.fori_loop(0, NJ, slices, 0)

    for u in range(2):
        e_first(1, u, DN)
    grad_of(NQ, 0)
    rs_turn()
    rs_begin(NQ)
    feed_grads(1)
    rs_begin(6)
    rs_begin(7)
    rs_turn()
    feed_grads(2)
    rs_begin(8)
    rs_begin(9)
    rs_turn()
    e_second(1, 0, DN)
    feed_grads(3)
    rs_begin(10)
    rs_begin(11)
    rs_turn()
    e_second(1, 1, DN)
    e_first(0, 0, OUT)
    e_first_y(0, 1, OUT)
    rs_turn()
    rs_turn()
    for u in range(2):
        e_last(1, u, DN)
    dn = DN[m_own]
    xhat = XH[...]
    gsum = jnp.sum(dn * xhat, axis=0, keepdims=True)
    bsum = jnp.sum(dn, axis=0, keepdims=True)
    for i in range(8):
        V[i : i + 1, :] = gsum[:, i * 128 : (i + 1) * 128]
        V[8 + i : 9 + i, :] = bsum[:, i * 128 : (i + 1) * 128]
    VS[0] = V[...]
    v_copy(0, dev_c).start()
    e = dn * gain_ref[...]
    me = jnp.mean(e, axis=-1, keepdims=True)
    mex = jnp.mean(e * xhat, axis=-1, keepdims=True)
    gin_ref[...] = (SA[m_own].astype(f32) + RSTD[:, 0:1] * (e - me - xhat * mex)).astype(bf16)
    v_step(0)
    rs_turn()
    e_first_x(0, 1, OUT)
    rs_turn()
    v_step(1)
    e_second(0, 0, OUT)
    rs_turn()
    v_step(2)
    rs_turn()
    e_second(0, 1, OUT)
    for k in rorder[:9]:
        rs_out(k)
    rs_turn()
    rs_out(rorder[9])
    for k in rorder[10:]:
        rs_out(k)
    for i in range(3):
        v_copy(3 + i, dev_z[i]).wait_recv()
    V[...] = VS[3] + VRV[3] + VRV[4] + VRV[5]
    index = 2 * dp + x
    lane4 = lax.rem(index, 4)
    for base, ref in ((0, lng_ref), (8, lnb_ref), (16, bbk_ref)):
        line = V[pl.ds(base + index // 4, 1), :]
        out = line[:, 0:32]
        for n in range(1, 4):
            out = jnp.where(lane4 == n, line[:, 32 * n : 32 * n + 32], out)
        ref[...] = out
    gbin_ref[...] = V[pl.ds(24 + 16 * x + dp, 1), :]
    for u in range(2):
        e_last(0, u, OUT)
    block_ref[...] = (XV[...].astype(f32) + OUT[m_own] + bback_ref[...]).astype(bf16)

    def later(f):
        lax.fori_loop(0, NK, lambda k, _: (f(k), 0)[1], 0)

    for k in range(NK + 1):
        ag_sent(k)
    for t in range(2):
        g_sent(t)
        e_sent(t)
    later(rs_sent)
    for i, dev in enumerate([dev_c, dev_x, dev_y] + dev_z):
        v_copy(i, dev).wait_send()


def write_kernel(*refs):
    srcs, dsts, sems = refs[:10], refs[10:20], refs[20]
    copies = [pltpu.make_async_copy(a, b, sems.at[i]) for i, (a, b) in enumerate(zip(srcs, dsts))]
    for copy in copies:
        copy.start()
    for copy in copies:
        copy.wait()


def rope_constants(rows):
    half = np.arange(ROT // 2, dtype=np.float32)
    rates = (10000.0 ** (-2.0 * half / ROT)).astype(np.float32)
    angle = np.arange(rows, dtype=np.float32)[:, None] * rates[None, :]
    angle = np.repeat(angle, 2, axis=1)
    cos = np.concatenate([np.cos(angle), np.ones((rows, HD - ROT))], axis=1)
    sin = np.concatenate([np.sin(angle), np.zeros((rows, HD - ROT))], axis=1)
    two = lambda t: np.concatenate([t, t], axis=1).astype(np.float32)
    return two(cos), two(sin)


def on_quad(
    residual_in,
    cotangent,
    ln_gain,
    ln_bias,
    w_qkv,
    w_out,
    w_in,
    b_in,
    w_back,
    b_back,
    bucket_ids,
    residue_counts,
):
    rows, width = residual_in.shape
    cos, sin = rope_constants(rows)
    f32, bf16 = jnp.float32, jnp.bfloat16
    vm = pl.BlockSpec(memory_space=pltpu.VMEM)
    sm = pl.BlockSpec(memory_space=pltpu.SMEM)
    anyspace = pl.BlockSpec(memory_space=pl.ANY)
    shard = width // (4 * NZ)
    sem = pltpu.SemaphoreType.DMA
    shapes = (
        jax.ShapeDtypeStruct((rows, width), bf16),
        jax.ShapeDtypeStruct((rows, width), bf16),
        jax.ShapeDtypeStruct((3, shard, 2 * TILE), f32),
        jax.ShapeDtypeStruct((shard, 2 * TILE), f32),
        jax.ShapeDtypeStruct((shard, 2 * NJ * TILE), f32),
        jax.ShapeDtypeStruct((shard, 2 * NJ * TILE), f32),
        jax.ShapeDtypeStruct((1, 32), f32),
        jax.ShapeDtypeStruct((1, 32), f32),
        jax.ShapeDtypeStruct((1, 32), f32),
        jax.ShapeDtypeStruct((1, 128), f32),
    )
    held = pl.pallas_call(
        layer_kernel,
        out_shape=tuple(pltpu.VMEM(v.shape, v.dtype) for v in shapes),
        in_specs=[sm, sm, anyspace, anyspace] + [vm] * 3 + [anyspace] * 2 + [vm] + [anyspace] * 4,
        out_specs=(vm,) * 10,
        scratch_shapes=[
            pltpu.VMEM((NZ, 2, 2, 16, 128), bf16),
            pltpu.VMEM((NK, NZ, 2, 2, shard, TILE), bf16),
            pltpu.VMEM((2, 4, rows, width), bf16),
            pltpu.VMEM((2, rows, TILE), f32),
            pltpu.VMEM((2, rows, TILE), f32),
            pltpu.VMEM((2, rows, rows), f32),
            pltpu.VMEM((4, rows, TILE), bf16),
            pltpu.VMEM((4, rows, TILE), bf16),
            pltpu.VMEM((4, rows, TILE), bf16),
            pltpu.VMEM((NK, 4 * rows, TILE), bf16),
            pltpu.VMEM((4 * rows, TILE), f32),
            pltpu.VMEM((rows, width), bf16),
            pltpu.VMEM((rows, width), bf16),
            pltpu.VMEM((rows, 128), f32),
            pltpu.VMEM((rows, 128), f32),
            sem((4,)),
            pltpu.VMEM((4, rows, width), f32),
            pltpu.VMEM((4, rows, width), f32),
            pltpu.VMEM((NK, NZ, 2, 2, shard, TILE), bf16),
            pltpu.VMEM((NK, NZ, 2, shard, TILE), bf16),
            pltpu.VMEM((NK, 5, 2, shard, TILE), bf16),
            pltpu.VMEM((2, shard, TILE), f32),
            pltpu.VMEM((NK, shard, TILE), bf16),
            pltpu.VMEM((NK, shard, TILE), bf16),
            pltpu.VMEM((rows, width), f32),
            pltpu.VMEM((rows, 128), f32),
            pltpu.VMEM((2, 2, rows, 384), bf16),
            pltpu.VMEM((2, 2, rows, 256), bf16),
            pltpu.VMEM((2, 2, rows, 256), bf16),
            pltpu.VMEM((2, 2, rows, 128), bf16),
            pltpu.VMEM((2, 2, rows, 384), bf16),
            pltpu.VMEM((2, 2, rows, 256), bf16),
            pltpu.VMEM((2, 2, rows, 256), bf16),
            pltpu.VMEM((2, 2, rows, 128), bf16),
            pltpu.VMEM((2, rows, 256), bf16),
            pltpu.VMEM((2, rows, 128), bf16),
            pltpu.VMEM((2, rows, 384), bf16),
            pltpu.VMEM((2, rows, 256), bf16),
            pltpu.VMEM((2, rows, 256), bf16),
            pltpu.VMEM((2, rows, 128), bf16),
            pltpu.VMEM((2, rows, 384), bf16),
            pltpu.VMEM((2, rows, 256), bf16),
            pltpu.VMEM((VROWS, 128), f32),
            pltpu.VMEM((4, VROWS, 128), f32),
            pltpu.VMEM((6, VROWS, 128), f32),
            sem((NK,)),
            sem((NK + 1,)),
            sem((NK + 1,)),
            sem((NK + 1, 2, 3)),
            sem((NK + 1, 2, 3)),
            sem((NK + 1, NZ)),
            sem((NK + 1, NZ)),
            sem((12,)),
            sem((12,)),
            sem((NK,)),
            sem((NK,)),
            sem((NK, NZ)),
            sem((NK, 5)),
            sem((NK,)),
            sem((NK,)),
            sem((2, 2, 4)),
            sem((2, 2, 4)),
            sem((6,)),
            sem((6,)),
        ],
        compiler_params=pltpu.CompilerParams(
            collective_id=0, has_side_effects=True, vmem_limit_bytes=58 << 20
        ),
        cost_estimate=pl.CostEstimate(
            flops=20 * 2**30, bytes_accessed=8 * 2**20, transcendentals=2**21
        ),
    )(
        bucket_ids,
        residue_counts.reshape(SLOTS),
        residual_in,
        cotangent,
        ln_gain.reshape(1, width),
        ln_bias.reshape(1, width),
        b_back.reshape(1, width),
        jnp.asarray(cos),
        jnp.asarray(sin),
        b_in.reshape(1, 128),
        w_qkv,
        w_out.T,
        w_in,
        w_back.T,
    )
    held = [pltpu.with_memory_space_constraint(v, pltpu.VMEM) for v in held]
    outs = pl.pallas_call(
        write_kernel,
        out_shape=shapes,
        in_specs=[vm] * 10,
        out_specs=(anyspace,) * 10,
        scratch_shapes=[sem((10,))],
    )(*held)
    block_out, grad_input, grad_w_qkv, gwo, grad_w_in, gwb, lng, lnb, bbk, gbin = outs
    return (
        block_out,
        grad_input,
        lng.reshape(32),
        lnb.reshape(32),
        grad_w_qkv,
        gwo.T,
        grad_w_in,
        gbin.reshape(128),
        gwb.T,
        bbk.reshape(32),
    )


def solution(mesh):
    placed = (
        P(("dp", "mp"), None),
        P(("dp", "mp"), None),
        P(),
        P(),
        P(None, "dp", "mp"),
        P("mp", "dp"),
        P("dp", "mp"),
        P(("mp", "dp")),
        P("mp", "dp"),
        P(),
        P("dp"),
        P("dp", None),
    )
    return jax.shard_map(
        on_quad if fits_quad(mesh) else on_device,
        mesh=mesh,
        in_specs=placed,
        out_specs=(
            P(("dp", "mp"), None),
            P(("dp", "mp"), None),
            P(("dp", "mp")),
            P(("dp", "mp")),
            P(None, "dp", "mp"),
            P("mp", "dp"),
            P("dp", "mp"),
            P(("mp", "dp")),
            P("mp", "dp"),
            P(("dp", "mp")),
        ),
        check_vma=False,
    )
```

```python
from functools import partial

import jax
import jax.numpy as jnp
import numpy as np
from jax import lax
from jax.experimental import pallas as pl
from jax.experimental.pallas import tpu as pltpu
from jax.sharding import PartitionSpec as P

HD = 64
ROT = 32
SLOTS = 16


NORM_EPS = 1e-05
MASKED_SCORE = -1e30


def norm_rows(inputs_now, norm_gain, norm_shift):
    centred = inputs_now - jnp.mean(inputs_now, axis=-1, keepdims=True)
    spread = jnp.mean(centred * centred, axis=-1, keepdims=True)
    return centred * lax.rsqrt(spread + NORM_EPS) * norm_gain + norm_shift


def slot_tables(bucket_one, residue_row, group_rows):
    slot_length = jnp.right_shift(jnp.int32(group_rows // 2), bucket_one)
    places = jnp.arange(group_rows, dtype=jnp.int32)
    slot_ids = places // slot_length
    inside = places - slot_ids * slot_length
    match_table = slot_ids[:, None] == jnp.arange(SLOTS, dtype=jnp.int32)[None, :]
    picked = jnp.sum(jnp.where(match_table, residue_row[None, :], 0), axis=1)
    live_rows = jnp.minimum(picked, slot_length)
    return (slot_ids, inside, inside < live_rows)


def rope_tables(inside):
    half_steps = jnp.arange(ROT // 2, dtype=jnp.float32)
    inverse_rates = 10000.0 ** (-2.0 * half_steps / ROT)
    angles = inside.astype(jnp.float32)[:, None] * inverse_rates[None, :]
    return (jnp.cos(angles), jnp.sin(angles))


def rotate(values, cosine_table, sine_table):
    row_count = values.shape[0]
    head_count = values.shape[1]
    paired = values[..., :ROT].reshape(row_count, head_count, ROT // 2, 2)
    even_part = paired[..., 0]
    odd_part = paired[..., 1]
    cosine_now = cosine_table[:, None, :]
    sine_now = sine_table[:, None, :]
    turned = jnp.stack(
        [
            even_part * cosine_now - odd_part * sine_now,
            odd_part * cosine_now + even_part * sine_now,
        ],
        axis=-1,
    )
    return jnp.concatenate([turned.reshape(row_count, head_count, ROT), values[..., ROT:]], axis=-1)


def mask_block(block_start, block_rows, slot_ids):
    query_places = block_start + jnp.arange(block_rows, dtype=jnp.int32)
    query_slots = lax.dynamic_slice_in_dim(slot_ids, block_start, block_rows, 0)
    key_places = jnp.arange(slot_ids.shape[0], dtype=jnp.int32)
    return (query_slots[:, None] == slot_ids[None, :]) & (
        key_places[None, :] <= query_places[:, None]
    )


def over_rows(first_op, second_op):
    return lax.dot_general(
        first_op, second_op, (((0,), (0,)), ((), ())), preferred_element_type=jnp.float32
    )


def against_weight(first_op, second_op):
    return lax.dot_general(
        first_op, second_op, (((1,), (1,)), ((), ())), preferred_element_type=jnp.float32
    )


def on_device(
    residual_in,
    cotangent,
    ln_gain,
    ln_bias,
    w_qkv,
    w_out,
    w_in,
    b_in,
    w_back,
    b_back,
    bucket_ids,
    residue_counts,
):
    model_count = lax.axis_size("mp")
    model_rank = lax.axis_index("mp")
    local_rows = residual_in.shape[0]
    group_rows = local_rows * model_count
    slot_ids, inside, valid_rows = slot_tables(bucket_ids[0], residue_counts[0], group_rows)
    cosine_table, sine_table = rope_tables(inside)
    qkv_all, out_all, in_all, bias_in, back_all = (
        lax.all_gather(w_qkv, "dp", axis=1, tiled=True),
        lax.all_gather(w_out, "dp", axis=1, tiled=True),
        lax.all_gather(w_in, "dp", axis=0, tiled=True),
        lax.all_gather(b_in, "dp", axis=0, tiled=True),
        lax.all_gather(w_back, "dp", axis=1, tiled=True),
    )
    x_local = residual_in.astype(jnp.float32)
    x_group = lax.all_gather(residual_in, "mp", axis=0, tiled=True).astype(jnp.float32)
    normed = norm_rows(x_group, ln_gain, ln_bias).astype(jnp.bfloat16)
    head_width = qkv_all.shape[2]
    head_count = head_width // HD
    score_scale = HD ** (-0.5)

    def project(member_index):
        return jnp.dot(normed, qkv_all[member_index], preferred_element_type=jnp.float32).reshape(
            group_rows, head_count, HD
        )

    queries = rotate(project(0), cosine_table, sine_table).astype(jnp.bfloat16)
    key_rows = rotate(project(1), cosine_table, sine_table).astype(jnp.bfloat16)
    value_rows = project(2).astype(jnp.bfloat16)
    block_rows = min(512, group_rows)
    starts = jnp.arange(group_rows // block_rows, dtype=jnp.int32) * block_rows

    def block_scores(block_start):
        query_block = lax.dynamic_slice_in_dim(queries, block_start, block_rows, 0)
        allowed = mask_block(block_start, block_rows, slot_ids)
        scores = (
            jnp.einsum("qhd,khd->hqk", query_block, key_rows, preferred_element_type=jnp.float32)
            * score_scale
        )
        return (query_block, jnp.where(allowed[None], scores, MASKED_SCORE))

    def forward_block(block_start):
        query_block, scores = block_scores(block_start)
        row_peak = jnp.max(scores, axis=-1, keepdims=True)
        exp_scores = jnp.exp(scores - row_peak)
        row_total = jnp.sum(exp_scores, axis=-1, keepdims=True)
        weights_now = (exp_scores / row_total).astype(jnp.bfloat16)
        attended = jnp.einsum(
            "hqk,khd->qhd", weights_now, value_rows, preferred_element_type=jnp.float32
        )
        return (attended.astype(jnp.bfloat16), (row_peak + jnp.log(row_total))[..., 0])

    attended_blocks, log_totals = lax.map(forward_block, starts)
    mixed_rows = attended_blocks.reshape(group_rows, head_width)
    hidden = jnp.dot(normed, in_all, preferred_element_type=jnp.float32) + bias_in.astype(
        jnp.float32
    )
    gelu_tanh = partial(jax.nn.gelu, approximate=True)
    active_value, gelu_pull = jax.vjp(gelu_tanh, hidden)
    active = active_value.astype(jnp.bfloat16)
    partial_out = jnp.dot(mixed_rows, out_all, preferred_element_type=jnp.float32) + jnp.dot(
        active, back_all, preferred_element_type=jnp.float32
    )
    summed_all = lax.psum(partial_out.astype(jnp.bfloat16), "mp").astype(jnp.float32)
    summed = lax.dynamic_slice_in_dim(summed_all, model_rank * local_rows, local_rows, 0)
    block_out = (x_local + summed + b_back).astype(jnp.bfloat16)
    cot_group = lax.all_gather(cotangent, "mp", axis=0, tiled=True)
    seed_rows = jnp.where(valid_rows[:, None], cot_group, jnp.zeros_like(cot_group))
    qkv_all, out_all, in_all, back_all = (
        lax.all_gather(w_qkv, "dp", axis=1, tiled=True),
        lax.all_gather(w_out, "dp", axis=1, tiled=True),
        lax.all_gather(w_in, "dp", axis=0, tiled=True),
        lax.all_gather(w_back, "dp", axis=1, tiled=True),
    )
    active_grad = against_weight(seed_rows, back_all)
    hidden_grad = gelu_pull(active_grad)[0].astype(jnp.bfloat16)
    grad_in_local = over_rows(normed, hidden_grad)
    grad_bias_in = jnp.sum(hidden_grad.astype(jnp.float32), axis=0)
    grad_back_local = over_rows(active, seed_rows)
    grad_out_local = over_rows(mixed_rows, seed_rows)
    normed_grad = against_weight(hidden_grad, in_all)
    mixed_grad = (
        against_weight(seed_rows, out_all).astype(jnp.bfloat16).reshape(group_rows, head_count, HD)
    )

    def backward_block(carry, inputs_now):
        key_acc, value_acc = carry
        block_start, log_total = inputs_now
        query_block, scores = block_scores(block_start)
        grad_block = lax.dynamic_slice_in_dim(mixed_grad, block_start, block_rows, 0)
        probs = jnp.exp(scores - log_total[..., None])
        probs_low = probs.astype(jnp.bfloat16)
        value_acc = value_acc + jnp.einsum(
            "hqk,qhd->khd", probs_low, grad_block, preferred_element_type=jnp.float32
        )
        probs_grad = jnp.einsum(
            "qhd,khd->hqk", grad_block, value_rows, preferred_element_type=jnp.float32
        )
        score_grad = probs * (probs_grad - jnp.sum(probs * probs_grad, axis=-1, keepdims=True))
        score_low = score_grad.astype(jnp.bfloat16)
        query_grad = (
            jnp.einsum("hqk,khd->qhd", score_low, key_rows, preferred_element_type=jnp.float32)
            * score_scale
        )
        key_acc = (
            key_acc
            + jnp.einsum("hqk,qhd->khd", score_low, query_block, preferred_element_type=jnp.float32)
            * score_scale
        )
        return ((key_acc, value_acc), query_grad)

    empty_heads = jnp.zeros((group_rows, head_count, HD), jnp.float32)
    (key_acc, value_acc), query_blocks = lax.scan(
        backward_block, (empty_heads, empty_heads), (starts, log_totals)
    )
    turn_back = partial(rotate, cosine_table=cosine_table, sine_table=sine_table)
    unturn = jax.vjp(turn_back, empty_heads)[1]
    query_pre_grad = (
        unturn(query_blocks.reshape(group_rows, head_count, HD))[0]
        .astype(jnp.bfloat16)
        .reshape(group_rows, head_width)
    )
    key_pre_grad = unturn(key_acc)[0].astype(jnp.bfloat16).reshape(group_rows, head_width)
    value_grad = value_acc.astype(jnp.bfloat16).reshape(group_rows, head_width)
    grad_qkv_local = jnp.stack(
        [
            over_rows(normed, query_pre_grad),
            over_rows(normed, key_pre_grad),
            over_rows(normed, value_grad),
        ],
        axis=0,
    )
    normed_grad = (
        normed_grad
        + against_weight(query_pre_grad, qkv_all[0])
        + against_weight(key_pre_grad, qkv_all[1])
        + against_weight(value_grad, qkv_all[2])
    )
    share_grad = lax.psum(normed_grad.astype(jnp.bfloat16), "mp").astype(jnp.float32)
    seed_group = seed_rows.astype(jnp.float32)
    norm_pull = jax.vjp(norm_rows, x_group, ln_gain, ln_bias)[1]
    input_part, gain_part, shift_part = norm_pull(share_grad)
    input_group = seed_group + input_part
    grad_input = lax.dynamic_slice_in_dim(
        input_group, model_rank * local_rows, local_rows, 0
    ).astype(jnp.bfloat16)
    back_part = jnp.sum(seed_group, axis=0)
    grad_w_qkv, grad_w_out, grad_w_in, grad_b_in, grad_w_back, gain_rows, shift_rows, back_rows = (
        lax.psum_scatter(
            grad_qkv_local.astype(jnp.bfloat16), "dp", scatter_dimension=1, tiled=True
        ).astype(jnp.float32),
        lax.psum_scatter(
            grad_out_local.astype(jnp.bfloat16), "dp", scatter_dimension=1, tiled=True
        ).astype(jnp.float32),
        lax.psum_scatter(
            grad_in_local.astype(jnp.bfloat16), "dp", scatter_dimension=0, tiled=True
        ).astype(jnp.float32),
        lax.psum_scatter(
            grad_bias_in.astype(jnp.bfloat16), "dp", scatter_dimension=0, tiled=True
        ).astype(jnp.float32),
        lax.psum_scatter(
            grad_back_local.astype(jnp.bfloat16), "dp", scatter_dimension=1, tiled=True
        ).astype(jnp.float32),
        lax.psum_scatter(
            gain_part.astype(jnp.bfloat16), "dp", scatter_dimension=0, tiled=True
        ).astype(jnp.float32),
        lax.psum_scatter(
            shift_part.astype(jnp.bfloat16), "dp", scatter_dimension=0, tiled=True
        ).astype(jnp.float32),
        lax.psum_scatter(
            back_part.astype(jnp.bfloat16), "dp", scatter_dimension=0, tiled=True
        ).astype(jnp.float32),
    )
    piece_width = gain_rows.shape[0] // model_count
    grad_ln_gain = lax.dynamic_slice_in_dim(gain_rows, model_rank * piece_width, piece_width, 0)
    grad_ln_bias = lax.dynamic_slice_in_dim(shift_rows, model_rank * piece_width, piece_width, 0)
    grad_b_back = lax.dynamic_slice_in_dim(back_rows, model_rank * piece_width, piece_width, 0)
    return (
        block_out,
        grad_input,
        grad_ln_gain,
        grad_ln_bias,
        grad_w_qkv,
        grad_w_out,
        grad_w_in,
        grad_b_in,
        grad_w_back,
        grad_b_back,
    )


MESH = pl.DeviceIdType.MESH
NZ = 4
TILE = 256
N_HEADS = TILE // HD
NQ = 4
NJ = 4
NK = NQ + 2 * NJ
VROWS = 56


def fits_quad(mesh):
    return mesh.shape["mp"] == 2 and mesh.shape["dp"] == 4 * NZ


def dot_nn(a, b):
    return lax.dot_general(a, b, (((1,), (0,)), ((), ())), preferred_element_type=jnp.float32)


def dot_nt(a, b):
    return lax.dot_general(a, b, (((1,), (1,)), ((), ())), preferred_element_type=jnp.float32)


def dot_tn(a, b):
    return lax.dot_general(a, b, (((0,), (0,)), ((), ())), preferred_element_type=jnp.float32)


def layer_kernel(
    bucket_ref,
    counts_ref,
    x_ref,
    cot_ref,
    gain_ref,
    bias_ref,
    bback_ref,
    cos_ref,
    sin_ref,
    bin_ref,
    wqkv_ref,
    wot_ref,
    win_ref,
    wbt_ref,
    block_ref,
    gin_ref,
    gqkv_ref,
    got_ref,
    gi_ref,
    gbt_ref,
    lng_ref,
    lnb_ref,
    bbk_ref,
    gbin_ref,
    B,
    W,
    NS,
    CT,
    SN,
    BM,
    QR,
    KR,
    VR,
    R,
    SL,
    XV,
    CV,
    COSV,
    SINV,
    ins,
    OUT,
    DN,
    GP,
    GC,
    RZ,
    FS,
    YS,
    YR,
    XH,
    RSTD,
    EXSa,
    EXSb,
    EYSa,
    EYSb,
    EXRa,
    EXRb,
    EYRa,
    EYRb,
    EXS2a,
    EXS2b,
    EYS2a,
    EYS2b,
    EXR2a,
    EXR2b,
    EYR2a,
    EYR2b,
    V,
    VS,
    VRV,
    loc_sem,
    ays,
    ayr,
    azs,
    azr,
    acs,
    acr,
    gs,
    gr,
    rcs,
    rcr,
    rzs,
    rzr,
    rys,
    ryr,
    exs,
    exr,
    vs,
    vr,
):
    EXS = (EXSa, EXSb)
    EYS = (EYSa, EYSb)
    EXR = (EXRa, EXRb)
    EYR = (EYRa, EYRb)
    EXS2 = (EXS2a, EXS2b)
    EYS2 = (EYS2a, EYS2b)
    EXR2 = (EXR2a, EXR2b)
    EYR2 = (EYR2a, EYR2b)
    f32, bf16 = jnp.float32, jnp.bfloat16
    dp, x = lax.axis_index("dp"), lax.axis_index("mp")
    z = dp // 4
    y = lax.rem(dp // 2, 2)
    c = lax.rem(dp, 2)
    rows = x_ref.shape[0]
    width = x_ref.shape[1]
    dev_x = (dp, 1 - x)
    dev_y = (dp + 2 - 4 * y, x)
    dev_c = (dp + 1 - 2 * c, x)
    dev_r = (lax.rem(dp + 4, 4 * NZ), x)
    dev_l = (lax.rem(dp + 4 * NZ - 4, 4 * NZ), x)
    dev_z = [(lax.rem(dp + 4 * i, 4 * NZ), x) for i in (1, 2, 3)]
    NA, SA = NS.at[0], NS.at[1]
    m_own = 2 * y + x
    m_x = 2 * y + 1 - x
    m_y = 2 - 2 * y + x
    m_d = 3 - m_own

    def rcp(src, dst, ss, rs, dev):
        return pltpu.make_async_remote_copy(
            src_ref=src, dst_ref=dst, send_sem=ss, recv_sem=rs, device_id=dev, device_id_type=MESH
        )

    barrier = pltpu.get_barrier_semaphore()
    peers = [dev_x, dev_y, dev_c] + dev_z
    for peer in peers:
        pl.semaphore_signal(barrier, inc=1, device_id=peer, device_id_type=MESH)

    def wsrc(k, q):
        if k == NK:
            return None
        if k < 3:
            return wqkv_ref.at[k, :, pl.ds(pl.multiple_of(q * TILE, TILE), TILE)]
        if k == 3:
            return wot_ref.at[:, pl.ds(pl.multiple_of(q * TILE, TILE), TILE)]
        ref = win_ref if k % 2 == 0 else wbt_ref
        j = (k - NQ) // 2
        return ref.at[:, pl.ds(pl.multiple_of(q * (NJ * TILE) + j * TILE, TILE), TILE)]

    def wv(k):
        return B if isinstance(k, int) and k == NK else W.at[k]

    def own_copy(k):
        return pltpu.make_async_copy(wsrc(k, y), W.at[k, z, y, c], loc_sem.at[k])

    def y_copy(k):
        if k == NK:
            return rcp(B.at[z, y, c], B.at[z, y, c], ays.at[k], ayr.at[k], dev_y)
        return rcp(wsrc(k, 1 - y), W.at[k, z, y, c], ays.at[k], ayr.at[k], dev_y)

    def y_arrived(k):
        here = wv(k).at[z, 1 - y, c]
        rcp(here, here, ays.at[k], ayr.at[k], dev_y).wait_recv()

    def z_copy(k, way, s, e):
        block = wv(k).at[e, :, c]
        return rcp(
            block, block, azs.at[k, way, s], azr.at[k, way, s], dev_r if way == 0 else dev_l
        )

    def c_copy(k, e):
        block = wv(k).at[e, :, c]
        return rcp(block, block, acs.at[k, e], acr.at[k, e], dev_c)

    def ag_own(k, copied=True):
        if copied:
            pltpu.make_async_copy(
                W.at[k, z, y, c], W.at[k, z, y, c], loc_sem.at[k]
            ).wait()
        y_arrived(k)

        @pl.when(z < NZ - 1)
        def _():
            z_copy(k, 0, 0, z).start()

        @pl.when(z > 0)
        def _():
            z_copy(k, 1, 0, z).start()

        c_copy(k, z).start()

    def ag_step(k, s):
        @pl.when(z - 1 - s >= 0)
        def _():
            e = z - 1 - s
            z_copy(k, 0, s, e).wait_recv()
            if s < NZ - 2:

                @pl.when(z < NZ - 1)
                def _():
                    z_copy(k, 0, s + 1, e).start()

            c_copy(k, e).start()

        @pl.when(z + 1 + s <= NZ - 1)
        def _():
            e = z + 1 + s
            z_copy(k, 1, s, e).wait_recv()
            if s < NZ - 2:

                @pl.when(z > 0)
                def _():
                    z_copy(k, 1, s + 1, e).start()

            c_copy(k, e).start()

    def ag_done(k):
        for e in range(NZ):
            block = wv(k).at[e, :, 1 - c]
            rcp(block, block, acs.at[k, e], acr.at[k, e], dev_c).wait_recv()

    def ag_sent(k, copied=True):
        y_copy(k).wait_send() if isinstance(k, int) else None
        for s in range(NZ - 1):

            @pl.when((z < NZ - 1) & (z - s >= 0))
            def _():
                z_copy(k, 0, s, z - s).wait_send()

            @pl.when((z > 0) & (z + s <= NZ - 1))
            def _():
                z_copy(k, 1, s, z + s).wait_send()

        for e in range(NZ):
            c_copy(k, e).wait_send()

    order = [0, NK] + list(range(1, NK))
    turns = iter([t for t in range(NK + NZ) if not 8 <= t <= 11])

    def ag_turn():
        t = next(turns, None)
        if t is None:
            return
        for n in range(2) if t == 0 else (t + 1,):
            if n <= NK:
                ag_own(order[n], copied=order[n] != NK)
        for s in range(NZ - 1):
            if 0 <= t - 1 - s <= NK:
                ag_step(order[t - 1 - s], s)

    def late_turn(t):
        ag_own(t)
        for s in range(NZ - 1):
            ag_step(t - 2 - s, s)

    P0 = 96
    parts = (pl.ds(0, P0), pl.ds(P0, rows - P0))
    BUF = (NA, SA)

    def g_copy(t, p, way, m):
        block = BUF[t].at[m, parts[p]]
        i = (t * 2 + p) * 3 + way
        dev = (dev_x, dev_y)[way] if way < 2 else (dev_y, dev_x)[p]
        return rcp(block, block, gs.at[i], gr.at[i], dev)

    def g_send(t):
        g_copy(t, 0, 0, m_own).start()
        g_copy(t, 1, 1, m_own).start()
        g_copy(t, 1, 0, m_own).start()
        g_copy(t, 0, 1, m_own).start()

    def g_near(t):
        g_copy(t, 0, 0, m_x).wait_recv()
        g_copy(t, 1, 1, m_y).wait_recv()

    def g_forward(t):
        g_copy(t, 0, 2, m_x).start()
        g_copy(t, 1, 2, m_y).start()

    def g_rest(t):
        g_copy(t, 1, 0, m_x).wait_recv()
        g_copy(t, 0, 1, m_y).wait_recv()

    def g_far(t):
        g_copy(t, 0, 2, m_d).wait_recv()
        g_copy(t, 1, 2, m_d).wait_recv()

    def g_sent(t):
        for p in (0, 1):
            for way in (0, 1):
                g_copy(t, p, way, m_own).wait_send()
        g_copy(t, 0, 2, m_x).wait_send()
        g_copy(t, 1, 2, m_y).wait_send()

    def rs_c(k):
        return rcp(GP.at[k, :, :, 1 - c], GC.at[k], rcs.at[k], rcr.at[k], dev_c)

    def rs_z(k, way, e, slot):
        return rcp(
            GP.at[k, e, :, c],
            RZ.at[k, slot],
            rzs.at[k, e],
            rzr.at[k, slot],
            dev_r if way == 0 else dev_l,
        )

    def rs_begin(k):
        rs_c(k).wait_recv()
        for e in range(NZ):
            GP[k, e, :, c] = (GP[k, e, :, c].astype(f32) + GC[k, e].astype(f32)).astype(bf16)

        @pl.when(z == 0)
        def _():
            for e in range(NZ - 1, 0, -1):
                rs_z(k, 0, e, e).start()

        @pl.when(z == NZ - 1)
        def _():
            for e in range(NZ - 1):
                rs_z(k, 1, e, e if e < NZ - 2 else 4).start()

    def pass_on(k, way, e, slot):
        rs_z(k, way, e, e).wait_recv()
        GP[k, e, :, c] = (GP[k, e, :, c].astype(f32) + RZ[k, e].astype(f32)).astype(bf16)
        rs_z(k, way, e, slot).start()

    def rs_hop1(k):
        @pl.when(z == 1)
        def _():
            pass_on(k, 0, 3, 3)
            pass_on(k, 0, 2, 2)

        @pl.when(z == 2)
        def _():
            pass_on(k, 1, 0, 0)
            pass_on(k, 1, 1, 4)

    def rs_hop2(k):
        @pl.when(z == 2)
        def _():
            pass_on(k, 0, 3, 3)

        @pl.when(z == 1)
        def _():
            pass_on(k, 1, 0, 4)

    def rs_y(k):
        return rcp(YS.at[k], YR.at[k], rys.at[k], ryr.at[k], dev_y)

    def put(k, q, value):
        if k < 3:
            gqkv_ref[k, :, pl.ds(pl.multiple_of(q * TILE, TILE), TILE)] = value
        elif k == 3:
            got_ref[:, pl.ds(pl.multiple_of(q * TILE, TILE), TILE)] = value
        else:
            ref = gi_ref if k % 2 == 0 else gbt_ref
            j = (k - NQ) // 2
            ref[:, pl.ds(pl.multiple_of(q * (NJ * TILE) + j * TILE, TILE), TILE)] = value

    def rs_final(k):
        FS[...] = GP[k, z, :, c].astype(f32)

        @pl.when(z > 0)
        def _():
            rs_z(k, 0, z, z).wait_recv()
            FS[...] += RZ[k, z].astype(f32)

        @pl.when(z < NZ - 1)
        def _():
            rs_z(k, 1, z, 4).wait_recv()
            FS[...] += RZ[k, 4].astype(f32)

        YS[k] = FS[1 - y].astype(bf16)
        rs_y(k).start()
        put(k, y, FS[y])

    def rs_out(k):
        rs_y(k).wait_recv()
        put(k, 1 - y, YR[k].astype(f32))

    rturns = iter(range(NK + 2))
    rorder = [NQ + 1] + [k for k in range(NK) if k != NQ + 1]

    def rs_turn():
        r = next(rturns, None)
        if r is None:
            return
        for s, f in enumerate((rs_hop1, rs_hop2, rs_final)):
            if 0 <= r - s < NK:
                f(rorder[r - s])

    def rs_sent(k):
        rs_c(k).wait_send()
        for e in range(NZ):

            @pl.when(z != e)
            def _():
                rs_z(k, 0, e, e).wait_send()

        rs_y(k).wait_send()

    def e_copy(t, u, i):
        src, dst, dev = (
            (EXS, EXR, dev_x),
            (EYS, EYR, dev_y),
            (EXS2, EXR2, dev_x),
            (EYS2, EYR2, dev_y),
        )[i]
        src, dst = src[u], dst[u]
        return rcp(src.at[t], dst.at[t], exs.at[t, u, i], exr.at[t, u, i], dev)

    wide = (384, 256)
    thin = (2 * 128, 128)

    def cols(u, half):
        if half == 0:
            return pl.ds(u * wide[0], wide[u])
        return pl.ds(sum(wide) + u * thin[0], thin[u])

    def e_first_x(t, u, P):
        for i in range(2):
            EXS[u][t, i] = P[2 * i + 1 - x, :, cols(u, 0)].astype(bf16)
        e_copy(t, u, 0).start()

    def e_first_y(t, u, P):
        for i in range(2):
            EYS[u][t, i] = P[2 - 2 * y + i, :, cols(u, 1)].astype(bf16)
        e_copy(t, u, 1).start()

    def e_first(t, u, P):
        e_first_x(t, u, P)
        e_first_y(t, u, P)

    def e_second(t, u, P):
        e_copy(t, u, 0).wait_recv()
        EYS2[u][t] = (P[m_y, :, cols(u, 0)] + EXR[u][t, 1 - y].astype(f32)).astype(bf16)
        e_copy(t, u, 3).start()
        e_copy(t, u, 1).wait_recv()
        EXS2[u][t] = (P[m_x, :, cols(u, 1)] + EYR[u][t, 1 - x].astype(f32)).astype(bf16)
        e_copy(t, u, 2).start()

    def e_last(t, u, P):
        e_copy(t, u, 3).wait_recv()
        P[m_own, :, cols(u, 0)] += EXR[u][t, y].astype(f32) + EYR2[u][t].astype(f32)
        e_copy(t, u, 2).wait_recv()
        P[m_own, :, cols(u, 1)] += EYR[u][t, x].astype(f32) + EXR2[u][t].astype(f32)

    def e_sent(t):
        for u in range(2):
            for i in range(4):
                e_copy(t, u, i).wait_send()

    inputs = [
        pltpu.make_async_copy(src, dst, ins.at[i])
        for i, (src, dst) in enumerate(
            ((x_ref, XV), (cot_ref, CV), (cos_ref, COSV), (sin_ref, SINV))
        )
    ]
    for copy in inputs:
        copy.start()
    for k in range(NK):
        own_copy(k).start()
    inputs[0].wait()
    xf = XV[...].astype(f32)
    centred = xf - jnp.mean(xf, axis=-1, keepdims=True)
    rstd = lax.rsqrt(jnp.mean(centred * centred, axis=-1, keepdims=True) + NORM_EPS)
    xhat = centred * rstd
    XH[...] = xhat
    RSTD[...] = jnp.broadcast_to(rstd, RSTD.shape)
    NA[m_own] = (xhat * gain_ref[...] + bias_ref[...]).astype(bf16)

    bucket = bucket_ref[0]
    B[z, y, c, 0:8] = jnp.broadcast_to(bin_ref[...].astype(f32), (8, 128)).astype(bf16)
    B[z, y, c, 8:16] = jnp.full((8, 128), bucket.astype(f32), f32).astype(bf16)

    slot = lax.shift_right_logical(jnp.int32(rows), bucket)
    shift_of = (rows.bit_length() - 1) - bucket
    row = x * rows + lax.broadcasted_iota(jnp.int32, (rows, 128), 0)
    slot_of = lax.shift_right_logical(row, jnp.full(row.shape, shift_of, jnp.int32))
    place = row & jnp.full(row.shape, slot - 1, jnp.int32)
    limit = jnp.zeros((rows, 128), jnp.int32)
    for s in range(SLOTS):
        limit = jnp.where(slot_of == s, counts_ref[s], limit)
    valid = jnp.where(place < limit, 1.0, 0.0)[:, 0:1]
    inputs[1].wait()
    seeds = CV[...].astype(f32) * valid
    SA[m_own] = seeds.astype(bf16)
    back_sum = jnp.sum(seeds, axis=0, keepdims=True)
    V[...] = jnp.zeros_like(V)
    for i in range(8):
        V[16 + i : 17 + i, :] = back_sum[:, i * 128 : (i + 1) * 128]
    pl.semaphore_wait(barrier, len(peers))
    for k in order[:6]:
        y_copy(k).start()
    g_send(0)
    for k in order[6:]:
        y_copy(k).start()
    g_send(1)
    ag_turn()
    ag_turn()

    lane = lax.broadcasted_iota(jnp.int32, (rows, TILE), 1)
    even = (lane & 1) == 0

    def table(g):
        brow = B[z, g, c].astype(f32)[8:9, :]
        ba = jnp.broadcast_to(brow, (rows, 128))

        def pick(ref):
            full = ref[...]
            out = full
            for b in range(1, 4):
                n = rows >> b
                out = jnp.where(ba == float(b), jnp.concatenate([full[:n]] * (1 << b), axis=0), out)
            return out

        cg, sg = pick(COSV), pick(SINV)
        CT[g] = jnp.concatenate([cg, cg], axis=1)
        SN[g] = jnp.concatenate([sg, sg], axis=1)
        size = jnp.full((rows, 128), rows, jnp.int32)
        for b in range(1, 4):
            size = jnp.where(ba == float(b), rows >> b, size)
        size = jnp.concatenate([size, size], axis=1)
        qi = lax.broadcasted_iota(jnp.int32, (rows, rows), 0)
        ki = lax.broadcasted_iota(jnp.int32, (rows, rows), 1)
        BM[g] = jnp.where((ki <= qi) & ((qi ^ ki) < size), 0.0, MASKED_SCORE)

    def tables():
        for g in range(2):
            table(g)

    def turn(v, g, sign):
        other = jnp.where(even, -pltpu.roll(v, TILE - 1, 1), pltpu.roll(v, 1, 1))
        return v * CT[g] + (sign * other) * SN[g]

    def weight(k):
        return W[k].reshape(width, TILE)

    scale = HD ** (-0.5)

    def project(m):
        g = m // 2
        nb = NA[m]
        QR[m] = turn(dot_nn(nb, weight(0)), g, 1.0).astype(bf16)
        KR[m] = turn(dot_nn(nb, weight(1)), g, 1.0).astype(bf16)
        VR[m] = dot_nn(nb, weight(2)).astype(bf16)

    def attend(m):
        g = m // 2
        q, kk, v = QR[m], KR[m], VR[m]
        da = dot_nn(SA[m], weight(3)).astype(bf16)
        zero = jnp.zeros((rows, TILE), bf16)
        ps, ss, qs, ks, vs_, ds = [], [], [], [], [], []
        for h in range(N_HEADS):
            mine = (lane // HD) == h
            qh, kh, vh, dh = (jnp.where(mine, t, zero) for t in (q, kk, v, da))
            s = dot_nt(qh, kk) * scale + BM[g]
            e = jnp.exp(s - jnp.max(s, axis=-1, keepdims=True))
            p = e * (1.0 / jnp.sum(e, axis=-1, keepdims=True))
            pg = dot_nt(dh, v)
            sg = p * (pg - jnp.sum(p * pg, axis=-1, keepdims=True))
            for held, t in ((ps, p), (ss, sg), (qs, qh), (ks, kh), (vs_, vh), (ds, dh)):
                held.append(t.astype(bf16))
        wide_p, wide_s = jnp.concatenate(ps, axis=1), jnp.concatenate(ss, axis=1)
        att = dot_nn(wide_p, jnp.concatenate(vs_, axis=0))
        dq = dot_nn(wide_s, jnp.concatenate(ks, axis=0))
        dk = dot_tn(jnp.concatenate(ss, axis=0), jnp.concatenate(qs, axis=0))
        dv = dot_tn(jnp.concatenate(ps, axis=0), jnp.concatenate(ds, axis=0))
        at = att.astype(bf16)
        dqb = turn(dq * scale, g, -1.0).astype(bf16)
        dkb = turn(dk * scale, g, -1.0).astype(bf16)
        dvb = dv.astype(bf16)
        rs = pl.ds(pl.multiple_of(m * rows, rows), rows)
        R[3, rs, :] = at
        R[0, rs, :] = dqb
        R[1, rs, :] = dkb
        R[2, rs, :] = dvb
        OUT[m] = dot_nt(at, weight(3))
        DN[m] = dot_nt(dqb, weight(0)) + dot_nt(dkb, weight(1)) + dot_nt(dvb, weight(2))

    def grad_of(k, left):
        total = dot_tn(NS[left].reshape(4 * rows, width), R[k])
        GP[k] = total.astype(bf16).reshape(NZ, 2, 2, 64, TILE)
        rs_c(k).start()

    def slice_of(j):
        return NQ + 2 * j, NQ + 1 + 2 * j

    def all_rows(ref):
        return ref[...].reshape(4 * rows, width)

    def feed(j):
        ki, kb = slice_of(j)
        b0 = B[2 * y + lax.div(j, 2), lax.rem(j, 2), 0].astype(f32)[0:1, :]
        b1 = B[2 * y + lax.div(j, 2), lax.rem(j, 2), 1].astype(f32)[0:1, :]
        u = dot_nn(all_rows(NA), weight(ki)) + jnp.concatenate([b0, b1], axis=1)
        u2 = u * u
        k0 = float(np.sqrt(2.0 / np.pi))
        t = jnp.tanh(k0 * u * (1.0 + 0.044715 * u2))
        R[kb] = (0.5 * u * (1.0 + t)).astype(bf16)
        SL[...] = 0.5 * (1.0 + t) + (0.5 * k0) * u * (1.0 - t * t) * (1.0 + 0.134145 * u2)

    def feed_back(j):
        ki, kb = slice_of(j)
        hg = (dot_nn(all_rows(SA), weight(kb)) * SL[...]).astype(bf16)
        R[ki] = hg
        OUT[...] += dot_nt(R[kb], weight(kb)).reshape(4, rows, width)
        DN[...] += dot_nt(hg, weight(ki)).reshape(4, rows, width)
        at = 24 + x * 16 + y * 8 + 2 * j
        total = jnp.sum(hg.astype(f32), axis=0, keepdims=True)
        V[pl.ds(at, 1), :] = total[:, :128]
        V[pl.ds(at + 1, 1), :] = total[:, 128:]

    def feed_grads(j):
        lax.fori_loop(0, 2, lambda i, _: (grad_of(NQ + 2 * j + i, i), 0)[1], 0)

    def v_copy(i, dev):
        return rcp(VS.at[min(i, 3)], VRV.at[i], vs.at[i], vr.at[i], dev)

    v_devs = (dev_c, dev_x, dev_y)

    def v_step(i):
        v_copy(i, v_devs[i]).wait_recv()
        VS[i + 1] = VS[i] + VRV[i]
        if i < 2:
            v_copy(i + 1, v_devs[i + 1]).start()
        else:
            for n, dev in enumerate(dev_z):
                v_copy(3 + n, dev).start()

    def arrived(*chunks):
        for k in chunks:
            ag_done(k)

    ag_turn()
    inputs[2].wait()
    inputs[3].wait()
    tables()
    ag_turn()
    ag_turn()
    ag_turn()
    g_near(0)
    g_forward(0)
    ag_turn()
    arrived(0, NK, 1, 2)
    g_rest(0)
    def near(i):
        ix, iy = lax.rem(i, 2), lax.div(i, 2)
        return 2 * (y + iy - 2 * y * iy) + x + ix - 2 * x * ix

    lax.fori_loop(0, 3, lambda i, _: (project(near(i)), 0)[1], 0)
    ag_turn()
    arrived(3)

    def rows_turn(i, _):
        @pl.when(i == 1)
        def _():
            g_near(1)
            g_forward(1)
            g_rest(1)

        @pl.when(i == 3)
        def _():
            g_far(1)
            grad_of(NQ + 1, 1)
            project(m_d)
            rs_begin(NQ + 1)

        attend(near(i))

        @pl.when(i == 2)
        def _():
            g_far(0)
            arrived(NQ)
            feed(0)

        @pl.when(i < 3)
        def _():
            late_turn(8 + i)

        return 0

    lax.fori_loop(0, 4, rows_turn, 0)

    def head_grads(k, _):
        grad_of(k, lax.div(k, 3))

        @pl.when(k == 1)
        def _():
            late_turn(11)

        @pl.when(k > 0)
        def _():
            rs_begin(k - 1)

        return 0

    lax.fori_loop(0, NQ, head_grads, 0)
    ag_turn()

    def slices(j, _):
        @pl.when(j > 0)
        def _():
            arrived(NQ + 2 * j)
            feed(j)

        arrived(NQ + 1 + 2 * j)
        feed_back(j)

        @pl.when(j == 0)
        def _():
            rs_begin(3)
            ag_turn()
            rs_turn()

        @pl.when(j == 1)
        def _():
            ag_turn()
            rs_turn()

        @pl.when(j == 2)
        def _():
            ag_turn()
            rs_turn()

        return 0

    lax.fori_loop(0, NJ, slices, 0)

    for u in range(2):
        e_first(1, u, DN)
    grad_of(NQ, 0)
    rs_turn()
    rs_begin(NQ)
    feed_grads(1)
    rs_begin(6)
    rs_begin(7)
    rs_turn()
    feed_grads(2)
    rs_begin(8)
    rs_begin(9)
    rs_turn()
    e_second(1, 0, DN)
    feed_grads(3)
    rs_begin(10)
    rs_begin(11)
    rs_turn()
    e_second(1, 1, DN)
    e_first(0, 0, OUT)
    e_first_y(0, 1, OUT)
    rs_turn()
    rs_turn()
    for u in range(2):
        e_last(1, u, DN)
    dn = DN[m_own]
    xhat = XH[...]
    gsum = jnp.sum(dn * xhat, axis=0, keepdims=True)
    bsum = jnp.sum(dn, axis=0, keepdims=True)
    for i in range(8):
        V[i : i + 1, :] = gsum[:, i * 128 : (i + 1) * 128]
        V[8 + i : 9 + i, :] = bsum[:, i * 128 : (i + 1) * 128]
    VS[0] = V[...]
    v_copy(0, dev_c).start()
    e = dn * gain_ref[...]
    me = jnp.mean(e, axis=-1, keepdims=True)
    mex = jnp.mean(e * xhat, axis=-1, keepdims=True)
    gin_ref[...] = (SA[m_own].astype(f32) + RSTD[:, 0:1] * (e - me - xhat * mex)).astype(bf16)
    v_step(0)
    rs_turn()
    e_first_x(0, 1, OUT)
    rs_turn()
    v_step(1)
    e_second(0, 0, OUT)
    rs_turn()
    v_step(2)
    rs_turn()
    e_second(0, 1, OUT)
    for k in rorder[:9]:
        rs_out(k)
    rs_turn()
    rs_out(rorder[9])
    for k in rorder[10:]:
        rs_out(k)
    for i in range(3):
        v_copy(3 + i, dev_z[i]).wait_recv()
    V[...] = VS[3] + VRV[3] + VRV[4] + VRV[5]
    index = 2 * dp + x
    lane4 = lax.rem(index, 4)
    for base, ref in ((0, lng_ref), (8, lnb_ref), (16, bbk_ref)):
        line = V[pl.ds(base + index // 4, 1), :]
        out = line[:, 0:32]
        for n in range(1, 4):
            out = jnp.where(lane4 == n, line[:, 32 * n : 32 * n + 32], out)
        ref[...] = out
    gbin_ref[...] = V[pl.ds(24 + 16 * x + dp, 1), :]
    for u in range(2):
        e_last(0, u, OUT)
    block_ref[...] = (XV[...].astype(f32) + OUT[m_own] + bback_ref[...]).astype(bf16)

    def later(f):
        lax.fori_loop(0, NK, lambda k, _: (f(k), 0)[1], 0)

    for k in range(NK + 1):
        ag_sent(k)
    for t in range(2):
        g_sent(t)
        e_sent(t)
    later(rs_sent)
    for i, dev in enumerate([dev_c, dev_x, dev_y] + dev_z):
        v_copy(i, dev).wait_send()


def write_kernel(*refs):
    srcs, dsts, sems = refs[:10], refs[10:20], refs[20]
    copies = [pltpu.make_async_copy(a, b, sems.at[i]) for i, (a, b) in enumerate(zip(srcs, dsts))]
    for copy in copies:
        copy.start()
    for copy in copies:
        copy.wait()


def rope_constants(rows):
    half = np.arange(ROT // 2, dtype=np.float32)
    rates = (10000.0 ** (-2.0 * half / ROT)).astype(np.float32)
    angle = np.arange(rows, dtype=np.float32)[:, None] * rates[None, :]
    angle = np.repeat(angle, 2, axis=1)
    cos = np.concatenate([np.cos(angle), np.ones((rows, HD - ROT))], axis=1)
    sin = np.concatenate([np.sin(angle), np.zeros((rows, HD - ROT))], axis=1)
    two = lambda t: np.concatenate([t, t], axis=1).astype(np.float32)
    return two(cos), two(sin)


def on_quad(
    residual_in,
    cotangent,
    ln_gain,
    ln_bias,
    w_qkv,
    w_out,
    w_in,
    b_in,
    w_back,
    b_back,
    bucket_ids,
    residue_counts,
):
    rows, width = residual_in.shape
    cos, sin = rope_constants(rows)
    f32, bf16 = jnp.float32, jnp.bfloat16
    vm = pl.BlockSpec(memory_space=pltpu.VMEM)
    sm = pl.BlockSpec(memory_space=pltpu.SMEM)
    anyspace = pl.BlockSpec(memory_space=pl.ANY)
    shard = width // (4 * NZ)
    sem = pltpu.SemaphoreType.DMA
    shapes = (
        jax.ShapeDtypeStruct((rows, width), bf16),
        jax.ShapeDtypeStruct((rows, width), bf16),
        jax.ShapeDtypeStruct((3, shard, 2 * TILE), f32),
        jax.ShapeDtypeStruct((shard, 2 * TILE), f32),
        jax.ShapeDtypeStruct((shard, 2 * NJ * TILE), f32),
        jax.ShapeDtypeStruct((shard, 2 * NJ * TILE), f32),
        jax.ShapeDtypeStruct((1, 32), f32),
        jax.ShapeDtypeStruct((1, 32), f32),
        jax.ShapeDtypeStruct((1, 32), f32),
        jax.ShapeDtypeStruct((1, 128), f32),
    )
    held = pl.pallas_call(
        layer_kernel,
        out_shape=tuple(pltpu.VMEM(v.shape, v.dtype) for v in shapes),
        in_specs=[sm, sm, anyspace, anyspace] + [vm] * 3 + [anyspace] * 2 + [vm] + [anyspace] * 4,
        out_specs=(vm,) * 10,
        scratch_shapes=[
            pltpu.VMEM((NZ, 2, 2, 16, 128), bf16),
            pltpu.VMEM((NK, NZ, 2, 2, shard, TILE), bf16),
            pltpu.VMEM((2, 4, rows, width), bf16),
            pltpu.VMEM((2, rows, TILE), f32),
            pltpu.VMEM((2, rows, TILE), f32),
            pltpu.VMEM((2, rows, rows), f32),
            pltpu.VMEM((4, rows, TILE), bf16),
            pltpu.VMEM((4, rows, TILE), bf16),
            pltpu.VMEM((4, rows, TILE), bf16),
            pltpu.VMEM((NK, 4 * rows, TILE), bf16),
            pltpu.VMEM((4 * rows, TILE), f32),
            pltpu.VMEM((rows, width), bf16),
            pltpu.VMEM((rows, width), bf16),
            pltpu.VMEM((rows, 128), f32),
            pltpu.VMEM((rows, 128), f32),
            sem((4,)),
            pltpu.VMEM((4, rows, width), f32),
            pltpu.VMEM((4, rows, width), f32),
            pltpu.VMEM((NK, NZ, 2, 2, shard, TILE), bf16),
            pltpu.VMEM((NK, NZ, 2, shard, TILE), bf16),
            pltpu.VMEM((NK, 5, 2, shard, TILE), bf16),
            pltpu.VMEM((2, shard, TILE), f32),
            pltpu.VMEM((NK, shard, TILE), bf16),
            pltpu.VMEM((NK, shard, TILE), bf16),
            pltpu.VMEM((rows, width), f32),
            pltpu.VMEM((rows, 128), f32),
            pltpu.VMEM((2, 2, rows, 384), bf16),
            pltpu.VMEM((2, 2, rows, 256), bf16),
            pltpu.VMEM((2, 2, rows, 256), bf16),
            pltpu.VMEM((2, 2, rows, 128), bf16),
            pltpu.VMEM((2, 2, rows, 384), bf16),
            pltpu.VMEM((2, 2, rows, 256), bf16),
            pltpu.VMEM((2, 2, rows, 256), bf16),
            pltpu.VMEM((2, 2, rows, 128), bf16),
            pltpu.VMEM((2, rows, 256), bf16),
            pltpu.VMEM((2, rows, 128), bf16),
            pltpu.VMEM((2, rows, 384), bf16),
            pltpu.VMEM((2, rows, 256), bf16),
            pltpu.VMEM((2, rows, 256), bf16),
            pltpu.VMEM((2, rows, 128), bf16),
            pltpu.VMEM((2, rows, 384), bf16),
            pltpu.VMEM((2, rows, 256), bf16),
            pltpu.VMEM((VROWS, 128), f32),
            pltpu.VMEM((4, VROWS, 128), f32),
            pltpu.VMEM((6, VROWS, 128), f32),
            sem((NK,)),
            sem((NK + 1,)),
            sem((NK + 1,)),
            sem((NK + 1, 2, 3)),
            sem((NK + 1, 2, 3)),
            sem((NK + 1, NZ)),
            sem((NK + 1, NZ)),
            sem((12,)),
            sem((12,)),
            sem((NK,)),
            sem((NK,)),
            sem((NK, NZ)),
            sem((NK, 5)),
            sem((NK,)),
            sem((NK,)),
            sem((2, 2, 4)),
            sem((2, 2, 4)),
            sem((6,)),
            sem((6,)),
        ],
        compiler_params=pltpu.CompilerParams(
            collective_id=0, has_side_effects=True, vmem_limit_bytes=58 << 20
        ),
        cost_estimate=pl.CostEstimate(
            flops=20 * 2**30, bytes_accessed=8 * 2**20, transcendentals=2**21
        ),
    )(
        bucket_ids,
        residue_counts.reshape(SLOTS),
        residual_in,
        cotangent,
        ln_gain.reshape(1, width),
        ln_bias.reshape(1, width),
        b_back.reshape(1, width),
        jnp.asarray(cos),
        jnp.asarray(sin),
        b_in.reshape(1, 128),
        w_qkv,
        w_out.T,
        w_in,
        w_back.T,
    )
    held = [pltpu.with_memory_space_constraint(v, pltpu.VMEM) for v in held]
    outs = pl.pallas_call(
        write_kernel,
        out_shape=shapes,
        in_specs=[vm] * 10,
        out_specs=(anyspace,) * 10,
        scratch_shapes=[sem((10,))],
    )(*held)
    block_out, grad_input, grad_w_qkv, gwo, grad_w_in, gwb, lng, lnb, bbk, gbin = outs
    return (
        block_out,
        grad_input,
        lng.reshape(32),
        lnb.reshape(32),
        grad_w_qkv,
        gwo.T,
        grad_w_in,
        gbin.reshape(128),
        gwb.T,
        bbk.reshape(32),
    )


def solution(mesh):
    placed = (
        P(("dp", "mp"), None),
        P(("dp", "mp"), None),
        P(),
        P(),
        P(None, "dp", "mp"),
        P("mp", "dp"),
        P("dp", "mp"),
        P(("mp", "dp")),
        P("mp", "dp"),
        P(),
        P("dp"),
        P("dp", None),
    )
    return jax.shard_map(
        on_quad if fits_quad(mesh) else on_device,
        mesh=mesh,
        in_specs=placed,
        out_specs=(
            P(("dp", "mp"), None),
            P(("dp", "mp"), None),
            P(("dp", "mp")),
            P(("dp", "mp")),
            P(None, "dp", "mp"),
            P("mp", "dp"),
            P("dp", "mp"),
            P(("mp", "dp")),
            P("mp", "dp"),
            P(("dp", "mp")),
        ),
        check_vma=False,
    )
```

```python
from functools import partial

import jax
import jax.numpy as jnp
import numpy as np
from jax import lax
from jax.experimental import pallas as pl
from jax.experimental.pallas import tpu as pltpu
from jax.sharding import PartitionSpec as P

HD = 64
ROT = 32
SLOTS = 16


NORM_EPS = 1e-05
MASKED_SCORE = -1e30


def norm_rows(inputs_now, norm_gain, norm_shift):
    centred = inputs_now - jnp.mean(inputs_now, axis=-1, keepdims=True)
    spread = jnp.mean(centred * centred, axis=-1, keepdims=True)
    return centred * lax.rsqrt(spread + NORM_EPS) * norm_gain + norm_shift


def slot_tables(bucket_one, residue_row, group_rows):
    slot_length = jnp.right_shift(jnp.int32(group_rows // 2), bucket_one)
    places = jnp.arange(group_rows, dtype=jnp.int32)
    slot_ids = places // slot_length
    inside = places - slot_ids * slot_length
    match_table = slot_ids[:, None] == jnp.arange(SLOTS, dtype=jnp.int32)[None, :]
    picked = jnp.sum(jnp.where(match_table, residue_row[None, :], 0), axis=1)
    live_rows = jnp.minimum(picked, slot_length)
    return (slot_ids, inside, inside < live_rows)


def rope_tables(inside):
    half_steps = jnp.arange(ROT // 2, dtype=jnp.float32)
    inverse_rates = 10000.0 ** (-2.0 * half_steps / ROT)
    angles = inside.astype(jnp.float32)[:, None] * inverse_rates[None, :]
    return (jnp.cos(angles), jnp.sin(angles))


def rotate(values, cosine_table, sine_table):
    row_count = values.shape[0]
    head_count = values.shape[1]
    paired = values[..., :ROT].reshape(row_count, head_count, ROT // 2, 2)
    even_part = paired[..., 0]
    odd_part = paired[..., 1]
    cosine_now = cosine_table[:, None, :]
    sine_now = sine_table[:, None, :]
    turned = jnp.stack(
        [
            even_part * cosine_now - odd_part * sine_now,
            odd_part * cosine_now + even_part * sine_now,
        ],
        axis=-1,
    )
    return jnp.concatenate([turned.reshape(row_count, head_count, ROT), values[..., ROT:]], axis=-1)


def mask_block(block_start, block_rows, slot_ids):
    query_places = block_start + jnp.arange(block_rows, dtype=jnp.int32)
    query_slots = lax.dynamic_slice_in_dim(slot_ids, block_start, block_rows, 0)
    key_places = jnp.arange(slot_ids.shape[0], dtype=jnp.int32)
    return (query_slots[:, None] == slot_ids[None, :]) & (
        key_places[None, :] <= query_places[:, None]
    )


def over_rows(first_op, second_op):
    return lax.dot_general(
        first_op, second_op, (((0,), (0,)), ((), ())), preferred_element_type=jnp.float32
    )


def against_weight(first_op, second_op):
    return lax.dot_general(
        first_op, second_op, (((1,), (1,)), ((), ())), preferred_element_type=jnp.float32
    )


def on_device(
    residual_in,
    cotangent,
    ln_gain,
    ln_bias,
    w_qkv,
    w_out,
    w_in,
    b_in,
    w_back,
    b_back,
    bucket_ids,
    residue_counts,
):
    model_count = lax.axis_size("mp")
    model_rank = lax.axis_index("mp")
    local_rows = residual_in.shape[0]
    group_rows = local_rows * model_count
    slot_ids, inside, valid_rows = slot_tables(bucket_ids[0], residue_counts[0], group_rows)
    cosine_table, sine_table = rope_tables(inside)
    qkv_all, out_all, in_all, bias_in, back_all = (
        lax.all_gather(w_qkv, "dp", axis=1, tiled=True),
        lax.all_gather(w_out, "dp", axis=1, tiled=True),
        lax.all_gather(w_in, "dp", axis=0, tiled=True),
        lax.all_gather(b_in, "dp", axis=0, tiled=True),
        lax.all_gather(w_back, "dp", axis=1, tiled=True),
    )
    x_local = residual_in.astype(jnp.float32)
    x_group = lax.all_gather(residual_in, "mp", axis=0, tiled=True).astype(jnp.float32)
    normed = norm_rows(x_group, ln_gain, ln_bias).astype(jnp.bfloat16)
    head_width = qkv_all.shape[2]
    head_count = head_width // HD
    score_scale = HD ** (-0.5)

    def project(member_index):
        return jnp.dot(normed, qkv_all[member_index], preferred_element_type=jnp.float32).reshape(
            group_rows, head_count, HD
        )

    queries = rotate(project(0), cosine_table, sine_table).astype(jnp.bfloat16)
    key_rows = rotate(project(1), cosine_table, sine_table).astype(jnp.bfloat16)
    value_rows = project(2).astype(jnp.bfloat16)
    block_rows = min(512, group_rows)
    starts = jnp.arange(group_rows // block_rows, dtype=jnp.int32) * block_rows

    def block_scores(block_start):
        query_block = lax.dynamic_slice_in_dim(queries, block_start, block_rows, 0)
        allowed = mask_block(block_start, block_rows, slot_ids)
        scores = (
            jnp.einsum("qhd,khd->hqk", query_block, key_rows, preferred_element_type=jnp.float32)
            * score_scale
        )
        return (query_block, jnp.where(allowed[None], scores, MASKED_SCORE))

    def forward_block(block_start):
        query_block, scores = block_scores(block_start)
        row_peak = jnp.max(scores, axis=-1, keepdims=True)
        exp_scores = jnp.exp(scores - row_peak)
        row_total = jnp.sum(exp_scores, axis=-1, keepdims=True)
        weights_now = (exp_scores / row_total).astype(jnp.bfloat16)
        attended = jnp.einsum(
            "hqk,khd->qhd", weights_now, value_rows, preferred_element_type=jnp.float32
        )
        return (attended.astype(jnp.bfloat16), (row_peak + jnp.log(row_total))[..., 0])

    attended_blocks, log_totals = lax.map(forward_block, starts)
    mixed_rows = attended_blocks.reshape(group_rows, head_width)
    hidden = jnp.dot(normed, in_all, preferred_element_type=jnp.float32) + bias_in.astype(
        jnp.float32
    )
    gelu_tanh = partial(jax.nn.gelu, approximate=True)
    active_value, gelu_pull = jax.vjp(gelu_tanh, hidden)
    active = active_value.astype(jnp.bfloat16)
    partial_out = jnp.dot(mixed_rows, out_all, preferred_element_type=jnp.float32) + jnp.dot(
        active, back_all, preferred_element_type=jnp.float32
    )
    summed_all = lax.psum(partial_out.astype(jnp.bfloat16), "mp").astype(jnp.float32)
    summed = lax.dynamic_slice_in_dim(summed_all, model_rank * local_rows, local_rows, 0)
    block_out = (x_local + summed + b_back).astype(jnp.bfloat16)
    cot_group = lax.all_gather(cotangent, "mp", axis=0, tiled=True)
    seed_rows = jnp.where(valid_rows[:, None], cot_group, jnp.zeros_like(cot_group))
    qkv_all, out_all, in_all, back_all = (
        lax.all_gather(w_qkv, "dp", axis=1, tiled=True),
        lax.all_gather(w_out, "dp", axis=1, tiled=True),
        lax.all_gather(w_in, "dp", axis=0, tiled=True),
        lax.all_gather(w_back, "dp", axis=1, tiled=True),
    )
    active_grad = against_weight(seed_rows, back_all)
    hidden_grad = gelu_pull(active_grad)[0].astype(jnp.bfloat16)
    grad_in_local = over_rows(normed, hidden_grad)
    grad_bias_in = jnp.sum(hidden_grad.astype(jnp.float32), axis=0)
    grad_back_local = over_rows(active, seed_rows)
    grad_out_local = over_rows(mixed_rows, seed_rows)
    normed_grad = against_weight(hidden_grad, in_all)
    mixed_grad = (
        against_weight(seed_rows, out_all).astype(jnp.bfloat16).reshape(group_rows, head_count, HD)
    )

    def backward_block(carry, inputs_now):
        key_acc, value_acc = carry
        block_start, log_total = inputs_now
        query_block, scores = block_scores(block_start)
        grad_block = lax.dynamic_slice_in_dim(mixed_grad, block_start, block_rows, 0)
        probs = jnp.exp(scores - log_total[..., None])
        probs_low = probs.astype(jnp.bfloat16)
        value_acc = value_acc + jnp.einsum(
            "hqk,qhd->khd", probs_low, grad_block, preferred_element_type=jnp.float32
        )
        probs_grad = jnp.einsum(
            "qhd,khd->hqk", grad_block, value_rows, preferred_element_type=jnp.float32
        )
        score_grad = probs * (probs_grad - jnp.sum(probs * probs_grad, axis=-1, keepdims=True))
        score_low = score_grad.astype(jnp.bfloat16)
        query_grad = (
            jnp.einsum("hqk,khd->qhd", score_low, key_rows, preferred_element_type=jnp.float32)
            * score_scale
        )
        key_acc = (
            key_acc
            + jnp.einsum("hqk,qhd->khd", score_low, query_block, preferred_element_type=jnp.float32)
            * score_scale
        )
        return ((key_acc, value_acc), query_grad)

    empty_heads = jnp.zeros((group_rows, head_count, HD), jnp.float32)
    (key_acc, value_acc), query_blocks = lax.scan(
        backward_block, (empty_heads, empty_heads), (starts, log_totals)
    )
    turn_back = partial(rotate, cosine_table=cosine_table, sine_table=sine_table)
    unturn = jax.vjp(turn_back, empty_heads)[1]
    query_pre_grad = (
        unturn(query_blocks.reshape(group_rows, head_count, HD))[0]
        .astype(jnp.bfloat16)
        .reshape(group_rows, head_width)
    )
    key_pre_grad = unturn(key_acc)[0].astype(jnp.bfloat16).reshape(group_rows, head_width)
    value_grad = value_acc.astype(jnp.bfloat16).reshape(group_rows, head_width)
    grad_qkv_local = jnp.stack(
        [
            over_rows(normed, query_pre_grad),
            over_rows(normed, key_pre_grad),
            over_rows(normed, value_grad),
        ],
        axis=0,
    )
    normed_grad = (
        normed_grad
        + against_weight(query_pre_grad, qkv_all[0])
        + against_weight(key_pre_grad, qkv_all[1])
        + against_weight(value_grad, qkv_all[2])
    )
    share_grad = lax.psum(normed_grad.astype(jnp.bfloat16), "mp").astype(jnp.float32)
    seed_group = seed_rows.astype(jnp.float32)
    norm_pull = jax.vjp(norm_rows, x_group, ln_gain, ln_bias)[1]
    input_part, gain_part, shift_part = norm_pull(share_grad)
    input_group = seed_group + input_part
    grad_input = lax.dynamic_slice_in_dim(
        input_group, model_rank * local_rows, local_rows, 0
    ).astype(jnp.bfloat16)
    back_part = jnp.sum(seed_group, axis=0)
    grad_w_qkv, grad_w_out, grad_w_in, grad_b_in, grad_w_back, gain_rows, shift_rows, back_rows = (
        lax.psum_scatter(
            grad_qkv_local.astype(jnp.bfloat16), "dp", scatter_dimension=1, tiled=True
        ).astype(jnp.float32),
        lax.psum_scatter(
            grad_out_local.astype(jnp.bfloat16), "dp", scatter_dimension=1, tiled=True
        ).astype(jnp.float32),
        lax.psum_scatter(
            grad_in_local.astype(jnp.bfloat16), "dp", scatter_dimension=0, tiled=True
        ).astype(jnp.float32),
        lax.psum_scatter(
            grad_bias_in.astype(jnp.bfloat16), "dp", scatter_dimension=0, tiled=True
        ).astype(jnp.float32),
        lax.psum_scatter(
            grad_back_local.astype(jnp.bfloat16), "dp", scatter_dimension=1, tiled=True
        ).astype(jnp.float32),
        lax.psum_scatter(
            gain_part.astype(jnp.bfloat16), "dp", scatter_dimension=0, tiled=True
        ).astype(jnp.float32),
        lax.psum_scatter(
            shift_part.astype(jnp.bfloat16), "dp", scatter_dimension=0, tiled=True
        ).astype(jnp.float32),
        lax.psum_scatter(
            back_part.astype(jnp.bfloat16), "dp", scatter_dimension=0, tiled=True
        ).astype(jnp.float32),
    )
    piece_width = gain_rows.shape[0] // model_count
    grad_ln_gain = lax.dynamic_slice_in_dim(gain_rows, model_rank * piece_width, piece_width, 0)
    grad_ln_bias = lax.dynamic_slice_in_dim(shift_rows, model_rank * piece_width, piece_width, 0)
    grad_b_back = lax.dynamic_slice_in_dim(back_rows, model_rank * piece_width, piece_width, 0)
    return (
        block_out,
        grad_input,
        grad_ln_gain,
        grad_ln_bias,
        grad_w_qkv,
        grad_w_out,
        grad_w_in,
        grad_b_in,
        grad_w_back,
        grad_b_back,
    )


MESH = pl.DeviceIdType.MESH
NZ = 4
TILE = 256
N_HEADS = TILE // HD
NQ = 4
NJ = 4
NK = NQ + 2 * NJ
VROWS = 56


def fits_quad(mesh):
    return mesh.shape["mp"] == 2 and mesh.shape["dp"] == 4 * NZ


def dot_nn(a, b):
    return lax.dot_general(a, b, (((1,), (0,)), ((), ())), preferred_element_type=jnp.float32)


def dot_nt(a, b):
    return lax.dot_general(a, b, (((1,), (1,)), ((), ())), preferred_element_type=jnp.float32)


def dot_tn(a, b):
    return lax.dot_general(a, b, (((0,), (0,)), ((), ())), preferred_element_type=jnp.float32)


def layer_kernel(
    bucket_ref,
    counts_ref,
    x_ref,
    cot_ref,
    gain_ref,
    bias_ref,
    bback_ref,
    cos_ref,
    sin_ref,
    bin_ref,
    wqkv_ref,
    wot_ref,
    win_ref,
    wbt_ref,
    block_ref,
    gin_ref,
    gqkv_ref,
    got_ref,
    gi_ref,
    gbt_ref,
    lng_ref,
    lnb_ref,
    bbk_ref,
    gbin_ref,
    B,
    W,
    NS,
    CT,
    SN,
    BM,
    QR,
    KR,
    VR,
    R,
    SL,
    XV,
    CV,
    COSV,
    SINV,
    ins,
    OUT,
    DN,
    GP,
    GC,
    RZ,
    FS,
    YS,
    YR,
    XH,
    RSTD,
    EXSa,
    EXSb,
    EYSa,
    EYSb,
    EXRa,
    EXRb,
    EYRa,
    EYRb,
    EXS2a,
    EXS2b,
    EYS2a,
    EYS2b,
    EXR2a,
    EXR2b,
    EYR2a,
    EYR2b,
    V,
    VS,
    VRV,
    loc_sem,
    ays,
    ayr,
    azs,
    azr,
    acs,
    acr,
    gs,
    gr,
    rcs,
    rcr,
    rzs,
    rzr,
    rys,
    ryr,
    exs,
    exr,
    vs,
    vr,
):
    EXS = (EXSa, EXSb)
    EYS = (EYSa, EYSb)
    EXR = (EXRa, EXRb)
    EYR = (EYRa, EYRb)
    EXS2 = (EXS2a, EXS2b)
    EYS2 = (EYS2a, EYS2b)
    EXR2 = (EXR2a, EXR2b)
    EYR2 = (EYR2a, EYR2b)
    f32, bf16 = jnp.float32, jnp.bfloat16
    dp, x = lax.axis_index("dp"), lax.axis_index("mp")
    z = dp // 4
    y = lax.rem(dp // 2, 2)
    c = lax.rem(dp, 2)
    rows = x_ref.shape[0]
    width = x_ref.shape[1]
    dev_x = (dp, 1 - x)
    dev_y = (dp + 2 - 4 * y, x)
    dev_c = (dp + 1 - 2 * c, x)
    dev_r = (lax.rem(dp + 4, 4 * NZ), x)
    dev_l = (lax.rem(dp + 4 * NZ - 4, 4 * NZ), x)
    dev_z = [(lax.rem(dp + 4 * i, 4 * NZ), x) for i in (1, 2, 3)]
    NA, SA = NS.at[0], NS.at[1]
    m_own = 2 * y + x
    m_x = 2 * y + 1 - x
    m_y = 2 - 2 * y + x
    m_d = 3 - m_own

    def rcp(src, dst, ss, rs, dev):
        return pltpu.make_async_remote_copy(
            src_ref=src, dst_ref=dst, send_sem=ss, recv_sem=rs, device_id=dev, device_id_type=MESH
        )

    barrier = pltpu.get_barrier_semaphore()
    peers = [dev_x, dev_y, dev_c] + dev_z
    for peer in peers:
        pl.semaphore_signal(barrier, inc=1, device_id=peer, device_id_type=MESH)

    def wsrc(k, q):
        if k == NK:
            return None
        if k < 3:
            return wqkv_ref.at[k, :, pl.ds(pl.multiple_of(q * TILE, TILE), TILE)]
        if k == 3:
            return wot_ref.at[:, pl.ds(pl.multiple_of(q * TILE, TILE), TILE)]
        ref = win_ref if k % 2 == 0 else wbt_ref
        j = (k - NQ) // 2
        return ref.at[:, pl.ds(pl.multiple_of(q * (NJ * TILE) + j * TILE, TILE), TILE)]

    def wv(k):
        return B if isinstance(k, int) and k == NK else W.at[k]

    def own_copy(k):
        return pltpu.make_async_copy(wsrc(k, y), W.at[k, z, y, c], loc_sem.at[k])

    def y_copy(k):
        if k == NK:
            return rcp(B.at[z, y, c], B.at[z, y, c], ays.at[k], ayr.at[k], dev_y)
        return rcp(wsrc(k, 1 - y), W.at[k, z, y, c], ays.at[k], ayr.at[k], dev_y)

    def y_arrived(k):
        here = wv(k).at[z, 1 - y, c]
        rcp(here, here, ays.at[k], ayr.at[k], dev_y).wait_recv()

    def z_copy(k, way, s, e):
        block = wv(k).at[e, :, c]
        return rcp(
            block, block, azs.at[k, way, s], azr.at[k, way, s], dev_r if way == 0 else dev_l
        )

    def c_copy(k, e):
        block = wv(k).at[e, :, c]
        return rcp(block, block, acs.at[k, e], acr.at[k, e], dev_c)

    def ag_own(k, copied=True):
        if copied:
            pltpu.make_async_copy(
                W.at[k, z, y, c], W.at[k, z, y, c], loc_sem.at[k]
            ).wait()
        y_arrived(k)

        @pl.when(z < NZ - 1)
        def _():
            z_copy(k, 0, 0, z).start()

        @pl.when(z > 0)
        def _():
            z_copy(k, 1, 0, z).start()

        c_copy(k, z).start()

    def ag_step(k, s):
        @pl.when(z - 1 - s >= 0)
        def _():
            e = z - 1 - s
            z_copy(k, 0, s, e).wait_recv()
            if s < NZ - 2:

                @pl.when(z < NZ - 1)
                def _():
                    z_copy(k, 0, s + 1, e).start()

            c_copy(k, e).start()

        @pl.when(z + 1 + s <= NZ - 1)
        def _():
            e = z + 1 + s
            z_copy(k, 1, s, e).wait_recv()
            if s < NZ - 2:

                @pl.when(z > 0)
                def _():
                    z_copy(k, 1, s + 1, e).start()

            c_copy(k, e).start()

    def ag_done(k):
        for e in range(NZ):
            block = wv(k).at[e, :, 1 - c]
            rcp(block, block, acs.at[k, e], acr.at[k, e], dev_c).wait_recv()

    def ag_sent(k, copied=True):
        y_copy(k).wait_send() if isinstance(k, int) else None
        for s in range(NZ - 1):

            @pl.when((z < NZ - 1) & (z - s >= 0))
            def _():
                z_copy(k, 0, s, z - s).wait_send()

            @pl.when((z > 0) & (z + s <= NZ - 1))
            def _():
                z_copy(k, 1, s, z + s).wait_send()

        for e in range(NZ):
            c_copy(k, e).wait_send()

    order = [0, NK] + list(range(1, NK))
    turns = iter([t for t in range(NK + NZ) if not 8 <= t <= 11])

    def ag_turn():
        t = next(turns, None)
        if t is None:
            return
        for n in range(2) if t == 0 else (t + 1,):
            if n <= NK:
                ag_own(order[n], copied=order[n] != NK)
        for s in range(NZ - 1):
            if 0 <= t - 1 - s <= NK:
                ag_step(order[t - 1 - s], s)

    def late_turn(t):
        ag_own(t)
        for s in range(NZ - 1):
            ag_step(t - 2 - s, s)

    P0 = 96
    parts = (pl.ds(0, P0), pl.ds(P0, rows - P0))
    BUF = (NA, SA)

    def g_copy(t, p, way, m):
        block = BUF[t].at[m, parts[p]]
        i = (t * 2 + p) * 3 + way
        dev = (dev_x, dev_y)[way] if way < 2 else (dev_y, dev_x)[p]
        return rcp(block, block, gs.at[i], gr.at[i], dev)

    def g_send(t):
        g_copy(t, 0, 0, m_own).start()
        g_copy(t, 1, 1, m_own).start()
        g_copy(t, 1, 0, m_own).start()
        g_copy(t, 0, 1, m_own).start()

    def g_near(t):
        g_copy(t, 0, 0, m_x).wait_recv()
        g_copy(t, 1, 1, m_y).wait_recv()

    def g_forward(t):
        g_copy(t, 0, 2, m_x).start()
        g_copy(t, 1, 2, m_y).start()

    def g_rest(t):
        g_copy(t, 1, 0, m_x).wait_recv()
        g_copy(t, 0, 1, m_y).wait_recv()

    def g_far(t):
        g_copy(t, 0, 2, m_d).wait_recv()
        g_copy(t, 1, 2, m_d).wait_recv()

    def g_sent(t):
        for p in (0, 1):
            for way in (0, 1):
                g_copy(t, p, way, m_own).wait_send()
        g_copy(t, 0, 2, m_x).wait_send()
        g_copy(t, 1, 2, m_y).wait_send()

    def rs_c(k):
        return rcp(GP.at[k, :, :, 1 - c], GC.at[k], rcs.at[k], rcr.at[k], dev_c)

    def rs_z(k, way, e, slot):
        return rcp(
            GP.at[k, e, :, c],
            RZ.at[k, slot],
            rzs.at[k, e],
            rzr.at[k, slot],
            dev_r if way == 0 else dev_l,
        )

    def rs_begin(k):
        rs_c(k).wait_recv()
        for e in range(NZ):
            GP[k, e, :, c] = (GP[k, e, :, c].astype(f32) + GC[k, e].astype(f32)).astype(bf16)

        @pl.when(z == 0)
        def _():
            for e in range(NZ - 1, 0, -1):
                rs_z(k, 0, e, e).start()

        @pl.when(z == NZ - 1)
        def _():
            for e in range(NZ - 1):
                rs_z(k, 1, e, e if e < NZ - 2 else 4).start()

    def pass_on(k, way, e, slot):
        rs_z(k, way, e, e).wait_recv()
        GP[k, e, :, c] = (GP[k, e, :, c].astype(f32) + RZ[k, e].astype(f32)).astype(bf16)
        rs_z(k, way, e, slot).start()

    def rs_hop1(k):
        @pl.when(z == 1)
        def _():
            pass_on(k, 0, 3, 3)
            pass_on(k, 0, 2, 2)

        @pl.when(z == 2)
        def _():
            pass_on(k, 1, 0, 0)
            pass_on(k, 1, 1, 4)

    def rs_hop2(k):
        @pl.when(z == 2)
        def _():
            pass_on(k, 0, 3, 3)

        @pl.when(z == 1)
        def _():
            pass_on(k, 1, 0, 4)

    def rs_y(k):
        return rcp(YS.at[k], YR.at[k], rys.at[k], ryr.at[k], dev_y)

    def put(k, q, value):
        if k < 3:
            gqkv_ref[k, :, pl.ds(pl.multiple_of(q * TILE, TILE), TILE)] = value
        elif k == 3:
            got_ref[:, pl.ds(pl.multiple_of(q * TILE, TILE), TILE)] = value
        else:
            ref = gi_ref if k % 2 == 0 else gbt_ref
            j = (k - NQ) // 2
            ref[:, pl.ds(pl.multiple_of(q * (NJ * TILE) + j * TILE, TILE), TILE)] = value

    def rs_final(k):
        FS[...] = GP[k, z, :, c].astype(f32)

        @pl.when(z > 0)
        def _():
            rs_z(k, 0, z, z).wait_recv()
            FS[...] += RZ[k, z].astype(f32)

        @pl.when(z < NZ - 1)
        def _():
            rs_z(k, 1, z, 4).wait_recv()
            FS[...] += RZ[k, 4].astype(f32)

        YS[k] = FS[1 - y].astype(bf16)
        rs_y(k).start()
        put(k, y, FS[y])

    def rs_out(k):
        rs_y(k).wait_recv()
        put(k, 1 - y, YR[k].astype(f32))

    rturns = iter(range(NK + 2))
    rorder = [NQ + 1] + [k for k in range(NK) if k != NQ + 1]

    def rs_turn():
        r = next(rturns, None)
        if r is None:
            return
        for s, f in enumerate((rs_hop1, rs_hop2, rs_final)):
            if 0 <= r - s < NK:
                f(rorder[r - s])

    def rs_sent(k):
        rs_c(k).wait_send()
        for e in range(NZ):

            @pl.when(z != e)
            def _():
                rs_z(k, 0, e, e).wait_send()

        rs_y(k).wait_send()

    def e_copy(t, u, i):
        src, dst, dev = (
            (EXS, EXR, dev_x),
            (EYS, EYR, dev_y),
            (EXS2, EXR2, dev_x),
            (EYS2, EYR2, dev_y),
        )[i]
        src, dst = src[u], dst[u]
        return rcp(src.at[t], dst.at[t], exs.at[t, u, i], exr.at[t, u, i], dev)

    wide = (384, 256)
    thin = (2 * 128, 128)

    def cols(u, half):
        if half == 0:
            return pl.ds(u * wide[0], wide[u])
        return pl.ds(sum(wide) + u * thin[0], thin[u])

    def e_first_x(t, u, P):
        for i in range(2):
            EXS[u][t, i] = P[2 * i + 1 - x, :, cols(u, 0)].astype(bf16)
        e_copy(t, u, 0).start()

    def e_first_y(t, u, P):
        for i in range(2):
            EYS[u][t, i] = P[2 - 2 * y + i, :, cols(u, 1)].astype(bf16)
        e_copy(t, u, 1).start()

    def e_first(t, u, P):
        e_first_x(t, u, P)
        e_first_y(t, u, P)

    def e_second(t, u, P):
        e_copy(t, u, 0).wait_recv()
        EYS2[u][t] = (P[m_y, :, cols(u, 0)] + EXR[u][t, 1 - y].astype(f32)).astype(bf16)
        e_copy(t, u, 3).start()
        e_copy(t, u, 1).wait_recv()
        EXS2[u][t] = (P[m_x, :, cols(u, 1)] + EYR[u][t, 1 - x].astype(f32)).astype(bf16)
        e_copy(t, u, 2).start()

    def e_last(t, u, P):
        e_copy(t, u, 3).wait_recv()
        P[m_own, :, cols(u, 0)] += EXR[u][t, y].astype(f32) + EYR2[u][t].astype(f32)
        e_copy(t, u, 2).wait_recv()
        P[m_own, :, cols(u, 1)] += EYR[u][t, x].astype(f32) + EXR2[u][t].astype(f32)

    def e_sent(t):
        for u in range(2):
            for i in range(4):
                e_copy(t, u, i).wait_send()

    inputs = [
        pltpu.make_async_copy(src, dst, ins.at[i])
        for i, (src, dst) in enumerate(
            ((x_ref, XV), (cot_ref, CV), (cos_ref, COSV), (sin_ref, SINV))
        )
    ]
    for copy in inputs:
        copy.start()
    for k in range(NK):
        own_copy(k).start()
    inputs[0].wait()
    xf = XV[...].astype(f32)
    centred = xf - jnp.mean(xf, axis=-1, keepdims=True)
    rstd = lax.rsqrt(jnp.mean(centred * centred, axis=-1, keepdims=True) + NORM_EPS)
    xhat = centred * rstd
    XH[...] = xhat
    RSTD[...] = jnp.broadcast_to(rstd, RSTD.shape)
    NA[m_own] = (xhat * gain_ref[...] + bias_ref[...]).astype(bf16)

    bucket = bucket_ref[0]
    B[z, y, c, 0:8] = jnp.broadcast_to(bin_ref[...].astype(f32), (8, 128)).astype(bf16)
    B[z, y, c, 8:16] = jnp.full((8, 128), bucket.astype(f32), f32).astype(bf16)

    slot = lax.shift_right_logical(jnp.int32(rows), bucket)
    shift_of = (rows.bit_length() - 1) - bucket
    row = x * rows + lax.broadcasted_iota(jnp.int32, (rows, 128), 0)
    slot_of = lax.shift_right_logical(row, jnp.full(row.shape, shift_of, jnp.int32))
    place = row & jnp.full(row.shape, slot - 1, jnp.int32)
    limit = jnp.zeros((rows, 128), jnp.int32)
    for s in range(SLOTS):
        limit = jnp.where(slot_of == s, counts_ref[s], limit)
    valid = jnp.where(place < limit, 1.0, 0.0)[:, 0:1]
    inputs[1].wait()
    seeds = CV[...].astype(f32) * valid
    SA[m_own] = seeds.astype(bf16)
    back_sum = jnp.sum(seeds, axis=0, keepdims=True)
    V[...] = jnp.zeros_like(V)
    for i in range(8):
        V[16 + i : 17 + i, :] = back_sum[:, i * 128 : (i + 1) * 128]
    pl.semaphore_wait(barrier, len(peers))
    for k in order[:6]:
        y_copy(k).start()
    g_send(0)
    g_copy(1, 0, 0, m_own).start()
    g_copy(1, 1, 0, m_own).start()
    for k in order[6:9]:
        y_copy(k).start()
    g_copy(1, 1, 1, m_own).start()
    for k in order[9:]:
        y_copy(k).start()
    g_copy(1, 0, 1, m_own).start()
    ag_turn()
    ag_turn()

    lane = lax.broadcasted_iota(jnp.int32, (rows, TILE), 1)
    even = (lane & 1) == 0

    def table(g):
        brow = B[z, g, c].astype(f32)[8:9, :]
        ba = jnp.broadcast_to(brow, (rows, 128))

        def pick(ref):
            full = ref[...]
            out = full
            for b in range(1, 4):
                n = rows >> b
                out = jnp.where(ba == float(b), jnp.concatenate([full[:n]] * (1 << b), axis=0), out)
            return out

        cg, sg = pick(COSV), pick(SINV)
        CT[g] = jnp.concatenate([cg, cg], axis=1)
        SN[g] = jnp.concatenate([sg, sg], axis=1)
        size = jnp.full((rows, 128), rows, jnp.int32)
        for b in range(1, 4):
            size = jnp.where(ba == float(b), rows >> b, size)
        size = jnp.concatenate([size, size], axis=1)
        qi = lax.broadcasted_iota(jnp.int32, (rows, rows), 0)
        ki = lax.broadcasted_iota(jnp.int32, (rows, rows), 1)
        BM[g] = jnp.where((ki <= qi) & ((qi ^ ki) < size), 0.0, MASKED_SCORE)

    def tables():
        for g in range(2):
            table(g)

    def turn(v, g, sign):
        other = jnp.where(even, -pltpu.roll(v, TILE - 1, 1), pltpu.roll(v, 1, 1))
        return v * CT[g] + (sign * other) * SN[g]

    def weight(k):
        return W[k].reshape(width, TILE)

    scale = HD ** (-0.5)

    def project(m):
        g = m // 2
        nb = NA[m]
        QR[m] = turn(dot_nn(nb, weight(0)), g, 1.0).astype(bf16)
        KR[m] = turn(dot_nn(nb, weight(1)), g, 1.0).astype(bf16)
        VR[m] = dot_nn(nb, weight(2)).astype(bf16)

    def attend(m):
        g = m // 2
        q, kk, v = QR[m], KR[m], VR[m]
        da = dot_nn(SA[m], weight(3)).astype(bf16)
        zero = jnp.zeros((rows, TILE), bf16)
        ps, ss, qs, ks, vs_, ds = [], [], [], [], [], []
        for h in range(N_HEADS):
            mine = (lane // HD) == h
            qh, kh, vh, dh = (jnp.where(mine, t, zero) for t in (q, kk, v, da))
            s = dot_nt(qh, kk) * scale + BM[g]
            e = jnp.exp(s - jnp.max(s, axis=-1, keepdims=True))
            p = e * (1.0 / jnp.sum(e, axis=-1, keepdims=True))
            pg = dot_nt(dh, v)
            sg = p * (pg - jnp.sum(p * pg, axis=-1, keepdims=True))
            for held, t in ((ps, p), (ss, sg), (qs, qh), (ks, kh), (vs_, vh), (ds, dh)):
                held.append(t.astype(bf16))
        wide_p, wide_s = jnp.concatenate(ps, axis=1), jnp.concatenate(ss, axis=1)
        att = dot_nn(wide_p, jnp.concatenate(vs_, axis=0))
        dq = dot_nn(wide_s, jnp.concatenate(ks, axis=0))
        dk = dot_tn(jnp.concatenate(ss, axis=0), jnp.concatenate(qs, axis=0))
        dv = dot_tn(jnp.concatenate(ps, axis=0), jnp.concatenate(ds, axis=0))
        at = att.astype(bf16)
        dqb = turn(dq * scale, g, -1.0).astype(bf16)
        dkb = turn(dk * scale, g, -1.0).astype(bf16)
        dvb = dv.astype(bf16)
        rs = pl.ds(pl.multiple_of(m * rows, rows), rows)
        R[3, rs, :] = at
        R[0, rs, :] = dqb
        R[1, rs, :] = dkb
        R[2, rs, :] = dvb
        OUT[m] = dot_nt(at, weight(3))
        DN[m] = dot_nt(dqb, weight(0)) + dot_nt(dkb, weight(1)) + dot_nt(dvb, weight(2))

    def grad_of(k, left):
        total = dot_tn(NS[left].reshape(4 * rows, width), R[k])
        GP[k] = total.astype(bf16).reshape(NZ, 2, 2, 64, TILE)
        rs_c(k).start()

    def slice_of(j):
        return NQ + 2 * j, NQ + 1 + 2 * j

    def all_rows(ref):
        return ref[...].reshape(4 * rows, width)

    def feed(j):
        ki, kb = slice_of(j)
        b0 = B[2 * y + lax.div(j, 2), lax.rem(j, 2), 0].astype(f32)[0:1, :]
        b1 = B[2 * y + lax.div(j, 2), lax.rem(j, 2), 1].astype(f32)[0:1, :]
        u = dot_nn(all_rows(NA), weight(ki)) + jnp.concatenate([b0, b1], axis=1)
        u2 = u * u
        k0 = float(np.sqrt(2.0 / np.pi))
        t = jnp.tanh(k0 * u * (1.0 + 0.044715 * u2))
        R[kb] = (0.5 * u * (1.0 + t)).astype(bf16)
        SL[...] = 0.5 * (1.0 + t) + (0.5 * k0) * u * (1.0 - t * t) * (1.0 + 0.134145 * u2)

    def feed_back(j):
        ki, kb = slice_of(j)
        hg = (dot_nn(all_rows(SA), weight(kb)) * SL[...]).astype(bf16)
        R[ki] = hg
        OUT[...] += dot_nt(R[kb], weight(kb)).reshape(4, rows, width)
        DN[...] += dot_nt(hg, weight(ki)).reshape(4, rows, width)
        at = 24 + x * 16 + y * 8 + 2 * j
        total = jnp.sum(hg.astype(f32), axis=0, keepdims=True)
        V[pl.ds(at, 1), :] = total[:, :128]
        V[pl.ds(at + 1, 1), :] = total[:, 128:]

    def feed_grads(j):
        lax.fori_loop(0, 2, lambda i, _: (grad_of(NQ + 2 * j + i, i), 0)[1], 0)

    def v_copy(i, dev):
        return rcp(VS.at[min(i, 3)], VRV.at[i], vs.at[i], vr.at[i], dev)

    v_devs = (dev_c, dev_x, dev_y)

    def v_step(i):
        v_copy(i, v_devs[i]).wait_recv()
        VS[i + 1] = VS[i] + VRV[i]
        if i < 2:
            v_copy(i + 1, v_devs[i + 1]).start()
        else:
            for n, dev in enumerate(dev_z):
                v_copy(3 + n, dev).start()

    def arrived(*chunks):
        for k in chunks:
            ag_done(k)

    ag_turn()
    inputs[2].wait()
    inputs[3].wait()
    tables()
    ag_turn()
    ag_turn()
    ag_turn()
    g_near(0)
    g_forward(0)
    ag_turn()
    arrived(0, NK, 1, 2)
    g_rest(0)
    def near(i):
        ix, iy = lax.rem(i, 2), lax.div(i, 2)
        return 2 * (y + iy - 2 * y * iy) + x + ix - 2 * x * ix

    lax.fori_loop(0, 3, lambda i, _: (project(near(i)), 0)[1], 0)
    ag_turn()
    arrived(3)

    def rows_turn(i, _):
        @pl.when(i == 1)
        def _():
            g_near(1)
            g_forward(1)
            g_rest(1)

        @pl.when(i == 3)
        def _():
            g_far(1)
            grad_of(NQ + 1, 1)
            project(m_d)
            rs_begin(NQ + 1)

        attend(near(i))

        @pl.when(i == 2)
        def _():
            g_far(0)
            arrived(NQ)
            feed(0)

        @pl.when(i < 3)
        def _():
            late_turn(8 + i)

        return 0

    lax.fori_loop(0, 4, rows_turn, 0)

    def head_grads(k, _):
        grad_of(k, lax.div(k, 3))

        @pl.when(k == 1)
        def _():
            late_turn(11)

        @pl.when(k > 0)
        def _():
            rs_begin(k - 1)

        return 0

    lax.fori_loop(0, NQ, head_grads, 0)
    ag_turn()

    def slices(j, _):
        @pl.when(j > 0)
        def _():
            arrived(NQ + 2 * j)
            feed(j)

        arrived(NQ + 1 + 2 * j)
        feed_back(j)

        @pl.when(j == 0)
        def _():
            rs_begin(3)
            ag_turn()
            rs_turn()

        @pl.when(j == 1)
        def _():
            ag_turn()
            rs_turn()

        @pl.when(j == 2)
        def _():
            ag_turn()
            rs_turn()

        return 0

    lax.fori_loop(0, NJ, slices, 0)

    for u in range(2):
        e_first(1, u, DN)
    grad_of(NQ, 0)
    rs_turn()
    rs_begin(NQ)
    feed_grads(1)
    rs_begin(6)
    rs_begin(7)
    rs_turn()
    feed_grads(2)
    rs_begin(8)
    rs_begin(9)
    rs_turn()
    e_second(1, 0, DN)
    feed_grads(3)
    rs_begin(10)
    rs_begin(11)
    rs_turn()
    e_second(1, 1, DN)
    e_first(0, 0, OUT)
    e_first_y(0, 1, OUT)
    rs_turn()
    rs_turn()
    for u in range(2):
        e_last(1, u, DN)
    dn = DN[m_own]
    xhat = XH[...]
    gsum = jnp.sum(dn * xhat, axis=0, keepdims=True)
    bsum = jnp.sum(dn, axis=0, keepdims=True)
    for i in range(8):
        V[i : i + 1, :] = gsum[:, i * 128 : (i + 1) * 128]
        V[8 + i : 9 + i, :] = bsum[:, i * 128 : (i + 1) * 128]
    VS[0] = V[...]
    v_copy(0, dev_c).start()
    e = dn * gain_ref[...]
    me = jnp.mean(e, axis=-1, keepdims=True)
    mex = jnp.mean(e * xhat, axis=-1, keepdims=True)
    gin_ref[...] = (SA[m_own].astype(f32) + RSTD[:, 0:1] * (e - me - xhat * mex)).astype(bf16)
    v_step(0)
    rs_turn()
    e_first_x(0, 1, OUT)
    rs_turn()
    v_step(1)
    e_second(0, 0, OUT)
    rs_turn()
    v_step(2)
    rs_turn()
    e_second(0, 1, OUT)
    for k in rorder[:9]:
        rs_out(k)
    rs_turn()
    rs_out(rorder[9])
    for k in rorder[10:]:
        rs_out(k)
    for i in range(3):
        v_copy(3 + i, dev_z[i]).wait_recv()
    V[...] = VS[3] + VRV[3] + VRV[4] + VRV[5]
    index = 2 * dp + x
    lane4 = lax.rem(index, 4)
    for base, ref in ((0, lng_ref), (8, lnb_ref), (16, bbk_ref)):
        line = V[pl.ds(base + index // 4, 1), :]
        out = line[:, 0:32]
        for n in range(1, 4):
            out = jnp.where(lane4 == n, line[:, 32 * n : 32 * n + 32], out)
        ref[...] = out
    gbin_ref[...] = V[pl.ds(24 + 16 * x + dp, 1), :]
    for u in range(2):
        e_last(0, u, OUT)
    block_ref[...] = (XV[...].astype(f32) + OUT[m_own] + bback_ref[...]).astype(bf16)

    def later(f):
        lax.fori_loop(0, NK, lambda k, _: (f(k), 0)[1], 0)

    for k in range(NK + 1):
        ag_sent(k)
    for t in range(2):
        g_sent(t)
        e_sent(t)
    later(rs_sent)
    for i, dev in enumerate([dev_c, dev_x, dev_y] + dev_z):
        v_copy(i, dev).wait_send()


def write_kernel(*refs):
    srcs, dsts, sems = refs[:10], refs[10:20], refs[20]
    copies = [pltpu.make_async_copy(a, b, sems.at[i]) for i, (a, b) in enumerate(zip(srcs, dsts))]
    for copy in copies:
        copy.start()
    for copy in copies:
        copy.wait()


def rope_constants(rows):
    half = np.arange(ROT // 2, dtype=np.float32)
    rates = (10000.0 ** (-2.0 * half / ROT)).astype(np.float32)
    angle = np.arange(rows, dtype=np.float32)[:, None] * rates[None, :]
    angle = np.repeat(angle, 2, axis=1)
    cos = np.concatenate([np.cos(angle), np.ones((rows, HD - ROT))], axis=1)
    sin = np.concatenate([np.sin(angle), np.zeros((rows, HD - ROT))], axis=1)
    two = lambda t: np.concatenate([t, t], axis=1).astype(np.float32)
    return two(cos), two(sin)


def on_quad(
    residual_in,
    cotangent,
    ln_gain,
    ln_bias,
    w_qkv,
    w_out,
    w_in,
    b_in,
    w_back,
    b_back,
    bucket_ids,
    residue_counts,
):
    rows, width = residual_in.shape
    cos, sin = rope_constants(rows)
    f32, bf16 = jnp.float32, jnp.bfloat16
    vm = pl.BlockSpec(memory_space=pltpu.VMEM)
    sm = pl.BlockSpec(memory_space=pltpu.SMEM)
    anyspace = pl.BlockSpec(memory_space=pl.ANY)
    shard = width // (4 * NZ)
    sem = pltpu.SemaphoreType.DMA
    shapes = (
        jax.ShapeDtypeStruct((rows, width), bf16),
        jax.ShapeDtypeStruct((rows, width), bf16),
        jax.ShapeDtypeStruct((3, shard, 2 * TILE), f32),
        jax.ShapeDtypeStruct((shard, 2 * TILE), f32),
        jax.ShapeDtypeStruct((shard, 2 * NJ * TILE), f32),
        jax.ShapeDtypeStruct((shard, 2 * NJ * TILE), f32),
        jax.ShapeDtypeStruct((1, 32), f32),
        jax.ShapeDtypeStruct((1, 32), f32),
        jax.ShapeDtypeStruct((1, 32), f32),
        jax.ShapeDtypeStruct((1, 128), f32),
    )
    held = pl.pallas_call(
        layer_kernel,
        out_shape=tuple(pltpu.VMEM(v.shape, v.dtype) for v in shapes),
        in_specs=[sm, sm, anyspace, anyspace] + [vm] * 3 + [anyspace] * 2 + [vm] + [anyspace] * 4,
        out_specs=(vm,) * 10,
        scratch_shapes=[
            pltpu.VMEM((NZ, 2, 2, 16, 128), bf16),
            pltpu.VMEM((NK, NZ, 2, 2, shard, TILE), bf16),
            pltpu.VMEM((2, 4, rows, width), bf16),
            pltpu.VMEM((2, rows, TILE), f32),
            pltpu.VMEM((2, rows, TILE), f32),
            pltpu.VMEM((2, rows, rows), f32),
            pltpu.VMEM((4, rows, TILE), bf16),
            pltpu.VMEM((4, rows, TILE), bf16),
            pltpu.VMEM((4, rows, TILE), bf16),
            pltpu.VMEM((NK, 4 * rows, TILE), bf16),
            pltpu.VMEM((4 * rows, TILE), f32),
            pltpu.VMEM((rows, width), bf16),
            pltpu.VMEM((rows, width), bf16),
            pltpu.VMEM((rows, 128), f32),
            pltpu.VMEM((rows, 128), f32),
            sem((4,)),
            pltpu.VMEM((4, rows, width), f32),
            pltpu.VMEM((4, rows, width), f32),
            pltpu.VMEM((NK, NZ, 2, 2, shard, TILE), bf16),
            pltpu.VMEM((NK, NZ, 2, shard, TILE), bf16),
            pltpu.VMEM((NK, 5, 2, shard, TILE), bf16),
            pltpu.VMEM((2, shard, TILE), f32),
            pltpu.VMEM((NK, shard, TILE), bf16),
            pltpu.VMEM((NK, shard, TILE), bf16),
            pltpu.VMEM((rows, width), f32),
            pltpu.VMEM((rows, 128), f32),
            pltpu.VMEM((2, 2, rows, 384), bf16),
            pltpu.VMEM((2, 2, rows, 256), bf16),
            pltpu.VMEM((2, 2, rows, 256), bf16),
            pltpu.VMEM((2, 2, rows, 128), bf16),
            pltpu.VMEM((2, 2, rows, 384), bf16),
            pltpu.VMEM((2, 2, rows, 256), bf16),
            pltpu.VMEM((2, 2, rows, 256), bf16),
            pltpu.VMEM((2, 2, rows, 128), bf16),
            pltpu.VMEM((2, rows, 256), bf16),
            pltpu.VMEM((2, rows, 128), bf16),
            pltpu.VMEM((2, rows, 384), bf16),
            pltpu.VMEM((2, rows, 256), bf16),
            pltpu.VMEM((2, rows, 256), bf16),
            pltpu.VMEM((2, rows, 128), bf16),
            pltpu.VMEM((2, rows, 384), bf16),
            pltpu.VMEM((2, rows, 256), bf16),
            pltpu.VMEM((VROWS, 128), f32),
            pltpu.VMEM((4, VROWS, 128), f32),
            pltpu.VMEM((6, VROWS, 128), f32),
            sem((NK,)),
            sem((NK + 1,)),
            sem((NK + 1,)),
            sem((NK + 1, 2, 3)),
            sem((NK + 1, 2, 3)),
            sem((NK + 1, NZ)),
            sem((NK + 1, NZ)),
            sem((12,)),
            sem((12,)),
            sem((NK,)),
            sem((NK,)),
            sem((NK, NZ)),
            sem((NK, 5)),
            sem((NK,)),
            sem((NK,)),
            sem((2, 2, 4)),
            sem((2, 2, 4)),
            sem((6,)),
            sem((6,)),
        ],
        compiler_params=pltpu.CompilerParams(
            collective_id=0, has_side_effects=True, vmem_limit_bytes=58 << 20
        ),
        cost_estimate=pl.CostEstimate(
            flops=20 * 2**30, bytes_accessed=8 * 2**20, transcendentals=2**21
        ),
    )(
        bucket_ids,
        residue_counts.reshape(SLOTS),
        residual_in,
        cotangent,
        ln_gain.reshape(1, width),
        ln_bias.reshape(1, width),
        b_back.reshape(1, width),
        jnp.asarray(cos),
        jnp.asarray(sin),
        b_in.reshape(1, 128),
        w_qkv,
        w_out.T,
        w_in,
        w_back.T,
    )
    held = [pltpu.with_memory_space_constraint(v, pltpu.VMEM) for v in held]
    outs = pl.pallas_call(
        write_kernel,
        out_shape=shapes,
        in_specs=[vm] * 10,
        out_specs=(anyspace,) * 10,
        scratch_shapes=[sem((10,))],
    )(*held)
    block_out, grad_input, grad_w_qkv, gwo, grad_w_in, gwb, lng, lnb, bbk, gbin = outs
    return (
        block_out,
        grad_input,
        lng.reshape(32),
        lnb.reshape(32),
        grad_w_qkv,
        gwo.T,
        grad_w_in,
        gbin.reshape(128),
        gwb.T,
        bbk.reshape(32),
    )


def solution(mesh):
    placed = (
        P(("dp", "mp"), None),
        P(("dp", "mp"), None),
        P(),
        P(),
        P(None, "dp", "mp"),
        P("mp", "dp"),
        P("dp", "mp"),
        P(("mp", "dp")),
        P("mp", "dp"),
        P(),
        P("dp"),
        P("dp", None),
    )
    return jax.shard_map(
        on_quad if fits_quad(mesh) else on_device,
        mesh=mesh,
        in_specs=placed,
        out_specs=(
            P(("dp", "mp"), None),
            P(("dp", "mp"), None),
            P(("dp", "mp")),
            P(("dp", "mp")),
            P(None, "dp", "mp"),
            P("mp", "dp"),
            P("dp", "mp"),
            P(("mp", "dp")),
            P("mp", "dp"),
            P(("dp", "mp")),
        ),
        check_vma=False,
    )
```
